32 devices in a mesh: slab: 8 (over z, y), strip: 4 (over x, core).
Axes of the slice: x: 2, y: 2, z: 4, core: 2. Of those that a mesh axis runs over, the one named last changes fastest.
Arguments:
- colors: bfloat16 [8, 4, 16, 32, 128], P('slab', 'strip'), may hold values from -6 to 6
- transmit: bfloat16 [8, 4, 16, 128], P('slab', 'strip'), may hold values from 0.099609375 to 1
- pair_counts: int32 [4, 8, 8], P('strip'), may hold values from 0 to 2, as said below
- slot_block: int32 [4, 8, 16], P('strip'), may hold values from 0 to 1023, as said below
- assign: int32 [4, 1024], P('strip'), may hold values from 0 to 1023, as said below
- depth_rank: int32 [8], replicated, may hold values from 0 to 7, each once
- w_in: bfloat16 [256, 32], replicated, may hold values from -1 to 1
- trans_weight: bfloat16 [256], replicated, may hold values from -6 to 6
- w_mid: bfloat16 [2, 256, 256], replicated, may hold values from -0.375 to 0.375
- w_out: bfloat16 [4, 256], replicated, may hold values from -0.375 to 0.375
Outputs:
- display: bfloat16 [8, 4, 128, 4, 128], P('slab', None, 'strip')
The draws below stay inside these ranges and needn't reach their ends.
Inputs may be any that keep to these rules, and one draw needn't show every extreme that they name: pair_counts[t, s, c] counts the span blocks renderer s of strip t sends to compositor c; in every strip one compositor gets 2 from every renderer. `slot_block`: the live slots of renderer s come first, grouped by compositor in increasing order, pair_counts[t, s, c] of them for compositor c, naming distinct blocks b with assign[t, b] // 128 = c; other slots are ignored. Each strip's row is a permutation: block b goes to compositor assign[t, b] // 128 at local position assign[t, b] % 128. `depth_rank`: a permutation.
All inputs are finite; a program needn't handle non-finite values.
Results may differ from the reference program's by a relative error of at most 0.0068.
Values may be sent and summed in bfloat16 or wider, within the bound.
No kernel may reach another device: no remote copies, remote signals or barrier semaphores. Data moves between devices by JAX's collectives and lax.ppermute only.
A program may use at most 128 MiB of HBM per device.

```python
import jax
import jax.numpy as jnp
from jax import lax

F = 32
H = 256
OUT = 4
SPAN = 128
MID = 2
MOST = 2
LB = 128
SLOTS = 16
NBLK = 1024
N_SLAB = 8
N_STRIP = 4


def layout_tables(key):
    assign_key = jax.random.fold_in(key, 101)
    assign_rows = jax.vmap(lambda sub_key: jax.random.permutation(sub_key, NBLK))(jax.random.split(assign_key, N_STRIP)).astype(jnp.int32)
    highest = jax.random.randint(jax.random.fold_in(key, 102), (N_STRIP, 1, N_SLAB), 1, MOST + 1)
    lowest = highest // 2
    spread = jax.random.randint(jax.random.fold_in(key, 103), (N_STRIP, N_SLAB, N_SLAB), 0, 1 << 20)
    counts = lowest + spread % (highest - lowest + 1)
    full_column = jax.random.randint(jax.random.fold_in(key, 104), (N_STRIP, 1, 1), 0, N_SLAB)
    column_ids = jnp.arange(N_SLAB)[None, None, :]
    counts = jnp.where(column_ids == full_column, MOST, counts).astype(jnp.int32)
    return (assign_rows, counts)


def draw_pair_counts(key, part):
    assign_rows, counts = layout_tables(key)
    return counts


def draw_assign(key, part):
    assign_rows, counts = layout_tables(key)
    return assign_rows


def draw_slot_block(key, part):
    assign_rows, counts = layout_tables(key)
    key = jax.random.fold_in(key, 7)
    inverse = jax.vmap(lambda row: jnp.zeros((NBLK,), jnp.int32).at[row].set(jnp.arange(NBLK, dtype=jnp.int32)))(assign_rows)
    start_pos = jax.random.randint(jax.random.fold_in(key, 1), (N_STRIP, N_SLAB, N_SLAB, 1), 0, LB)
    step_sizes = jax.random.randint(jax.random.fold_in(key, 2), (N_STRIP, N_SLAB, N_SLAB, MOST), 1, LB // MOST + 1)
    step_sizes = step_sizes.at[..., 0].set(0)
    local_pos = (start_pos + jnp.cumsum(step_sizes, axis=-1)) % LB
    position = jnp.arange(N_SLAB)[None, None, :, None] * LB + local_pos
    blocks = jax.vmap(lambda inverse_row, position_rows: inverse_row[position_rows])(inverse, position)
    offsets = jnp.cumsum(counts, axis=-1) - counts
    slot_rank = jnp.arange(MOST)[None, None, None, :]
    target = jnp.where(slot_rank < counts[..., None], offsets[..., None] + slot_rank, SLOTS)
    filler = jax.random.randint(jax.random.fold_in(key, 3), (N_STRIP, N_SLAB, SLOTS), 0, NBLK)
    strip_ids = jnp.arange(N_STRIP)[:, None, None, None]
    slab_ids = jnp.arange(N_SLAB)[None, :, None, None]
    return filler.at[strip_ids, slab_ids, target].set(blocks, mode='drop').astype(jnp.int32)


def steps_of(own_key, extent, pieces, low, largest):
    def one(axis_at, shards_of):
        steps = jax.random.uniform(jax.random.fold_in(jax.random.fold_in(own_key, 6), axis_at), (shards_of,), jnp.float32, low / len(pieces), largest / len(pieces))
        return jnp.repeat(jnp.exp(steps), extent[axis_at] // shards_of).reshape((-1,) + (1,) * (len(extent) - axis_at - 1))

    factor_of = one(*pieces[0])
    for cut in pieces[1:]:
        factor_of = factor_of * one(*cut)
    return factor_of


def centred(stream_key, extent, scale, bound, cuts=(), held_as=jnp.bfloat16):
    drawn = jax.random.normal(stream_key, extent, jnp.float32) * scale
    if len(cuts) > 0:
        drawn = steps_of(stream_key, extent, cuts, -0.22, 0.18) * drawn
    return jnp.clip(drawn, min=-bound, max=bound).astype(held_as)


def setup_inputs(seed: int = 0) -> dict:
    key_of = jax.random.split(jax.random.key(seed), 11)
    colors = centred(key_of[0], (N_SLAB, N_STRIP, SLOTS, F, SPAN), 1.0, 6.0, ((0, 8), (1, 4)))
    transmit = jnp.clip(0.099609375 + 0.9003906 * jax.random.uniform(key_of[1], (N_SLAB, N_STRIP, SLOTS, SPAN), jnp.float32) ** steps_of(key_of[1], (N_SLAB, N_STRIP, SLOTS, SPAN), ((0, 8), (1, 4)), -0.2, 0.2), 0.099609375, 1.0).astype(jnp.bfloat16)
    pair_counts = draw_pair_counts(jax.random.fold_in(key_of[10], 71), 0)
    slot_block = draw_slot_block(jax.random.fold_in(key_of[10], 71), 0)
    assign = draw_assign(jax.random.fold_in(key_of[10], 71), 0)
    depth_rank = jax.random.permutation(key_of[5], N_SLAB).astype(jnp.int32)
    w_in = centred(key_of[6], (H, F), F ** -0.5, 1.0)
    trans_weight = centred(key_of[7], (H,), 1.0, 6.0)
    w_mid = centred(key_of[8], (MID, H, H), H ** -0.5, 0.375)
    w_out = centred(key_of[9], (OUT, H), H ** -0.5, 0.375)
    return {"colors": colors, "transmit": transmit, "pair_counts": pair_counts, "slot_block": slot_block, "assign": assign, "depth_rank": depth_rank, "w_in": w_in, "trans_weight": trans_weight, "w_mid": w_mid, "w_out": w_out}


def shade_blocks(blend_color, trans_field, w_in, trans_weight, w_mid, w_out):
    summed = jnp.einsum('hf,lfp->lhp', w_in.astype(jnp.float32), blend_color.astype(jnp.float32))
    summed = summed + trans_weight.astype(jnp.float32)[None, :, None] * trans_field[:, None, :]
    hidden = jax.nn.silu(summed).astype(jnp.bfloat16)
    for layer_index in range(MID):
        hidden = jax.nn.silu(jnp.einsum('hg,lgp->lhp', w_mid[layer_index].astype(jnp.float32), hidden.astype(jnp.float32))).astype(jnp.bfloat16)
    return jnp.einsum('oh,lhp->lop', w_out.astype(jnp.float32), hidden.astype(jnp.float32)).astype(jnp.bfloat16)


def composite_strip(colors_strip, trans_strip, counts_strip, blocks_strip, assign_strip, depth_order):
    slot_range = jnp.arange(SLOTS, dtype=jnp.int32)

    def absorb(carry, slab_index):
        color_sum, log_sum = carry
        live_total = jnp.sum(counts_strip[slab_index])
        live_slot = slot_range < live_total
        where_at = assign_strip[blocks_strip[slab_index]]
        front_share = jnp.where(live_slot[:, None], jnp.exp(log_sum[where_at]), 0.0)
        color_sum = color_sum.at[where_at].add(front_share[:, None, :] * colors_strip[slab_index].astype(jnp.float32))
        log_trans = jnp.where(live_slot[:, None], jnp.log(trans_strip[slab_index].astype(jnp.float32)), 0.0)
        log_sum = log_sum.at[where_at].add(log_trans)
        return (color_sum, log_sum), None

    start_state = (jnp.zeros((NBLK, F, SPAN), jnp.float32), jnp.zeros((NBLK, SPAN), jnp.float32))
    (color_sum, log_sum), _ = lax.scan(absorb, start_state, depth_order)
    return color_sum.astype(jnp.bfloat16), jnp.exp(log_sum)


def reference(colors, transmit, pair_counts, slot_block, assign, depth_rank, w_in, trans_weight, w_mid, w_out):
    depth_order = jnp.zeros((N_SLAB,), jnp.int32).at[depth_rank].set(jnp.arange(N_SLAB, dtype=jnp.int32))
    shaded_strips = []
    for strip_index in range(N_STRIP):
        blend_color, trans_field = composite_strip(colors[:, strip_index], transmit[:, strip_index], pair_counts[strip_index], slot_block[strip_index], assign[strip_index], depth_order)

        def shade_one(compositor_pair):
            return shade_blocks(compositor_pair[0], compositor_pair[1], w_in, trans_weight, w_mid, w_out)

        shaded = lax.map(shade_one, (blend_color.reshape(N_SLAB, LB, F, SPAN), trans_field.reshape(N_SLAB, LB, SPAN)))
        shaded_strips.append(shaded)
    return jnp.stack(shaded_strips, axis=1)
```

```python
import functools

import jax
import jax.numpy as jnp
from jax import lax
from jax.experimental import pallas as pl
from jax.experimental.pallas import tpu as pltpu
from jax.sharding import PartitionSpec as P

MOST = 2
LB = 128


EXACT_PRECISION = lax.Precision.HIGHEST


def shade_blocks(blend_color, trans_field, w_in, trans_weight, w_mid, w_out):
    summed = jnp.einsum("hf,lfp->lhp", w_in, blend_color, preferred_element_type=jnp.float32)
    summed = summed + trans_weight.astype(jnp.float32)[None, :, None] * trans_field[:, None, :]
    hidden = jax.nn.silu(summed).astype(jnp.bfloat16)
    for layer_index in range(w_mid.shape[0]):
        hidden = jax.nn.silu(
            jnp.einsum(
                "hg,lgp->lhp", w_mid[layer_index], hidden, preferred_element_type=jnp.float32
            )
        ).astype(jnp.bfloat16)
    return jnp.einsum("oh,lhp->lop", w_out, hidden, preferred_element_type=jnp.float32).astype(
        jnp.bfloat16
    )


def dense_device(
    colors, transmit, pair_counts, slot_block, assign, depth_rank, w_in, trans_weight, w_mid, w_out
):
    myself = lax.axis_index("slab")
    counts = pair_counts[0]
    blocks_all = slot_block[0]
    assign_row = assign[0]
    offsets = jnp.cumsum(counts, axis=1) - counts
    slot_rank = jnp.arange(MOST, dtype=jnp.int32)
    my_counts = lax.dynamic_index_in_dim(counts, myself, 0, keepdims=False)
    my_offsets = lax.dynamic_index_in_dim(offsets, myself, 0, keepdims=False)
    send_slots = jnp.where(
        slot_rank[None, :] < my_counts[:, None], my_offsets[:, None] + slot_rank[None, :], 0
    )
    send_color = colors[0, 0][send_slots]
    send_trans = transmit[0, 0][send_slots][:, :, None, :]
    incoming = lax.dynamic_index_in_dim(counts, myself, 1, keepdims=False)
    in_offsets = lax.dynamic_index_in_dim(offsets, myself, 1, keepdims=False)
    live_slot = slot_rank[None, :] < incoming[:, None]
    recv_slots = jnp.where(live_slot, in_offsets[:, None] + slot_rank[None, :], 0)
    recv_blocks = jnp.take_along_axis(blocks_all, recv_slots, axis=1)
    local_pos = assign_row[recv_blocks] - myself * LB
    live_flat = live_slot.reshape(-1)
    local_flat = jnp.where(live_flat, local_pos.reshape(-1), -1)
    depth_flat = jnp.repeat(depth_rank, MOST)
    ahead_table = (
        (local_flat[:, None] == local_flat[None, :])
        & (depth_flat[None, :] < depth_flat[:, None])
        & live_flat[None, :]
    )
    ahead_table = ahead_table.astype(jnp.float32)
    owner_table = (jnp.arange(LB, dtype=jnp.int32)[:, None] == local_flat[None, :]).astype(
        jnp.float32
    )
    got_color = lax.all_to_all(send_color, "slab", split_axis=0, concat_axis=0, tiled=True)
    got_trans = lax.all_to_all(send_trans, "slab", split_axis=0, concat_axis=0, tiled=True)
    pixel_count = got_color.shape[3]
    item_count = got_color.shape[0] * got_color.shape[1]
    log_trans = jnp.log(got_trans.reshape(item_count, pixel_count).astype(jnp.float32))
    log_trans = jnp.where(live_flat[:, None], log_trans, 0.0)
    front_log = jnp.dot(ahead_table, log_trans, precision=EXACT_PRECISION)
    front_share = jnp.where(live_flat[:, None], jnp.exp(front_log), 0.0)
    weighted = front_share[:, None, :] * got_color.reshape(item_count, -1, pixel_count).astype(
        jnp.float32
    )
    blend_sum = jnp.dot(owner_table, weighted.reshape(item_count, -1), precision=EXACT_PRECISION)
    blend_color = blend_sum.reshape(LB, -1, pixel_count).astype(jnp.bfloat16)
    trans_field = jnp.exp(jnp.dot(owner_table, log_trans, precision=EXACT_PRECISION))
    shaded = shade_blocks(blend_color, trans_field, w_in, trans_weight, w_mid, w_out)
    display_tiles = lax.all_to_all(shaded[None], "strip", split_axis=1, concat_axis=0, tiled=True)
    return display_tiles[None]


SMEM = pltpu.SMEM
VMEM = pltpu.VMEM


def pack_kernel(
    n_slab, counts, blocks, assign, depth, colors, transmit, table, *rest
):
    sends, sem = rest[:n_slab], rest[n_slab]
    me = lax.axis_index("slab")
    slots, feats = colors.shape[2], colors.shape[3]
    offset = jnp.int32(0)
    offsets = []
    for c in range(n_slab):
        offsets.append(offset)
        offset = offset + counts[0, me, c]
    copies = []
    for k in range(n_slab):
        peer = me ^ k
        off = offsets[0]
        for c in range(1, n_slab):
            off = jnp.where(peer == c, offsets[c], off)
        for r in range(MOST):
            slot = jnp.minimum(off + r, slots - 1)
            copies.append(
                pltpu.make_async_copy(
                    colors.at[0, 0, slot], sends[k].at[pl.ds(r * feats, feats)], sem.at[0]
                )
            )
        copies.append(
            pltpu.make_async_copy(
                transmit.at[0, 0], sends[k].at[pl.ds(MOST * feats, slots)], sem.at[0]
            )
        )
    for copy in copies:
        copy.start()
    pos = []
    for k in range(n_slab):
        peer = me ^ k
        off = jnp.int32(0)
        for c in range(n_slab):
            off = off + jnp.where(c < me, counts[0, peer, c], 0)
        count = counts[0, peer, me]
        for r in range(MOST):
            i = k * MOST + r
            slot = jnp.minimum(off + r, slots - 1)
            here = assign[0, blocks[0, peer, slot]] - me * LB
            here = jnp.where(r < count, here, -1)
            first = jnp.int32(i)
            for j in reversed(range(i)):
                first = jnp.where(pos[j] == here, j, first)
            pos.append(here)
            table[0, i] = here
            table[1, i] = depth[peer]
            table[2, i] = first
            table[3, i] = slot
    for copy in copies:
        copy.wait()


def silu_half(u):
    return (u + u * jnp.tanh(u)).astype(jnp.bfloat16)


def shade_kernel(n_slab, n_strip, feats, table, *refs):
    got = refs[:n_slab]
    w_first, w_mid, w_out = refs[n_slab : n_slab + 3]
    pieces = refs[n_slab + 3 : n_slab + 3 + n_strip]
    acc, tall, xs, ys = refs[n_slab + 3 + n_strip :]
    items = n_slab * MOST
    span = xs.shape[1] // (items + 1)
    slots = got[0].shape[0] - MOST * feats
    strip_me = lax.axis_index("strip")

    for k in range(n_slab):
        tall[pl.ds(k * slots, slots), :] = got[k][pl.ds(MOST * feats, slots), :].astype(jnp.float32)
    row = lax.broadcasted_iota(jnp.int32, (items, span), 0)
    posv = jnp.zeros((items, span), jnp.int32)
    depthv = jnp.zeros((items, span), jnp.int32)
    for i in range(items):
        posv = jnp.where(row == i, table[0, i], posv)
        depthv = jnp.where(row == i, table[1, i], depthv)
    front = jnp.ones((items, span), jnp.float32)
    total = jnp.ones((items, span), jnp.float32)
    for j in range(items):
        trans_j = tall[pl.ds((j // MOST) * slots + table[3, j], 1), :]
        same = posv == table[0, j]
        total = jnp.where(same, total * trans_j, total)
        front = jnp.where(same & (depthv > table[1, j]), front * trans_j, front)
    acc[...] = jnp.zeros_like(acc)
    for j in range(items):
        k, r = divmod(j, MOST)
        color = got[k][pl.ds(r * feats, feats), :].astype(jnp.float32)
        at = table[2, j]
        acc[at] = acc[at] + front[j : j + 1, :] * color
    total_hi = total.astype(jnp.bfloat16)
    total_lo = (total - total_hi.astype(jnp.float32)).astype(jnp.bfloat16)
    extra = xs.shape[0] - feats
    sub = lax.broadcasted_iota(jnp.int32, (extra, span), 0)
    for i in range(items):
        cols = pl.ds(i * span, span)
        xs[pl.ds(0, feats), cols] = acc[i].astype(jnp.bfloat16)
        hi = total_hi[i : i + 1, :].astype(jnp.float32)
        lo = total_lo[i : i + 1, :].astype(jnp.float32)
        tail = jnp.where(sub == 0, hi, jnp.where(sub == 1, lo, 0.0))
        xs[pl.ds(feats, extra), cols] = tail.astype(jnp.bfloat16)
    cols = pl.ds(items * span, span)
    xs[pl.ds(0, feats), cols] = jnp.zeros((feats, span), jnp.bfloat16)
    xs[pl.ds(feats, extra), cols] = jnp.where(sub == 0, 1.0, 0.0).astype(jnp.bfloat16)

    width = xs.shape[1]
    step = 4 * span
    for start in range(0, width, step):
        size = min(step, width - start)
        x = xs[:, pl.ds(start, size)]
        h = silu_half(
            lax.dot_general(
                w_first[...], x, (((0,), (0,)), ((), ())), preferred_element_type=jnp.float32
            )
        )
        for m in range(w_mid.shape[0]):
            h = silu_half(jnp.dot(w_mid[m], h, preferred_element_type=jnp.float32))
        y = jnp.dot(w_out[...], h, preferred_element_type=jnp.float32).astype(jnp.bfloat16)
        for i in range(size // span):
            ys[start // span + i] = y[:, i * span : (i + 1) * span]

    tile = pieces[0].shape[0]
    empty = jnp.broadcast_to(ys[items][None], pieces[0].shape)
    for k in range(n_strip):
        pieces[k][...] = empty
    for i in range(items):
        here = table[0, i]
        owner = (here // tile) ^ strip_me
        for k in range(n_strip):

            @pl.when((here >= 0) & (table[2, i] == i) & (owner == k))
            def _():
                pieces[k][here % tile] = ys[i]


def join_kernel(n_strip, *refs):
    got, out, sem = refs[:n_strip], refs[n_strip], refs[n_strip + 1]
    me = lax.axis_index("strip")
    copies = [
        pltpu.make_async_copy(got[k], out.at[0, me ^ k], sem.at[0]) for k in range(n_strip)
    ]
    for copy in copies:
        copy.start()
    for copy in copies:
        copy.wait()


def compact_device(
    n_slab,
    n_strip,
    colors,
    transmit,
    pair_counts,
    slot_block,
    assign,
    depth_rank,
    w_in,
    trans_weight,
    w_mid,
    w_out,
):
    slots, feats, span = colors.shape[2:]
    items = n_slab * MOST
    outs = w_out.shape[0]
    buf = jax.ShapeDtypeStruct((MOST * feats + slots, span), jnp.bfloat16)
    smem = pl.BlockSpec(memory_space=SMEM)
    vmem = pl.BlockSpec(memory_space=VMEM)
    anywhere = pl.BlockSpec(memory_space=pl.ANY)
    table, *sends = pl.pallas_call(
        functools.partial(pack_kernel, n_slab),
        out_shape=[jax.ShapeDtypeStruct((4, items), jnp.int32)] + [buf] * n_slab,
        in_specs=[smem] * 4 + [anywhere] * 2,
        out_specs=[smem] + [anywhere] * n_slab,
        scratch_shapes=[pltpu.SemaphoreType.DMA((1,))],
        name="pack",
    )(pair_counts, slot_block, assign, depth_rank, colors, transmit)
    got = [sends[0]] + [
        lax.ppermute(sends[k], "slab", [(s, s ^ k) for s in range(n_slab)])
        for k in range(1, n_slab)
    ]
    hidden = w_in.shape[0]
    extra = 16
    w_first = jnp.concatenate(
        [
            w_in.T,
            trans_weight[None],
            trans_weight[None],
            jnp.zeros((extra - 2, hidden), jnp.bfloat16),
        ]
    )
    half = jnp.bfloat16(0.5)
    pieces = pl.pallas_call(
        functools.partial(shade_kernel, n_slab, n_strip, feats),
        out_shape=[jax.ShapeDtypeStruct((LB // n_strip, outs, span), jnp.bfloat16)] * n_strip,
        in_specs=[smem] + [vmem] * (n_slab + 3),
        out_specs=[vmem] * n_strip,
        scratch_shapes=[
            pltpu.VMEM((items, feats, span), jnp.float32),
            pltpu.VMEM((n_slab * slots, span), jnp.float32),
            pltpu.VMEM((feats + extra, (items + 1) * span), jnp.bfloat16),
            pltpu.VMEM((items + 1, outs, span), jnp.bfloat16),
        ],
        compiler_params=pltpu.CompilerParams(vmem_limit_bytes=32 * 1024 * 1024),
        name="shade",
    )(table, *got, w_first * half, w_mid * half, w_out)
    tiles = [pieces[0]] + [
        lax.ppermute(pieces[k], "strip", [(s, s ^ k) for s in range(n_strip)])
        for k in range(1, n_strip)
    ]
    return pl.pallas_call(
        functools.partial(join_kernel, n_strip),
        out_shape=jax.ShapeDtypeStruct((1, n_strip, LB // n_strip, outs, span), jnp.bfloat16),
        in_specs=[anywhere] * n_strip,
        out_specs=anywhere,
        scratch_shapes=[pltpu.SemaphoreType.DMA((1,))],
        name="join",
    )(*tiles)


def solution(mesh):
    n_slab, n_strip = mesh.shape["slab"], mesh.shape["strip"]
    placed = (
        P("slab", "strip", None, None, None),
        P("slab", "strip", None, None),
        P("strip", None, None),
        P("strip", None, None),
        P("strip", None),
        P(),
        P(),
        P(),
        P(),
        P(),
    )
    powers = n_slab & (n_slab - 1) == 0 and n_strip & (n_strip - 1) == 0
    compact = powers and 4 * MOST * n_slab <= LB
    return jax.shard_map(
        functools.partial(compact_device, n_slab, n_strip) if compact else dense_device,
        mesh=mesh,
        in_specs=placed,
        out_specs=P("slab", None, "strip", None, None),
        check_vma=False,
    )
```

```python
import functools

import jax
import jax.numpy as jnp
from jax import lax
from jax.experimental import pallas as pl
from jax.experimental.pallas import tpu as pltpu
from jax.sharding import PartitionSpec as P

MOST = 2
LB = 128


EXACT_PRECISION = lax.Precision.HIGHEST


def shade_blocks(blend_color, trans_field, w_in, trans_weight, w_mid, w_out):
    summed = jnp.einsum("hf,lfp->lhp", w_in, blend_color, preferred_element_type=jnp.float32)
    summed = summed + trans_weight.astype(jnp.float32)[None, :, None] * trans_field[:, None, :]
    hidden = jax.nn.silu(summed).astype(jnp.bfloat16)
    for layer_index in range(w_mid.shape[0]):
        hidden = jax.nn.silu(
            jnp.einsum(
                "hg,lgp->lhp", w_mid[layer_index], hidden, preferred_element_type=jnp.float32
            )
        ).astype(jnp.bfloat16)
    return jnp.einsum("oh,lhp->lop", w_out, hidden, preferred_element_type=jnp.float32).astype(
        jnp.bfloat16
    )


def dense_device(
    colors, transmit, pair_counts, slot_block, assign, depth_rank, w_in, trans_weight, w_mid, w_out
):
    myself = lax.axis_index("slab")
    counts = pair_counts[0]
    blocks_all = slot_block[0]
    assign_row = assign[0]
    offsets = jnp.cumsum(counts, axis=1) - counts
    slot_rank = jnp.arange(MOST, dtype=jnp.int32)
    my_counts = lax.dynamic_index_in_dim(counts, myself, 0, keepdims=False)
    my_offsets = lax.dynamic_index_in_dim(offsets, myself, 0, keepdims=False)
    send_slots = jnp.where(
        slot_rank[None, :] < my_counts[:, None], my_offsets[:, None] + slot_rank[None, :], 0
    )
    send_color = colors[0, 0][send_slots]
    send_trans = transmit[0, 0][send_slots][:, :, None, :]
    incoming = lax.dynamic_index_in_dim(counts, myself, 1, keepdims=False)
    in_offsets = lax.dynamic_index_in_dim(offsets, myself, 1, keepdims=False)
    live_slot = slot_rank[None, :] < incoming[:, None]
    recv_slots = jnp.where(live_slot, in_offsets[:, None] + slot_rank[None, :], 0)
    recv_blocks = jnp.take_along_axis(blocks_all, recv_slots, axis=1)
    local_pos = assign_row[recv_blocks] - myself * LB
    live_flat = live_slot.reshape(-1)
    local_flat = jnp.where(live_flat, local_pos.reshape(-1), -1)
    depth_flat = jnp.repeat(depth_rank, MOST)
    ahead_table = (
        (local_flat[:, None] == local_flat[None, :])
        & (depth_flat[None, :] < depth_flat[:, None])
        & live_flat[None, :]
    )
    ahead_table = ahead_table.astype(jnp.float32)
    owner_table = (jnp.arange(LB, dtype=jnp.int32)[:, None] == local_flat[None, :]).astype(
        jnp.float32
    )
    got_color = lax.all_to_all(send_color, "slab", split_axis=0, concat_axis=0, tiled=True)
    got_trans = lax.all_to_all(send_trans, "slab", split_axis=0, concat_axis=0, tiled=True)
    pixel_count = got_color.shape[3]
    item_count = got_color.shape[0] * got_color.shape[1]
    log_trans = jnp.log(got_trans.reshape(item_count, pixel_count).astype(jnp.float32))
    log_trans = jnp.where(live_flat[:, None], log_trans, 0.0)
    front_log = jnp.dot(ahead_table, log_trans, precision=EXACT_PRECISION)
    front_share = jnp.where(live_flat[:, None], jnp.exp(front_log), 0.0)
    weighted = front_share[:, None, :] * got_color.reshape(item_count, -1, pixel_count).astype(
        jnp.float32
    )
    blend_sum = jnp.dot(owner_table, weighted.reshape(item_count, -1), precision=EXACT_PRECISION)
    blend_color = blend_sum.reshape(LB, -1, pixel_count).astype(jnp.bfloat16)
    trans_field = jnp.exp(jnp.dot(owner_table, log_trans, precision=EXACT_PRECISION))
    shaded = shade_blocks(blend_color, trans_field, w_in, trans_weight, w_mid, w_out)
    display_tiles = lax.all_to_all(shaded[None], "strip", split_axis=1, concat_axis=0, tiled=True)
    return display_tiles[None]


SMEM = pltpu.SMEM
VMEM = pltpu.VMEM


def plan_kernel(n_slab, slots, counts, blocks, assign, depth, table):
    me = lax.axis_index("slab")
    pos = []
    for s in range(n_slab):
        off = jnp.int32(0)
        for c in range(n_slab):
            off = off + jnp.where(c < me, counts[0, s, c], 0)
        count = counts[0, s, me]
        for r in range(MOST):
            i = s * MOST + r
            slot = jnp.minimum(off + r, slots - 1)
            here = assign[0, blocks[0, s, slot]] - me * LB
            here = jnp.where(r < count, here, -1)
            first = jnp.int32(i)
            for j in reversed(range(i)):
                first = jnp.where(pos[j] == here, j, first)
            pos.append(here)
            table[0, i] = here
            table[1, i] = depth[s]
            table[2, i] = first
            table[3, i] = slot


def silu_half(u):
    return (u + u * jnp.tanh(u)).astype(jnp.bfloat16)


def shade_kernel(table, colors, transmit, w_first, w_mid, w_out, ys, acc, tall, xs):
    n_slab, slots, feats = colors.shape[:3]
    items = n_slab * MOST
    span = xs.shape[1] // (items + 1)

    tall[...] = transmit[...].astype(jnp.float32).reshape(tall.shape)
    row = lax.broadcasted_iota(jnp.int32, (items, span), 0)
    posv = jnp.zeros((items, span), jnp.int32)
    depthv = jnp.zeros((items, span), jnp.int32)
    for i in range(items):
        posv = jnp.where(row == i, table[0, i], posv)
        depthv = jnp.where(row == i, table[1, i], depthv)
    front = jnp.ones((items, span), jnp.float32)
    total = jnp.ones((items, span), jnp.float32)
    for j in range(items):
        trans_j = tall[pl.ds((j // MOST) * slots + table[3, j], 1), :]
        same = posv == table[0, j]
        total = jnp.where(same, total * trans_j, total)
        front = jnp.where(same & (depthv > table[1, j]), front * trans_j, front)
    acc[...] = jnp.zeros_like(acc)
    for j in range(items):
        color = colors[j // MOST, table[3, j]].astype(jnp.float32)
        at = table[2, j]
        acc[at] = acc[at] + front[j : j + 1, :] * color
    total_hi = total.astype(jnp.bfloat16)
    total_lo = (total - total_hi.astype(jnp.float32)).astype(jnp.bfloat16)
    extra = xs.shape[0] - feats
    sub = lax.broadcasted_iota(jnp.int32, (extra, span), 0)
    for i in range(items):
        cols = pl.ds(i * span, span)
        xs[pl.ds(0, feats), cols] = acc[i].astype(jnp.bfloat16)
        hi = total_hi[i : i + 1, :].astype(jnp.float32)
        lo = total_lo[i : i + 1, :].astype(jnp.float32)
        tail = jnp.where(sub == 0, hi, jnp.where(sub == 1, lo, 0.0))
        xs[pl.ds(feats, extra), cols] = tail.astype(jnp.bfloat16)
    cols = pl.ds(items * span, span)
    xs[pl.ds(0, feats), cols] = jnp.zeros((feats, span), jnp.bfloat16)
    xs[pl.ds(feats, extra), cols] = jnp.where(sub == 0, 1.0, 0.0).astype(jnp.bfloat16)

    width = xs.shape[1]
    step = 4 * span
    for start in range(0, width, step):
        size = min(step, width - start)
        x = xs[:, pl.ds(start, size)]
        h = silu_half(
            lax.dot_general(
                w_first[...], x, (((0,), (0,)), ((), ())), preferred_element_type=jnp.float32
            )
        )
        for m in range(w_mid.shape[0]):
            h = silu_half(jnp.dot(w_mid[m], h, preferred_element_type=jnp.float32))
        y = jnp.dot(w_out[...], h, preferred_element_type=jnp.float32).astype(jnp.bfloat16)
        for i in range(size // span):
            ys[start // span + i] = y[:, i * span : (i + 1) * span]


def join_kernel(tables, got, out):
    _, n_strip, tile, outs, span = out.shape
    items = got.shape[1] - 1
    low = lax.axis_index("strip") * tile
    out[...] = jnp.broadcast_to(got[0, items][None, None, None], out.shape)
    for t in range(n_strip):
        for i in range(items):
            at = tables[t, 0, i] - low

            @pl.when((at >= 0) & (at < tile) & (tables[t, 2, i] == i))
            def _():
                out[0, t, at] = got[t, i]


def compact_device(
    n_slab,
    n_strip,
    colors,
    transmit,
    pair_counts,
    slot_block,
    assign,
    depth_rank,
    w_in,
    trans_weight,
    w_mid,
    w_out,
):
    slots, feats, span = colors.shape[2:]
    items = n_slab * MOST
    outs = w_out.shape[0]
    smem = pl.BlockSpec(memory_space=SMEM)
    vmem = pl.BlockSpec(memory_space=VMEM)
    all_colors = lax.all_gather(colors[0, 0], "slab")
    all_transmit = lax.all_gather(transmit[0, 0], "slab")
    table = pl.pallas_call(
        functools.partial(plan_kernel, n_slab, slots),
        out_shape=jax.ShapeDtypeStruct((4, items), jnp.int32),
        in_specs=[smem] * 4,
        out_specs=smem,
        name="plan",
    )(pair_counts, slot_block, assign, depth_rank)
    tables = lax.all_gather(table, "strip")
    hidden = w_in.shape[0]
    extra = 16
    w_first = jnp.concatenate(
        [
            w_in.T,
            trans_weight[None],
            trans_weight[None],
            jnp.zeros((extra - 2, hidden), jnp.bfloat16),
        ]
    )
    half = jnp.bfloat16(0.5)
    shaded = pl.pallas_call(
        shade_kernel,
        out_shape=jax.ShapeDtypeStruct((items + 1, outs, span), jnp.bfloat16),
        in_specs=[smem] + [vmem] * 5,
        out_specs=vmem,
        scratch_shapes=[
            pltpu.VMEM((items, feats, span), jnp.float32),
            pltpu.VMEM((n_slab * slots, span), jnp.float32),
            pltpu.VMEM((feats + extra, (items + 1) * span), jnp.bfloat16),
        ],
        compiler_params=pltpu.CompilerParams(vmem_limit_bytes=32 * 1024 * 1024),
        name="shade",
    )(table, all_colors, all_transmit, w_first * half, w_mid * half, w_out)
    all_shaded = lax.all_gather(shaded, "strip")
    return pl.pallas_call(
        join_kernel,
        out_shape=jax.ShapeDtypeStruct((1, n_strip, LB // n_strip, outs, span), jnp.bfloat16),
        in_specs=[smem, vmem],
        out_specs=vmem,
        name="join",
    )(tables, all_shaded)


def solution(mesh):
    n_slab, n_strip = mesh.shape["slab"], mesh.shape["strip"]
    placed = (
        P("slab", "strip", None, None, None),
        P("slab", "strip", None, None),
        P("strip", None, None),
        P("strip", None, None),
        P("strip", None),
        P(),
        P(),
        P(),
        P(),
        P(),
    )
    compact = 4 * MOST * n_slab <= LB
    return jax.shard_map(
        functools.partial(compact_device, n_slab, n_strip) if compact else dense_device,
        mesh=mesh,
        in_specs=placed,
        out_specs=P("slab", None, "strip", None, None),
        check_vma=False,
    )
```

```python
import functools

import jax
import jax.numpy as jnp
from jax import lax
from jax.experimental import pallas as pl
from jax.experimental.pallas import tpu as pltpu
from jax.sharding import PartitionSpec as P

MOST = 2
LB = 128


EXACT_PRECISION = lax.Precision.HIGHEST


def shade_blocks(blend_color, trans_field, w_in, trans_weight, w_mid, w_out):
    summed = jnp.einsum("hf,lfp->lhp", w_in, blend_color, preferred_element_type=jnp.float32)
    summed = summed + trans_weight.astype(jnp.float32)[None, :, None] * trans_field[:, None, :]
    hidden = jax.nn.silu(summed).astype(jnp.bfloat16)
    for layer_index in range(w_mid.shape[0]):
        hidden = jax.nn.silu(
            jnp.einsum(
                "hg,lgp->lhp", w_mid[layer_index], hidden, preferred_element_type=jnp.float32
            )
        ).astype(jnp.bfloat16)
    return jnp.einsum("oh,lhp->lop", w_out, hidden, preferred_element_type=jnp.float32).astype(
        jnp.bfloat16
    )


def dense_device(
    colors, transmit, pair_counts, slot_block, assign, depth_rank, w_in, trans_weight, w_mid, w_out
):
    myself = lax.axis_index("slab")
    counts = pair_counts[0]
    blocks_all = slot_block[0]
    assign_row = assign[0]
    offsets = jnp.cumsum(counts, axis=1) - counts
    slot_rank = jnp.arange(MOST, dtype=jnp.int32)
    my_counts = lax.dynamic_index_in_dim(counts, myself, 0, keepdims=False)
    my_offsets = lax.dynamic_index_in_dim(offsets, myself, 0, keepdims=False)
    send_slots = jnp.where(
        slot_rank[None, :] < my_counts[:, None], my_offsets[:, None] + slot_rank[None, :], 0
    )
    send_color = colors[0, 0][send_slots]
    send_trans = transmit[0, 0][send_slots][:, :, None, :]
    incoming = lax.dynamic_index_in_dim(counts, myself, 1, keepdims=False)
    in_offsets = lax.dynamic_index_in_dim(offsets, myself, 1, keepdims=False)
    live_slot = slot_rank[None, :] < incoming[:, None]
    recv_slots = jnp.where(live_slot, in_offsets[:, None] + slot_rank[None, :], 0)
    recv_blocks = jnp.take_along_axis(blocks_all, recv_slots, axis=1)
    local_pos = assign_row[recv_blocks] - myself * LB
    live_flat = live_slot.reshape(-1)
    local_flat = jnp.where(live_flat, local_pos.reshape(-1), -1)
    depth_flat = jnp.repeat(depth_rank, MOST)
    ahead_table = (
        (local_flat[:, None] == local_flat[None, :])
        & (depth_flat[None, :] < depth_flat[:, None])
        & live_flat[None, :]
    )
    ahead_table = ahead_table.astype(jnp.float32)
    owner_table = (jnp.arange(LB, dtype=jnp.int32)[:, None] == local_flat[None, :]).astype(
        jnp.float32
    )
    got_color = lax.all_to_all(send_color, "slab", split_axis=0, concat_axis=0, tiled=True)
    got_trans = lax.all_to_all(send_trans, "slab", split_axis=0, concat_axis=0, tiled=True)
    pixel_count = got_color.shape[3]
    item_count = got_color.shape[0] * got_color.shape[1]
    log_trans = jnp.log(got_trans.reshape(item_count, pixel_count).astype(jnp.float32))
    log_trans = jnp.where(live_flat[:, None], log_trans, 0.0)
    front_log = jnp.dot(ahead_table, log_trans, precision=EXACT_PRECISION)
    front_share = jnp.where(live_flat[:, None], jnp.exp(front_log), 0.0)
    weighted = front_share[:, None, :] * got_color.reshape(item_count, -1, pixel_count).astype(
        jnp.float32
    )
    blend_sum = jnp.dot(owner_table, weighted.reshape(item_count, -1), precision=EXACT_PRECISION)
    blend_color = blend_sum.reshape(LB, -1, pixel_count).astype(jnp.bfloat16)
    trans_field = jnp.exp(jnp.dot(owner_table, log_trans, precision=EXACT_PRECISION))
    shaded = shade_blocks(blend_color, trans_field, w_in, trans_weight, w_mid, w_out)
    display_tiles = lax.all_to_all(shaded[None], "strip", split_axis=1, concat_axis=0, tiled=True)
    return display_tiles[None]


SMEM = pltpu.SMEM
VMEM = pltpu.VMEM


def pack_kernel(counts, colors, transmit, sends):
    n_slab = sends.shape[0]
    slots, feats = colors.shape[2], colors.shape[3]
    me = lax.axis_index("slab")
    off = jnp.int32(0)
    for c in range(n_slab):
        for r in range(MOST):
            slot = jnp.minimum(off + r, slots - 1)
            sends[c, pl.ds(r * feats, feats), :] = colors[0, 0, slot]
        sends[c, pl.ds(MOST * feats, slots), :] = transmit[0, 0]
        off = off + counts[0, me, c]


def plan_kernel(n_slab, slots, counts, blocks, assign, depth, table):
    me = lax.axis_index("slab")
    pos = []
    for s in range(n_slab):
        off = jnp.int32(0)
        for c in range(n_slab):
            off = off + jnp.where(c < me, counts[0, s, c], 0)
        count = counts[0, s, me]
        for r in range(MOST):
            i = s * MOST + r
            slot = jnp.minimum(off + r, slots - 1)
            here = assign[0, blocks[0, s, slot]] - me * LB
            here = jnp.where(r < count, here, -1)
            first = jnp.int32(i)
            for j in reversed(range(i)):
                first = jnp.where(pos[j] == here, j, first)
            pos.append(here)
            table[0, i] = here
            table[1, i] = depth[s]
            table[2, i] = first
            table[3, i] = slot


def silu_half(u):
    return (u + u * jnp.tanh(u)).astype(jnp.bfloat16)


def shade_kernel(n_slab, n_strip, feats, table, got, w_first, w_mid, w_out, *refs):
    pieces = refs[:n_strip]
    acc, tall, xs, ys = refs[n_strip:]
    items = n_slab * MOST
    span = xs.shape[1] // (items + 1)
    slots = got.shape[1] - MOST * feats
    strip_me = lax.axis_index("strip")

    for k in range(n_slab):
        tall[pl.ds(k * slots, slots), :] = got[k, pl.ds(MOST * feats, slots), :].astype(jnp.float32)
    row = lax.broadcasted_iota(jnp.int32, (items, span), 0)
    posv = jnp.zeros((items, span), jnp.int32)
    depthv = jnp.zeros((items, span), jnp.int32)
    for i in range(items):
        posv = jnp.where(row == i, table[0, i], posv)
        depthv = jnp.where(row == i, table[1, i], depthv)
    front = jnp.ones((items, span), jnp.float32)
    total = jnp.ones((items, span), jnp.float32)
    for j in range(items):
        trans_j = tall[pl.ds((j // MOST) * slots + table[3, j], 1), :]
        same = posv == table[0, j]
        total = jnp.where(same, total * trans_j, total)
        front = jnp.where(same & (depthv > table[1, j]), front * trans_j, front)
    acc[...] = jnp.zeros_like(acc)
    for j in range(items):
        k, r = divmod(j, MOST)
        color = got[k, pl.ds(r * feats, feats), :].astype(jnp.float32)
        at = table[2, j]
        acc[at] = acc[at] + front[j : j + 1, :] * color
    total_hi = total.astype(jnp.bfloat16)
    total_lo = (total - total_hi.astype(jnp.float32)).astype(jnp.bfloat16)
    extra = xs.shape[0] - feats
    sub = lax.broadcasted_iota(jnp.int32, (extra, span), 0)
    for i in range(items):
        cols = pl.ds(i * span, span)
        xs[pl.ds(0, feats), cols] = acc[i].astype(jnp.bfloat16)
        hi = total_hi[i : i + 1, :].astype(jnp.float32)
        lo = total_lo[i : i + 1, :].astype(jnp.float32)
        tail = jnp.where(sub == 0, hi, jnp.where(sub == 1, lo, 0.0))
        xs[pl.ds(feats, extra), cols] = tail.astype(jnp.bfloat16)
    cols = pl.ds(items * span, span)
    xs[pl.ds(0, feats), cols] = jnp.zeros((feats, span), jnp.bfloat16)
    xs[pl.ds(feats, extra), cols] = jnp.where(sub == 0, 1.0, 0.0).astype(jnp.bfloat16)

    width = xs.shape[1]
    step = 4 * span
    for start in range(0, width, step):
        size = min(step, width - start)
        x = xs[:, pl.ds(start, size)]
        h = silu_half(
            lax.dot_general(
                w_first[...], x, (((0,), (0,)), ((), ())), preferred_element_type=jnp.float32
            )
        )
        for m in range(w_mid.shape[0]):
            h = silu_half(jnp.dot(w_mid[m], h, preferred_element_type=jnp.float32))
        y = jnp.dot(w_out[...], h, preferred_element_type=jnp.float32).astype(jnp.bfloat16)
        for i in range(size // span):
            ys[start // span + i] = y[:, i * span : (i + 1) * span]

    tile = pieces[0].shape[0]
    empty = jnp.broadcast_to(ys[items][None], pieces[0].shape)
    for k in range(n_strip):
        pieces[k][...] = empty
    for i in range(items):
        here = table[0, i]
        owner = (here // tile) ^ strip_me
        for k in range(n_strip):

            @pl.when((here >= 0) & (table[2, i] == i) & (owner == k))
            def _():
                pieces[k][here % tile] = ys[i]


def join_kernel(*refs):
    *got, out = refs
    me = lax.axis_index("strip")
    for k in range(len(got)):
        out[0, me ^ k] = got[k][...]


def compact_device(
    n_slab,
    n_strip,
    colors,
    transmit,
    pair_counts,
    slot_block,
    assign,
    depth_rank,
    w_in,
    trans_weight,
    w_mid,
    w_out,
):
    slots, feats, span = colors.shape[2:]
    items = n_slab * MOST
    outs = w_out.shape[0]
    smem = pl.BlockSpec(memory_space=SMEM)
    vmem = pl.BlockSpec(memory_space=VMEM)
    sends = pl.pallas_call(
        pack_kernel,
        out_shape=jax.ShapeDtypeStruct((n_slab, MOST * feats + slots, span), jnp.bfloat16),
        in_specs=[smem, pl.BlockSpec(), pl.BlockSpec()],
        out_specs=vmem,
        name="pack",
    )(pair_counts, colors, transmit)
    got = lax.all_to_all(sends, "slab", split_axis=0, concat_axis=0, tiled=True)
    table = pl.pallas_call(
        functools.partial(plan_kernel, n_slab, slots),
        out_shape=jax.ShapeDtypeStruct((4, items), jnp.int32),
        in_specs=[smem] * 4,
        out_specs=smem,
        cost_estimate=pl.CostEstimate(flops=10**5, bytes_accessed=10**6, transcendentals=0),
        name="plan",
    )(pair_counts, slot_block, assign, depth_rank)
    hidden = w_in.shape[0]
    extra = 16
    w_first = jnp.concatenate(
        [
            w_in.T,
            trans_weight[None],
            trans_weight[None],
            jnp.zeros((extra - 2, hidden), jnp.bfloat16),
        ]
    )
    half = jnp.bfloat16(0.5)
    pieces = pl.pallas_call(
        functools.partial(shade_kernel, n_slab, n_strip, feats),
        out_shape=[jax.ShapeDtypeStruct((LB // n_strip, outs, span), jnp.bfloat16)] * n_strip,
        in_specs=[smem] + [vmem] * 4,
        out_specs=[vmem] * n_strip,
        scratch_shapes=[
            pltpu.VMEM((items, feats, span), jnp.float32),
            pltpu.VMEM((n_slab * slots, span), jnp.float32),
            pltpu.VMEM((feats + extra, (items + 1) * span), jnp.bfloat16),
            pltpu.VMEM((items + 1, outs, span), jnp.bfloat16),
        ],
        compiler_params=pltpu.CompilerParams(vmem_limit_bytes=32 * 1024 * 1024),
        name="shade",
    )(table, got, w_first * half, w_mid * half, w_out)
    tiles = [pieces[0]] + [
        lax.ppermute(pieces[k], "strip", [(s, s ^ k) for s in range(n_strip)])
        for k in range(1, n_strip)
    ]
    return pl.pallas_call(
        join_kernel,
        out_shape=jax.ShapeDtypeStruct((1, n_strip, LB // n_strip, outs, span), jnp.bfloat16),
        in_specs=[vmem] * n_strip,
        out_specs=pl.BlockSpec(),
        name="join",
    )(*tiles)


def solution(mesh):
    n_slab, n_strip = mesh.shape["slab"], mesh.shape["strip"]
    placed = (
        P("slab", "strip", None, None, None),
        P("slab", "strip", None, None),
        P("strip", None, None),
        P("strip", None, None),
        P("strip", None),
        P(),
        P(),
        P(),
        P(),
        P(),
    )
    compact = n_strip & (n_strip - 1) == 0 and 4 * MOST * n_slab <= LB
    return jax.shard_map(
        functools.partial(compact_device, n_slab, n_strip) if compact else dense_device,
        mesh=mesh,
        in_specs=placed,
        out_specs=P("slab", None, "strip", None, None),
        check_vma=False,
    )
```

```python
import functools

import jax
import jax.numpy as jnp
from jax import lax
from jax.experimental import pallas as pl
from jax.experimental.pallas import tpu as pltpu
from jax.sharding import PartitionSpec as P

MOST = 2
LB = 128


EXACT_PRECISION = lax.Precision.HIGHEST


def shade_blocks(blend_color, trans_field, w_in, trans_weight, w_mid, w_out):
    summed = jnp.einsum("hf,lfp->lhp", w_in, blend_color, preferred_element_type=jnp.float32)
    summed = summed + trans_weight.astype(jnp.float32)[None, :, None] * trans_field[:, None, :]
    hidden = jax.nn.silu(summed).astype(jnp.bfloat16)
    for layer_index in range(w_mid.shape[0]):
        hidden = jax.nn.silu(
            jnp.einsum(
                "hg,lgp->lhp", w_mid[layer_index], hidden, preferred_element_type=jnp.float32
            )
        ).astype(jnp.bfloat16)
    return jnp.einsum("oh,lhp->lop", w_out, hidden, preferred_element_type=jnp.float32).astype(
        jnp.bfloat16
    )


def dense_device(
    colors, transmit, pair_counts, slot_block, assign, depth_rank, w_in, trans_weight, w_mid, w_out
):
    myself = lax.axis_index("slab")
    counts = pair_counts[0]
    blocks_all = slot_block[0]
    assign_row = assign[0]
    offsets = jnp.cumsum(counts, axis=1) - counts
    slot_rank = jnp.arange(MOST, dtype=jnp.int32)
    my_counts = lax.dynamic_index_in_dim(counts, myself, 0, keepdims=False)
    my_offsets = lax.dynamic_index_in_dim(offsets, myself, 0, keepdims=False)
    send_slots = jnp.where(
        slot_rank[None, :] < my_counts[:, None], my_offsets[:, None] + slot_rank[None, :], 0
    )
    send_color = colors[0, 0][send_slots]
    send_trans = transmit[0, 0][send_slots][:, :, None, :]
    incoming = lax.dynamic_index_in_dim(counts, myself, 1, keepdims=False)
    in_offsets = lax.dynamic_index_in_dim(offsets, myself, 1, keepdims=False)
    live_slot = slot_rank[None, :] < incoming[:, None]
    recv_slots = jnp.where(live_slot, in_offsets[:, None] + slot_rank[None, :], 0)
    recv_blocks = jnp.take_along_axis(blocks_all, recv_slots, axis=1)
    local_pos = assign_row[recv_blocks] - myself * LB
    live_flat = live_slot.reshape(-1)
    local_flat = jnp.where(live_flat, local_pos.reshape(-1), -1)
    depth_flat = jnp.repeat(depth_rank, MOST)
    ahead_table = (
        (local_flat[:, None] == local_flat[None, :])
        & (depth_flat[None, :] < depth_flat[:, None])
        & live_flat[None, :]
    )
    ahead_table = ahead_table.astype(jnp.float32)
    owner_table = (jnp.arange(LB, dtype=jnp.int32)[:, None] == local_flat[None, :]).astype(
        jnp.float32
    )
    got_color = lax.all_to_all(send_color, "slab", split_axis=0, concat_axis=0, tiled=True)
    got_trans = lax.all_to_all(send_trans, "slab", split_axis=0, concat_axis=0, tiled=True)
    pixel_count = got_color.shape[3]
    item_count = got_color.shape[0] * got_color.shape[1]
    log_trans = jnp.log(got_trans.reshape(item_count, pixel_count).astype(jnp.float32))
    log_trans = jnp.where(live_flat[:, None], log_trans, 0.0)
    front_log = jnp.dot(ahead_table, log_trans, precision=EXACT_PRECISION)
    front_share = jnp.where(live_flat[:, None], jnp.exp(front_log), 0.0)
    weighted = front_share[:, None, :] * got_color.reshape(item_count, -1, pixel_count).astype(
        jnp.float32
    )
    blend_sum = jnp.dot(owner_table, weighted.reshape(item_count, -1), precision=EXACT_PRECISION)
    blend_color = blend_sum.reshape(LB, -1, pixel_count).astype(jnp.bfloat16)
    trans_field = jnp.exp(jnp.dot(owner_table, log_trans, precision=EXACT_PRECISION))
    shaded = shade_blocks(blend_color, trans_field, w_in, trans_weight, w_mid, w_out)
    display_tiles = lax.all_to_all(shaded[None], "strip", split_axis=1, concat_axis=0, tiled=True)
    return display_tiles[None]


SMEM = pltpu.SMEM
VMEM = pltpu.VMEM
ROWS = 8


def pack_kernel(counts, colors, transmit, sends, tall):
    n_slab = sends.shape[0]
    slots, feats, span = colors.shape[2:]
    me = lax.axis_index("slab")
    tall[...] = transmit[0, 0].astype(jnp.float32)
    row = lax.broadcasted_iota(jnp.int32, (ROWS, span), 0)
    off = jnp.int32(0)
    for c in range(n_slab):
        tail = jnp.ones((ROWS, span), jnp.float32)
        for r in range(MOST):
            slot = jnp.minimum(off + r, slots - 1)
            sends[c, pl.ds(r * feats, feats), :] = colors[0, 0, slot]
            tail = jnp.where(row == r, tall[pl.ds(slot, 1), :], tail)
        sends[c, pl.ds(MOST * feats, ROWS), :] = tail.astype(jnp.bfloat16)
        off = off + counts[0, me, c]


def plan_kernel(n_slab, slots, counts, blocks, assign, depth, table, rows):
    items = n_slab * MOST
    me = lax.axis_index("slab")
    row = lax.broadcasted_iota(jnp.int32, rows.shape[1:], 0)
    posv = jnp.zeros(rows.shape[1:], jnp.int32)
    depthv = jnp.zeros(rows.shape[1:], jnp.int32)
    pos, firsts = [], []
    spare_to, spare_from = jnp.int32(0), jnp.int32(items)
    for s in range(n_slab):
        off = jnp.int32(0)
        for c in range(n_slab):
            off = off + jnp.where(c < me, counts[0, s, c], 0)
        count = counts[0, s, me]
        for r in range(MOST):
            i = s * MOST + r
            slot = jnp.minimum(off + r, slots - 1)
            here = assign[0, blocks[0, s, slot]] - me * LB
            here = jnp.where(r < count, here, -1)
            first = jnp.int32(i)
            for j in reversed(range(i)):
                first = jnp.where(pos[j] == here, j, first)
            pos.append(here)
            firsts.append(first)
            spare_to = jnp.where(here >= 0, here, spare_to)
            spare_from = jnp.where(here >= 0, first, spare_from)
            posv = jnp.where(row == i, here, posv)
            depthv = jnp.where(row == i, depth[s], depthv)
    for i in range(items):
        table[0, i] = firsts[i]
        table[1, i] = jnp.where(pos[i] >= 0, pos[i], spare_to)
        table[2, i] = jnp.where(pos[i] >= 0, firsts[i], spare_from)
    rows[0] = posv
    rows[1] = depthv


def silu_half(u):
    return (u + u * jnp.tanh(u)).astype(jnp.bfloat16)


def shade_kernel(n_strip, table, rows, got, w_first, w_mid, w_out, *refs):
    pieces = refs[:n_strip]
    acc, xs, ys, full = refs[n_strip:]
    items, feats, span = acc.shape
    strip_me = lax.axis_index("strip")

    posv, depthv = rows[0], rows[1]
    front = jnp.ones((items, span), jnp.float32)
    total = jnp.ones((items, span), jnp.float32)
    for k in range(items // MOST):
        tail = got[k, pl.ds(MOST * feats, ROWS), :].astype(jnp.float32)
        for r in range(MOST):
            j = k * MOST + r
            trans_j = tail[r : r + 1, :]
            same = posv == posv[j : j + 1, :]
            total = jnp.where(same, total * trans_j, total)
            front = jnp.where(same & (depthv > depthv[j : j + 1, :]), front * trans_j, front)
    acc[...] = jnp.zeros_like(acc)
    for j in range(items):
        k, r = divmod(j, MOST)
        color = got[k, pl.ds(r * feats, feats), :].astype(jnp.float32)
        at = table[0, j]
        acc[at] = acc[at] + front[j : j + 1, :] * color
    total_hi = total.astype(jnp.bfloat16)
    total_lo = (total - total_hi.astype(jnp.float32)).astype(jnp.bfloat16)
    extra = xs.shape[0] - feats
    sub = lax.broadcasted_iota(jnp.int32, (extra, span), 0)
    for i in range(items):
        cols = pl.ds(i * span, span)
        xs[pl.ds(0, feats), cols] = acc[i].astype(jnp.bfloat16)
        hi = total_hi[i : i + 1, :].astype(jnp.float32)
        lo = total_lo[i : i + 1, :].astype(jnp.float32)
        tail = jnp.where(sub == 0, hi, jnp.where(sub == 1, lo, 0.0))
        xs[pl.ds(feats, extra), cols] = tail.astype(jnp.bfloat16)
    cols = pl.ds(items * span, span)
    xs[pl.ds(0, feats), cols] = jnp.zeros((feats, span), jnp.bfloat16)
    xs[pl.ds(feats, extra), cols] = jnp.where(sub == 0, 1.0, 0.0).astype(jnp.bfloat16)

    width = xs.shape[1]
    step = 4 * span
    for start in range(0, width, step):
        size = min(step, width - start)
        x = xs[:, pl.ds(start, size)]
        h = silu_half(
            lax.dot_general(
                w_first[...], x, (((0,), (0,)), ((), ())), preferred_element_type=jnp.float32
            )
        )
        for m in range(w_mid.shape[0]):
            h = silu_half(jnp.dot(w_mid[m], h, preferred_element_type=jnp.float32))
        y = jnp.dot(w_out[...], h, preferred_element_type=jnp.float32).astype(jnp.bfloat16)
        for i in range(size // span):
            ys[start // span + i] = y[:, i * span : (i + 1) * span]

    full[...] = jnp.broadcast_to(ys[items][None], full.shape)
    for i in range(items):
        full[table[1, i]] = ys[table[2, i]]
    tile = pieces[0].shape[0]
    for k in range(n_strip):
        pieces[k][...] = full[pl.ds((strip_me ^ k) * tile, tile)]


def join_kernel(*refs):
    *got, out = refs
    me = lax.axis_index("strip")
    for k in range(len(got)):
        out[0, me ^ k] = got[k][...]


def compact_device(
    n_slab,
    n_strip,
    colors,
    transmit,
    pair_counts,
    slot_block,
    assign,
    depth_rank,
    w_in,
    trans_weight,
    w_mid,
    w_out,
):
    slots, feats, span = colors.shape[2:]
    items = n_slab * MOST
    outs = w_out.shape[0]
    smem = pl.BlockSpec(memory_space=SMEM)
    vmem = pl.BlockSpec(memory_space=VMEM)
    small = pltpu.CompilerParams(vmem_limit_bytes=4 * 1024 * 1024)
    sends = pl.pallas_call(
        pack_kernel,
        out_shape=jax.ShapeDtypeStruct((n_slab, MOST * feats + ROWS, span), jnp.bfloat16),
        in_specs=[smem, vmem, vmem],
        out_specs=vmem,
        scratch_shapes=[pltpu.VMEM((slots, span), jnp.float32)],
        compiler_params=small,
        name="pack",
    )(pair_counts, colors, transmit)
    got = lax.all_to_all(sends, "slab", split_axis=0, concat_axis=0, tiled=True)
    table, rows = pl.pallas_call(
        functools.partial(plan_kernel, n_slab, slots),
        out_shape=[
            jax.ShapeDtypeStruct((3, items), jnp.int32),
            jax.ShapeDtypeStruct((2, items, span), jnp.int32),
        ],
        in_specs=[smem] * 4,
        out_specs=[smem, vmem],
        compiler_params=small,
        cost_estimate=pl.CostEstimate(flops=10**5, bytes_accessed=10**6, transcendentals=0),
        name="plan",
    )(pair_counts, slot_block, assign, depth_rank)
    hidden = w_in.shape[0]
    extra = 16
    w_first = jnp.concatenate(
        [
            w_in.T,
            trans_weight[None],
            trans_weight[None],
            jnp.zeros((extra - 2, hidden), jnp.bfloat16),
        ]
    )
    half = jnp.bfloat16(0.5)
    pieces = pl.pallas_call(
        functools.partial(shade_kernel, n_strip),
        out_shape=[jax.ShapeDtypeStruct((LB // n_strip, outs, span), jnp.bfloat16)] * n_strip,
        in_specs=[smem] + [vmem] * 5,
        out_specs=[vmem] * n_strip,
        scratch_shapes=[
            pltpu.VMEM((items, feats, span), jnp.float32),
            pltpu.VMEM((feats + extra, (items + 1) * span), jnp.bfloat16),
            pltpu.VMEM((items + 1, outs, span), jnp.bfloat16),
            pltpu.VMEM((LB, outs, span), jnp.bfloat16),
        ],
        compiler_params=pltpu.CompilerParams(vmem_limit_bytes=16 * 1024 * 1024),
        name="shade",
    )(table, rows, got, w_first * half, w_mid * half, w_out)
    tiles = [pieces[0]] + [
        lax.ppermute(pieces[k], "strip", [(s, s ^ k) for s in range(n_strip)])
        for k in range(1, n_strip)
    ]
    return pl.pallas_call(
        join_kernel,
        out_shape=jax.ShapeDtypeStruct((1, n_strip, LB // n_strip, outs, span), jnp.bfloat16),
        in_specs=[vmem] * n_strip,
        out_specs=pl.BlockSpec(),
        compiler_params=small,
        name="join",
    )(*tiles)


def solution(mesh):
    n_slab, n_strip = mesh.shape["slab"], mesh.shape["strip"]
    placed = (
        P("slab", "strip", None, None, None),
        P("slab", "strip", None, None),
        P("strip", None, None),
        P("strip", None, None),
        P("strip", None),
        P(),
        P(),
        P(),
        P(),
        P(),
    )
    compact = n_strip & (n_strip - 1) == 0 and 4 * MOST * n_slab <= LB
    return jax.shard_map(
        functools.partial(compact_device, n_slab, n_strip) if compact else dense_device,
        mesh=mesh,
        in_specs=placed,
        out_specs=P("slab", None, "strip", None, None),
        check_vma=False,
    )
```

```python
import functools

import jax
import jax.numpy as jnp
from jax import lax
from jax.experimental import pallas as pl
from jax.experimental.pallas import tpu as pltpu
from jax.sharding import PartitionSpec as P

MOST = 2
LB = 128


EXACT_PRECISION = lax.Precision.HIGHEST


def shade_blocks(blend_color, trans_field, w_in, trans_weight, w_mid, w_out):
    summed = jnp.einsum("hf,lfp->lhp", w_in, blend_color, preferred_element_type=jnp.float32)
    summed = summed + trans_weight.astype(jnp.float32)[None, :, None] * trans_field[:, None, :]
    hidden = jax.nn.silu(summed).astype(jnp.bfloat16)
    for layer_index in range(w_mid.shape[0]):
        hidden = jax.nn.silu(
            jnp.einsum(
                "hg,lgp->lhp", w_mid[layer_index], hidden, preferred_element_type=jnp.float32
            )
        ).astype(jnp.bfloat16)
    return jnp.einsum("oh,lhp->lop", w_out, hidden, preferred_element_type=jnp.float32).astype(
        jnp.bfloat16
    )


def dense_device(
    colors, transmit, pair_counts, slot_block, assign, depth_rank, w_in, trans_weight, w_mid, w_out
):
    myself = lax.axis_index("slab")
    counts = pair_counts[0]
    blocks_all = slot_block[0]
    assign_row = assign[0]
    offsets = jnp.cumsum(counts, axis=1) - counts
    slot_rank = jnp.arange(MOST, dtype=jnp.int32)
    my_counts = lax.dynamic_index_in_dim(counts, myself, 0, keepdims=False)
    my_offsets = lax.dynamic_index_in_dim(offsets, myself, 0, keepdims=False)
    send_slots = jnp.where(
        slot_rank[None, :] < my_counts[:, None], my_offsets[:, None] + slot_rank[None, :], 0
    )
    send_color = colors[0, 0][send_slots]
    send_trans = transmit[0, 0][send_slots][:, :, None, :]
    incoming = lax.dynamic_index_in_dim(counts, myself, 1, keepdims=False)
    in_offsets = lax.dynamic_index_in_dim(offsets, myself, 1, keepdims=False)
    live_slot = slot_rank[None, :] < incoming[:, None]
    recv_slots = jnp.where(live_slot, in_offsets[:, None] + slot_rank[None, :], 0)
    recv_blocks = jnp.take_along_axis(blocks_all, recv_slots, axis=1)
    local_pos = assign_row[recv_blocks] - myself * LB
    live_flat = live_slot.reshape(-1)
    local_flat = jnp.where(live_flat, local_pos.reshape(-1), -1)
    depth_flat = jnp.repeat(depth_rank, MOST)
    ahead_table = (
        (local_flat[:, None] == local_flat[None, :])
        & (depth_flat[None, :] < depth_flat[:, None])
        & live_flat[None, :]
    )
    ahead_table = ahead_table.astype(jnp.float32)
    owner_table = (jnp.arange(LB, dtype=jnp.int32)[:, None] == local_flat[None, :]).astype(
        jnp.float32
    )
    got_color = lax.all_to_all(send_color, "slab", split_axis=0, concat_axis=0, tiled=True)
    got_trans = lax.all_to_all(send_trans, "slab", split_axis=0, concat_axis=0, tiled=True)
    pixel_count = got_color.shape[3]
    item_count = got_color.shape[0] * got_color.shape[1]
    log_trans = jnp.log(got_trans.reshape(item_count, pixel_count).astype(jnp.float32))
    log_trans = jnp.where(live_flat[:, None], log_trans, 0.0)
    front_log = jnp.dot(ahead_table, log_trans, precision=EXACT_PRECISION)
    front_share = jnp.where(live_flat[:, None], jnp.exp(front_log), 0.0)
    weighted = front_share[:, None, :] * got_color.reshape(item_count, -1, pixel_count).astype(
        jnp.float32
    )
    blend_sum = jnp.dot(owner_table, weighted.reshape(item_count, -1), precision=EXACT_PRECISION)
    blend_color = blend_sum.reshape(LB, -1, pixel_count).astype(jnp.bfloat16)
    trans_field = jnp.exp(jnp.dot(owner_table, log_trans, precision=EXACT_PRECISION))
    shaded = shade_blocks(blend_color, trans_field, w_in, trans_weight, w_mid, w_out)
    display_tiles = lax.all_to_all(shaded[None], "strip", split_axis=1, concat_axis=0, tiled=True)
    return display_tiles[None]


SMEM = pltpu.SMEM
VMEM = pltpu.VMEM
ROWS = 8


def fetch(sources, targets, sems):
    copies = [
        pltpu.make_async_copy(source, target, sems.at[i])
        for i, (source, target) in enumerate(zip(sources, targets))
    ]
    for copy in copies:
        copy.start()
    for copy in copies:
        copy.wait()


def pack_kernel(far_counts, far_colors, far_transmit, sends, counts, colors, transmit, tall, sems):
    n_slab = sends.shape[0]
    slots, feats, span = colors.shape[2:]
    me = lax.axis_index("slab")
    fetch((far_counts, far_colors, far_transmit), (counts, colors, transmit), sems)
    tall[...] = transmit[0, 0].astype(jnp.float32)
    row = lax.broadcasted_iota(jnp.int32, (ROWS, span), 0)
    off = jnp.int32(0)
    for c in range(n_slab):
        tail = jnp.ones((ROWS, span), jnp.float32)
        for r in range(MOST):
            slot = jnp.minimum(off + r, slots - 1)
            sends[c, pl.ds(r * feats, feats), :] = colors[0, 0, slot]
            tail = jnp.where(row == r, tall[pl.ds(slot, 1), :], tail)
        sends[c, pl.ds(MOST * feats, ROWS), :] = tail.astype(jnp.bfloat16)
        off = off + counts[0, me, c]


def plan_kernel(n_slab, slots, *refs):
    far, (table, rows), near, sems = refs[:4], refs[4:6], refs[6:10], refs[10]
    counts, blocks, assign, depth = near
    items = n_slab * MOST
    me = lax.axis_index("slab")
    fetch(far, near, sems)
    row = lax.broadcasted_iota(jnp.int32, rows.shape[1:], 0)
    posv = jnp.zeros(rows.shape[1:], jnp.int32)
    depthv = jnp.zeros(rows.shape[1:], jnp.int32)
    pos, firsts = [], []
    spare_to, spare_from = jnp.int32(0), jnp.int32(items)
    for s in range(n_slab):
        off = jnp.int32(0)
        for c in range(n_slab):
            off = off + jnp.where(c < me, counts[0, s, c], 0)
        count = counts[0, s, me]
        for r in range(MOST):
            i = s * MOST + r
            slot = jnp.minimum(off + r, slots - 1)
            here = assign[0, blocks[0, s, slot]] - me * LB
            here = jnp.where(r < count, here, -1)
            first = jnp.int32(i)
            for j in reversed(range(i)):
                first = jnp.where(pos[j] == here, j, first)
            pos.append(here)
            firsts.append(first)
            spare_to = jnp.where(here >= 0, here, spare_to)
            spare_from = jnp.where(here >= 0, first, spare_from)
            posv = jnp.where(row == i, here, posv)
            depthv = jnp.where(row == i, depth[s], depthv)
    for i in range(items):
        table[0, i] = firsts[i]
        table[1, i] = jnp.where(pos[i] >= 0, pos[i], spare_to)
        table[2, i] = jnp.where(pos[i] >= 0, firsts[i], spare_from)
    rows[0] = posv
    rows[1] = depthv


def silu_half(u):
    return (u + u * jnp.tanh(u)).astype(jnp.bfloat16)


def shade_kernel(n_strip, table, rows, got, w_first, w_mid, w_out, *refs):
    pieces = refs[:n_strip]
    acc, xs, ys, full = refs[n_strip:]
    items, feats, span = acc.shape
    strip_me = lax.axis_index("strip")

    posv, depthv = rows[0], rows[1]
    front = jnp.ones((items, span), jnp.float32)
    total = jnp.ones((items, span), jnp.float32)
    for k in range(items // MOST):
        tail = got[k, pl.ds(MOST * feats, ROWS), :].astype(jnp.float32)
        for r in range(MOST):
            j = k * MOST + r
            trans_j = tail[r : r + 1, :]
            same = posv == posv[j : j + 1, :]
            total = jnp.where(same, total * trans_j, total)
            front = jnp.where(same & (depthv > depthv[j : j + 1, :]), front * trans_j, front)
    acc[...] = jnp.zeros_like(acc)
    for j in range(items):
        k, r = divmod(j, MOST)
        color = got[k, pl.ds(r * feats, feats), :].astype(jnp.float32)
        at = table[0, j]
        acc[at] = acc[at] + front[j : j + 1, :] * color
    total_hi = total.astype(jnp.bfloat16)
    total_lo = (total - total_hi.astype(jnp.float32)).astype(jnp.bfloat16)
    extra = xs.shape[0] - feats
    sub = lax.broadcasted_iota(jnp.int32, (extra, span), 0)
    for i in range(items):
        cols = pl.ds(i * span, span)
        xs[pl.ds(0, feats), cols] = acc[i].astype(jnp.bfloat16)
        hi = total_hi[i : i + 1, :].astype(jnp.float32)
        lo = total_lo[i : i + 1, :].astype(jnp.float32)
        tail = jnp.where(sub == 0, hi, jnp.where(sub == 1, lo, 0.0))
        xs[pl.ds(feats, extra), cols] = tail.astype(jnp.bfloat16)
    cols = pl.ds(items * span, span)
    xs[pl.ds(0, feats), cols] = jnp.zeros((feats, span), jnp.bfloat16)
    xs[pl.ds(feats, extra), cols] = jnp.where(sub == 0, 1.0, 0.0).astype(jnp.bfloat16)

    width = xs.shape[1]
    step = 4 * span
    for start in range(0, width, step):
        size = min(step, width - start)
        x = xs[:, pl.ds(start, size)]
        h = silu_half(
            lax.dot_general(
                w_first[...], x, (((0,), (0,)), ((), ())), preferred_element_type=jnp.float32
            )
        )
        for m in range(w_mid.shape[0]):
            h = silu_half(jnp.dot(w_mid[m], h, preferred_element_type=jnp.float32))
        y = jnp.dot(w_out[...], h, preferred_element_type=jnp.float32).astype(jnp.bfloat16)
        for i in range(size // span):
            ys[start // span + i] = y[:, i * span : (i + 1) * span]

    full[...] = jnp.broadcast_to(ys[items][None], full.shape)
    for i in range(items):
        full[table[1, i]] = ys[table[2, i]]
    tile = pieces[0].shape[0]
    for k in range(n_strip):
        pieces[k][...] = full[pl.ds((strip_me ^ k) * tile, tile)]


def join_kernel(*refs):
    *got, out = refs
    me = lax.axis_index("strip")
    for k in range(len(got)):
        out[0, me ^ k] = got[k][...]


def compact_device(
    n_slab,
    n_strip,
    colors,
    transmit,
    pair_counts,
    slot_block,
    assign,
    depth_rank,
    w_in,
    trans_weight,
    w_mid,
    w_out,
):
    slots, feats, span = colors.shape[2:]
    items = n_slab * MOST
    outs = w_out.shape[0]
    smem = pl.BlockSpec(memory_space=SMEM)
    vmem = pl.BlockSpec(memory_space=VMEM)
    hbm = pl.BlockSpec(memory_space=pltpu.HBM)
    small = pltpu.CompilerParams(vmem_limit_bytes=4 * 1024 * 1024)
    sends = pl.pallas_call(
        pack_kernel,
        out_shape=jax.ShapeDtypeStruct((n_slab, MOST * feats + ROWS, span), jnp.bfloat16),
        in_specs=[hbm] * 3,
        out_specs=vmem,
        scratch_shapes=[
            pltpu.SMEM(pair_counts.shape, jnp.int32),
            pltpu.VMEM(colors.shape, colors.dtype),
            pltpu.VMEM(transmit.shape, transmit.dtype),
            pltpu.VMEM((slots, span), jnp.float32),
            pltpu.SemaphoreType.DMA((3,)),
        ],
        compiler_params=small,
        name="pack",
    )(pair_counts, colors, transmit)
    got = lax.all_to_all(sends, "slab", split_axis=0, concat_axis=0, tiled=True)
    table, rows = pl.pallas_call(
        functools.partial(plan_kernel, n_slab, slots),
        out_shape=[
            jax.ShapeDtypeStruct((3, items), jnp.int32),
            jax.ShapeDtypeStruct((2, items, span), jnp.int32),
        ],
        in_specs=[hbm] * 4,
        out_specs=[smem, vmem],
        scratch_shapes=[
            pltpu.SMEM(a.shape, jnp.int32) for a in (pair_counts, slot_block, assign, depth_rank)
        ]
        + [pltpu.SemaphoreType.DMA((4,))],
        compiler_params=small,
        cost_estimate=pl.CostEstimate(flops=10**5, bytes_accessed=10**6, transcendentals=0),
        name="plan",
    )(pair_counts, slot_block, assign, depth_rank)
    hidden = w_in.shape[0]
    extra = 16
    w_first = jnp.concatenate(
        [
            w_in.T,
            trans_weight[None],
            trans_weight[None],
            jnp.zeros((extra - 2, hidden), jnp.bfloat16),
        ]
    )
    half = jnp.bfloat16(0.5)
    pieces = pl.pallas_call(
        functools.partial(shade_kernel, n_strip),
        out_shape=[jax.ShapeDtypeStruct((LB // n_strip, outs, span), jnp.bfloat16)] * n_strip,
        in_specs=[smem] + [vmem] * 5,
        out_specs=[vmem] * n_strip,
        scratch_shapes=[
            pltpu.VMEM((items, feats, span), jnp.float32),
            pltpu.VMEM((feats + extra, (items + 1) * span), jnp.bfloat16),
            pltpu.VMEM((items + 1, outs, span), jnp.bfloat16),
            pltpu.VMEM((LB, outs, span), jnp.bfloat16),
        ],
        compiler_params=pltpu.CompilerParams(vmem_limit_bytes=16 * 1024 * 1024),
        name="shade",
    )(table, rows, got, w_first * half, w_mid * half, w_out)
    tiles = [pieces[0]] + [
        lax.ppermute(pieces[k], "strip", [(s, s ^ k) for s in range(n_strip)])
        for k in range(1, n_strip)
    ]
    return pl.pallas_call(
        join_kernel,
        out_shape=jax.ShapeDtypeStruct((1, n_strip, LB // n_strip, outs, span), jnp.bfloat16),
        in_specs=[vmem] * n_strip,
        out_specs=pl.BlockSpec(),
        compiler_params=small,
        name="join",
    )(*tiles)


def solution(mesh):
    n_slab, n_strip = mesh.shape["slab"], mesh.shape["strip"]
    placed = (
        P("slab", "strip", None, None, None),
        P("slab", "strip", None, None),
        P("strip", None, None),
        P("strip", None, None),
        P("strip", None),
        P(),
        P(),
        P(),
        P(),
        P(),
    )
    compact = n_strip & (n_strip - 1) == 0 and 4 * MOST * n_slab <= LB
    return jax.shard_map(
        functools.partial(compact_device, n_slab, n_strip) if compact else dense_device,
        mesh=mesh,
        in_specs=placed,
        out_specs=P("slab", None, "strip", None, None),
        check_vma=False,
    )
```

```python
import functools

import jax
import jax.numpy as jnp
from jax import lax
from jax.experimental import pallas as pl
from jax.experimental.pallas import tpu as pltpu
from jax.sharding import PartitionSpec as P

MOST = 2
LB = 128


EXACT_PRECISION = lax.Precision.HIGHEST


def shade_blocks(blend_color, trans_field, w_in, trans_weight, w_mid, w_out):
    summed = jnp.einsum("hf,lfp->lhp", w_in, blend_color, preferred_element_type=jnp.float32)
    summed = summed + trans_weight.astype(jnp.float32)[None, :, None] * trans_field[:, None, :]
    hidden = jax.nn.silu(summed).astype(jnp.bfloat16)
    for layer_index in range(w_mid.shape[0]):
        hidden = jax.nn.silu(
            jnp.einsum(
                "hg,lgp->lhp", w_mid[layer_index], hidden, preferred_element_type=jnp.float32
            )
        ).astype(jnp.bfloat16)
    return jnp.einsum("oh,lhp->lop", w_out, hidden, preferred_element_type=jnp.float32).astype(
        jnp.bfloat16
    )


def dense_device(
    colors, transmit, pair_counts, slot_block, assign, depth_rank, w_in, trans_weight, w_mid, w_out
):
    myself = lax.axis_index("slab")
    counts = pair_counts[0]
    blocks_all = slot_block[0]
    assign_row = assign[0]
    offsets = jnp.cumsum(counts, axis=1) - counts
    slot_rank = jnp.arange(MOST, dtype=jnp.int32)
    my_counts = lax.dynamic_index_in_dim(counts, myself, 0, keepdims=False)
    my_offsets = lax.dynamic_index_in_dim(offsets, myself, 0, keepdims=False)
    send_slots = jnp.where(
        slot_rank[None, :] < my_counts[:, None], my_offsets[:, None] + slot_rank[None, :], 0
    )
    send_color = colors[0, 0][send_slots]
    send_trans = transmit[0, 0][send_slots][:, :, None, :]
    incoming = lax.dynamic_index_in_dim(counts, myself, 1, keepdims=False)
    in_offsets = lax.dynamic_index_in_dim(offsets, myself, 1, keepdims=False)
    live_slot = slot_rank[None, :] < incoming[:, None]
    recv_slots = jnp.where(live_slot, in_offsets[:, None] + slot_rank[None, :], 0)
    recv_blocks = jnp.take_along_axis(blocks_all, recv_slots, axis=1)
    local_pos = assign_row[recv_blocks] - myself * LB
    live_flat = live_slot.reshape(-1)
    local_flat = jnp.where(live_flat, local_pos.reshape(-1), -1)
    depth_flat = jnp.repeat(depth_rank, MOST)
    ahead_table = (
        (local_flat[:, None] == local_flat[None, :])
        & (depth_flat[None, :] < depth_flat[:, None])
        & live_flat[None, :]
    )
    ahead_table = ahead_table.astype(jnp.float32)
    owner_table = (jnp.arange(LB, dtype=jnp.int32)[:, None] == local_flat[None, :]).astype(
        jnp.float32
    )
    got_color = lax.all_to_all(send_color, "slab", split_axis=0, concat_axis=0, tiled=True)
    got_trans = lax.all_to_all(send_trans, "slab", split_axis=0, concat_axis=0, tiled=True)
    pixel_count = got_color.shape[3]
    item_count = got_color.shape[0] * got_color.shape[1]
    log_trans = jnp.log(got_trans.reshape(item_count, pixel_count).astype(jnp.float32))
    log_trans = jnp.where(live_flat[:, None], log_trans, 0.0)
    front_log = jnp.dot(ahead_table, log_trans, precision=EXACT_PRECISION)
    front_share = jnp.where(live_flat[:, None], jnp.exp(front_log), 0.0)
    weighted = front_share[:, None, :] * got_color.reshape(item_count, -1, pixel_count).astype(
        jnp.float32
    )
    blend_sum = jnp.dot(owner_table, weighted.reshape(item_count, -1), precision=EXACT_PRECISION)
    blend_color = blend_sum.reshape(LB, -1, pixel_count).astype(jnp.bfloat16)
    trans_field = jnp.exp(jnp.dot(owner_table, log_trans, precision=EXACT_PRECISION))
    shaded = shade_blocks(blend_color, trans_field, w_in, trans_weight, w_mid, w_out)
    display_tiles = lax.all_to_all(shaded[None], "strip", split_axis=1, concat_axis=0, tiled=True)
    return display_tiles[None]


SMEM = pltpu.SMEM
VMEM = pltpu.VMEM
ROWS = 8


def fetch(sources, targets, sems):
    copies = [
        pltpu.make_async_copy(source, target, sems.at[i])
        for i, (source, target) in enumerate(zip(sources, targets))
    ]
    for copy in copies:
        copy.start()
    for copy in copies:
        copy.wait()


def pack_kernel(far_counts, far_colors, far_transmit, sends, counts, colors, transmit, tall, sems):
    n_slab = sends.shape[0]
    slots, feats, span = colors.shape[2:]
    me = lax.axis_index("slab")
    fetch((far_counts, far_colors, far_transmit), (counts, colors, transmit), sems)
    tall[...] = transmit[0, 0].astype(jnp.float32)
    row = lax.broadcasted_iota(jnp.int32, (ROWS, span), 0)
    off = jnp.int32(0)
    for c in range(n_slab):
        tail = jnp.ones((ROWS, span), jnp.float32)
        for r in range(MOST):
            slot = jnp.minimum(off + r, slots - 1)
            sends[c, pl.ds(r * feats, feats), :] = colors[0, 0, slot]
            tail = jnp.where(row == r, tall[pl.ds(slot, 1), :], tail)
        sends[c, pl.ds(MOST * feats, ROWS), :] = tail.astype(jnp.bfloat16)
        off = off + counts[0, me, c]


def plan_kernel(n_slab, slots, *refs):
    far, (table, rows), near, sems = refs[:4], refs[4:6], refs[6:10], refs[10]
    counts, blocks, assign, depth = near
    items = n_slab * MOST
    me = lax.axis_index("slab")
    fetch(far, near, sems)
    row = lax.broadcasted_iota(jnp.int32, rows.shape[1:], 0)
    posv = jnp.zeros(rows.shape[1:], jnp.int32)
    depthv = jnp.zeros(rows.shape[1:], jnp.int32)
    pos, firsts = [], []
    spare_to, spare_from = jnp.int32(0), jnp.int32(items)
    for s in range(n_slab):
        off = jnp.int32(0)
        for c in range(n_slab):
            off = off + jnp.where(c < me, counts[0, s, c], 0)
        count = counts[0, s, me]
        for r in range(MOST):
            i = s * MOST + r
            slot = jnp.minimum(off + r, slots - 1)
            here = assign[0, blocks[0, s, slot]] - me * LB
            here = jnp.where(r < count, here, -1)
            first = jnp.int32(i)
            for j in reversed(range(i)):
                first = jnp.where(pos[j] == here, j, first)
            pos.append(here)
            firsts.append(first)
            spare_to = jnp.where(here >= 0, here, spare_to)
            spare_from = jnp.where(here >= 0, first, spare_from)
            posv = jnp.where(row == i, here, posv)
            depthv = jnp.where(row == i, depth[s], depthv)
    for i in range(items):
        table[0, i] = firsts[i]
        table[1, i] = jnp.where(pos[i] >= 0, pos[i], spare_to)
        table[2, i] = jnp.where(pos[i] >= 0, firsts[i], spare_from)
    rows[0] = posv
    rows[1] = depthv


def silu_half(u):
    return (u + u * jnp.tanh(u)).astype(jnp.bfloat16)


def shade_kernel(n_strip, table, rows, got, w_first, w_mid, w_out, *refs):
    pieces = refs[:n_strip]
    acc, xs, ys, full = refs[n_strip:]
    items, feats, span = acc.shape
    strip_me = lax.axis_index("strip")

    posv, depthv = rows[0], rows[1]
    front = jnp.ones((items, span), jnp.float32)
    total = jnp.ones((items, span), jnp.float32)
    for k in range(items // MOST):
        tail = got[k, pl.ds(MOST * feats, ROWS), :].astype(jnp.float32)
        for r in range(MOST):
            j = k * MOST + r
            trans_j = tail[r : r + 1, :]
            same = posv == posv[j : j + 1, :]
            total = jnp.where(same, total * trans_j, total)
            front = jnp.where(same & (depthv > depthv[j : j + 1, :]), front * trans_j, front)
    acc[...] = jnp.zeros_like(acc)
    for j in range(items):
        k, r = divmod(j, MOST)
        color = got[k, pl.ds(r * feats, feats), :].astype(jnp.float32)
        at = table[0, j]
        acc[at] = acc[at] + front[j : j + 1, :] * color
    total_hi = total.astype(jnp.bfloat16)
    total_lo = (total - total_hi.astype(jnp.float32)).astype(jnp.bfloat16)
    extra = xs.shape[0] - feats
    sub = lax.broadcasted_iota(jnp.int32, (extra, span), 0)
    for i in range(items):
        cols = pl.ds(i * span, span)
        xs[pl.ds(0, feats), cols] = acc[i].astype(jnp.bfloat16)
        hi = total_hi[i : i + 1, :].astype(jnp.float32)
        lo = total_lo[i : i + 1, :].astype(jnp.float32)
        tail = jnp.where(sub == 0, hi, jnp.where(sub == 1, lo, 0.0))
        xs[pl.ds(feats, extra), cols] = tail.astype(jnp.bfloat16)
    cols = pl.ds(items * span, span)
    xs[pl.ds(0, feats), cols] = jnp.zeros((feats, span), jnp.bfloat16)
    xs[pl.ds(feats, extra), cols] = jnp.where(sub == 0, 1.0, 0.0).astype(jnp.bfloat16)

    width = xs.shape[1]
    step = 4 * span
    for start in range(0, width, step):
        size = min(step, width - start)
        x = xs[:, pl.ds(start, size)]
        h = silu_half(
            lax.dot_general(
                x, w_first[...], (((0,), (0,)), ((), ())), preferred_element_type=jnp.float32
            )
        )
        for m in range(w_mid.shape[0]):
            h = silu_half(jnp.dot(h, w_mid[m], preferred_element_type=jnp.float32))
        y = lax.dot_general(
            w_out[...], h, (((1,), (1,)), ((), ())), preferred_element_type=jnp.float32
        ).astype(jnp.bfloat16)
        for i in range(size // span):
            ys[start // span + i] = y[:, i * span : (i + 1) * span]

    full[...] = jnp.broadcast_to(ys[items][None], full.shape)
    for i in range(items):
        full[table[1, i]] = ys[table[2, i]]
    tile = pieces[0].shape[0]
    for k in range(n_strip):
        pieces[k][...] = full[pl.ds((strip_me ^ k) * tile, tile)]


def join_kernel(*refs):
    *got, out = refs
    me = lax.axis_index("strip")
    for k in range(len(got)):
        out[0, me ^ k] = got[k][...]


def compact_device(
    n_slab,
    n_strip,
    colors,
    transmit,
    pair_counts,
    slot_block,
    assign,
    depth_rank,
    w_in,
    trans_weight,
    w_mid,
    w_out,
):
    slots, feats, span = colors.shape[2:]
    items = n_slab * MOST
    outs = w_out.shape[0]
    smem = pl.BlockSpec(memory_space=SMEM)
    vmem = pl.BlockSpec(memory_space=VMEM)
    hbm = pl.BlockSpec(memory_space=pltpu.HBM)
    small = pltpu.CompilerParams(vmem_limit_bytes=4 * 1024 * 1024)
    sends = pl.pallas_call(
        pack_kernel,
        out_shape=jax.ShapeDtypeStruct((n_slab, MOST * feats + ROWS, span), jnp.bfloat16),
        in_specs=[hbm] * 3,
        out_specs=vmem,
        scratch_shapes=[
            pltpu.SMEM(pair_counts.shape, jnp.int32),
            pltpu.VMEM(colors.shape, colors.dtype),
            pltpu.VMEM(transmit.shape, transmit.dtype),
            pltpu.VMEM((slots, span), jnp.float32),
            pltpu.SemaphoreType.DMA((3,)),
        ],
        name="pack",
    )(pair_counts, colors, transmit)
    got = lax.all_to_all(sends, "slab", split_axis=0, concat_axis=0, tiled=True)
    table, rows = pl.pallas_call(
        functools.partial(plan_kernel, n_slab, slots),
        out_shape=[
            jax.ShapeDtypeStruct((3, items), jnp.int32),
            jax.ShapeDtypeStruct((2, items, span), jnp.int32),
        ],
        in_specs=[hbm] * 4,
        out_specs=[smem, vmem],
        scratch_shapes=[
            pltpu.SMEM(a.shape, jnp.int32) for a in (pair_counts, slot_block, assign, depth_rank)
        ]
        + [pltpu.SemaphoreType.DMA((4,))],
        cost_estimate=pl.CostEstimate(flops=10**5, bytes_accessed=10**6, transcendentals=0),
        name="plan",
    )(pair_counts, slot_block, assign, depth_rank)
    hidden = w_in.shape[0]
    extra = 16
    w_first = jnp.concatenate(
        [
            w_in.T,
            trans_weight[None],
            trans_weight[None],
            jnp.zeros((extra - 2, hidden), jnp.bfloat16),
        ]
    )
    half = jnp.bfloat16(0.5)
    pieces = pl.pallas_call(
        functools.partial(shade_kernel, n_strip),
        out_shape=[jax.ShapeDtypeStruct((LB // n_strip, outs, span), jnp.bfloat16)] * n_strip,
        in_specs=[smem] + [vmem] * 5,
        out_specs=[vmem] * n_strip,
        scratch_shapes=[
            pltpu.VMEM((items, feats, span), jnp.float32),
            pltpu.VMEM((feats + extra, (items + 1) * span), jnp.bfloat16),
            pltpu.VMEM((items + 1, outs, span), jnp.bfloat16),
            pltpu.VMEM((LB, outs, span), jnp.bfloat16),
        ],
        compiler_params=pltpu.CompilerParams(vmem_limit_bytes=16 * 1024 * 1024),
        name="shade",
    )(table, rows, got, w_first * half, jnp.swapaxes(w_mid, 1, 2) * half, w_out)
    tiles = [pieces[0]] + [
        lax.ppermute(pieces[k], "strip", [(s, s ^ k) for s in range(n_strip)])
        for k in range(1, n_strip)
    ]
    return pl.pallas_call(
        join_kernel,
        out_shape=jax.ShapeDtypeStruct((1, n_strip, LB // n_strip, outs, span), jnp.bfloat16),
        in_specs=[vmem] * n_strip,
        out_specs=pl.BlockSpec(),
        compiler_params=small,
        name="join",
    )(*tiles)


def solution(mesh):
    n_slab, n_strip = mesh.shape["slab"], mesh.shape["strip"]
    placed = (
        P("slab", "strip", None, None, None),
        P("slab", "strip", None, None),
        P("strip", None, None),
        P("strip", None, None),
        P("strip", None),
        P(),
        P(),
        P(),
        P(),
        P(),
    )
    compact = n_strip & (n_strip - 1) == 0 and 4 * MOST * n_slab <= LB
    return jax.shard_map(
        functools.partial(compact_device, n_slab, n_strip) if compact else dense_device,
        mesh=mesh,
        in_specs=placed,
        out_specs=P("slab", None, "strip", None, None),
        check_vma=False,
    )
```

```python
import functools

import jax
import jax.numpy as jnp
from jax import lax
from jax.experimental import pallas as pl
from jax.experimental.pallas import tpu as pltpu
from jax.sharding import PartitionSpec as P

MOST = 2
LB = 128


EXACT_PRECISION = lax.Precision.HIGHEST


def shade_blocks(blend_color, trans_field, w_in, trans_weight, w_mid, w_out):
    summed = jnp.einsum("hf,lfp->lhp", w_in, blend_color, preferred_element_type=jnp.float32)
    summed = summed + trans_weight.astype(jnp.float32)[None, :, None] * trans_field[:, None, :]
    hidden = jax.nn.silu(summed).astype(jnp.bfloat16)
    for layer_index in range(w_mid.shape[0]):
        hidden = jax.nn.silu(
            jnp.einsum(
                "hg,lgp->lhp", w_mid[layer_index], hidden, preferred_element_type=jnp.float32
            )
        ).astype(jnp.bfloat16)
    return jnp.einsum("oh,lhp->lop", w_out, hidden, preferred_element_type=jnp.float32).astype(
        jnp.bfloat16
    )


def dense_device(
    colors, transmit, pair_counts, slot_block, assign, depth_rank, w_in, trans_weight, w_mid, w_out
):
    myself = lax.axis_index("slab")
    counts = pair_counts[0]
    blocks_all = slot_block[0]
    assign_row = assign[0]
    offsets = jnp.cumsum(counts, axis=1) - counts
    slot_rank = jnp.arange(MOST, dtype=jnp.int32)
    my_counts = lax.dynamic_index_in_dim(counts, myself, 0, keepdims=False)
    my_offsets = lax.dynamic_index_in_dim(offsets, myself, 0, keepdims=False)
    send_slots = jnp.where(
        slot_rank[None, :] < my_counts[:, None], my_offsets[:, None] + slot_rank[None, :], 0
    )
    send_color = colors[0, 0][send_slots]
    send_trans = transmit[0, 0][send_slots][:, :, None, :]
    incoming = lax.dynamic_index_in_dim(counts, myself, 1, keepdims=False)
    in_offsets = lax.dynamic_index_in_dim(offsets, myself, 1, keepdims=False)
    live_slot = slot_rank[None, :] < incoming[:, None]
    recv_slots = jnp.where(live_slot, in_offsets[:, None] + slot_rank[None, :], 0)
    recv_blocks = jnp.take_along_axis(blocks_all, recv_slots, axis=1)
    local_pos = assign_row[recv_blocks] - myself * LB
    live_flat = live_slot.reshape(-1)
    local_flat = jnp.where(live_flat, local_pos.reshape(-1), -1)
    depth_flat = jnp.repeat(depth_rank, MOST)
    ahead_table = (
        (local_flat[:, None] == local_flat[None, :])
        & (depth_flat[None, :] < depth_flat[:, None])
        & live_flat[None, :]
    )
    ahead_table = ahead_table.astype(jnp.float32)
    owner_table = (jnp.arange(LB, dtype=jnp.int32)[:, None] == local_flat[None, :]).astype(
        jnp.float32
    )
    got_color = lax.all_to_all(send_color, "slab", split_axis=0, concat_axis=0, tiled=True)
    got_trans = lax.all_to_all(send_trans, "slab", split_axis=0, concat_axis=0, tiled=True)
    pixel_count = got_color.shape[3]
    item_count = got_color.shape[0] * got_color.shape[1]
    log_trans = jnp.log(got_trans.reshape(item_count, pixel_count).astype(jnp.float32))
    log_trans = jnp.where(live_flat[:, None], log_trans, 0.0)
    front_log = jnp.dot(ahead_table, log_trans, precision=EXACT_PRECISION)
    front_share = jnp.where(live_flat[:, None], jnp.exp(front_log), 0.0)
    weighted = front_share[:, None, :] * got_color.reshape(item_count, -1, pixel_count).astype(
        jnp.float32
    )
    blend_sum = jnp.dot(owner_table, weighted.reshape(item_count, -1), precision=EXACT_PRECISION)
    blend_color = blend_sum.reshape(LB, -1, pixel_count).astype(jnp.bfloat16)
    trans_field = jnp.exp(jnp.dot(owner_table, log_trans, precision=EXACT_PRECISION))
    shaded = shade_blocks(blend_color, trans_field, w_in, trans_weight, w_mid, w_out)
    display_tiles = lax.all_to_all(shaded[None], "strip", split_axis=1, concat_axis=0, tiled=True)
    return display_tiles[None]


SMEM = pltpu.SMEM
VMEM = pltpu.VMEM
ROWS = 8
GROUP = 4


def fetch(sources, targets, sems):
    copies = [
        pltpu.make_async_copy(source, target, sems.at[i])
        for i, (source, target) in enumerate(zip(sources, targets))
    ]
    for copy in copies:
        copy.start()
    for copy in copies:
        copy.wait()


def pack_kernel(far_counts, far_colors, far_transmit, sends, counts, colors, transmit, tall, sems):
    n_slab = sends.shape[0]
    slots, feats, span = colors.shape[2:]
    me = lax.axis_index("slab")
    fetch((far_counts, far_colors, far_transmit), (counts, colors, transmit), sems)
    tall[...] = transmit[0, 0].astype(jnp.float32)
    row = lax.broadcasted_iota(jnp.int32, (ROWS, span), 0)
    off = jnp.int32(0)
    for c in range(n_slab):
        tail = jnp.ones((ROWS, span), jnp.float32)
        for r in range(MOST):
            slot = jnp.minimum(off + r, slots - 1)
            sends[c, pl.ds(r * feats, feats), :] = colors[0, 0, slot]
            tail = jnp.where(row == r, tall[pl.ds(slot, 1), :], tail)
        sends[c, pl.ds(MOST * feats, ROWS), :] = tail.astype(jnp.bfloat16)
        off = off + counts[0, me, c]


def plan_kernel(n_slab, slots, *refs):
    far, (w_in, trans_weight), (table, rows, codes, w_first) = refs[:4], refs[4:6], refs[6:10]
    near, sems = refs[10:14], refs[14]
    counts, blocks, assign, depth = near
    items = n_slab * MOST
    outs = codes.shape[1] // (2 * items)
    me = lax.axis_index("slab")
    copies = [pltpu.make_async_copy(far[i], near[i], sems.at[i]) for i in range(4)]
    for copy in copies:
        copy.start()
    feats, hidden = w_in.shape
    half_in = (w_in[...].astype(jnp.float32) * 0.5).astype(jnp.bfloat16)
    half_trans = trans_weight[...].astype(jnp.float32) * 0.5
    sub = lax.broadcasted_iota(jnp.int32, (16, hidden), 0)
    w_first[...] = jnp.zeros_like(w_first)
    for a in range(GROUP):
        w_first[a, pl.ds(a * feats, feats), :] = half_in
        tail = jnp.where(sub // 2 == a, half_trans, 0.0)
        w_first[a, pl.ds(GROUP * feats, 16), :] = tail.astype(jnp.bfloat16)
    for copy in copies:
        copy.wait()
    row = lax.broadcasted_iota(jnp.int32, rows.shape[1:], 0)
    item_lane = lax.broadcasted_iota(jnp.int32, codes.shape, 1) // outs
    posv = jnp.zeros(rows.shape[1:], jnp.int32)
    depthv = jnp.zeros(rows.shape[1:], jnp.int32)
    codev = jnp.full(codes.shape, -1, jnp.int32)
    pos = []
    for s in range(n_slab):
        off = jnp.int32(0)
        for c in range(n_slab):
            off = off + jnp.where(c < me, counts[0, s, c], 0)
        count = counts[0, s, me]
        for r in range(MOST):
            i = s * MOST + r
            slot = jnp.minimum(off + r, slots - 1)
            here = assign[0, blocks[0, s, slot]] - me * LB
            here = jnp.where(r < count, here, -1)
            first = jnp.int32(i)
            for j in reversed(range(i)):
                first = jnp.where(pos[j] == here, j, first)
            pos.append(here)
            table[0, i] = first
            posv = jnp.where(row == i, here, posv)
            depthv = jnp.where(row == i, depth[s], depthv)
            codev = jnp.where(item_lane == i, jnp.where(first == i, here, -1), codev)
    rows[0] = posv
    rows[1] = depthv
    codes[...] = codev.astype(jnp.float32).astype(jnp.bfloat16)


def silu_half(u):
    return (u + u * jnp.tanh(u)).astype(jnp.bfloat16)


def later_layers(h, w_mid, w_out):
    for m in range(w_mid.shape[0]):
        h = silu_half(jnp.dot(h, w_mid[m], preferred_element_type=jnp.float32))
    y = lax.dot_general(
        w_out[...], h, (((1,), (1,)), ((), ())), preferred_element_type=jnp.float32
    )
    return y.astype(jnp.bfloat16).astype(jnp.float32)


def empty_kernel(trans_weight, w_mid, w_out, out):
    u = trans_weight[...].astype(jnp.float32) * 0.5
    h = silu_half(jnp.broadcast_to(u, (out.shape[1], u.shape[1])))
    y = later_layers(h, w_mid, w_out)
    outs = w_out.shape[0]
    for at in range(0, out.shape[0], outs):
        out[pl.ds(at, outs), :] = y


def shade_kernel(table, rows, codes, got, w_first, w_mid, w_out, out, acc, xt, ys):
    items, feats, span = acc.shape
    outs = w_out.shape[0]

    posv, depthv = rows[0], rows[1]
    front = jnp.ones((items, span), jnp.float32)
    total = jnp.ones((items, span), jnp.float32)
    for k in range(items // MOST):
        tail = got[k, pl.ds(MOST * feats, ROWS), :].astype(jnp.float32)
        for r in range(MOST):
            j = k * MOST + r
            trans_j = tail[r : r + 1, :]
            same = posv == posv[j : j + 1, :]
            total = jnp.where(same, total * trans_j, total)
            front = jnp.where(same & (depthv > depthv[j : j + 1, :]), front * trans_j, front)
    acc[...] = jnp.zeros_like(acc)
    for j in range(items):
        k, r = divmod(j, MOST)
        color = got[k, pl.ds(r * feats, feats), :].astype(jnp.float32)
        at = table[0, j]
        acc[at] = acc[at] + front[j : j + 1, :] * color
    total_hi = total.astype(jnp.bfloat16).astype(jnp.float32)
    total_lo = total - total_hi
    groups = items // GROUP
    sub = lax.broadcasted_iota(jnp.int32, (16, span), 0)
    xt[...] = jnp.zeros_like(xt)
    for q in range(groups):
        block = acc[pl.ds(q * GROUP, GROUP)].reshape(GROUP * feats, span)
        tail = jnp.zeros((16, span), jnp.float32)
        for a in range(GROUP):
            i = q * GROUP + a
            tail = jnp.where(sub == 2 * a, total_hi[i : i + 1, :], tail)
            tail = jnp.where(sub == 2 * a + 1, total_lo[i : i + 1, :], tail)
        lines = pl.ds(q * span, span)
        xt[lines, pl.ds(0, GROUP * feats)] = block.T.astype(jnp.bfloat16)
        xt[lines, pl.ds(GROUP * feats, 16)] = tail.T.astype(jnp.bfloat16)

    x = xt[...]
    for start in range(0, GROUP, 2):
        h = jnp.concatenate(
            [
                silu_half(jnp.dot(x, w_first[a], preferred_element_type=jnp.float32))
                for a in range(start, start + 2)
            ]
        )
        y = later_layers(h, w_mid, w_out)
        for a in range(start, start + 2):
            for q in range(groups):
                at = ((a - start) * groups + q) * span
                ys[pl.ds((q * GROUP + a) * outs, outs), :] = y[:, at : at + span]
    out[pl.ds(0, items * outs), :] = ys[...].astype(jnp.bfloat16)
    out[pl.ds(items * outs, ROWS), :] = codes[...]


def join_kernel(*refs):
    *got, empty, out = refs
    _, n_strip, tile, outs, span = out.shape
    lines = tile * outs
    count = got[0].shape[0] - ROWS
    me = lax.axis_index("strip")
    want = lax.broadcasted_iota(jnp.int32, (lines, count), 0) + me * lines
    chan = lax.broadcasted_iota(jnp.int32, (lines, count), 1) % outs
    filler = jnp.concatenate([empty[...]] * (lines // ROWS))
    ones = jnp.ones((count, span), jnp.bfloat16)
    for k in range(n_strip):
        pos = got[k][pl.ds(count, ROWS), :].astype(jnp.float32)[:1, :count].astype(jnp.int32)
        hit = pos * outs + chan == want
        pick = jnp.where(hit, 1.0, 0.0).astype(jnp.bfloat16)
        blocks = got[k][pl.ds(0, count), :]
        placed = jnp.dot(pick, blocks, preferred_element_type=jnp.float32)
        filled = jnp.dot(pick, ones, preferred_element_type=jnp.float32)
        value = jnp.where(filled > 0.5, placed, filler)
        out[0, me ^ k] = value.reshape(tile, outs, span).astype(jnp.bfloat16)


def compact_device(
    n_slab,
    n_strip,
    colors,
    transmit,
    pair_counts,
    slot_block,
    assign,
    depth_rank,
    w_in,
    trans_weight,
    w_mid,
    w_out,
):
    slots, feats, span = colors.shape[2:]
    items = n_slab * MOST
    outs = w_out.shape[0]
    smem = pl.BlockSpec(memory_space=SMEM)
    vmem = pl.BlockSpec(memory_space=VMEM)
    hbm = pl.BlockSpec(memory_space=pltpu.HBM)
    small = pltpu.CompilerParams(vmem_limit_bytes=4 * 1024 * 1024)
    sends = pl.pallas_call(
        pack_kernel,
        out_shape=jax.ShapeDtypeStruct((n_slab, MOST * feats + ROWS, span), jnp.bfloat16),
        in_specs=[hbm] * 3,
        out_specs=vmem,
        scratch_shapes=[
            pltpu.SMEM(pair_counts.shape, jnp.int32),
            pltpu.VMEM(colors.shape, colors.dtype),
            pltpu.VMEM(transmit.shape, transmit.dtype),
            pltpu.VMEM((slots, span), jnp.float32),
            pltpu.SemaphoreType.DMA((3,)),
        ],
        name="pack",
    )(pair_counts, colors, transmit)
    got = lax.all_to_all(sends, "slab", split_axis=0, concat_axis=0, tiled=True)
    hidden = w_in.shape[0]
    rough = pl.CostEstimate(flops=10**5, bytes_accessed=10**6, transcendentals=0)
    roomy = pltpu.CompilerParams(vmem_limit_bytes=16 * 1024 * 1024)
    trans_row = trans_weight[None]
    table, rows, codes, w_first = pl.pallas_call(
        functools.partial(plan_kernel, n_slab, slots),
        out_shape=[
            jax.ShapeDtypeStruct((1, items), jnp.int32),
            jax.ShapeDtypeStruct((2, items, span), jnp.int32),
            jax.ShapeDtypeStruct((ROWS, span), jnp.bfloat16),
            jax.ShapeDtypeStruct((GROUP, 2 * GROUP * feats, hidden), jnp.bfloat16),
        ],
        in_specs=[hbm] * 4 + [vmem] * 2,
        out_specs=[smem] + [vmem] * 3,
        scratch_shapes=[
            pltpu.SMEM(a.shape, jnp.int32) for a in (pair_counts, slot_block, assign, depth_rank)
        ]
        + [pltpu.SemaphoreType.DMA((4,))],
        cost_estimate=rough,
        name="plan",
    )(pair_counts, slot_block, assign, depth_rank, w_in.T, trans_row)
    w_later = jnp.swapaxes(w_mid, 1, 2) * jnp.bfloat16(0.5)
    empty = pl.pallas_call(
        empty_kernel,
        out_shape=jax.ShapeDtypeStruct((ROWS, span), jnp.float32),
        in_specs=[vmem] * 3,
        out_specs=vmem,
        compiler_params=roomy,
        cost_estimate=rough,
        name="empty",
    )(trans_row, w_later, w_out)
    shaded = pl.pallas_call(
        shade_kernel,
        out_shape=jax.ShapeDtypeStruct((items * outs + ROWS, span), jnp.bfloat16),
        in_specs=[smem] + [vmem] * 6,
        out_specs=vmem,
        scratch_shapes=[
            pltpu.VMEM((items, feats, span), jnp.float32),
            pltpu.VMEM((items // GROUP * span, 2 * GROUP * feats), jnp.bfloat16),
            pltpu.VMEM((items * outs, span), jnp.float32),
        ],
        compiler_params=roomy,
        name="shade",
    )(table, rows, codes, got, w_first, w_later, w_out)
    tiles = {0: shaded}
    for k in sorted(range(1, n_strip), key=lambda k: k % 2 == 1 and k < 2):
        tiles[k] = lax.ppermute(shaded, "strip", [(s, s ^ k) for s in range(n_strip)])
    return pl.pallas_call(
        join_kernel,
        out_shape=jax.ShapeDtypeStruct((1, n_strip, LB // n_strip, outs, span), jnp.bfloat16),
        in_specs=[vmem] * (n_strip + 1),
        out_specs=pl.BlockSpec(),
        compiler_params=small,
        name="join",
    )(*[tiles[k] for k in range(n_strip)], empty)


def solution(mesh):
    n_slab, n_strip = mesh.shape["slab"], mesh.shape["strip"]
    placed = (
        P("slab", "strip", None, None, None),
        P("slab", "strip", None, None),
        P("strip", None, None),
        P("strip", None, None),
        P("strip", None),
        P(),
        P(),
        P(),
        P(),
        P(),
    )
    compact = n_strip & (n_strip - 1) == 0 and 4 * MOST * n_slab <= LB
    return jax.shard_map(
        functools.partial(compact_device, n_slab, n_strip) if compact else dense_device,
        mesh=mesh,
        in_specs=placed,
        out_specs=P("slab", None, "strip", None, None),
        check_vma=False,
    )
```

```python
import functools

import jax
import jax.numpy as jnp
from jax import lax
from jax.experimental import pallas as pl
from jax.experimental.pallas import tpu as pltpu
from jax.sharding import PartitionSpec as P

MOST = 2
LB = 128


EXACT_PRECISION = lax.Precision.HIGHEST


def shade_blocks(blend_color, trans_field, w_in, trans_weight, w_mid, w_out):
    summed = jnp.einsum("hf,lfp->lhp", w_in, blend_color, preferred_element_type=jnp.float32)
    summed = summed + trans_weight.astype(jnp.float32)[None, :, None] * trans_field[:, None, :]
    hidden = jax.nn.silu(summed).astype(jnp.bfloat16)
    for layer_index in range(w_mid.shape[0]):
        hidden = jax.nn.silu(
            jnp.einsum(
                "hg,lgp->lhp", w_mid[layer_index], hidden, preferred_element_type=jnp.float32
            )
        ).astype(jnp.bfloat16)
    return jnp.einsum("oh,lhp->lop", w_out, hidden, preferred_element_type=jnp.float32).astype(
        jnp.bfloat16
    )


def dense_device(
    colors, transmit, pair_counts, slot_block, assign, depth_rank, w_in, trans_weight, w_mid, w_out
):
    myself = lax.axis_index("slab")
    counts = pair_counts[0]
    blocks_all = slot_block[0]
    assign_row = assign[0]
    offsets = jnp.cumsum(counts, axis=1) - counts
    slot_rank = jnp.arange(MOST, dtype=jnp.int32)
    my_counts = lax.dynamic_index_in_dim(counts, myself, 0, keepdims=False)
    my_offsets = lax.dynamic_index_in_dim(offsets, myself, 0, keepdims=False)
    send_slots = jnp.where(
        slot_rank[None, :] < my_counts[:, None], my_offsets[:, None] + slot_rank[None, :], 0
    )
    send_color = colors[0, 0][send_slots]
    send_trans = transmit[0, 0][send_slots][:, :, None, :]
    incoming = lax.dynamic_index_in_dim(counts, myself, 1, keepdims=False)
    in_offsets = lax.dynamic_index_in_dim(offsets, myself, 1, keepdims=False)
    live_slot = slot_rank[None, :] < incoming[:, None]
    recv_slots = jnp.where(live_slot, in_offsets[:, None] + slot_rank[None, :], 0)
    recv_blocks = jnp.take_along_axis(blocks_all, recv_slots, axis=1)
    local_pos = assign_row[recv_blocks] - myself * LB
    live_flat = live_slot.reshape(-1)
    local_flat = jnp.where(live_flat, local_pos.reshape(-1), -1)
    depth_flat = jnp.repeat(depth_rank, MOST)
    ahead_table = (
        (local_flat[:, None] == local_flat[None, :])
        & (depth_flat[None, :] < depth_flat[:, None])
        & live_flat[None, :]
    )
    ahead_table = ahead_table.astype(jnp.float32)
    owner_table = (jnp.arange(LB, dtype=jnp.int32)[:, None] == local_flat[None, :]).astype(
        jnp.float32
    )
    got_color = lax.all_to_all(send_color, "slab", split_axis=0, concat_axis=0, tiled=True)
    got_trans = lax.all_to_all(send_trans, "slab", split_axis=0, concat_axis=0, tiled=True)
    pixel_count = got_color.shape[3]
    item_count = got_color.shape[0] * got_color.shape[1]
    log_trans = jnp.log(got_trans.reshape(item_count, pixel_count).astype(jnp.float32))
    log_trans = jnp.where(live_flat[:, None], log_trans, 0.0)
    front_log = jnp.dot(ahead_table, log_trans, precision=EXACT_PRECISION)
    front_share = jnp.where(live_flat[:, None], jnp.exp(front_log), 0.0)
    weighted = front_share[:, None, :] * got_color.reshape(item_count, -1, pixel_count).astype(
        jnp.float32
    )
    blend_sum = jnp.dot(owner_table, weighted.reshape(item_count, -1), precision=EXACT_PRECISION)
    blend_color = blend_sum.reshape(LB, -1, pixel_count).astype(jnp.bfloat16)
    trans_field = jnp.exp(jnp.dot(owner_table, log_trans, precision=EXACT_PRECISION))
    shaded = shade_blocks(blend_color, trans_field, w_in, trans_weight, w_mid, w_out)
    display_tiles = lax.all_to_all(shaded[None], "strip", split_axis=1, concat_axis=0, tiled=True)
    return display_tiles[None]


SMEM = pltpu.SMEM
VMEM = pltpu.VMEM
ROWS = 8
GROUP = 4


def fetch(sources, targets, sems):
    copies = [
        pltpu.make_async_copy(source, target, sems.at[i])
        for i, (source, target) in enumerate(zip(sources, targets))
    ]
    for copy in copies:
        copy.start()
    for copy in copies:
        copy.wait()


def pack_kernel(far_counts, far_colors, far_transmit, sends, counts, colors, transmit, tall, sems):
    n_slab = sends.shape[0]
    slots, feats, span = colors.shape[2:]
    me = lax.axis_index("slab")
    fetch((far_counts, far_colors, far_transmit), (counts, colors, transmit), sems)
    tall[...] = transmit[0, 0].astype(jnp.float32)
    row = lax.broadcasted_iota(jnp.int32, (ROWS, span), 0)
    off = jnp.int32(0)
    for c in range(n_slab):
        tail = jnp.ones((ROWS, span), jnp.float32)
        for r in range(MOST):
            slot = jnp.minimum(off + r, slots - 1)
            sends[c, pl.ds(r * feats, feats), :] = colors[0, 0, slot]
            tail = jnp.where(row == r, tall[pl.ds(slot, 1), :], tail)
        sends[c, pl.ds(MOST * feats, ROWS), :] = tail.astype(jnp.bfloat16)
        off = off + counts[0, me, c]


def plan_kernel(n_slab, slots, *refs):
    (counts, blocks, assign, depth), (table, rows, codes) = refs[:4], refs[4:]
    items = n_slab * MOST
    outs = codes.shape[1] // (2 * items)
    me = lax.axis_index("slab")
    row = lax.broadcasted_iota(jnp.int32, rows.shape[1:], 0)
    item_lane = lax.broadcasted_iota(jnp.int32, codes.shape, 1) // outs
    posv = jnp.zeros(rows.shape[1:], jnp.int32)
    depthv = jnp.zeros(rows.shape[1:], jnp.int32)
    codev = jnp.full(codes.shape, -1, jnp.int32)
    pos = []
    for s in range(n_slab):
        off = jnp.int32(0)
        for c in range(n_slab):
            off = off + jnp.where(c < me, counts[0, s, c], 0)
        count = counts[0, s, me]
        for r in range(MOST):
            i = s * MOST + r
            slot = jnp.minimum(off + r, slots - 1)
            here = assign[0, blocks[0, s, slot]] - me * LB
            here = jnp.where(r < count, here, -1)
            first = jnp.int32(i)
            for j in reversed(range(i)):
                first = jnp.where(pos[j] == here, j, first)
            pos.append(here)
            table[0, i] = first
            posv = jnp.where(row == i, here, posv)
            depthv = jnp.where(row == i, depth[s], depthv)
            codev = jnp.where(item_lane == i, jnp.where(first == i, here, -1), codev)
    rows[0] = posv
    rows[1] = depthv
    codes[...] = codev.astype(jnp.float32).astype(jnp.bfloat16)


def place_kernel(w_in, trans_weight, w_first):
    feats, hidden = w_in.shape
    half_in = (w_in[...].astype(jnp.float32) * 0.5).astype(jnp.bfloat16)
    half_trans = trans_weight[...].astype(jnp.float32) * 0.5
    sub = lax.broadcasted_iota(jnp.int32, (16, hidden), 0)
    w_first[...] = jnp.zeros_like(w_first)
    for a in range(GROUP):
        w_first[a, pl.ds(a * feats, feats), :] = half_in
        tail = jnp.where(sub // 2 == a, half_trans, 0.0)
        w_first[a, pl.ds(GROUP * feats, 16), :] = tail.astype(jnp.bfloat16)


def silu_half(u):
    return (u + u * jnp.tanh(u)).astype(jnp.bfloat16)


def later_layers(h, w_mid, w_out):
    for m in range(w_mid.shape[0]):
        h = silu_half(jnp.dot(h, w_mid[m], preferred_element_type=jnp.float32))
    y = lax.dot_general(
        w_out[...], h, (((1,), (1,)), ((), ())), preferred_element_type=jnp.float32
    )
    return y.astype(jnp.bfloat16).astype(jnp.float32)


def empty_kernel(trans_weight, w_mid, w_out, out):
    u = trans_weight[...].astype(jnp.float32) * 0.5
    h = silu_half(jnp.broadcast_to(u, (out.shape[1], u.shape[1])))
    y = later_layers(h, w_mid, w_out)
    outs = w_out.shape[0]
    for at in range(0, out.shape[0], outs):
        out[pl.ds(at, outs), :] = y


def shade_kernel(table, rows, codes, got, w_first, w_mid, w_out, out, acc, xt, ys):
    items, feats, span = acc.shape
    outs = w_out.shape[0]

    posv, depthv = rows[0], rows[1]
    front = jnp.ones((items, span), jnp.float32)
    total = jnp.ones((items, span), jnp.float32)
    for k in range(items // MOST):
        tail = got[k, pl.ds(MOST * feats, ROWS), :].astype(jnp.float32)
        for r in range(MOST):
            j = k * MOST + r
            trans_j = tail[r : r + 1, :]
            same = posv == posv[j : j + 1, :]
            total = jnp.where(same, total * trans_j, total)
            front = jnp.where(same & (depthv > depthv[j : j + 1, :]), front * trans_j, front)
    acc[...] = jnp.zeros_like(acc)
    for j in range(items):
        k, r = divmod(j, MOST)
        color = got[k, pl.ds(r * feats, feats), :].astype(jnp.float32)
        at = table[0, j]
        acc[at] = acc[at] + front[j : j + 1, :] * color
    total_hi = total.astype(jnp.bfloat16).astype(jnp.float32)
    total_lo = total - total_hi
    groups = items // GROUP
    sub = lax.broadcasted_iota(jnp.int32, (16, span), 0)
    xt[...] = jnp.zeros_like(xt)
    for q in range(groups):
        block = acc[pl.ds(q * GROUP, GROUP)].reshape(GROUP * feats, span)
        tail = jnp.zeros((16, span), jnp.float32)
        for a in range(GROUP):
            i = q * GROUP + a
            tail = jnp.where(sub == 2 * a, total_hi[i : i + 1, :], tail)
            tail = jnp.where(sub == 2 * a + 1, total_lo[i : i + 1, :], tail)
        lines = pl.ds(q * span, span)
        xt[lines, pl.ds(0, GROUP * feats)] = block.T.astype(jnp.bfloat16)
        xt[lines, pl.ds(GROUP * feats, 16)] = tail.T.astype(jnp.bfloat16)

    x = xt[...]
    stride = GROUP
    for start in range(0, GROUP, stride):
        h = jnp.concatenate(
            [
                silu_half(jnp.dot(x, w_first[a], preferred_element_type=jnp.float32))
                for a in range(start, start + stride)
            ]
        )
        y = later_layers(h, w_mid, w_out)
        for a in range(start, start + stride):
            for q in range(groups):
                at = ((a - start) * groups + q) * span
                ys[pl.ds((q * GROUP + a) * outs, outs), :] = y[:, at : at + span]
    out[pl.ds(0, items * outs), :] = ys[...].astype(jnp.bfloat16)
    out[pl.ds(items * outs, ROWS), :] = codes[...]


def join_kernel(*refs):
    *got, empty, out = refs
    _, n_strip, tile, outs, span = out.shape
    lines = tile * outs
    count = got[0].shape[0] - ROWS
    me = lax.axis_index("strip")
    want = lax.broadcasted_iota(jnp.int32, (lines, count), 0) + me * lines
    chan = lax.broadcasted_iota(jnp.int32, (lines, count), 1) % outs
    filler = jnp.concatenate([empty[...]] * (lines // ROWS))
    ones = jnp.ones((count, span), jnp.bfloat16)
    for k in range(n_strip):
        pos = got[k][pl.ds(count, ROWS), :].astype(jnp.float32)[:1, :count].astype(jnp.int32)
        hit = pos * outs + chan == want
        pick = jnp.where(hit, 1.0, 0.0).astype(jnp.bfloat16)
        blocks = got[k][pl.ds(0, count), :]
        placed = jnp.dot(pick, blocks, preferred_element_type=jnp.float32)
        filled = jnp.dot(pick, ones, preferred_element_type=jnp.float32)
        value = jnp.where(filled > 0.5, placed, filler)
        out[0, me ^ (n_strip - 1 - k)] = value.reshape(tile, outs, span).astype(jnp.bfloat16)


def compact_device(
    n_slab,
    n_strip,
    colors,
    transmit,
    pair_counts,
    slot_block,
    assign,
    depth_rank,
    w_in,
    trans_weight,
    w_mid,
    w_out,
):
    slots, feats, span = colors.shape[2:]
    items = n_slab * MOST
    outs = w_out.shape[0]
    smem = pl.BlockSpec(memory_space=SMEM)
    vmem = pl.BlockSpec(memory_space=VMEM)
    hbm = pl.BlockSpec(memory_space=pltpu.HBM)
    small = pltpu.CompilerParams(vmem_limit_bytes=4 * 1024 * 1024)
    sends = pl.pallas_call(
        pack_kernel,
        out_shape=jax.ShapeDtypeStruct((n_slab, MOST * feats + ROWS, span), jnp.bfloat16),
        in_specs=[hbm] * 3,
        out_specs=vmem,
        scratch_shapes=[
            pltpu.SMEM(pair_counts.shape, jnp.int32),
            pltpu.VMEM(colors.shape, colors.dtype),
            pltpu.VMEM(transmit.shape, transmit.dtype),
            pltpu.VMEM((slots, span), jnp.float32),
            pltpu.SemaphoreType.DMA((3,)),
        ],
        name="pack",
    )(pair_counts, colors, transmit)
    got = lax.all_to_all(sends, "slab", split_axis=0, concat_axis=0, tiled=True)
    hidden = w_in.shape[0]
    rough = pl.CostEstimate(flops=10**5, bytes_accessed=10**6, transcendentals=0)
    roomy = pltpu.CompilerParams(vmem_limit_bytes=16 * 1024 * 1024)
    trans_row = trans_weight[None]
    table, rows, codes = pl.pallas_call(
        functools.partial(plan_kernel, n_slab, slots),
        out_shape=[
            jax.ShapeDtypeStruct((1, items), jnp.int32),
            jax.ShapeDtypeStruct((2, items, span), jnp.int32),
            jax.ShapeDtypeStruct((ROWS, span), jnp.bfloat16),
        ],
        in_specs=[smem] * 4,
        out_specs=[smem] + [vmem] * 2,
        compiler_params=small,
        cost_estimate=rough,
        name="plan",
    )(pair_counts, slot_block, assign, depth_rank)
    w_first = pl.pallas_call(
        place_kernel,
        out_shape=jax.ShapeDtypeStruct((GROUP, 2 * GROUP * feats, hidden), jnp.bfloat16),
        in_specs=[vmem] * 2,
        out_specs=vmem,
        compiler_params=small,
        cost_estimate=rough,
        name="place",
    )(w_in.T, trans_row)
    w_later = jnp.swapaxes(w_mid, 1, 2) * jnp.bfloat16(0.5)
    empty = pl.pallas_call(
        empty_kernel,
        out_shape=jax.ShapeDtypeStruct((ROWS, span), jnp.float32),
        in_specs=[vmem] * 3,
        out_specs=vmem,
        compiler_params=roomy,
        cost_estimate=rough,
        name="empty",
    )(trans_row, w_later, w_out)
    shaded = pl.pallas_call(
        shade_kernel,
        out_shape=jax.ShapeDtypeStruct((items * outs + ROWS, span), jnp.bfloat16),
        in_specs=[smem] + [vmem] * 6,
        out_specs=vmem,
        scratch_shapes=[
            pltpu.VMEM((items, feats, span), jnp.float32),
            pltpu.VMEM((items // GROUP * span, 2 * GROUP * feats), jnp.bfloat16),
            pltpu.VMEM((items * outs, span), jnp.float32),
        ],
        compiler_params=roomy,
        name="shade",
    )(table, rows, codes, got, w_first, w_later, w_out)
    tiles = [
        lax.ppermute(shaded, "strip", [(s, s ^ k) for s in range(n_strip)])
        for k in reversed(range(1, n_strip))
    ] + [shaded]
    return pl.pallas_call(
        join_kernel,
        out_shape=jax.ShapeDtypeStruct((1, n_strip, LB // n_strip, outs, span), jnp.bfloat16),
        in_specs=[vmem] * (n_strip + 1),
        out_specs=pl.BlockSpec(),
        compiler_params=small,
        name="join",
    )(*tiles, empty)


def solution(mesh):
    n_slab, n_strip = mesh.shape["slab"], mesh.shape["strip"]
    placed = (
        P("slab", "strip", None, None, None),
        P("slab", "strip", None, None),
        P("strip", None, None),
        P("strip", None, None),
        P("strip", None),
        P(),
        P(),
        P(),
        P(),
        P(),
    )
    compact = n_strip & (n_strip - 1) == 0 and 4 * MOST * n_slab <= LB
    return jax.shard_map(
        functools.partial(compact_device, n_slab, n_strip) if compact else dense_device,
        mesh=mesh,
        in_specs=placed,
        out_specs=P("slab", None, "strip", None, None),
        check_vma=False,
    )
```

```python
import functools

import jax
import jax.numpy as jnp
from jax import lax
from jax.experimental import pallas as pl
from jax.experimental.pallas import tpu as pltpu
from jax.sharding import PartitionSpec as P

MOST = 2
LB = 128


EXACT_PRECISION = lax.Precision.HIGHEST


def shade_blocks(blend_color, trans_field, w_in, trans_weight, w_mid, w_out):
    summed = jnp.einsum("hf,lfp->lhp", w_in, blend_color, preferred_element_type=jnp.float32)
    summed = summed + trans_weight.astype(jnp.float32)[None, :, None] * trans_field[:, None, :]
    hidden = jax.nn.silu(summed).astype(jnp.bfloat16)
    for layer_index in range(w_mid.shape[0]):
        hidden = jax.nn.silu(
            jnp.einsum(
                "hg,lgp->lhp", w_mid[layer_index], hidden, preferred_element_type=jnp.float32
            )
        ).astype(jnp.bfloat16)
    return jnp.einsum("oh,lhp->lop", w_out, hidden, preferred_element_type=jnp.float32).astype(
        jnp.bfloat16
    )


def dense_device(
    colors, transmit, pair_counts, slot_block, assign, depth_rank, w_in, trans_weight, w_mid, w_out
):
    myself = lax.axis_index("slab")
    counts = pair_counts[0]
    blocks_all = slot_block[0]
    assign_row = assign[0]
    offsets = jnp.cumsum(counts, axis=1) - counts
    slot_rank = jnp.arange(MOST, dtype=jnp.int32)
    my_counts = lax.dynamic_index_in_dim(counts, myself, 0, keepdims=False)
    my_offsets = lax.dynamic_index_in_dim(offsets, myself, 0, keepdims=False)
    send_slots = jnp.where(
        slot_rank[None, :] < my_counts[:, None], my_offsets[:, None] + slot_rank[None, :], 0
    )
    send_color = colors[0, 0][send_slots]
    send_trans = transmit[0, 0][send_slots][:, :, None, :]
    incoming = lax.dynamic_index_in_dim(counts, myself, 1, keepdims=False)
    in_offsets = lax.dynamic_index_in_dim(offsets, myself, 1, keepdims=False)
    live_slot = slot_rank[None, :] < incoming[:, None]
    recv_slots = jnp.where(live_slot, in_offsets[:, None] + slot_rank[None, :], 0)
    recv_blocks = jnp.take_along_axis(blocks_all, recv_slots, axis=1)
    local_pos = assign_row[recv_blocks] - myself * LB
    live_flat = live_slot.reshape(-1)
    local_flat = jnp.where(live_flat, local_pos.reshape(-1), -1)
    depth_flat = jnp.repeat(depth_rank, MOST)
    ahead_table = (
        (local_flat[:, None] == local_flat[None, :])
        & (depth_flat[None, :] < depth_flat[:, None])
        & live_flat[None, :]
    )
    ahead_table = ahead_table.astype(jnp.float32)
    owner_table = (jnp.arange(LB, dtype=jnp.int32)[:, None] == local_flat[None, :]).astype(
        jnp.float32
    )
    got_color = lax.all_to_all(send_color, "slab", split_axis=0, concat_axis=0, tiled=True)
    got_trans = lax.all_to_all(send_trans, "slab", split_axis=0, concat_axis=0, tiled=True)
    pixel_count = got_color.shape[3]
    item_count = got_color.shape[0] * got_color.shape[1]
    log_trans = jnp.log(got_trans.reshape(item_count, pixel_count).astype(jnp.float32))
    log_trans = jnp.where(live_flat[:, None], log_trans, 0.0)
    front_log = jnp.dot(ahead_table, log_trans, precision=EXACT_PRECISION)
    front_share = jnp.where(live_flat[:, None], jnp.exp(front_log), 0.0)
    weighted = front_share[:, None, :] * got_color.reshape(item_count, -1, pixel_count).astype(
        jnp.float32
    )
    blend_sum = jnp.dot(owner_table, weighted.reshape(item_count, -1), precision=EXACT_PRECISION)
    blend_color = blend_sum.reshape(LB, -1, pixel_count).astype(jnp.bfloat16)
    trans_field = jnp.exp(jnp.dot(owner_table, log_trans, precision=EXACT_PRECISION))
    shaded = shade_blocks(blend_color, trans_field, w_in, trans_weight, w_mid, w_out)
    display_tiles = lax.all_to_all(shaded[None], "strip", split_axis=1, concat_axis=0, tiled=True)
    return display_tiles[None]


SMEM = pltpu.SMEM
VMEM = pltpu.VMEM
ROWS = 8
GROUP = 4


def fetch(sources, targets, sems):
    copies = [
        pltpu.make_async_copy(source, target, sems.at[i])
        for i, (source, target) in enumerate(zip(sources, targets))
    ]
    for copy in copies:
        copy.start()
    for copy in copies:
        copy.wait()


def pack_kernel(far_counts, far_colors, far_transmit, sends, counts, colors, transmit, tall, sems):
    n_slab = sends.shape[0]
    slots, feats, span = colors.shape[2:]
    me = lax.axis_index("slab")
    fetch((far_counts, far_colors, far_transmit), (counts, colors, transmit), sems)
    tall[...] = transmit[0, 0].astype(jnp.float32)
    row = lax.broadcasted_iota(jnp.int32, (ROWS, span), 0)
    off = jnp.int32(0)
    for c in range(n_slab):
        tail = jnp.ones((ROWS, span), jnp.float32)
        for r in range(MOST):
            slot = jnp.minimum(off + r, slots - 1)
            sends[c, pl.ds(r * feats, feats), :] = colors[0, 0, slot]
            tail = jnp.where(row == r, tall[pl.ds(slot, 1), :], tail)
        sends[c, pl.ds(MOST * feats, ROWS), :] = tail.astype(jnp.bfloat16)
        off = off + counts[0, me, c]


def plan_kernel(n_slab, slots, *refs):
    (counts, blocks, assign, depth), (table, rows, codes) = refs[:4], refs[4:]
    items = n_slab * MOST
    outs = codes.shape[1] // (2 * items)
    me = lax.axis_index("slab")
    row = lax.broadcasted_iota(jnp.int32, rows.shape[1:], 0)
    item_lane = lax.broadcasted_iota(jnp.int32, codes.shape, 1) // outs
    posv = jnp.zeros(rows.shape[1:], jnp.int32)
    depthv = jnp.zeros(rows.shape[1:], jnp.int32)
    codev = jnp.full(codes.shape, -1, jnp.int32)
    pos = []
    for s in range(n_slab):
        off = jnp.int32(0)
        for c in range(n_slab):
            off = off + jnp.where(c < me, counts[0, s, c], 0)
        count = counts[0, s, me]
        for r in range(MOST):
            i = s * MOST + r
            slot = jnp.minimum(off + r, slots - 1)
            here = assign[0, blocks[0, s, slot]] - me * LB
            here = jnp.where(r < count, here, -1)
            first = jnp.int32(i)
            for j in reversed(range(i)):
                first = jnp.where(pos[j] == here, j, first)
            pos.append(here)
            table[0, i] = first
            posv = jnp.where(row == i, here, posv)
            depthv = jnp.where(row == i, depth[s], depthv)
            codev = jnp.where(item_lane == i, jnp.where(first == i, here, -1), codev)
    rows[0] = posv
    rows[1] = depthv
    codes[...] = codev.astype(jnp.float32).astype(jnp.bfloat16)


def place_kernel(w_in, trans_weight, far_out, w_first, w_out):
    feats, hidden = w_in.shape
    half_in = (w_in[...].astype(jnp.float32) * 0.5).astype(jnp.bfloat16)
    half_trans = trans_weight[...].astype(jnp.float32) * 0.5
    sub = lax.broadcasted_iota(jnp.int32, (16, hidden), 0)
    w_first[...] = jnp.zeros_like(w_first)
    for a in range(GROUP):
        w_first[a, pl.ds(a * feats, feats), :] = half_in
        tail = jnp.where(sub // 2 == a, half_trans, 0.0)
        w_first[a, pl.ds(GROUP * feats, 16), :] = tail.astype(jnp.bfloat16)
    w_out[...] = far_out[...]


def silu_half(u):
    return (u + u * jnp.tanh(u)).astype(jnp.bfloat16)


def later_layers(h, w_mid, w_out):
    for m in range(w_mid.shape[0]):
        h = silu_half(jnp.dot(h, w_mid[m], preferred_element_type=jnp.float32))
    y = lax.dot_general(
        w_out[...], h, (((1,), (1,)), ((), ())), preferred_element_type=jnp.float32
    )
    return y.astype(jnp.bfloat16).astype(jnp.float32)


def empty_kernel(trans_weight, w_mid, w_out, out):
    u = trans_weight[...].astype(jnp.float32) * 0.5
    h = silu_half(jnp.broadcast_to(u, (out.shape[1], u.shape[1])))
    y = later_layers(h, w_mid, w_out)
    outs = w_out.shape[0]
    for at in range(0, out.shape[0], outs):
        out[pl.ds(at, outs), :] = y


def shade_kernel(table, rows, codes, got, w_first, w_mid, w_out, out, acc, xt, ys):
    items, feats, span = acc.shape
    outs = w_out.shape[0]

    posv, depthv = rows[0], rows[1]
    front = jnp.ones((items, span), jnp.float32)
    total = jnp.ones((items, span), jnp.float32)
    for k in range(items // MOST):
        tail = got[k, pl.ds(MOST * feats, ROWS), :].astype(jnp.float32)
        for r in range(MOST):
            j = k * MOST + r
            trans_j = tail[r : r + 1, :]
            same = posv == posv[j : j + 1, :]
            total = jnp.where(same, total * trans_j, total)
            front = jnp.where(same & (depthv > depthv[j : j + 1, :]), front * trans_j, front)
    acc[...] = jnp.zeros_like(acc)
    for j in range(items):
        k, r = divmod(j, MOST)
        color = got[k, pl.ds(r * feats, feats), :].astype(jnp.float32)
        at = table[0, j]
        acc[at] = acc[at] + front[j : j + 1, :] * color
    total_hi = total.astype(jnp.bfloat16).astype(jnp.float32)
    total_lo = total - total_hi
    groups = items // GROUP
    sub = lax.broadcasted_iota(jnp.int32, (16, span), 0)
    xt[...] = jnp.zeros_like(xt)
    for q in range(groups):
        block = acc[pl.ds(q * GROUP, GROUP)].reshape(GROUP * feats, span)
        tail = jnp.zeros((16, span), jnp.float32)
        for a in range(GROUP):
            i = q * GROUP + a
            tail = jnp.where(sub == 2 * a, total_hi[i : i + 1, :], tail)
            tail = jnp.where(sub == 2 * a + 1, total_lo[i : i + 1, :], tail)
        lines = pl.ds(q * span, span)
        xt[lines, pl.ds(0, GROUP * feats)] = block.T.astype(jnp.bfloat16)
        xt[lines, pl.ds(GROUP * feats, 16)] = tail.T.astype(jnp.bfloat16)

    x = xt[...]
    stride = GROUP
    for start in range(0, GROUP, stride):
        h = jnp.concatenate(
            [
                silu_half(jnp.dot(x, w_first[a], preferred_element_type=jnp.float32))
                for a in range(start, start + stride)
            ]
        )
        y = later_layers(h, w_mid, w_out)
        for a in range(start, start + stride):
            for q in range(groups):
                at = ((a - start) * groups + q) * span
                ys[pl.ds((q * GROUP + a) * outs, outs), :] = y[:, at : at + span]
    out[pl.ds(0, items * outs), :] = ys[...].astype(jnp.bfloat16)
    out[pl.ds(items * outs, ROWS), :] = codes[...]


def join_kernel(*refs):
    *got, empty, out = refs
    _, n_strip, tile, outs, span = out.shape
    lines = tile * outs
    count = got[0].shape[0] - ROWS
    me = lax.axis_index("strip")
    want = lax.broadcasted_iota(jnp.int32, (lines, count), 0) + me * lines
    chan = lax.broadcasted_iota(jnp.int32, (lines, count), 1) % outs
    filler = jnp.concatenate([empty[...]] * (lines // ROWS))
    ones = jnp.ones((count, span), jnp.bfloat16)
    for k in range(n_strip):
        pos = got[k][pl.ds(count, ROWS), :].astype(jnp.float32)[:1, :count].astype(jnp.int32)
        hit = pos * outs + chan == want
        pick = jnp.where(hit, 1.0, 0.0).astype(jnp.bfloat16)
        blocks = got[k][pl.ds(0, count), :]
        placed = jnp.dot(pick, blocks, preferred_element_type=jnp.float32)
        filled = jnp.dot(pick, ones, preferred_element_type=jnp.float32)
        value = jnp.where(filled > 0.5, placed, filler)
        out[0, me ^ (n_strip - 1 - k)] = value.reshape(tile, outs, span).astype(jnp.bfloat16)


def compact_device(
    n_slab,
    n_strip,
    colors,
    transmit,
    pair_counts,
    slot_block,
    assign,
    depth_rank,
    w_in,
    trans_weight,
    w_mid,
    w_out,
):
    slots, feats, span = colors.shape[2:]
    items = n_slab * MOST
    outs = w_out.shape[0]
    smem = pl.BlockSpec(memory_space=SMEM)
    vmem = pl.BlockSpec(memory_space=VMEM)
    hbm = pl.BlockSpec(memory_space=pltpu.HBM)
    small = pltpu.CompilerParams(vmem_limit_bytes=4 * 1024 * 1024)
    message = MOST * feats + ROWS
    sends = pl.pallas_call(
        pack_kernel,
        out_shape=jax.ShapeDtypeStruct((n_slab, message, span), jnp.bfloat16),
        in_specs=[hbm] * 3,
        out_specs=vmem,
        scratch_shapes=[
            pltpu.SMEM(pair_counts.shape, jnp.int32),
            pltpu.VMEM(colors.shape, colors.dtype),
            pltpu.VMEM(transmit.shape, transmit.dtype),
            pltpu.VMEM((slots, span), jnp.float32),
            pltpu.SemaphoreType.DMA((3,)),
        ],
        name="pack",
    )(pair_counts, colors, transmit)
    got = lax.all_to_all(sends, "slab", split_axis=0, concat_axis=0, tiled=True)
    hidden = w_in.shape[0]
    rough = pl.CostEstimate(flops=10**5, bytes_accessed=10**6, transcendentals=0)
    roomy = pltpu.CompilerParams(vmem_limit_bytes=16 * 1024 * 1024)
    trans_row = trans_weight[None]
    table, rows, codes = pl.pallas_call(
        functools.partial(plan_kernel, n_slab, slots),
        out_shape=[
            jax.ShapeDtypeStruct((1, items), jnp.int32),
            jax.ShapeDtypeStruct((2, items, span), jnp.int32),
            jax.ShapeDtypeStruct((ROWS, span), jnp.bfloat16),
        ],
        in_specs=[smem] * 4,
        out_specs=[smem] + [vmem] * 2,
        compiler_params=small,
        cost_estimate=rough,
        name="plan",
    )(pair_counts, slot_block, assign, depth_rank)
    w_first, w_last = pl.pallas_call(
        place_kernel,
        out_shape=[
            jax.ShapeDtypeStruct((GROUP, 2 * GROUP * feats, hidden), jnp.bfloat16),
            jax.ShapeDtypeStruct(w_out.shape, jnp.bfloat16),
        ],
        in_specs=[vmem] * 3,
        out_specs=[vmem] * 2,
        compiler_params=small,
        cost_estimate=rough,
        name="place",
    )(w_in.T, trans_row, w_out)
    w_later = jnp.swapaxes(w_mid, 1, 2) * jnp.bfloat16(0.5)
    empty = pl.pallas_call(
        empty_kernel,
        out_shape=jax.ShapeDtypeStruct((ROWS, span), jnp.float32),
        in_specs=[vmem] * 3,
        out_specs=vmem,
        compiler_params=roomy,
        cost_estimate=rough,
        name="empty",
    )(trans_row, w_later, w_last)
    shaded = pl.pallas_call(
        shade_kernel,
        out_shape=jax.ShapeDtypeStruct((items * outs + ROWS, span), jnp.bfloat16),
        in_specs=[smem] + [vmem] * 6,
        out_specs=vmem,
        scratch_shapes=[
            pltpu.VMEM((items, feats, span), jnp.float32),
            pltpu.VMEM((items // GROUP * span, 2 * GROUP * feats), jnp.bfloat16),
            pltpu.VMEM((items * outs, span), jnp.float32),
        ],
        compiler_params=roomy,
        name="shade",
    )(table, rows, codes, got, w_first, w_later, w_last)
    tiles = [
        lax.ppermute(shaded, "strip", [(s, s ^ k) for s in range(n_strip)])
        for k in reversed(range(1, n_strip))
    ] + [shaded]
    return pl.pallas_call(
        join_kernel,
        out_shape=jax.ShapeDtypeStruct((1, n_strip, LB // n_strip, outs, span), jnp.bfloat16),
        in_specs=[vmem] * (n_strip + 1),
        out_specs=pl.BlockSpec(),
        compiler_params=small,
        name="join",
    )(*tiles, empty)


def solution(mesh):
    n_slab, n_strip = mesh.shape["slab"], mesh.shape["strip"]
    placed = (
        P("slab", "strip", None, None, None),
        P("slab", "strip", None, None),
        P("strip", None, None),
        P("strip", None, None),
        P("strip", None),
        P(),
        P(),
        P(),
        P(),
        P(),
    )
    compact = n_strip & (n_strip - 1) == 0 and 4 * MOST * n_slab <= LB
    return jax.shard_map(
        functools.partial(compact_device, n_slab, n_strip) if compact else dense_device,
        mesh=mesh,
        in_specs=placed,
        out_specs=P("slab", None, "strip", None, None),
        check_vma=False,
    )
```

```python
import functools

import jax
import jax.numpy as jnp
from jax import lax
from jax.experimental import pallas as pl
from jax.experimental.pallas import tpu as pltpu
from jax.sharding import PartitionSpec as P

MOST = 2
LB = 128


EXACT_PRECISION = lax.Precision.HIGHEST


def shade_blocks(blend_color, trans_field, w_in, trans_weight, w_mid, w_out):
    summed = jnp.einsum("hf,lfp->lhp", w_in, blend_color, preferred_element_type=jnp.float32)
    summed = summed + trans_weight.astype(jnp.float32)[None, :, None] * trans_field[:, None, :]
    hidden = jax.nn.silu(summed).astype(jnp.bfloat16)
    for layer_index in range(w_mid.shape[0]):
        hidden = jax.nn.silu(
            jnp.einsum(
                "hg,lgp->lhp", w_mid[layer_index], hidden, preferred_element_type=jnp.float32
            )
        ).astype(jnp.bfloat16)
    return jnp.einsum("oh,lhp->lop", w_out, hidden, preferred_element_type=jnp.float32).astype(
        jnp.bfloat16
    )


def dense_device(
    colors, transmit, pair_counts, slot_block, assign, depth_rank, w_in, trans_weight, w_mid, w_out
):
    myself = lax.axis_index("slab")
    counts = pair_counts[0]
    blocks_all = slot_block[0]
    assign_row = assign[0]
    offsets = jnp.cumsum(counts, axis=1) - counts
    slot_rank = jnp.arange(MOST, dtype=jnp.int32)
    my_counts = lax.dynamic_index_in_dim(counts, myself, 0, keepdims=False)
    my_offsets = lax.dynamic_index_in_dim(offsets, myself, 0, keepdims=False)
    send_slots = jnp.where(
        slot_rank[None, :] < my_counts[:, None], my_offsets[:, None] + slot_rank[None, :], 0
    )
    send_color = colors[0, 0][send_slots]
    send_trans = transmit[0, 0][send_slots][:, :, None, :]
    incoming = lax.dynamic_index_in_dim(counts, myself, 1, keepdims=False)
    in_offsets = lax.dynamic_index_in_dim(offsets, myself, 1, keepdims=False)
    live_slot = slot_rank[None, :] < incoming[:, None]
    recv_slots = jnp.where(live_slot, in_offsets[:, None] + slot_rank[None, :], 0)
    recv_blocks = jnp.take_along_axis(blocks_all, recv_slots, axis=1)
    local_pos = assign_row[recv_blocks] - myself * LB
    live_flat = live_slot.reshape(-1)
    local_flat = jnp.where(live_flat, local_pos.reshape(-1), -1)
    depth_flat = jnp.repeat(depth_rank, MOST)
    ahead_table = (
        (local_flat[:, None] == local_flat[None, :])
        & (depth_flat[None, :] < depth_flat[:, None])
        & live_flat[None, :]
    )
    ahead_table = ahead_table.astype(jnp.float32)
    owner_table = (jnp.arange(LB, dtype=jnp.int32)[:, None] == local_flat[None, :]).astype(
        jnp.float32
    )
    got_color = lax.all_to_all(send_color, "slab", split_axis=0, concat_axis=0, tiled=True)
    got_trans = lax.all_to_all(send_trans, "slab", split_axis=0, concat_axis=0, tiled=True)
    pixel_count = got_color.shape[3]
    item_count = got_color.shape[0] * got_color.shape[1]
    log_trans = jnp.log(got_trans.reshape(item_count, pixel_count).astype(jnp.float32))
    log_trans = jnp.where(live_flat[:, None], log_trans, 0.0)
    front_log = jnp.dot(ahead_table, log_trans, precision=EXACT_PRECISION)
    front_share = jnp.where(live_flat[:, None], jnp.exp(front_log), 0.0)
    weighted = front_share[:, None, :] * got_color.reshape(item_count, -1, pixel_count).astype(
        jnp.float32
    )
    blend_sum = jnp.dot(owner_table, weighted.reshape(item_count, -1), precision=EXACT_PRECISION)
    blend_color = blend_sum.reshape(LB, -1, pixel_count).astype(jnp.bfloat16)
    trans_field = jnp.exp(jnp.dot(owner_table, log_trans, precision=EXACT_PRECISION))
    shaded = shade_blocks(blend_color, trans_field, w_in, trans_weight, w_mid, w_out)
    display_tiles = lax.all_to_all(shaded[None], "strip", split_axis=1, concat_axis=0, tiled=True)
    return display_tiles[None]


SMEM = pltpu.SMEM
VMEM = pltpu.VMEM
ROWS = 8
GROUP = 4


def fetch(sources, targets, sems):
    copies = [
        pltpu.make_async_copy(source, target, sems.at[i])
        for i, (source, target) in enumerate(zip(sources, targets))
    ]
    for copy in copies:
        copy.start()
    for copy in copies:
        copy.wait()


def pack_kernel(far_counts, far_colors, far_transmit, sends, counts, colors, transmit, tall, sems):
    n_slab = sends.shape[0]
    slots, feats, span = colors.shape[2:]
    me = lax.axis_index("slab")
    fetch((far_counts, far_colors, far_transmit), (counts, colors, transmit), sems)
    tall[...] = transmit[0, 0].astype(jnp.float32)
    row = lax.broadcasted_iota(jnp.int32, (ROWS, span), 0)
    off = jnp.int32(0)
    for c in range(n_slab):
        tail = jnp.ones((ROWS, span), jnp.float32)
        for r in range(MOST):
            slot = jnp.minimum(off + r, slots - 1)
            sends[c, pl.ds(r * feats, feats), :] = colors[0, 0, slot]
            tail = jnp.where(row == r, tall[pl.ds(slot, 1), :], tail)
        sends[c, pl.ds(MOST * feats, ROWS), :] = tail.astype(jnp.bfloat16)
        off = off + counts[0, me, c]


def plan_kernel(n_slab, slots, *refs):
    (counts, blocks, assign, depth), (table, rows, codes) = refs[:4], refs[4:]
    items = n_slab * MOST
    outs = codes.shape[1] // (2 * items)
    me = lax.axis_index("slab")
    row = lax.broadcasted_iota(jnp.int32, rows.shape[1:], 0)
    item_lane = lax.broadcasted_iota(jnp.int32, codes.shape, 1) // outs
    posv = jnp.zeros(rows.shape[1:], jnp.int32)
    depthv = jnp.zeros(rows.shape[1:], jnp.int32)
    codev = jnp.full(codes.shape, -1, jnp.int32)
    pos = []
    for s in range(n_slab):
        off = jnp.int32(0)
        for c in range(n_slab):
            off = off + jnp.where(c < me, counts[0, s, c], 0)
        count = counts[0, s, me]
        for r in range(MOST):
            i = s * MOST + r
            slot = jnp.minimum(off + r, slots - 1)
            here = assign[0, blocks[0, s, slot]] - me * LB
            here = jnp.where(r < count, here, -1)
            first = jnp.int32(i)
            for j in reversed(range(i)):
                first = jnp.where(pos[j] == here, j, first)
            pos.append(here)
            table[0, i] = first
            posv = jnp.where(row == i, here, posv)
            depthv = jnp.where(row == i, depth[s], depthv)
            codev = jnp.where(item_lane == i, jnp.where(first == i, here, -1), codev)
    rows[0] = posv
    rows[1] = depthv
    codes[...] = codev.astype(jnp.float32).astype(jnp.bfloat16)


def place_kernel(w_in, trans_weight, far_out, w_first, w_out):
    feats, hidden = w_in.shape
    half_in = (w_in[...].astype(jnp.float32) * 0.5).astype(jnp.bfloat16)
    half_trans = trans_weight[...].astype(jnp.float32) * 0.5
    sub = lax.broadcasted_iota(jnp.int32, (16, hidden), 0)
    w_first[...] = jnp.zeros_like(w_first)
    for a in range(GROUP):
        w_first[a, pl.ds(a * feats, feats), :] = half_in
        tail = jnp.where(sub // 2 == a, half_trans, 0.0)
        w_first[a, pl.ds(GROUP * feats, 16), :] = tail.astype(jnp.bfloat16)
    w_out[...] = far_out[...]


def silu_half(u):
    return (u + u * jnp.tanh(u)).astype(jnp.bfloat16)


def later_layers(h, w_mid, w_out):
    for m in range(w_mid.shape[0]):
        h = silu_half(jnp.dot(h, w_mid[m], preferred_element_type=jnp.float32))
    y = lax.dot_general(
        w_out[...], h, (((1,), (1,)), ((), ())), preferred_element_type=jnp.float32
    )
    return y.astype(jnp.bfloat16).astype(jnp.float32)


def empty_kernel(trans_weight, w_mid, w_out, out):
    u = trans_weight[...].astype(jnp.float32) * 0.5
    h = silu_half(jnp.broadcast_to(u, (out.shape[1], u.shape[1])))
    y = later_layers(h, w_mid, w_out)
    outs = w_out.shape[0]
    for at in range(0, out.shape[0], outs):
        out[pl.ds(at, outs), :] = y


def shade_kernel(table, rows, codes, got, w_first, w_mid, w_out, out, acc, xt, ys):
    items, feats, span = acc.shape
    outs = w_out.shape[0]

    posv, depthv = rows[0], rows[1]
    front = jnp.ones((items, span), jnp.float32)
    total = jnp.ones((items, span), jnp.float32)
    for k in range(items // MOST):
        tail = got[k, pl.ds(MOST * feats, ROWS), :].astype(jnp.float32)
        for r in range(MOST):
            j = k * MOST + r
            trans_j = tail[r : r + 1, :]
            same = posv == posv[j : j + 1, :]
            total = jnp.where(same, total * trans_j, total)
            front = jnp.where(same & (depthv > depthv[j : j + 1, :]), front * trans_j, front)
    acc[...] = jnp.zeros_like(acc)
    for j in range(items):
        k, r = divmod(j, MOST)
        color = got[k, pl.ds(r * feats, feats), :].astype(jnp.float32)
        at = table[0, j]
        acc[at] = acc[at] + front[j : j + 1, :] * color
    total_hi = total.astype(jnp.bfloat16).astype(jnp.float32)
    total_lo = total - total_hi
    groups = items // GROUP
    sub = lax.broadcasted_iota(jnp.int32, (16, span), 0)
    xt[...] = jnp.zeros_like(xt)
    for q in range(groups):
        block = acc[pl.ds(q * GROUP, GROUP)].reshape(GROUP * feats, span)
        tail = jnp.zeros((16, span), jnp.float32)
        for a in range(GROUP):
            i = q * GROUP + a
            tail = jnp.where(sub == 2 * a, total_hi[i : i + 1, :], tail)
            tail = jnp.where(sub == 2 * a + 1, total_lo[i : i + 1, :], tail)
        lines = pl.ds(q * span, span)
        xt[lines, pl.ds(0, GROUP * feats)] = block.T.astype(jnp.bfloat16)
        xt[lines, pl.ds(GROUP * feats, 16)] = tail.T.astype(jnp.bfloat16)

    x = xt[...]
    stride = GROUP
    for start in range(0, GROUP, stride):
        h = jnp.concatenate(
            [
                silu_half(jnp.dot(x, w_first[a], preferred_element_type=jnp.float32))
                for a in range(start, start + stride)
            ]
        )
        y = later_layers(h, w_mid, w_out)
        for a in range(start, start + stride):
            for q in range(groups):
                at = ((a - start) * groups + q) * span
                ys[pl.ds((q * GROUP + a) * outs, outs), :] = y[:, at : at + span]
    out[pl.ds(0, items * outs), :] = ys[...].astype(jnp.bfloat16)
    out[pl.ds(items * outs, ROWS), :] = codes[...]


def join_kernel(*refs):
    *got, empty, out = refs
    _, n_strip, tile, outs, span = out.shape
    lines = tile * outs
    count = got[0].shape[0] - ROWS
    me = lax.axis_index("strip")
    want = lax.broadcasted_iota(jnp.int32, (lines, count), 0) + me * lines
    chan = lax.broadcasted_iota(jnp.int32, (lines, count), 1) % outs
    filler = jnp.concatenate([empty[...]] * (lines // ROWS))
    ones = jnp.ones((count, span), jnp.bfloat16)
    for k in range(n_strip):
        pos = got[k][pl.ds(count, ROWS), :].astype(jnp.float32)[:1, :count].astype(jnp.int32)
        hit = pos * outs + chan == want
        pick = jnp.where(hit, 1.0, 0.0).astype(jnp.bfloat16)
        blocks = got[k][pl.ds(0, count), :]
        placed = jnp.dot(pick, blocks, preferred_element_type=jnp.float32)
        filled = jnp.dot(pick, ones, preferred_element_type=jnp.float32)
        value = jnp.where(filled > 0.5, placed, filler)
        out[0, me ^ ((k + 1) % n_strip)] = value.reshape(tile, outs, span).astype(jnp.bfloat16)


def compact_device(
    n_slab,
    n_strip,
    colors,
    transmit,
    pair_counts,
    slot_block,
    assign,
    depth_rank,
    w_in,
    trans_weight,
    w_mid,
    w_out,
):
    slots, feats, span = colors.shape[2:]
    items = n_slab * MOST
    outs = w_out.shape[0]
    smem = pl.BlockSpec(memory_space=SMEM)
    vmem = pl.BlockSpec(memory_space=VMEM)
    hbm = pl.BlockSpec(memory_space=pltpu.HBM)
    small = pltpu.CompilerParams(vmem_limit_bytes=4 * 1024 * 1024)
    message = MOST * feats + ROWS
    sends = pl.pallas_call(
        pack_kernel,
        out_shape=jax.ShapeDtypeStruct((n_slab, message, span), jnp.bfloat16),
        in_specs=[hbm] * 3,
        out_specs=vmem,
        scratch_shapes=[
            pltpu.SMEM(pair_counts.shape, jnp.int32),
            pltpu.VMEM(colors.shape, colors.dtype),
            pltpu.VMEM(transmit.shape, transmit.dtype),
            pltpu.VMEM((slots, span), jnp.float32),
            pltpu.SemaphoreType.DMA((3,)),
        ],
        name="pack",
    )(pair_counts, colors, transmit)
    got = lax.all_to_all(sends, "slab", split_axis=0, concat_axis=0, tiled=True)
    hidden = w_in.shape[0]
    rough = pl.CostEstimate(flops=10**5, bytes_accessed=10**6, transcendentals=0)
    roomy = pltpu.CompilerParams(vmem_limit_bytes=16 * 1024 * 1024)
    trans_row = trans_weight[None]
    table, rows, codes = pl.pallas_call(
        functools.partial(plan_kernel, n_slab, slots),
        out_shape=[
            jax.ShapeDtypeStruct((1, items), jnp.int32),
            jax.ShapeDtypeStruct((2, items, span), jnp.int32),
            jax.ShapeDtypeStruct((ROWS, span), jnp.bfloat16),
        ],
        in_specs=[smem] * 4,
        out_specs=[smem] + [vmem] * 2,
        compiler_params=small,
        cost_estimate=rough,
        name="plan",
    )(pair_counts, slot_block, assign, depth_rank)
    w_first, w_last = pl.pallas_call(
        place_kernel,
        out_shape=[
            jax.ShapeDtypeStruct((GROUP, 2 * GROUP * feats, hidden), jnp.bfloat16),
            jax.ShapeDtypeStruct(w_out.shape, jnp.bfloat16),
        ],
        in_specs=[vmem] * 3,
        out_specs=[vmem] * 2,
        compiler_params=small,
        cost_estimate=rough,
        name="place",
    )(w_in.T, trans_row, w_out)
    w_later = jnp.swapaxes(w_mid, 1, 2) * jnp.bfloat16(0.5)
    empty = pl.pallas_call(
        empty_kernel,
        out_shape=jax.ShapeDtypeStruct((ROWS, span), jnp.float32),
        in_specs=[vmem] * 3,
        out_specs=vmem,
        compiler_params=roomy,
        cost_estimate=rough,
        name="empty",
    )(trans_row, w_later, w_last)
    shaded = pl.pallas_call(
        shade_kernel,
        out_shape=jax.ShapeDtypeStruct((items * outs + ROWS, span), jnp.bfloat16),
        in_specs=[smem] + [vmem] * 6,
        out_specs=vmem,
        scratch_shapes=[
            pltpu.VMEM((items, feats, span), jnp.float32),
            pltpu.VMEM((items // GROUP * span, 2 * GROUP * feats), jnp.bfloat16),
            pltpu.VMEM((items * outs, span), jnp.float32),
        ],
        compiler_params=roomy,
        name="shade",
    )(table, rows, codes, got, w_first, w_later, w_last)
    tiles = [
        lax.ppermute(shaded, "strip", [(s, s ^ k) for s in range(n_strip)])
        for k in range(1, n_strip)
    ] + [shaded]
    return pl.pallas_call(
        join_kernel,
        out_shape=jax.ShapeDtypeStruct((1, n_strip, LB // n_strip, outs, span), jnp.bfloat16),
        in_specs=[vmem] * (n_strip + 1),
        out_specs=pl.BlockSpec(),
        compiler_params=small,
        name="join",
    )(*tiles, empty)


def solution(mesh):
    n_slab, n_strip = mesh.shape["slab"], mesh.shape["strip"]
    placed = (
        P("slab", "strip", None, None, None),
        P("slab", "strip", None, None),
        P("strip", None, None),
        P("strip", None, None),
        P("strip", None),
        P(),
        P(),
        P(),
        P(),
        P(),
    )
    compact = n_strip & (n_strip - 1) == 0 and 4 * MOST * n_slab <= LB
    return jax.shard_map(
        functools.partial(compact_device, n_slab, n_strip) if compact else dense_device,
        mesh=mesh,
        in_specs=placed,
        out_specs=P("slab", None, "strip", None, None),
        check_vma=False,
    )
```

```python
import functools

import jax
import jax.numpy as jnp
from jax import lax
from jax.experimental import pallas as pl
from jax.experimental.pallas import tpu as pltpu
from jax.sharding import PartitionSpec as P

MOST = 2
LB = 128


EXACT_PRECISION = lax.Precision.HIGHEST


def shade_blocks(blend_color, trans_field, w_in, trans_weight, w_mid, w_out):
    summed = jnp.einsum("hf,lfp->lhp", w_in, blend_color, preferred_element_type=jnp.float32)
    summed = summed + trans_weight.astype(jnp.float32)[None, :, None] * trans_field[:, None, :]
    hidden = jax.nn.silu(summed).astype(jnp.bfloat16)
    for layer_index in range(w_mid.shape[0]):
        hidden = jax.nn.silu(
            jnp.einsum(
                "hg,lgp->lhp", w_mid[layer_index], hidden, preferred_element_type=jnp.float32
            )
        ).astype(jnp.bfloat16)
    return jnp.einsum("oh,lhp->lop", w_out, hidden, preferred_element_type=jnp.float32).astype(
        jnp.bfloat16
    )


def dense_device(
    colors, transmit, pair_counts, slot_block, assign, depth_rank, w_in, trans_weight, w_mid, w_out
):
    myself = lax.axis_index("slab")
    counts = pair_counts[0]
    blocks_all = slot_block[0]
    assign_row = assign[0]
    offsets = jnp.cumsum(counts, axis=1) - counts
    slot_rank = jnp.arange(MOST, dtype=jnp.int32)
    my_counts = lax.dynamic_index_in_dim(counts, myself, 0, keepdims=False)
    my_offsets = lax.dynamic_index_in_dim(offsets, myself, 0, keepdims=False)
    send_slots = jnp.where(
        slot_rank[None, :] < my_counts[:, None], my_offsets[:, None] + slot_rank[None, :], 0
    )
    send_color = colors[0, 0][send_slots]
    send_trans = transmit[0, 0][send_slots][:, :, None, :]
    incoming = lax.dynamic_index_in_dim(counts, myself, 1, keepdims=False)
    in_offsets = lax.dynamic_index_in_dim(offsets, myself, 1, keepdims=False)
    live_slot = slot_rank[None, :] < incoming[:, None]
    recv_slots = jnp.where(live_slot, in_offsets[:, None] + slot_rank[None, :], 0)
    recv_blocks = jnp.take_along_axis(blocks_all, recv_slots, axis=1)
    local_pos = assign_row[recv_blocks] - myself * LB
    live_flat = live_slot.reshape(-1)
    local_flat = jnp.where(live_flat, local_pos.reshape(-1), -1)
    depth_flat = jnp.repeat(depth_rank, MOST)
    ahead_table = (
        (local_flat[:, None] == local_flat[None, :])
        & (depth_flat[None, :] < depth_flat[:, None])
        & live_flat[None, :]
    )
    ahead_table = ahead_table.astype(jnp.float32)
    owner_table = (jnp.arange(LB, dtype=jnp.int32)[:, None] == local_flat[None, :]).astype(
        jnp.float32
    )
    got_color = lax.all_to_all(send_color, "slab", split_axis=0, concat_axis=0, tiled=True)
    got_trans = lax.all_to_all(send_trans, "slab", split_axis=0, concat_axis=0, tiled=True)
    pixel_count = got_color.shape[3]
    item_count = got_color.shape[0] * got_color.shape[1]
    log_trans = jnp.log(got_trans.reshape(item_count, pixel_count).astype(jnp.float32))
    log_trans = jnp.where(live_flat[:, None], log_trans, 0.0)
    front_log = jnp.dot(ahead_table, log_trans, precision=EXACT_PRECISION)
    front_share = jnp.where(live_flat[:, None], jnp.exp(front_log), 0.0)
    weighted = front_share[:, None, :] * got_color.reshape(item_count, -1, pixel_count).astype(
        jnp.float32
    )
    blend_sum = jnp.dot(owner_table, weighted.reshape(item_count, -1), precision=EXACT_PRECISION)
    blend_color = blend_sum.reshape(LB, -1, pixel_count).astype(jnp.bfloat16)
    trans_field = jnp.exp(jnp.dot(owner_table, log_trans, precision=EXACT_PRECISION))
    shaded = shade_blocks(blend_color, trans_field, w_in, trans_weight, w_mid, w_out)
    display_tiles = lax.all_to_all(shaded[None], "strip", split_axis=1, concat_axis=0, tiled=True)
    return display_tiles[None]


SMEM = pltpu.SMEM
VMEM = pltpu.VMEM
ROWS = 8
GROUP = 4


def fetch(sources, targets, sems):
    copies = [
        pltpu.make_async_copy(source, target, sems.at[i])
        for i, (source, target) in enumerate(zip(sources, targets))
    ]
    for copy in copies:
        copy.start()
    for copy in copies:
        copy.wait()


def pack_kernel(far_counts, far_colors, far_transmit, sends, counts, colors, transmit, tall, sems):
    n_slab = sends.shape[0]
    slots, feats, span = colors.shape[2:]
    me = lax.axis_index("slab")
    fetch((far_counts, far_colors, far_transmit), (counts, colors, transmit), sems)
    tall[...] = transmit[0, 0].astype(jnp.float32)
    row = lax.broadcasted_iota(jnp.int32, (ROWS, span), 0)
    off = jnp.int32(0)
    for c in range(n_slab):
        tail = jnp.ones((ROWS, span), jnp.float32)
        for r in range(MOST):
            slot = jnp.minimum(off + r, slots - 1)
            sends[c, pl.ds(r * feats, feats), :] = colors[0, 0, slot]
            tail = jnp.where(row == r, tall[pl.ds(slot, 1), :], tail)
        sends[c, pl.ds(MOST * feats, ROWS), :] = tail.astype(jnp.bfloat16)
        off = off + counts[0, me, c]


def plan_kernel(n_slab, slots, *refs):
    (counts, blocks, assign, depth), (table, rows, codes) = refs[:4], refs[4:]
    items = n_slab * MOST
    outs = codes.shape[1] // (2 * items)
    me = lax.axis_index("slab")
    row = lax.broadcasted_iota(jnp.int32, rows.shape[1:], 0)
    item_lane = lax.broadcasted_iota(jnp.int32, codes.shape, 1) // outs
    posv = jnp.zeros(rows.shape[1:], jnp.int32)
    depthv = jnp.zeros(rows.shape[1:], jnp.int32)
    codev = jnp.full(codes.shape, -1, jnp.int32)
    pos = []
    for s in range(n_slab):
        off = jnp.int32(0)
        for c in range(n_slab):
            off = off + jnp.where(c < me, counts[0, s, c], 0)
        count = counts[0, s, me]
        for r in range(MOST):
            i = s * MOST + r
            slot = jnp.minimum(off + r, slots - 1)
            here = assign[0, blocks[0, s, slot]] - me * LB
            here = jnp.where(r < count, here, -1)
            first = jnp.int32(i)
            for j in reversed(range(i)):
                first = jnp.where(pos[j] == here, j, first)
            pos.append(here)
            table[0, i] = first
            posv = jnp.where(row == i, here, posv)
            depthv = jnp.where(row == i, depth[s], depthv)
            codev = jnp.where(item_lane == i, jnp.where(first == i, here, -1), codev)
    rows[0] = posv
    rows[1] = depthv
    codes[...] = codev.astype(jnp.float32).astype(jnp.bfloat16)


def place_kernel(w_in, trans_weight, far_out, w_first, w_out):
    feats, hidden = w_in.shape
    half_in = (w_in[...].astype(jnp.float32) * 0.5).astype(jnp.bfloat16)
    half_trans = trans_weight[...].astype(jnp.float32) * 0.5
    sub = lax.broadcasted_iota(jnp.int32, (16, hidden), 0)
    w_first[...] = jnp.zeros_like(w_first)
    for a in range(GROUP):
        w_first[a, pl.ds(a * feats, feats), :] = half_in
        tail = jnp.where(sub // 2 == a, half_trans, 0.0)
        w_first[a, pl.ds(GROUP * feats, 16), :] = tail.astype(jnp.bfloat16)
    w_out[...] = far_out[...]


def silu_half(u):
    return (u + u * jnp.tanh(u)).astype(jnp.bfloat16)


def later_layers(h, w_mid, w_out):
    for m in range(w_mid.shape[0]):
        h = silu_half(jnp.dot(h, w_mid[m], preferred_element_type=jnp.float32))
    y = lax.dot_general(
        w_out[...], h, (((1,), (1,)), ((), ())), preferred_element_type=jnp.float32
    )
    return y.astype(jnp.bfloat16).astype(jnp.float32)


def empty_kernel(trans_weight, w_mid, w_out, out):
    u = trans_weight[...].astype(jnp.float32) * 0.5
    h = silu_half(jnp.broadcast_to(u, (out.shape[1], u.shape[1])))
    y = later_layers(h, w_mid, w_out)
    outs = w_out.shape[0]
    for at in range(0, out.shape[0], outs):
        out[pl.ds(at, outs), :] = y


def shade_kernel(table, rows, codes, got, w_first, w_mid, w_out, out, acc, xt, ys):
    items, feats, span = acc.shape
    outs = w_out.shape[0]

    posv, depthv = rows[0], rows[1]
    front = jnp.ones((items, span), jnp.float32)
    total = jnp.ones((items, span), jnp.float32)
    for k in range(items // MOST):
        tail = got[k, pl.ds(MOST * feats, ROWS), :].astype(jnp.float32)
        for r in range(MOST):
            j = k * MOST + r
            trans_j = tail[r : r + 1, :]
            same = posv == posv[j : j + 1, :]
            total = jnp.where(same, total * trans_j, total)
            front = jnp.where(same & (depthv > depthv[j : j + 1, :]), front * trans_j, front)
    acc[...] = jnp.zeros_like(acc)
    for j in range(items):
        k, r = divmod(j, MOST)
        color = got[k, pl.ds(r * feats, feats), :].astype(jnp.float32)
        at = table[0, j]
        acc[at] = acc[at] + front[j : j + 1, :] * color
    total_hi = total.astype(jnp.bfloat16).astype(jnp.float32)
    total_lo = total - total_hi
    groups = items // GROUP
    sub = lax.broadcasted_iota(jnp.int32, (16, span), 0)
    xt[...] = jnp.zeros_like(xt)
    for q in range(groups):
        block = acc[pl.ds(q * GROUP, GROUP)].reshape(GROUP * feats, span)
        tail = jnp.zeros((16, span), jnp.float32)
        for a in range(GROUP):
            i = q * GROUP + a
            tail = jnp.where(sub == 2 * a, total_hi[i : i + 1, :], tail)
            tail = jnp.where(sub == 2 * a + 1, total_lo[i : i + 1, :], tail)
        lines = pl.ds(q * span, span)
        xt[lines, pl.ds(0, GROUP * feats)] = block.T.astype(jnp.bfloat16)
        xt[lines, pl.ds(GROUP * feats, 16)] = tail.T.astype(jnp.bfloat16)

    x = xt[...]
    stride = GROUP
    for start in range(0, GROUP, stride):
        h = jnp.concatenate(
            [
                silu_half(jnp.dot(x, w_first[a], preferred_element_type=jnp.float32))
                for a in range(start, start + stride)
            ]
        )
        y = later_layers(h, w_mid, w_out)
        for a in range(start, start + stride):
            for q in range(groups):
                at = ((a - start) * groups + q) * span
                ys[pl.ds((q * GROUP + a) * outs, outs), :] = y[:, at : at + span]
    out[pl.ds(0, items * outs), :] = ys[...].astype(jnp.bfloat16)
    out[pl.ds(items * outs, ROWS), :] = codes[...]


def join_kernel(*refs):
    *got, empty, out = refs
    _, n_strip, tile, outs, span = out.shape
    lines = tile * outs
    count = got[0].shape[0] - ROWS
    me = lax.axis_index("strip")
    want = lax.broadcasted_iota(jnp.int32, (lines, count), 0) + me * lines
    chan = lax.broadcasted_iota(jnp.int32, (lines, count), 1) % outs
    filler = jnp.concatenate([empty[...]] * (lines // ROWS))
    ones = jnp.ones((count, span), jnp.bfloat16)
    for k in range(n_strip):
        pos = got[k][pl.ds(count, ROWS), :].astype(jnp.float32)[:1, :count].astype(jnp.int32)
        hit = pos * outs + chan == want
        pick = jnp.where(hit, 1.0, 0.0).astype(jnp.bfloat16)
        blocks = got[k][pl.ds(0, count), :]
        placed = jnp.dot(pick, blocks, preferred_element_type=jnp.float32)
        filled = jnp.dot(pick, ones, preferred_element_type=jnp.float32)
        value = jnp.where(filled > 0.5, placed, filler)
        out[0, me ^ ((k + 1) % n_strip)] = value.reshape(tile, outs, span).astype(jnp.bfloat16)


def compact_device(
    n_slab,
    n_strip,
    colors,
    transmit,
    pair_counts,
    slot_block,
    assign,
    depth_rank,
    w_in,
    trans_weight,
    w_mid,
    w_out,
):
    slots, feats, span = colors.shape[2:]
    items = n_slab * MOST
    outs = w_out.shape[0]
    smem = pl.BlockSpec(memory_space=SMEM)
    vmem = pl.BlockSpec(memory_space=VMEM)
    hbm = pl.BlockSpec(memory_space=pltpu.HBM)
    small = pltpu.CompilerParams(vmem_limit_bytes=4 * 1024 * 1024)
    message = MOST * feats + ROWS
    sends = pl.pallas_call(
        pack_kernel,
        out_shape=jax.ShapeDtypeStruct((n_slab, message, span), jnp.bfloat16),
        in_specs=[hbm] * 3,
        out_specs=vmem,
        scratch_shapes=[
            pltpu.SMEM(pair_counts.shape, jnp.int32),
            pltpu.VMEM(colors.shape, colors.dtype),
            pltpu.VMEM(transmit.shape, transmit.dtype),
            pltpu.VMEM((slots, span), jnp.float32),
            pltpu.SemaphoreType.DMA((3,)),
        ],
        compiler_params=small,
        name="pack",
    )(*[pltpu.with_memory_space_constraint(a, pltpu.HBM) for a in (pair_counts, colors, transmit)])
    got = lax.all_to_all(sends, "slab", split_axis=0, concat_axis=0, tiled=True)
    hidden = w_in.shape[0]
    rough = pl.CostEstimate(flops=10**5, bytes_accessed=10**6, transcendentals=0)
    roomy = pltpu.CompilerParams(vmem_limit_bytes=16 * 1024 * 1024)
    trans_row = trans_weight[None]
    table, rows, codes = pl.pallas_call(
        functools.partial(plan_kernel, n_slab, slots),
        out_shape=[
            jax.ShapeDtypeStruct((1, items), jnp.int32),
            jax.ShapeDtypeStruct((2, items, span), jnp.int32),
            jax.ShapeDtypeStruct((ROWS, span), jnp.bfloat16),
        ],
        in_specs=[smem] * 4,
        out_specs=[smem] + [vmem] * 2,
        compiler_params=small,
        cost_estimate=rough,
        name="plan",
    )(pair_counts, slot_block, assign, depth_rank)
    w_first, w_last = pl.pallas_call(
        place_kernel,
        out_shape=[
            jax.ShapeDtypeStruct((GROUP, 2 * GROUP * feats, hidden), jnp.bfloat16),
            jax.ShapeDtypeStruct(w_out.shape, jnp.bfloat16),
        ],
        in_specs=[vmem] * 3,
        out_specs=[vmem] * 2,
        compiler_params=small,
        cost_estimate=rough,
        name="place",
    )(w_in.T, trans_row, w_out)
    w_later = jnp.swapaxes(w_mid, 1, 2) * jnp.bfloat16(0.5)
    empty = pl.pallas_call(
        empty_kernel,
        out_shape=jax.ShapeDtypeStruct((ROWS, span), jnp.float32),
        in_specs=[vmem] * 3,
        out_specs=vmem,
        compiler_params=roomy,
        cost_estimate=rough,
        name="empty",
    )(trans_row, w_later, w_last)
    shaded = pl.pallas_call(
        shade_kernel,
        out_shape=jax.ShapeDtypeStruct((items * outs + ROWS, span), jnp.bfloat16),
        in_specs=[smem] + [vmem] * 6,
        out_specs=vmem,
        scratch_shapes=[
            pltpu.VMEM((items, feats, span), jnp.float32),
            pltpu.VMEM((items // GROUP * span, 2 * GROUP * feats), jnp.bfloat16),
            pltpu.VMEM((items * outs, span), jnp.float32),
        ],
        compiler_params=roomy,
        name="shade",
    )(table, rows, codes, got, w_first, w_later, w_last)
    tiles = [
        lax.ppermute(shaded, "strip", [(s, s ^ k) for s in range(n_strip)])
        for k in range(1, n_strip)
    ] + [shaded]
    return pl.pallas_call(
        join_kernel,
        out_shape=jax.ShapeDtypeStruct((1, n_strip, LB // n_strip, outs, span), jnp.bfloat16),
        in_specs=[vmem] * (n_strip + 1),
        out_specs=pl.BlockSpec(),
        compiler_params=small,
        name="join",
    )(*tiles, empty)


def solution(mesh):
    n_slab, n_strip = mesh.shape["slab"], mesh.shape["strip"]
    placed = (
        P("slab", "strip", None, None, None),
        P("slab", "strip", None, None),
        P("strip", None, None),
        P("strip", None, None),
        P("strip", None),
        P(),
        P(),
        P(),
        P(),
        P(),
    )
    compact = n_strip & (n_strip - 1) == 0 and 4 * MOST * n_slab <= LB
    return jax.shard_map(
        functools.partial(compact_device, n_slab, n_strip) if compact else dense_device,
        mesh=mesh,
        in_specs=placed,
        out_specs=P("slab", None, "strip", None, None),
        check_vma=False,
    )
```

```python
import functools

import jax
import jax.numpy as jnp
from jax import lax
from jax.experimental import pallas as pl
from jax.experimental.pallas import tpu as pltpu
from jax.sharding import PartitionSpec as P

MOST = 2
LB = 128


EXACT_PRECISION = lax.Precision.HIGHEST


def shade_blocks(blend_color, trans_field, w_in, trans_weight, w_mid, w_out):
    summed = jnp.einsum("hf,lfp->lhp", w_in, blend_color, preferred_element_type=jnp.float32)
    summed = summed + trans_weight.astype(jnp.float32)[None, :, None] * trans_field[:, None, :]
    hidden = jax.nn.silu(summed).astype(jnp.bfloat16)
    for layer_index in range(w_mid.shape[0]):
        hidden = jax.nn.silu(
            jnp.einsum(
                "hg,lgp->lhp", w_mid[layer_index], hidden, preferred_element_type=jnp.float32
            )
        ).astype(jnp.bfloat16)
    return jnp.einsum("oh,lhp->lop", w_out, hidden, preferred_element_type=jnp.float32).astype(
        jnp.bfloat16
    )


def dense_device(
    colors, transmit, pair_counts, slot_block, assign, depth_rank, w_in, trans_weight, w_mid, w_out
):
    myself = lax.axis_index("slab")
    counts = pair_counts[0]
    blocks_all = slot_block[0]
    assign_row = assign[0]
    offsets = jnp.cumsum(counts, axis=1) - counts
    slot_rank = jnp.arange(MOST, dtype=jnp.int32)
    my_counts = lax.dynamic_index_in_dim(counts, myself, 0, keepdims=False)
    my_offsets = lax.dynamic_index_in_dim(offsets, myself, 0, keepdims=False)
    send_slots = jnp.where(
        slot_rank[None, :] < my_counts[:, None], my_offsets[:, None] + slot_rank[None, :], 0
    )
    send_color = colors[0, 0][send_slots]
    send_trans = transmit[0, 0][send_slots][:, :, None, :]
    incoming = lax.dynamic_index_in_dim(counts, myself, 1, keepdims=False)
    in_offsets = lax.dynamic_index_in_dim(offsets, myself, 1, keepdims=False)
    live_slot = slot_rank[None, :] < incoming[:, None]
    recv_slots = jnp.where(live_slot, in_offsets[:, None] + slot_rank[None, :], 0)
    recv_blocks = jnp.take_along_axis(blocks_all, recv_slots, axis=1)
    local_pos = assign_row[recv_blocks] - myself * LB
    live_flat = live_slot.reshape(-1)
    local_flat = jnp.where(live_flat, local_pos.reshape(-1), -1)
    depth_flat = jnp.repeat(depth_rank, MOST)
    ahead_table = (
        (local_flat[:, None] == local_flat[None, :])
        & (depth_flat[None, :] < depth_flat[:, None])
        & live_flat[None, :]
    )
    ahead_table = ahead_table.astype(jnp.float32)
    owner_table = (jnp.arange(LB, dtype=jnp.int32)[:, None] == local_flat[None, :]).astype(
        jnp.float32
    )
    got_color = lax.all_to_all(send_color, "slab", split_axis=0, concat_axis=0, tiled=True)
    got_trans = lax.all_to_all(send_trans, "slab", split_axis=0, concat_axis=0, tiled=True)
    pixel_count = got_color.shape[3]
    item_count = got_color.shape[0] * got_color.shape[1]
    log_trans = jnp.log(got_trans.reshape(item_count, pixel_count).astype(jnp.float32))
    log_trans = jnp.where(live_flat[:, None], log_trans, 0.0)
    front_log = jnp.dot(ahead_table, log_trans, precision=EXACT_PRECISION)
    front_share = jnp.where(live_flat[:, None], jnp.exp(front_log), 0.0)
    weighted = front_share[:, None, :] * got_color.reshape(item_count, -1, pixel_count).astype(
        jnp.float32
    )
    blend_sum = jnp.dot(owner_table, weighted.reshape(item_count, -1), precision=EXACT_PRECISION)
    blend_color = blend_sum.reshape(LB, -1, pixel_count).astype(jnp.bfloat16)
    trans_field = jnp.exp(jnp.dot(owner_table, log_trans, precision=EXACT_PRECISION))
    shaded = shade_blocks(blend_color, trans_field, w_in, trans_weight, w_mid, w_out)
    display_tiles = lax.all_to_all(shaded[None], "strip", split_axis=1, concat_axis=0, tiled=True)
    return display_tiles[None]


SMEM = pltpu.SMEM
VMEM = pltpu.VMEM
ROWS = 8
GROUP = 4


def fetch(sources, targets, sems):
    copies = [
        pltpu.make_async_copy(source, target, sems.at[i])
        for i, (source, target) in enumerate(zip(sources, targets))
    ]
    for copy in copies:
        copy.start()
    for copy in copies:
        copy.wait()


def pack_kernel(far_counts, far_colors, far_transmit, sends, counts, colors, transmit, tall, sems):
    n_slab = sends.shape[0]
    slots, feats, span = colors.shape[2:]
    me = lax.axis_index("slab")
    fetch((far_counts, far_colors, far_transmit), (counts, colors, transmit), sems)
    tall[...] = transmit[0, 0].astype(jnp.float32)
    row = lax.broadcasted_iota(jnp.int32, (ROWS, span), 0)
    off = jnp.int32(0)
    for c in range(n_slab):
        tail = jnp.ones((ROWS, span), jnp.float32)
        for r in range(MOST):
            slot = jnp.minimum(off + r, slots - 1)
            sends[c, pl.ds(r * feats, feats), :] = colors[0, 0, slot]
            tail = jnp.where(row == r, tall[pl.ds(slot, 1), :], tail)
        sends[c, pl.ds(MOST * feats, ROWS), :] = tail.astype(jnp.bfloat16)
        off = off + counts[0, me, c]


def plan_kernel(n_slab, slots, *refs):
    (counts, blocks, assign, depth), (rows, codes) = refs[:4], refs[4:]
    items = n_slab * MOST
    outs = codes.shape[1] // (2 * items)
    me = lax.axis_index("slab")
    row = lax.broadcasted_iota(jnp.int32, rows.shape[1:], 0)
    item_lane = lax.broadcasted_iota(jnp.int32, codes.shape, 1) // outs
    posv = jnp.zeros(rows.shape[1:], jnp.int32)
    depthv = jnp.zeros(rows.shape[1:], jnp.int32)
    firstv = jnp.zeros(rows.shape[1:], jnp.int32)
    codev = jnp.full(codes.shape, -1, jnp.int32)
    pos = []
    for s in range(n_slab):
        off = jnp.int32(0)
        for c in range(n_slab):
            off = off + jnp.where(c < me, counts[0, s, c], 0)
        count = counts[0, s, me]
        for r in range(MOST):
            i = s * MOST + r
            slot = jnp.minimum(off + r, slots - 1)
            here = assign[0, blocks[0, s, slot]] - me * LB
            here = jnp.where(r < count, here, -1)
            first = jnp.int32(i)
            for j in reversed(range(i)):
                first = jnp.where(pos[j] == here, j, first)
            pos.append(here)
            firstv = jnp.where(row == i, first, firstv)
            posv = jnp.where(row == i, here, posv)
            depthv = jnp.where(row == i, depth[s], depthv)
            codev = jnp.where(item_lane == i, jnp.where(first == i, here, -1), codev)
    rows[0] = posv
    rows[1] = depthv
    rows[2] = firstv
    codes[...] = codev.astype(jnp.float32).astype(jnp.bfloat16)


def place_kernel(w_in, trans_weight, far_out, w_first, w_out):
    feats, hidden = w_in.shape
    half_in = (w_in[...].astype(jnp.float32) * 0.5).astype(jnp.bfloat16)
    half_trans = trans_weight[...].astype(jnp.float32) * 0.5
    sub = lax.broadcasted_iota(jnp.int32, (16, hidden), 0)
    w_first[...] = jnp.zeros_like(w_first)
    for a in range(GROUP):
        w_first[a, pl.ds(a * feats, feats), :] = half_in
        tail = jnp.where(sub // 2 == a, half_trans, 0.0)
        w_first[a, pl.ds(GROUP * feats, 16), :] = tail.astype(jnp.bfloat16)
    w_out[...] = far_out[...]


def silu_half(u):
    return (u + u * jnp.tanh(u)).astype(jnp.bfloat16)


def later_layers(h, w_mid, w_out):
    for m in range(w_mid.shape[0]):
        h = silu_half(jnp.dot(h, w_mid[m], preferred_element_type=jnp.float32))
    y = lax.dot_general(
        w_out[...], h, (((1,), (1,)), ((), ())), preferred_element_type=jnp.float32
    )
    return y.astype(jnp.bfloat16).astype(jnp.float32)


def empty_kernel(trans_weight, w_mid, w_out, out):
    u = trans_weight[...].astype(jnp.float32) * 0.5
    h = silu_half(jnp.broadcast_to(u, (out.shape[1], u.shape[1])))
    y = later_layers(h, w_mid, w_out)
    outs = w_out.shape[0]
    for at in range(0, out.shape[0], outs):
        out[pl.ds(at, outs), :] = y


def shade_kernel(rows, codes, got, w_first, w_mid, w_out, out, acc, xt, ys):
    items, feats, span = acc.shape
    outs = w_out.shape[0]

    posv, depthv = rows[0], rows[1]
    front = jnp.ones((items, span), jnp.float32)
    total = jnp.ones((items, span), jnp.float32)
    for k in range(items // MOST):
        tail = got[k, pl.ds(MOST * feats, ROWS), :].astype(jnp.float32)
        for r in range(MOST):
            j = k * MOST + r
            trans_j = tail[r : r + 1, :]
            same = posv == posv[j : j + 1, :]
            total = jnp.where(same, total * trans_j, total)
            front = jnp.where(same & (depthv > depthv[j : j + 1, :]), front * trans_j, front)
    acc[...] = jnp.zeros_like(acc)
    for j in range(items):
        k, r = divmod(j, MOST)
        color = got[k, pl.ds(r * feats, feats), :].astype(jnp.float32)
        at = rows[2, j, 0]
        acc[at] = acc[at] + front[j : j + 1, :] * color
    total_hi = total.astype(jnp.bfloat16).astype(jnp.float32)
    total_lo = total - total_hi
    groups = items // GROUP
    sub = lax.broadcasted_iota(jnp.int32, (16, span), 0)
    xt[...] = jnp.zeros_like(xt)
    for q in range(groups):
        block = acc[pl.ds(q * GROUP, GROUP)].reshape(GROUP * feats, span)
        tail = jnp.zeros((16, span), jnp.float32)
        for a in range(GROUP):
            i = q * GROUP + a
            tail = jnp.where(sub == 2 * a, total_hi[i : i + 1, :], tail)
            tail = jnp.where(sub == 2 * a + 1, total_lo[i : i + 1, :], tail)
        lines = pl.ds(q * span, span)
        xt[lines, pl.ds(0, GROUP * feats)] = block.T.astype(jnp.bfloat16)
        xt[lines, pl.ds(GROUP * feats, 16)] = tail.T.astype(jnp.bfloat16)

    x = xt[...]
    stride = GROUP
    for start in range(0, GROUP, stride):
        h = jnp.concatenate(
            [
                silu_half(jnp.dot(x, w_first[a], preferred_element_type=jnp.float32))
                for a in range(start, start + stride)
            ]
        )
        y = later_layers(h, w_mid, w_out)
        for a in range(start, start + stride):
            for q in range(groups):
                at = ((a - start) * groups + q) * span
                ys[pl.ds((q * GROUP + a) * outs, outs), :] = y[:, at : at + span]
    out[pl.ds(0, items * outs), :] = ys[...].astype(jnp.bfloat16)
    out[pl.ds(items * outs, ROWS), :] = codes[...]


def join_kernel(*refs):
    *got, empty, out = refs
    _, n_strip, tile, outs, span = out.shape
    lines = tile * outs
    count = got[0].shape[0] - ROWS
    me = lax.axis_index("strip")
    want = lax.broadcasted_iota(jnp.int32, (lines, count), 0) + me * lines
    chan = lax.broadcasted_iota(jnp.int32, (lines, count), 1) % outs
    filler = jnp.concatenate([empty[...]] * (lines // ROWS))
    ones = jnp.ones((count, span), jnp.bfloat16)
    for k in range(n_strip):
        pos = got[k][pl.ds(count, ROWS), :].astype(jnp.float32)[:1, :count].astype(jnp.int32)
        hit = pos * outs + chan == want
        pick = jnp.where(hit, 1.0, 0.0).astype(jnp.bfloat16)
        blocks = got[k][pl.ds(0, count), :]
        placed = jnp.dot(pick, blocks, preferred_element_type=jnp.float32)
        filled = jnp.dot(pick, ones, preferred_element_type=jnp.float32)
        value = jnp.where(filled > 0.5, placed, filler)
        out[0, me ^ ((k + 1) % n_strip)] = value.reshape(tile, outs, span).astype(jnp.bfloat16)


def compact_device(
    n_slab,
    n_strip,
    colors,
    transmit,
    pair_counts,
    slot_block,
    assign,
    depth_rank,
    w_in,
    trans_weight,
    w_mid,
    w_out,
):
    slots, feats, span = colors.shape[2:]
    items = n_slab * MOST
    outs = w_out.shape[0]
    smem = pl.BlockSpec(memory_space=SMEM)
    vmem = pl.BlockSpec(memory_space=VMEM)
    hbm = pl.BlockSpec(memory_space=pltpu.HBM)
    small = pltpu.CompilerParams(vmem_limit_bytes=4 * 1024 * 1024)
    message = MOST * feats + ROWS
    sends = pl.pallas_call(
        pack_kernel,
        out_shape=jax.ShapeDtypeStruct((n_slab, message, span), jnp.bfloat16),
        in_specs=[hbm] * 3,
        out_specs=vmem,
        scratch_shapes=[
            pltpu.VMEM(pair_counts.shape, jnp.int32),
            pltpu.VMEM(colors.shape, colors.dtype),
            pltpu.VMEM(transmit.shape, transmit.dtype),
            pltpu.VMEM((slots, span), jnp.float32),
            pltpu.SemaphoreType.DMA((3,)),
        ],
        compiler_params=small,
        name="pack",
    )(*[pltpu.with_memory_space_constraint(a, pltpu.HBM) for a in (pair_counts, colors, transmit)])
    got = lax.all_to_all(sends, "slab", split_axis=0, concat_axis=0, tiled=True)
    hidden = w_in.shape[0]
    rough = pl.CostEstimate(flops=10**5, bytes_accessed=10**6, transcendentals=0)
    roomy = pltpu.CompilerParams(vmem_limit_bytes=16 * 1024 * 1024)
    trans_row = trans_weight[None]
    rows, codes = pl.pallas_call(
        functools.partial(plan_kernel, n_slab, slots),
        out_shape=[
            jax.ShapeDtypeStruct((3, items, span), jnp.int32),
            jax.ShapeDtypeStruct((ROWS, span), jnp.bfloat16),
        ],
        in_specs=[smem] * 4,
        out_specs=[vmem] * 2,
        compiler_params=small,
        cost_estimate=rough,
        name="plan",
    )(pair_counts, slot_block, assign, depth_rank)
    w_first, w_last = pl.pallas_call(
        place_kernel,
        out_shape=[
            jax.ShapeDtypeStruct((GROUP, 2 * GROUP * feats, hidden), jnp.bfloat16),
            jax.ShapeDtypeStruct(w_out.shape, jnp.bfloat16),
        ],
        in_specs=[vmem] * 3,
        out_specs=[vmem] * 2,
        compiler_params=small,
        cost_estimate=rough,
        name="place",
    )(w_in.T, trans_row, w_out)
    w_later = jnp.swapaxes(w_mid, 1, 2) * jnp.bfloat16(0.5)
    empty = pl.pallas_call(
        empty_kernel,
        out_shape=jax.ShapeDtypeStruct((ROWS, span), jnp.float32),
        in_specs=[vmem] * 3,
        out_specs=vmem,
        compiler_params=roomy,
        cost_estimate=rough,
        name="empty",
    )(trans_row, w_later, w_last)
    shaded = pl.pallas_call(
        shade_kernel,
        out_shape=jax.ShapeDtypeStruct((items * outs + ROWS, span), jnp.bfloat16),
        in_specs=[vmem] * 6,
        out_specs=vmem,
        scratch_shapes=[
            pltpu.VMEM((items, feats, span), jnp.float32),
            pltpu.VMEM((items // GROUP * span, 2 * GROUP * feats), jnp.bfloat16),
            pltpu.VMEM((items * outs, span), jnp.float32),
        ],
        compiler_params=roomy,
        name="shade",
    )(rows, codes, got, w_first, w_later, w_last)
    tiles = [
        lax.ppermute(shaded, "strip", [(s, s ^ k) for s in range(n_strip)])
        for k in range(1, n_strip)
    ] + [shaded]
    return pl.pallas_call(
        join_kernel,
        out_shape=jax.ShapeDtypeStruct((1, n_strip, LB // n_strip, outs, span), jnp.bfloat16),
        in_specs=[vmem] * (n_strip + 1),
        out_specs=pl.BlockSpec(),
        compiler_params=small,
        name="join",
    )(*tiles, empty)


def solution(mesh):
    n_slab, n_strip = mesh.shape["slab"], mesh.shape["strip"]
    placed = (
        P("slab", "strip", None, None, None),
        P("slab", "strip", None, None),
        P("strip", None, None),
        P("strip", None, None),
        P("strip", None),
        P(),
        P(),
        P(),
        P(),
        P(),
    )
    compact = n_strip & (n_strip - 1) == 0 and 4 * MOST * n_slab <= LB
    return jax.shard_map(
        functools.partial(compact_device, n_slab, n_strip) if compact else dense_device,
        mesh=mesh,
        in_specs=placed,
        out_specs=P("slab", None, "strip", None, None),
        check_vma=False,
    )
```

```python
import functools

import jax
import jax.numpy as jnp
from jax import lax
from jax.experimental import pallas as pl
from jax.experimental.pallas import tpu as pltpu
from jax.sharding import PartitionSpec as P

MOST = 2
LB = 128


EXACT_PRECISION = lax.Precision.HIGHEST


def shade_blocks(blend_color, trans_field, w_in, trans_weight, w_mid, w_out):
    summed = jnp.einsum("hf,lfp->lhp", w_in, blend_color, preferred_element_type=jnp.float32)
    summed = summed + trans_weight.astype(jnp.float32)[None, :, None] * trans_field[:, None, :]
    hidden = jax.nn.silu(summed).astype(jnp.bfloat16)
    for layer_index in range(w_mid.shape[0]):
        hidden = jax.nn.silu(
            jnp.einsum(
                "hg,lgp->lhp", w_mid[layer_index], hidden, preferred_element_type=jnp.float32
            )
        ).astype(jnp.bfloat16)
    return jnp.einsum("oh,lhp->lop", w_out, hidden, preferred_element_type=jnp.float32).astype(
        jnp.bfloat16
    )


def dense_device(
    colors, transmit, pair_counts, slot_block, assign, depth_rank, w_in, trans_weight, w_mid, w_out
):
    myself = lax.axis_index("slab")
    counts = pair_counts[0]
    blocks_all = slot_block[0]
    assign_row = assign[0]
    offsets = jnp.cumsum(counts, axis=1) - counts
    slot_rank = jnp.arange(MOST, dtype=jnp.int32)
    my_counts = lax.dynamic_index_in_dim(counts, myself, 0, keepdims=False)
    my_offsets = lax.dynamic_index_in_dim(offsets, myself, 0, keepdims=False)
    send_slots = jnp.where(
        slot_rank[None, :] < my_counts[:, None], my_offsets[:, None] + slot_rank[None, :], 0
    )
    send_color = colors[0, 0][send_slots]
    send_trans = transmit[0, 0][send_slots][:, :, None, :]
    incoming = lax.dynamic_index_in_dim(counts, myself, 1, keepdims=False)
    in_offsets = lax.dynamic_index_in_dim(offsets, myself, 1, keepdims=False)
    live_slot = slot_rank[None, :] < incoming[:, None]
    recv_slots = jnp.where(live_slot, in_offsets[:, None] + slot_rank[None, :], 0)
    recv_blocks = jnp.take_along_axis(blocks_all, recv_slots, axis=1)
    local_pos = assign_row[recv_blocks] - myself * LB
    live_flat = live_slot.reshape(-1)
    local_flat = jnp.where(live_flat, local_pos.reshape(-1), -1)
    depth_flat = jnp.repeat(depth_rank, MOST)
    ahead_table = (
        (local_flat[:, None] == local_flat[None, :])
        & (depth_flat[None, :] < depth_flat[:, None])
        & live_flat[None, :]
    )
    ahead_table = ahead_table.astype(jnp.float32)
    owner_table = (jnp.arange(LB, dtype=jnp.int32)[:, None] == local_flat[None, :]).astype(
        jnp.float32
    )
    got_color = lax.all_to_all(send_color, "slab", split_axis=0, concat_axis=0, tiled=True)
    got_trans = lax.all_to_all(send_trans, "slab", split_axis=0, concat_axis=0, tiled=True)
    pixel_count = got_color.shape[3]
    item_count = got_color.shape[0] * got_color.shape[1]
    log_trans = jnp.log(got_trans.reshape(item_count, pixel_count).astype(jnp.float32))
    log_trans = jnp.where(live_flat[:, None], log_trans, 0.0)
    front_log = jnp.dot(ahead_table, log_trans, precision=EXACT_PRECISION)
    front_share = jnp.where(live_flat[:, None], jnp.exp(front_log), 0.0)
    weighted = front_share[:, None, :] * got_color.reshape(item_count, -1, pixel_count).astype(
        jnp.float32
    )
    blend_sum = jnp.dot(owner_table, weighted.reshape(item_count, -1), precision=EXACT_PRECISION)
    blend_color = blend_sum.reshape(LB, -1, pixel_count).astype(jnp.bfloat16)
    trans_field = jnp.exp(jnp.dot(owner_table, log_trans, precision=EXACT_PRECISION))
    shaded = shade_blocks(blend_color, trans_field, w_in, trans_weight, w_mid, w_out)
    display_tiles = lax.all_to_all(shaded[None], "strip", split_axis=1, concat_axis=0, tiled=True)
    return display_tiles[None]


SMEM = pltpu.SMEM
VMEM = pltpu.VMEM
ROWS = 8
GROUP = 4


def pack_kernel(far_counts, colors, far_transmit, sends, counts, transmit, tall, sems, slot_sems):
    n_slab = sends.shape[0]
    slots, feats, span = colors.shape[2:]
    me = lax.axis_index("slab")
    get_counts = pltpu.make_async_copy(far_counts, counts, sems.at[0])
    get_transmit = pltpu.make_async_copy(far_transmit, transmit, sems.at[1])
    get_counts.start()
    get_transmit.start()
    get_counts.wait()
    off = jnp.int32(0)
    picks, copies = [], []
    for c in range(n_slab):
        for r in range(MOST):
            slot = jnp.minimum(off + r, slots - 1)
            copy = pltpu.make_async_copy(
                colors.at[0, 0, slot],
                sends.at[c, pl.ds(r * feats, feats)],
                slot_sems.at[c * MOST + r],
            )
            copy.start()
            picks.append(slot)
            copies.append(copy)
        off = off + counts[0, me, c]
    get_transmit.wait()
    tall[...] = transmit[0, 0].astype(jnp.float32)
    row = lax.broadcasted_iota(jnp.int32, (ROWS, span), 0)
    for c in range(n_slab):
        tail = jnp.ones((ROWS, span), jnp.float32)
        for r in range(MOST):
            tail = jnp.where(row == r, tall[pl.ds(picks[c * MOST + r], 1), :], tail)
        sends[c, pl.ds(MOST * feats, ROWS), :] = tail.astype(jnp.bfloat16)
    for copy in copies:
        copy.wait()


def plan_kernel(n_slab, slots, *refs):
    (counts, blocks, assign, depth), (rows, codes) = refs[:4], refs[4:]
    items = n_slab * MOST
    outs = codes.shape[1] // (2 * items)
    me = lax.axis_index("slab")
    row = lax.broadcasted_iota(jnp.int32, rows.shape[1:], 0)
    item_lane = lax.broadcasted_iota(jnp.int32, codes.shape, 1) // outs
    posv = jnp.zeros(rows.shape[1:], jnp.int32)
    depthv = jnp.zeros(rows.shape[1:], jnp.int32)
    firstv = jnp.zeros(rows.shape[1:], jnp.int32)
    codev = jnp.full(codes.shape, -1, jnp.int32)
    pos = []
    for s in range(n_slab):
        off = jnp.int32(0)
        for c in range(n_slab):
            off = off + jnp.where(c < me, counts[0, s, c], 0)
        count = counts[0, s, me]
        for r in range(MOST):
            i = s * MOST + r
            slot = jnp.minimum(off + r, slots - 1)
            here = assign[0, blocks[0, s, slot]] - me * LB
            here = jnp.where(r < count, here, -1)
            first = jnp.int32(i)
            for j in reversed(range(i)):
                first = jnp.where(pos[j] == here, j, first)
            pos.append(here)
            firstv = jnp.where(row == i, first, firstv)
            posv = jnp.where(row == i, here, posv)
            depthv = jnp.where(row == i, depth[s], depthv)
            codev = jnp.where(item_lane == i, jnp.where(first == i, here, -1), codev)
    rows[0] = posv
    rows[1] = depthv
    rows[2] = firstv
    codes[...] = codev.astype(jnp.float32).astype(jnp.bfloat16)


def place_kernel(w_in, trans_weight, far_out, w_first, w_out):
    feats, hidden = w_in.shape
    half_in = (w_in[...].astype(jnp.float32) * 0.5).astype(jnp.bfloat16)
    half_trans = trans_weight[...].astype(jnp.float32) * 0.5
    sub = lax.broadcasted_iota(jnp.int32, (16, hidden), 0)
    w_first[...] = jnp.zeros_like(w_first)
    for a in range(GROUP):
        w_first[a, pl.ds(a * feats, feats), :] = half_in
        tail = jnp.where(sub // 2 == a, half_trans, 0.0)
        w_first[a, pl.ds(GROUP * feats, 16), :] = tail.astype(jnp.bfloat16)
    w_out[...] = far_out[...]


def silu_half(u):
    return (u + u * jnp.tanh(u)).astype(jnp.bfloat16)


def later_layers(h, w_mid, w_out):
    for m in range(w_mid.shape[0]):
        h = silu_half(jnp.dot(h, w_mid[m], preferred_element_type=jnp.float32))
    y = lax.dot_general(
        w_out[...], h, (((1,), (1,)), ((), ())), preferred_element_type=jnp.float32
    )
    return y.astype(jnp.bfloat16).astype(jnp.float32)


def empty_kernel(trans_weight, w_mid, w_out, out):
    u = trans_weight[...].astype(jnp.float32) * 0.5
    h = silu_half(jnp.broadcast_to(u, (out.shape[1], u.shape[1])))
    y = later_layers(h, w_mid, w_out)
    outs = w_out.shape[0]
    for at in range(0, out.shape[0], outs):
        out[pl.ds(at, outs), :] = y


def shade_kernel(rows, codes, got, w_first, w_mid, w_out, out, acc, xt, ys):
    items, feats, span = acc.shape
    outs = w_out.shape[0]

    posv, depthv = rows[0], rows[1]
    front = jnp.ones((items, span), jnp.float32)
    total = jnp.ones((items, span), jnp.float32)
    for k in range(items // MOST):
        tail = got[k, pl.ds(MOST * feats, ROWS), :].astype(jnp.float32)
        for r in range(MOST):
            j = k * MOST + r
            trans_j = tail[r : r + 1, :]
            same = posv == posv[j : j + 1, :]
            total = jnp.where(same, total * trans_j, total)
            front = jnp.where(same & (depthv > depthv[j : j + 1, :]), front * trans_j, front)
    acc[...] = jnp.zeros_like(acc)
    for j in range(items):
        k, r = divmod(j, MOST)
        color = got[k, pl.ds(r * feats, feats), :].astype(jnp.float32)
        at = rows[2, j, 0]
        acc[at] = acc[at] + front[j : j + 1, :] * color
    total_hi = total.astype(jnp.bfloat16).astype(jnp.float32)
    total_lo = total - total_hi
    groups = items // GROUP
    sub = lax.broadcasted_iota(jnp.int32, (16, span), 0)
    xt[...] = jnp.zeros_like(xt)
    for q in range(groups):
        block = acc[pl.ds(q * GROUP, GROUP)].reshape(GROUP * feats, span)
        tail = jnp.zeros((16, span), jnp.float32)
        for a in range(GROUP):
            i = q * GROUP + a
            tail = jnp.where(sub == 2 * a, total_hi[i : i + 1, :], tail)
            tail = jnp.where(sub == 2 * a + 1, total_lo[i : i + 1, :], tail)
        lines = pl.ds(q * span, span)
        xt[lines, pl.ds(0, GROUP * feats)] = block.T.astype(jnp.bfloat16)
        xt[lines, pl.ds(GROUP * feats, 16)] = tail.T.astype(jnp.bfloat16)

    x = xt[...]
    stride = GROUP
    for start in range(0, GROUP, stride):
        h = jnp.concatenate(
            [
                silu_half(jnp.dot(x, w_first[a], preferred_element_type=jnp.float32))
                for a in range(start, start + stride)
            ]
        )
        y = later_layers(h, w_mid, w_out)
        for a in range(start, start + stride):
            for q in range(groups):
                at = ((a - start) * groups + q) * span
                ys[pl.ds((q * GROUP + a) * outs, outs), :] = y[:, at : at + span]
    out[pl.ds(0, items * outs), :] = ys[...].astype(jnp.bfloat16)
    out[pl.ds(items * outs, ROWS), :] = codes[...]


def join_kernel(*refs):
    *got, empty, out = refs
    _, n_strip, tile, outs, span = out.shape
    lines = tile * outs
    count = got[0].shape[0] - ROWS
    me = lax.axis_index("strip")
    want = lax.broadcasted_iota(jnp.int32, (lines, count), 0) + me * lines
    chan = lax.broadcasted_iota(jnp.int32, (lines, count), 1) % outs
    filler = jnp.concatenate([empty[...]] * (lines // ROWS))
    ones = jnp.ones((count, span), jnp.bfloat16)
    for k in range(n_strip):
        pos = got[k][pl.ds(count, ROWS), :].astype(jnp.float32)[:1, :count].astype(jnp.int32)
        hit = pos * outs + chan == want
        pick = jnp.where(hit, 1.0, 0.0).astype(jnp.bfloat16)
        blocks = got[k][pl.ds(0, count), :]
        placed = jnp.dot(pick, blocks, preferred_element_type=jnp.float32)
        filled = jnp.dot(pick, ones, preferred_element_type=jnp.float32)
        value = jnp.where(filled > 0.5, placed, filler)
        out[0, me ^ ((k + 1) % n_strip)] = value.reshape(tile, outs, span).astype(jnp.bfloat16)


def compact_device(
    n_slab,
    n_strip,
    colors,
    transmit,
    pair_counts,
    slot_block,
    assign,
    depth_rank,
    w_in,
    trans_weight,
    w_mid,
    w_out,
):
    slots, feats, span = colors.shape[2:]
    items = n_slab * MOST
    outs = w_out.shape[0]
    smem = pl.BlockSpec(memory_space=SMEM)
    vmem = pl.BlockSpec(memory_space=VMEM)
    hbm = pl.BlockSpec(memory_space=pltpu.HBM)
    small = pltpu.CompilerParams(vmem_limit_bytes=4 * 1024 * 1024)
    message = MOST * feats + ROWS
    sends = pl.pallas_call(
        pack_kernel,
        out_shape=jax.ShapeDtypeStruct((n_slab, message, span), jnp.bfloat16),
        in_specs=[hbm] * 3,
        out_specs=vmem,
        scratch_shapes=[
            pltpu.VMEM(pair_counts.shape, jnp.int32),
            pltpu.VMEM(transmit.shape, transmit.dtype),
            pltpu.VMEM((slots, span), jnp.float32),
            pltpu.SemaphoreType.DMA((2,)),
            pltpu.SemaphoreType.DMA((n_slab * MOST,)),
        ],
        compiler_params=small,
        name="pack",
    )(*[pltpu.with_memory_space_constraint(a, pltpu.HBM) for a in (pair_counts, colors, transmit)])
    got = lax.all_to_all(sends, "slab", split_axis=0, concat_axis=0, tiled=True)
    hidden = w_in.shape[0]
    rough = pl.CostEstimate(flops=10**5, bytes_accessed=10**6, transcendentals=0)
    roomy = pltpu.CompilerParams(vmem_limit_bytes=16 * 1024 * 1024)
    trans_row = trans_weight[None]
    rows, codes = pl.pallas_call(
        functools.partial(plan_kernel, n_slab, slots),
        out_shape=[
            jax.ShapeDtypeStruct((3, items, span), jnp.int32),
            jax.ShapeDtypeStruct((ROWS, span), jnp.bfloat16),
        ],
        in_specs=[smem] * 4,
        out_specs=[vmem] * 2,
        compiler_params=small,
        cost_estimate=rough,
        name="plan",
    )(pair_counts, slot_block, assign, depth_rank)
    w_first, w_last = pl.pallas_call(
        place_kernel,
        out_shape=[
            jax.ShapeDtypeStruct((GROUP, 2 * GROUP * feats, hidden), jnp.bfloat16),
            jax.ShapeDtypeStruct(w_out.shape, jnp.bfloat16),
        ],
        in_specs=[vmem] * 3,
        out_specs=[vmem] * 2,
        compiler_params=small,
        cost_estimate=rough,
        name="place",
    )(w_in.T, trans_row, w_out)
    w_later = jnp.swapaxes(w_mid, 1, 2) * jnp.bfloat16(0.5)
    empty = pl.pallas_call(
        empty_kernel,
        out_shape=jax.ShapeDtypeStruct((ROWS, span), jnp.float32),
        in_specs=[vmem] * 3,
        out_specs=vmem,
        compiler_params=roomy,
        cost_estimate=rough,
        name="empty",
    )(trans_row, w_later, w_last)
    shaded = pl.pallas_call(
        shade_kernel,
        out_shape=jax.ShapeDtypeStruct((items * outs + ROWS, span), jnp.bfloat16),
        in_specs=[vmem] * 6,
        out_specs=vmem,
        scratch_shapes=[
            pltpu.VMEM((items, feats, span), jnp.float32),
            pltpu.VMEM((items // GROUP * span, 2 * GROUP * feats), jnp.bfloat16),
            pltpu.VMEM((items * outs, span), jnp.float32),
        ],
        compiler_params=roomy,
        name="shade",
    )(rows, codes, got, w_first, w_later, w_last)
    tiles = [
        lax.ppermute(shaded, "strip", [(s, s ^ k) for s in range(n_strip)])
        for k in range(1, n_strip)
    ] + [shaded]
    return pl.pallas_call(
        join_kernel,
        out_shape=jax.ShapeDtypeStruct((1, n_strip, LB // n_strip, outs, span), jnp.bfloat16),
        in_specs=[vmem] * (n_strip + 1),
        out_specs=pl.BlockSpec(),
        compiler_params=small,
        name="join",
    )(*tiles, empty)


def solution(mesh):
    n_slab, n_strip = mesh.shape["slab"], mesh.shape["strip"]
    placed = (
        P("slab", "strip", None, None, None),
        P("slab", "strip", None, None),
        P("strip", None, None),
        P("strip", None, None),
        P("strip", None),
        P(),
        P(),
        P(),
        P(),
        P(),
    )
    compact = n_strip & (n_strip - 1) == 0 and 4 * MOST * n_slab <= LB
    return jax.shard_map(
        functools.partial(compact_device, n_slab, n_strip) if compact else dense_device,
        mesh=mesh,
        in_specs=placed,
        out_specs=P("slab", None, "strip", None, None),
        check_vma=False,
    )
```

```python
import functools

import jax
import jax.numpy as jnp
from jax import lax
from jax.experimental import pallas as pl
from jax.experimental.pallas import tpu as pltpu
from jax.sharding import PartitionSpec as P

MOST = 2
LB = 128


EXACT_PRECISION = lax.Precision.HIGHEST


def shade_blocks(blend_color, trans_field, w_in, trans_weight, w_mid, w_out):
    summed = jnp.einsum("hf,lfp->lhp", w_in, blend_color, preferred_element_type=jnp.float32)
    summed = summed + trans_weight.astype(jnp.float32)[None, :, None] * trans_field[:, None, :]
    hidden = jax.nn.silu(summed).astype(jnp.bfloat16)
    for layer_index in range(w_mid.shape[0]):
        hidden = jax.nn.silu(
            jnp.einsum(
                "hg,lgp->lhp", w_mid[layer_index], hidden, preferred_element_type=jnp.float32
            )
        ).astype(jnp.bfloat16)
    return jnp.einsum("oh,lhp->lop", w_out, hidden, preferred_element_type=jnp.float32).astype(
        jnp.bfloat16
    )


def dense_device(
    colors, transmit, pair_counts, slot_block, assign, depth_rank, w_in, trans_weight, w_mid, w_out
):
    myself = lax.axis_index("slab")
    counts = pair_counts[0]
    blocks_all = slot_block[0]
    assign_row = assign[0]
    offsets = jnp.cumsum(counts, axis=1) - counts
    slot_rank = jnp.arange(MOST, dtype=jnp.int32)
    my_counts = lax.dynamic_index_in_dim(counts, myself, 0, keepdims=False)
    my_offsets = lax.dynamic_index_in_dim(offsets, myself, 0, keepdims=False)
    send_slots = jnp.where(
        slot_rank[None, :] < my_counts[:, None], my_offsets[:, None] + slot_rank[None, :], 0
    )
    send_color = colors[0, 0][send_slots]
    send_trans = transmit[0, 0][send_slots][:, :, None, :]
    incoming = lax.dynamic_index_in_dim(counts, myself, 1, keepdims=False)
    in_offsets = lax.dynamic_index_in_dim(offsets, myself, 1, keepdims=False)
    live_slot = slot_rank[None, :] < incoming[:, None]
    recv_slots = jnp.where(live_slot, in_offsets[:, None] + slot_rank[None, :], 0)
    recv_blocks = jnp.take_along_axis(blocks_all, recv_slots, axis=1)
    local_pos = assign_row[recv_blocks] - myself * LB
    live_flat = live_slot.reshape(-1)
    local_flat = jnp.where(live_flat, local_pos.reshape(-1), -1)
    depth_flat = jnp.repeat(depth_rank, MOST)
    ahead_table = (
        (local_flat[:, None] == local_flat[None, :])
        & (depth_flat[None, :] < depth_flat[:, None])
        & live_flat[None, :]
    )
    ahead_table = ahead_table.astype(jnp.float32)
    owner_table = (jnp.arange(LB, dtype=jnp.int32)[:, None] == local_flat[None, :]).astype(
        jnp.float32
    )
    got_color = lax.all_to_all(send_color, "slab", split_axis=0, concat_axis=0, tiled=True)
    got_trans = lax.all_to_all(send_trans, "slab", split_axis=0, concat_axis=0, tiled=True)
    pixel_count = got_color.shape[3]
    item_count = got_color.shape[0] * got_color.shape[1]
    log_trans = jnp.log(got_trans.reshape(item_count, pixel_count).astype(jnp.float32))
    log_trans = jnp.where(live_flat[:, None], log_trans, 0.0)
    front_log = jnp.dot(ahead_table, log_trans, precision=EXACT_PRECISION)
    front_share = jnp.where(live_flat[:, None], jnp.exp(front_log), 0.0)
    weighted = front_share[:, None, :] * got_color.reshape(item_count, -1, pixel_count).astype(
        jnp.float32
    )
    blend_sum = jnp.dot(owner_table, weighted.reshape(item_count, -1), precision=EXACT_PRECISION)
    blend_color = blend_sum.reshape(LB, -1, pixel_count).astype(jnp.bfloat16)
    trans_field = jnp.exp(jnp.dot(owner_table, log_trans, precision=EXACT_PRECISION))
    shaded = shade_blocks(blend_color, trans_field, w_in, trans_weight, w_mid, w_out)
    display_tiles = lax.all_to_all(shaded[None], "strip", split_axis=1, concat_axis=0, tiled=True)
    return display_tiles[None]


SMEM = pltpu.SMEM
VMEM = pltpu.VMEM
ROWS = 8
GROUP = 4


def pack_kernel(far_counts, far_colors, far_transmit, sends, counts, colors, transmit, sems):
    n_slab = sends.shape[0]
    slots, feats, span = colors.shape[2:]
    me = lax.axis_index("slab")
    copies = [
        pltpu.make_async_copy(far, near, sems.at[i])
        for i, (far, near) in enumerate(
            ((far_counts, counts), (far_transmit, transmit), (far_colors, colors))
        )
    ]
    for copy in copies:
        copy.start()
    copies[0].wait()
    mine = counts[0, pl.ds(me, 1), :].astype(jnp.float32)
    before = lax.broadcasted_iota(jnp.int32, mine.shape, 1)
    row = lax.broadcasted_iota(jnp.int32, (ROWS, slots), 0).astype(jnp.float32)
    lane = lax.broadcasted_iota(jnp.int32, (ROWS, slots), 1).astype(jnp.float32)
    offs, picks = [], []
    for c in range(n_slab):
        off = jnp.sum(jnp.where(before < c, mine, 0.0), axis=1, keepdims=True)
        offs.append(off)
        hit = (row < MOST) & (lane - row == off)
        picks.append(jnp.where(hit, 1.0, 0.0))
    pick = jnp.concatenate(picks).astype(jnp.bfloat16)
    copies[1].wait()
    tails = jnp.dot(pick, transmit[0, 0], preferred_element_type=jnp.float32)
    for c in range(n_slab):
        tail = tails[c * ROWS : (c + 1) * ROWS]
        sends[c, pl.ds(MOST * feats, ROWS), :] = tail.astype(jnp.bfloat16)
    copies[2].wait()
    for c in range(n_slab):
        off = jnp.broadcast_to(offs[c], (feats, span)).astype(jnp.bfloat16)
        for r in range(MOST):
            last = min(MOST * c + r, slots - 1)
            block = colors[0, 0, last]
            for slot in range(r, last):
                block = jnp.where(off == slot - r, colors[0, 0, slot], block)
            sends[c, pl.ds(r * feats, feats), :] = block


def plan_kernel(n_slab, slots, *refs):
    (counts, blocks, assign, depth), (rows, codes) = refs[:4], refs[4:]
    items = n_slab * MOST
    outs = codes.shape[1] // (2 * items)
    me = lax.axis_index("slab")
    row = lax.broadcasted_iota(jnp.int32, rows.shape[1:], 0)
    item_lane = lax.broadcasted_iota(jnp.int32, codes.shape, 1) // outs
    posv = jnp.zeros(rows.shape[1:], jnp.int32)
    depthv = jnp.zeros(rows.shape[1:], jnp.int32)
    firstv = jnp.zeros(rows.shape[1:], jnp.int32)
    codev = jnp.full(codes.shape, -1, jnp.int32)
    pos = []
    for s in range(n_slab):
        off = jnp.int32(0)
        for c in range(n_slab):
            off = off + jnp.where(c < me, counts[0, s, c], 0)
        count = counts[0, s, me]
        for r in range(MOST):
            i = s * MOST + r
            slot = jnp.minimum(off + r, slots - 1)
            here = assign[0, blocks[0, s, slot]] - me * LB
            here = jnp.where(r < count, here, -1)
            first = jnp.int32(i)
            for j in reversed(range(i)):
                first = jnp.where(pos[j] == here, j, first)
            pos.append(here)
            firstv = jnp.where(row == i, first, firstv)
            posv = jnp.where(row == i, here, posv)
            depthv = jnp.where(row == i, depth[s], depthv)
            codev = jnp.where(item_lane == i, jnp.where(first == i, here, -1), codev)
    rows[0] = posv
    rows[1] = depthv
    rows[2] = firstv
    codes[...] = codev.astype(jnp.float32).astype(jnp.bfloat16)


def place_kernel(w_in, trans_weight, far_out, w_first, w_out):
    feats, hidden = w_in.shape
    half_in = (w_in[...].astype(jnp.float32) * 0.5).astype(jnp.bfloat16)
    half_trans = trans_weight[...].astype(jnp.float32) * 0.5
    sub = lax.broadcasted_iota(jnp.int32, (16, hidden), 0)
    w_first[...] = jnp.zeros_like(w_first)
    for a in range(GROUP):
        w_first[a, pl.ds(a * feats, feats), :] = half_in
        tail = jnp.where(sub // 2 == a, half_trans, 0.0)
        w_first[a, pl.ds(GROUP * feats, 16), :] = tail.astype(jnp.bfloat16)
    w_out[...] = far_out[...]


def silu_half(u):
    return (u + u * jnp.tanh(u)).astype(jnp.bfloat16)


def later_layers(h, w_mid, w_out):
    for m in range(w_mid.shape[0]):
        h = silu_half(jnp.dot(h, w_mid[m], preferred_element_type=jnp.float32))
    y = lax.dot_general(
        w_out[...], h, (((1,), (1,)), ((), ())), preferred_element_type=jnp.float32
    )
    return y.astype(jnp.bfloat16).astype(jnp.float32)


def empty_kernel(trans_weight, w_mid, w_out, out):
    u = trans_weight[...].astype(jnp.float32) * 0.5
    h = silu_half(jnp.broadcast_to(u, (out.shape[1], u.shape[1])))
    y = later_layers(h, w_mid, w_out)
    outs = w_out.shape[0]
    for at in range(0, out.shape[0], outs):
        out[pl.ds(at, outs), :] = y


def shade_kernel(rows, codes, got, w_first, w_mid, w_out, out, acc, xt, ys):
    items, feats, span = acc.shape
    outs = w_out.shape[0]

    posv, depthv = rows[0], rows[1]
    front = jnp.ones((items, span), jnp.float32)
    total = jnp.ones((items, span), jnp.float32)
    for k in range(items // MOST):
        tail = got[k, pl.ds(MOST * feats, ROWS), :].astype(jnp.float32)
        for r in range(MOST):
            j = k * MOST + r
            trans_j = tail[r : r + 1, :]
            same = posv == posv[j : j + 1, :]
            total = jnp.where(same, total * trans_j, total)
            front = jnp.where(same & (depthv > depthv[j : j + 1, :]), front * trans_j, front)
    acc[...] = jnp.zeros_like(acc)
    for j in range(items):
        k, r = divmod(j, MOST)
        color = got[k, pl.ds(r * feats, feats), :].astype(jnp.float32)
        at = rows[2, j, 0]
        acc[at] = acc[at] + front[j : j + 1, :] * color
    total_hi = total.astype(jnp.bfloat16).astype(jnp.float32)
    total_lo = total - total_hi
    groups = items // GROUP
    sub = lax.broadcasted_iota(jnp.int32, (16, span), 0)
    xt[...] = jnp.zeros_like(xt)
    for q in range(groups):
        block = acc[pl.ds(q * GROUP, GROUP)].reshape(GROUP * feats, span)
        tail = jnp.zeros((16, span), jnp.float32)
        for a in range(GROUP):
            i = q * GROUP + a
            tail = jnp.where(sub == 2 * a, total_hi[i : i + 1, :], tail)
            tail = jnp.where(sub == 2 * a + 1, total_lo[i : i + 1, :], tail)
        lines = pl.ds(q * span, span)
        xt[lines, pl.ds(0, GROUP * feats)] = block.T.astype(jnp.bfloat16)
        xt[lines, pl.ds(GROUP * feats, 16)] = tail.T.astype(jnp.bfloat16)

    x = xt[...]
    stride = GROUP
    for start in range(0, GROUP, stride):
        h = jnp.concatenate(
            [
                silu_half(jnp.dot(x, w_first[a], preferred_element_type=jnp.float32))
                for a in range(start, start + stride)
            ]
        )
        y = later_layers(h, w_mid, w_out)
        for a in range(start, start + stride):
            for q in range(groups):
                at = ((a - start) * groups + q) * span
                ys[pl.ds((q * GROUP + a) * outs, outs), :] = y[:, at : at + span]
    out[pl.ds(0, items * outs), :] = ys[...].astype(jnp.bfloat16)
    out[pl.ds(items * outs, ROWS), :] = codes[...]


def join_kernel(*refs):
    *got, empty, out = refs
    _, n_strip, tile, outs, span = out.shape
    lines = tile * outs
    count = got[0].shape[0] - ROWS
    me = lax.axis_index("strip")
    want = lax.broadcasted_iota(jnp.int32, (lines, count), 0) + me * lines
    chan = lax.broadcasted_iota(jnp.int32, (lines, count), 1) % outs
    filler = jnp.concatenate([empty[...]] * (lines // ROWS))
    ones = jnp.ones((count, span), jnp.bfloat16)
    for k in range(n_strip):
        pos = got[k][pl.ds(count, ROWS), :].astype(jnp.float32)[:1, :count].astype(jnp.int32)
        hit = pos * outs + chan == want
        pick = jnp.where(hit, 1.0, 0.0).astype(jnp.bfloat16)
        blocks = got[k][pl.ds(0, count), :]
        placed = jnp.dot(pick, blocks, preferred_element_type=jnp.float32)
        filled = jnp.dot(pick, ones, preferred_element_type=jnp.float32)
        value = jnp.where(filled > 0.5, placed, filler)
        out[0, me ^ ((k + 1) % n_strip)] = value.reshape(tile, outs, span).astype(jnp.bfloat16)


def compact_device(
    n_slab,
    n_strip,
    colors,
    transmit,
    pair_counts,
    slot_block,
    assign,
    depth_rank,
    w_in,
    trans_weight,
    w_mid,
    w_out,
):
    slots, feats, span = colors.shape[2:]
    items = n_slab * MOST
    outs = w_out.shape[0]
    smem = pl.BlockSpec(memory_space=SMEM)
    vmem = pl.BlockSpec(memory_space=VMEM)
    hbm = pl.BlockSpec(memory_space=pltpu.HBM)
    small = pltpu.CompilerParams(vmem_limit_bytes=4 * 1024 * 1024)
    message = MOST * feats + ROWS
    sends = pl.pallas_call(
        pack_kernel,
        out_shape=jax.ShapeDtypeStruct((n_slab, message, span), jnp.bfloat16),
        in_specs=[hbm] * 3,
        out_specs=vmem,
        scratch_shapes=[
            pltpu.VMEM(pair_counts.shape, jnp.int32),
            pltpu.VMEM(colors.shape, colors.dtype),
            pltpu.VMEM(transmit.shape, transmit.dtype),
            pltpu.SemaphoreType.DMA((3,)),
        ],
        compiler_params=small,
        name="pack",
    )(*[pltpu.with_memory_space_constraint(a, pltpu.HBM) for a in (pair_counts, colors, transmit)])
    got = lax.all_to_all(sends, "slab", split_axis=0, concat_axis=0, tiled=True)
    hidden = w_in.shape[0]
    rough = pl.CostEstimate(flops=10**5, bytes_accessed=10**6, transcendentals=0)
    roomy = pltpu.CompilerParams(vmem_limit_bytes=16 * 1024 * 1024)
    trans_row = trans_weight[None]
    rows, codes = pl.pallas_call(
        functools.partial(plan_kernel, n_slab, slots),
        out_shape=[
            jax.ShapeDtypeStruct((3, items, span), jnp.int32),
            jax.ShapeDtypeStruct((ROWS, span), jnp.bfloat16),
        ],
        in_specs=[smem] * 4,
        out_specs=[vmem] * 2,
        compiler_params=small,
        cost_estimate=rough,
        name="plan",
    )(pair_counts, slot_block, assign, depth_rank)
    w_first, w_last = pl.pallas_call(
        place_kernel,
        out_shape=[
            jax.ShapeDtypeStruct((GROUP, 2 * GROUP * feats, hidden), jnp.bfloat16),
            jax.ShapeDtypeStruct(w_out.shape, jnp.bfloat16),
        ],
        in_specs=[vmem] * 3,
        out_specs=[vmem] * 2,
        compiler_params=small,
        cost_estimate=rough,
        name="place",
    )(w_in.T, trans_row, w_out)
    w_later = jnp.swapaxes(w_mid, 1, 2) * jnp.bfloat16(0.5)
    empty = pl.pallas_call(
        empty_kernel,
        out_shape=jax.ShapeDtypeStruct((ROWS, span), jnp.float32),
        in_specs=[vmem] * 3,
        out_specs=vmem,
        compiler_params=roomy,
        cost_estimate=rough,
        name="empty",
    )(trans_row, w_later, w_last)
    shaded = pl.pallas_call(
        shade_kernel,
        out_shape=jax.ShapeDtypeStruct((items * outs + ROWS, span), jnp.bfloat16),
        in_specs=[vmem] * 6,
        out_specs=vmem,
        scratch_shapes=[
            pltpu.VMEM((items, feats, span), jnp.float32),
            pltpu.VMEM((items // GROUP * span, 2 * GROUP * feats), jnp.bfloat16),
            pltpu.VMEM((items * outs, span), jnp.float32),
        ],
        compiler_params=roomy,
        name="shade",
    )(rows, codes, got, w_first, w_later, w_last)
    tiles = [
        lax.ppermute(shaded, "strip", [(s, s ^ k) for s in range(n_strip)])
        for k in range(1, n_strip)
    ] + [shaded]
    return pl.pallas_call(
        join_kernel,
        out_shape=jax.ShapeDtypeStruct((1, n_strip, LB // n_strip, outs, span), jnp.bfloat16),
        in_specs=[vmem] * (n_strip + 1),
        out_specs=pl.BlockSpec(),
        compiler_params=small,
        name="join",
    )(*tiles, empty)


def solution(mesh):
    n_slab, n_strip = mesh.shape["slab"], mesh.shape["strip"]
    placed = (
        P("slab", "strip", None, None, None),
        P("slab", "strip", None, None),
        P("strip", None, None),
        P("strip", None, None),
        P("strip", None),
        P(),
        P(),
        P(),
        P(),
        P(),
    )
    compact = n_strip & (n_strip - 1) == 0 and 4 * MOST * n_slab <= LB
    return jax.shard_map(
        functools.partial(compact_device, n_slab, n_strip) if compact else dense_device,
        mesh=mesh,
        in_specs=placed,
        out_specs=P("slab", None, "strip", None, None),
        check_vma=False,
    )
```

```python
import functools

import jax
import jax.numpy as jnp
from jax import lax
from jax.experimental import pallas as pl
from jax.experimental.pallas import tpu as pltpu
from jax.sharding import PartitionSpec as P

MOST = 2
LB = 128


EXACT_PRECISION = lax.Precision.HIGHEST


def shade_blocks(blend_color, trans_field, w_in, trans_weight, w_mid, w_out):
    summed = jnp.einsum("hf,lfp->lhp", w_in, blend_color, preferred_element_type=jnp.float32)
    summed = summed + trans_weight.astype(jnp.float32)[None, :, None] * trans_field[:, None, :]
    hidden = jax.nn.silu(summed).astype(jnp.bfloat16)
    for layer_index in range(w_mid.shape[0]):
        hidden = jax.nn.silu(
            jnp.einsum(
                "hg,lgp->lhp", w_mid[layer_index], hidden, preferred_element_type=jnp.float32
            )
        ).astype(jnp.bfloat16)
    return jnp.einsum("oh,lhp->lop", w_out, hidden, preferred_element_type=jnp.float32).astype(
        jnp.bfloat16
    )


def dense_device(
    colors, transmit, pair_counts, slot_block, assign, depth_rank, w_in, trans_weight, w_mid, w_out
):
    myself = lax.axis_index("slab")
    counts = pair_counts[0]
    blocks_all = slot_block[0]
    assign_row = assign[0]
    offsets = jnp.cumsum(counts, axis=1) - counts
    slot_rank = jnp.arange(MOST, dtype=jnp.int32)
    my_counts = lax.dynamic_index_in_dim(counts, myself, 0, keepdims=False)
    my_offsets = lax.dynamic_index_in_dim(offsets, myself, 0, keepdims=False)
    send_slots = jnp.where(
        slot_rank[None, :] < my_counts[:, None], my_offsets[:, None] + slot_rank[None, :], 0
    )
    send_color = colors[0, 0][send_slots]
    send_trans = transmit[0, 0][send_slots][:, :, None, :]
    incoming = lax.dynamic_index_in_dim(counts, myself, 1, keepdims=False)
    in_offsets = lax.dynamic_index_in_dim(offsets, myself, 1, keepdims=False)
    live_slot = slot_rank[None, :] < incoming[:, None]
    recv_slots = jnp.where(live_slot, in_offsets[:, None] + slot_rank[None, :], 0)
    recv_blocks = jnp.take_along_axis(blocks_all, recv_slots, axis=1)
    local_pos = assign_row[recv_blocks] - myself * LB
    live_flat = live_slot.reshape(-1)
    local_flat = jnp.where(live_flat, local_pos.reshape(-1), -1)
    depth_flat = jnp.repeat(depth_rank, MOST)
    ahead_table = (
        (local_flat[:, None] == local_flat[None, :])
        & (depth_flat[None, :] < depth_flat[:, None])
        & live_flat[None, :]
    )
    ahead_table = ahead_table.astype(jnp.float32)
    owner_table = (jnp.arange(LB, dtype=jnp.int32)[:, None] == local_flat[None, :]).astype(
        jnp.float32
    )
    got_color = lax.all_to_all(send_color, "slab", split_axis=0, concat_axis=0, tiled=True)
    got_trans = lax.all_to_all(send_trans, "slab", split_axis=0, concat_axis=0, tiled=True)
    pixel_count = got_color.shape[3]
    item_count = got_color.shape[0] * got_color.shape[1]
    log_trans = jnp.log(got_trans.reshape(item_count, pixel_count).astype(jnp.float32))
    log_trans = jnp.where(live_flat[:, None], log_trans, 0.0)
    front_log = jnp.dot(ahead_table, log_trans, precision=EXACT_PRECISION)
    front_share = jnp.where(live_flat[:, None], jnp.exp(front_log), 0.0)
    weighted = front_share[:, None, :] * got_color.reshape(item_count, -1, pixel_count).astype(
        jnp.float32
    )
    blend_sum = jnp.dot(owner_table, weighted.reshape(item_count, -1), precision=EXACT_PRECISION)
    blend_color = blend_sum.reshape(LB, -1, pixel_count).astype(jnp.bfloat16)
    trans_field = jnp.exp(jnp.dot(owner_table, log_trans, precision=EXACT_PRECISION))
    shaded = shade_blocks(blend_color, trans_field, w_in, trans_weight, w_mid, w_out)
    display_tiles = lax.all_to_all(shaded[None], "strip", split_axis=1, concat_axis=0, tiled=True)
    return display_tiles[None]


SMEM = pltpu.SMEM
VMEM = pltpu.VMEM
ROWS = 8
GROUP = 4


def pack_kernel(far_counts, far_colors, far_transmit, sends, counts, colors, transmit, sems):
    n_slab = sends.shape[0]
    slots, feats, span = colors.shape[2:]
    me = lax.axis_index("slab")
    copies = [
        pltpu.make_async_copy(far, near, sems.at[i])
        for i, (far, near) in enumerate(
            ((far_counts, counts), (far_transmit, transmit), (far_colors, colors))
        )
    ]
    for copy in copies:
        copy.start()
    copies[0].wait()
    mine = counts[0, pl.ds(me, 1), :].astype(jnp.float32)
    before = lax.broadcasted_iota(jnp.int32, mine.shape, 1)
    row = lax.broadcasted_iota(jnp.int32, (ROWS, slots), 0).astype(jnp.float32)
    lane = lax.broadcasted_iota(jnp.int32, (ROWS, slots), 1).astype(jnp.float32)
    offs, picks = [], []
    for c in range(n_slab):
        off = jnp.sum(jnp.where(before < c, mine, 0.0), axis=1, keepdims=True)
        offs.append(off)
        hit = (row < MOST) & (lane - row == off)
        picks.append(jnp.where(hit, 1.0, 0.0))
    pick = jnp.concatenate(picks).astype(jnp.bfloat16)
    copies[1].wait()
    tails = jnp.dot(pick, transmit[0, 0], preferred_element_type=jnp.float32)
    for c in range(n_slab):
        tail = tails[c * ROWS : (c + 1) * ROWS]
        sends[c, pl.ds(MOST * feats, ROWS), :] = tail.astype(jnp.bfloat16)
    copies[2].wait()
    for c in range(n_slab):
        off = jnp.broadcast_to(offs[c], (feats, span)).astype(jnp.bfloat16)
        for r in range(MOST):
            last = min(MOST * c + r, slots - 1)
            block = colors[0, 0, last]
            for slot in range(r, last):
                block = jnp.where(off == slot - r, colors[0, 0, slot], block)
            sends[c, pl.ds(r * feats, feats), :] = block


def plan_kernel(n_slab, slots, *refs):
    (counts, blocks, assign, depth), (rows, codes) = refs[:4], refs[4:]
    items = n_slab * MOST
    outs = codes.shape[1] // (2 * items)
    me = lax.axis_index("slab")
    row = lax.broadcasted_iota(jnp.int32, rows.shape[1:], 0)
    item_lane = lax.broadcasted_iota(jnp.int32, codes.shape, 1) // outs
    posv = jnp.zeros(rows.shape[1:], jnp.int32)
    depthv = jnp.zeros(rows.shape[1:], jnp.int32)
    firstv = jnp.zeros(rows.shape[1:], jnp.int32)
    codev = jnp.full(codes.shape, -1, jnp.int32)
    pos = []
    for s in range(n_slab):
        off = jnp.int32(0)
        for c in range(n_slab):
            off = off + jnp.where(c < me, counts[0, s, c], 0)
        count = counts[0, s, me]
        for r in range(MOST):
            i = s * MOST + r
            slot = jnp.minimum(off + r, slots - 1)
            here = assign[0, blocks[0, s, slot]] - me * LB
            here = jnp.where(r < count, here, -1)
            first = jnp.int32(i)
            for j in reversed(range(i)):
                first = jnp.where(pos[j] == here, j, first)
            pos.append(here)
            firstv = jnp.where(row == i, first, firstv)
            posv = jnp.where(row == i, here, posv)
            depthv = jnp.where(row == i, depth[s], depthv)
            codev = jnp.where(item_lane == i, jnp.where(first == i, here, -1), codev)
    rows[0] = posv
    rows[1] = depthv
    rows[2] = firstv
    codes[...] = codev.astype(jnp.float32).astype(jnp.bfloat16)


def place_kernel(w_in, trans_weight, far_out, far_mid, w_first, w_out, w_later, w_mid, sems):
    copy = pltpu.make_async_copy(far_mid, w_mid, sems.at[0])
    copy.start()
    feats, hidden = w_in.shape
    half_in = (w_in[...].astype(jnp.float32) * 0.5).astype(jnp.bfloat16)
    half_trans = trans_weight[...].astype(jnp.float32) * 0.5
    sub = lax.broadcasted_iota(jnp.int32, (16, hidden), 0)
    w_first[...] = jnp.zeros_like(w_first)
    for a in range(GROUP):
        w_first[a, pl.ds(a * feats, feats), :] = half_in
        tail = jnp.where(sub // 2 == a, half_trans, 0.0)
        w_first[a, pl.ds(GROUP * feats, 16), :] = tail.astype(jnp.bfloat16)
    w_out[...] = far_out[...]
    copy.wait()
    for m in range(w_mid.shape[0]):
        w_later[m] = (w_mid[m].astype(jnp.float32).T * 0.5).astype(jnp.bfloat16)


def silu_half(u):
    return (u + u * jnp.tanh(u)).astype(jnp.bfloat16)


def later_layers(h, w_mid, w_out):
    for m in range(w_mid.shape[0]):
        h = silu_half(jnp.dot(h, w_mid[m], preferred_element_type=jnp.float32))
    y = lax.dot_general(
        w_out[...], h, (((1,), (1,)), ((), ())), preferred_element_type=jnp.float32
    )
    return y.astype(jnp.bfloat16).astype(jnp.float32)


def empty_kernel(trans_weight, w_mid, w_out, out):
    u = trans_weight[...].astype(jnp.float32) * 0.5
    h = silu_half(jnp.broadcast_to(u, (out.shape[1], u.shape[1])))
    y = later_layers(h, w_mid, w_out)
    outs = w_out.shape[0]
    for at in range(0, out.shape[0], outs):
        out[pl.ds(at, outs), :] = y


def shade_kernel(rows, codes, got, w_first, w_mid, w_out, out, acc, xt, ys):
    items, feats, span = acc.shape
    outs = w_out.shape[0]

    posv, depthv = rows[0], rows[1]
    front = jnp.ones((items, span), jnp.float32)
    total = jnp.ones((items, span), jnp.float32)
    for k in range(items // MOST):
        tail = got[k, pl.ds(MOST * feats, ROWS), :].astype(jnp.float32)
        for r in range(MOST):
            j = k * MOST + r
            trans_j = tail[r : r + 1, :]
            same = posv == posv[j : j + 1, :]
            total = jnp.where(same, total * trans_j, total)
            front = jnp.where(same & (depthv > depthv[j : j + 1, :]), front * trans_j, front)
    acc[...] = jnp.zeros_like(acc)
    for j in range(items):
        k, r = divmod(j, MOST)
        color = got[k, pl.ds(r * feats, feats), :].astype(jnp.float32)
        at = rows[2, j, 0]
        acc[at] = acc[at] + front[j : j + 1, :] * color
    total_hi = total.astype(jnp.bfloat16).astype(jnp.float32)
    total_lo = total - total_hi
    groups = items // GROUP
    sub = lax.broadcasted_iota(jnp.int32, (16, span), 0)
    xt[...] = jnp.zeros_like(xt)
    for q in range(groups):
        block = acc[pl.ds(q * GROUP, GROUP)].reshape(GROUP * feats, span)
        tail = jnp.zeros((16, span), jnp.float32)
        for a in range(GROUP):
            i = q * GROUP + a
            tail = jnp.where(sub == 2 * a, total_hi[i : i + 1, :], tail)
            tail = jnp.where(sub == 2 * a + 1, total_lo[i : i + 1, :], tail)
        lines = pl.ds(q * span, span)
        xt[lines, pl.ds(0, GROUP * feats)] = block.T.astype(jnp.bfloat16)
        xt[lines, pl.ds(GROUP * feats, 16)] = tail.T.astype(jnp.bfloat16)

    x = xt[...]
    stride = GROUP
    for start in range(0, GROUP, stride):
        h = jnp.concatenate(
            [
                silu_half(jnp.dot(x, w_first[a], preferred_element_type=jnp.float32))
                for a in range(start, start + stride)
            ]
        )
        y = later_layers(h, w_mid, w_out)
        for a in range(start, start + stride):
            for q in range(groups):
                at = ((a - start) * groups + q) * span
                ys[pl.ds((q * GROUP + a) * outs, outs), :] = y[:, at : at + span]
    out[pl.ds(0, items * outs), :] = ys[...].astype(jnp.bfloat16)
    out[pl.ds(items * outs, ROWS), :] = codes[...]


def join_kernel(*refs):
    *got, empty, out = refs
    _, n_strip, tile, outs, span = out.shape
    lines = tile * outs
    count = got[0].shape[0] - ROWS
    me = lax.axis_index("strip")
    want = lax.broadcasted_iota(jnp.int32, (lines, count), 0) + me * lines
    chan = lax.broadcasted_iota(jnp.int32, (lines, count), 1) % outs
    filler = jnp.concatenate([empty[...]] * (lines // ROWS))
    ones = jnp.ones((count, span), jnp.bfloat16)
    for k in range(n_strip):
        pos = got[k][pl.ds(count, ROWS), :].astype(jnp.float32)[:1, :count].astype(jnp.int32)
        hit = pos * outs + chan == want
        pick = jnp.where(hit, 1.0, 0.0).astype(jnp.bfloat16)
        blocks = got[k][pl.ds(0, count), :]
        placed = jnp.dot(pick, blocks, preferred_element_type=jnp.float32)
        filled = jnp.dot(pick, ones, preferred_element_type=jnp.float32)
        value = jnp.where(filled > 0.5, placed, filler)
        out[0, me ^ ((k + 1) % n_strip)] = value.reshape(tile, outs, span).astype(jnp.bfloat16)


def compact_device(
    n_slab,
    n_strip,
    colors,
    transmit,
    pair_counts,
    slot_block,
    assign,
    depth_rank,
    w_in,
    trans_weight,
    w_mid,
    w_out,
):
    slots, feats, span = colors.shape[2:]
    items = n_slab * MOST
    outs = w_out.shape[0]
    smem = pl.BlockSpec(memory_space=SMEM)
    vmem = pl.BlockSpec(memory_space=VMEM)
    hbm = pl.BlockSpec(memory_space=pltpu.HBM)
    held = functools.partial(pltpu.with_memory_space_constraint, memory_space=pltpu.HBM)
    small = pltpu.CompilerParams(vmem_limit_bytes=4 * 1024 * 1024)
    message = MOST * feats + ROWS
    sends = pl.pallas_call(
        pack_kernel,
        out_shape=jax.ShapeDtypeStruct((n_slab, message, span), jnp.bfloat16),
        in_specs=[hbm] * 3,
        out_specs=vmem,
        scratch_shapes=[
            pltpu.VMEM(pair_counts.shape, jnp.int32),
            pltpu.VMEM(colors.shape, colors.dtype),
            pltpu.VMEM(transmit.shape, transmit.dtype),
            pltpu.SemaphoreType.DMA((3,)),
        ],
        compiler_params=small,
        name="pack",
    )(held(pair_counts), held(colors), held(transmit))
    got = lax.all_to_all(sends, "slab", split_axis=0, concat_axis=0, tiled=True)
    hidden = w_in.shape[0]
    rough = pl.CostEstimate(flops=10**5, bytes_accessed=10**6, transcendentals=0)
    roomy = pltpu.CompilerParams(vmem_limit_bytes=16 * 1024 * 1024)
    trans_row = trans_weight[None]
    rows, codes = pl.pallas_call(
        functools.partial(plan_kernel, n_slab, slots),
        out_shape=[
            jax.ShapeDtypeStruct((3, items, span), jnp.int32),
            jax.ShapeDtypeStruct((ROWS, span), jnp.bfloat16),
        ],
        in_specs=[smem] * 4,
        out_specs=[vmem] * 2,
        compiler_params=small,
        cost_estimate=rough,
        name="plan",
    )(pair_counts, slot_block, assign, depth_rank)
    w_first, w_last, w_later = pl.pallas_call(
        place_kernel,
        out_shape=[
            jax.ShapeDtypeStruct((GROUP, 2 * GROUP * feats, hidden), jnp.bfloat16),
            jax.ShapeDtypeStruct(w_out.shape, jnp.bfloat16),
            jax.ShapeDtypeStruct(w_mid.shape, jnp.bfloat16),
        ],
        in_specs=[vmem] * 3 + [hbm],
        out_specs=[vmem] * 3,
        scratch_shapes=[
            pltpu.VMEM(w_mid.shape, jnp.bfloat16),
            pltpu.SemaphoreType.DMA((1,)),
        ],
        compiler_params=small,
        cost_estimate=rough,
        name="place",
    )(w_in.T, trans_row, w_out, held(w_mid))
    empty = pl.pallas_call(
        empty_kernel,
        out_shape=jax.ShapeDtypeStruct((ROWS, span), jnp.float32),
        in_specs=[vmem] * 3,
        out_specs=vmem,
        compiler_params=roomy,
        cost_estimate=rough,
        name="empty",
    )(trans_row, w_later, w_last)
    shaded = pl.pallas_call(
        shade_kernel,
        out_shape=jax.ShapeDtypeStruct((items * outs + ROWS, span), jnp.bfloat16),
        in_specs=[vmem] * 6,
        out_specs=vmem,
        scratch_shapes=[
            pltpu.VMEM((items, feats, span), jnp.float32),
            pltpu.VMEM((items // GROUP * span, 2 * GROUP * feats), jnp.bfloat16),
            pltpu.VMEM((items * outs, span), jnp.float32),
        ],
        compiler_params=roomy,
        name="shade",
    )(rows, codes, got, w_first, w_later, w_last)
    tiles = [
        lax.ppermute(shaded, "strip", [(s, s ^ k) for s in range(n_strip)])
        for k in range(1, n_strip)
    ] + [shaded]
    return pl.pallas_call(
        join_kernel,
        out_shape=jax.ShapeDtypeStruct((1, n_strip, LB // n_strip, outs, span), jnp.bfloat16),
        in_specs=[vmem] * (n_strip + 1),
        out_specs=pl.BlockSpec(),
        compiler_params=small,
        name="join",
    )(*tiles, empty)


def solution(mesh):
    n_slab, n_strip = mesh.shape["slab"], mesh.shape["strip"]
    placed = (
        P("slab", "strip", None, None, None),
        P("slab", "strip", None, None),
        P("strip", None, None),
        P("strip", None, None),
        P("strip", None),
        P(),
        P(),
        P(),
        P(),
        P(),
    )
    compact = n_strip & (n_strip - 1) == 0 and 4 * MOST * n_slab <= LB
    return jax.shard_map(
        functools.partial(compact_device, n_slab, n_strip) if compact else dense_device,
        mesh=mesh,
        in_specs=placed,
        out_specs=P("slab", None, "strip", None, None),
        check_vma=False,
    )
```

```python
import functools

import jax
import jax.numpy as jnp
from jax import lax
from jax.experimental import pallas as pl
from jax.experimental.pallas import tpu as pltpu
from jax.sharding import PartitionSpec as P

MOST = 2
LB = 128


EXACT_PRECISION = lax.Precision.HIGHEST


def shade_blocks(blend_color, trans_field, w_in, trans_weight, w_mid, w_out):
    summed = jnp.einsum("hf,lfp->lhp", w_in, blend_color, preferred_element_type=jnp.float32)
    summed = summed + trans_weight.astype(jnp.float32)[None, :, None] * trans_field[:, None, :]
    hidden = jax.nn.silu(summed).astype(jnp.bfloat16)
    for layer_index in range(w_mid.shape[0]):
        hidden = jax.nn.silu(
            jnp.einsum(
                "hg,lgp->lhp", w_mid[layer_index], hidden, preferred_element_type=jnp.float32
            )
        ).astype(jnp.bfloat16)
    return jnp.einsum("oh,lhp->lop", w_out, hidden, preferred_element_type=jnp.float32).astype(
        jnp.bfloat16
    )


def dense_device(
    colors, transmit, pair_counts, slot_block, assign, depth_rank, w_in, trans_weight, w_mid, w_out
):
    myself = lax.axis_index("slab")
    counts = pair_counts[0]
    blocks_all = slot_block[0]
    assign_row = assign[0]
    offsets = jnp.cumsum(counts, axis=1) - counts
    slot_rank = jnp.arange(MOST, dtype=jnp.int32)
    my_counts = lax.dynamic_index_in_dim(counts, myself, 0, keepdims=False)
    my_offsets = lax.dynamic_index_in_dim(offsets, myself, 0, keepdims=False)
    send_slots = jnp.where(
        slot_rank[None, :] < my_counts[:, None], my_offsets[:, None] + slot_rank[None, :], 0
    )
    send_color = colors[0, 0][send_slots]
    send_trans = transmit[0, 0][send_slots][:, :, None, :]
    incoming = lax.dynamic_index_in_dim(counts, myself, 1, keepdims=False)
    in_offsets = lax.dynamic_index_in_dim(offsets, myself, 1, keepdims=False)
    live_slot = slot_rank[None, :] < incoming[:, None]
    recv_slots = jnp.where(live_slot, in_offsets[:, None] + slot_rank[None, :], 0)
    recv_blocks = jnp.take_along_axis(blocks_all, recv_slots, axis=1)
    local_pos = assign_row[recv_blocks] - myself * LB
    live_flat = live_slot.reshape(-1)
    local_flat = jnp.where(live_flat, local_pos.reshape(-1), -1)
    depth_flat = jnp.repeat(depth_rank, MOST)
    ahead_table = (
        (local_flat[:, None] == local_flat[None, :])
        & (depth_flat[None, :] < depth_flat[:, None])
        & live_flat[None, :]
    )
    ahead_table = ahead_table.astype(jnp.float32)
    owner_table = (jnp.arange(LB, dtype=jnp.int32)[:, None] == local_flat[None, :]).astype(
        jnp.float32
    )
    got_color = lax.all_to_all(send_color, "slab", split_axis=0, concat_axis=0, tiled=True)
    got_trans = lax.all_to_all(send_trans, "slab", split_axis=0, concat_axis=0, tiled=True)
    pixel_count = got_color.shape[3]
    item_count = got_color.shape[0] * got_color.shape[1]
    log_trans = jnp.log(got_trans.reshape(item_count, pixel_count).astype(jnp.float32))
    log_trans = jnp.where(live_flat[:, None], log_trans, 0.0)
    front_log = jnp.dot(ahead_table, log_trans, precision=EXACT_PRECISION)
    front_share = jnp.where(live_flat[:, None], jnp.exp(front_log), 0.0)
    weighted = front_share[:, None, :] * got_color.reshape(item_count, -1, pixel_count).astype(
        jnp.float32
    )
    blend_sum = jnp.dot(owner_table, weighted.reshape(item_count, -1), precision=EXACT_PRECISION)
    blend_color = blend_sum.reshape(LB, -1, pixel_count).astype(jnp.bfloat16)
    trans_field = jnp.exp(jnp.dot(owner_table, log_trans, precision=EXACT_PRECISION))
    shaded = shade_blocks(blend_color, trans_field, w_in, trans_weight, w_mid, w_out)
    display_tiles = lax.all_to_all(shaded[None], "strip", split_axis=1, concat_axis=0, tiled=True)
    return display_tiles[None]


SMEM = pltpu.SMEM
VMEM = pltpu.VMEM
ROWS = 8
GROUP = 4
FIRST = 5


def pack_kernel(far_counts, far_colors, far_transmit, sends, counts, colors, transmit, sems):
    n_slab = sends.shape[0]
    slots, feats, span = colors.shape[2:]
    me = lax.axis_index("slab")
    copies = [
        pltpu.make_async_copy(far, near, sems.at[i])
        for i, (far, near) in enumerate(
            ((far_counts, counts), (far_transmit, transmit), (far_colors, colors))
        )
    ]
    for copy in copies:
        copy.start()
    copies[0].wait()
    mine = counts[0, pl.ds(me, 1), :].astype(jnp.float32)
    before = lax.broadcasted_iota(jnp.int32, mine.shape, 1)
    row = lax.broadcasted_iota(jnp.int32, (ROWS, slots), 0).astype(jnp.float32)
    lane = lax.broadcasted_iota(jnp.int32, (ROWS, slots), 1).astype(jnp.float32)
    offs, picks = [], []
    for c in range(n_slab):
        off = jnp.sum(jnp.where(before < c, mine, 0.0), axis=1, keepdims=True)
        offs.append(off)
        hit = (row < MOST) & (lane - row == off)
        picks.append(jnp.where(hit, 1.0, 0.0))
    pick = jnp.concatenate(picks).astype(jnp.bfloat16)
    copies[1].wait()
    tails = jnp.dot(pick, transmit[0, 0], preferred_element_type=jnp.float32)
    for c in range(n_slab):
        tail = tails[c * ROWS : (c + 1) * ROWS]
        sends[(c - FIRST) % n_slab, pl.ds(MOST * feats, ROWS), :] = tail.astype(jnp.bfloat16)
    copies[2].wait()
    for c in range(n_slab):
        off = jnp.broadcast_to(offs[c], (feats, span)).astype(jnp.bfloat16)
        for r in range(MOST):
            last = min(MOST * c + r, slots - 1)
            block = colors[0, 0, last]
            for slot in range(r, last):
                block = jnp.where(off == slot - r, colors[0, 0, slot], block)
            sends[(c - FIRST) % n_slab, pl.ds(r * feats, feats), :] = block


def plan_kernel(n_slab, slots, *refs):
    (counts, blocks, assign, depth), (rows, codes) = refs[:4], refs[4:]
    items = n_slab * MOST
    outs = codes.shape[1] // (2 * items)
    me = lax.axis_index("slab")
    row = lax.broadcasted_iota(jnp.int32, rows.shape[1:], 0)
    item_lane = lax.broadcasted_iota(jnp.int32, codes.shape, 1) // outs
    posv = jnp.zeros(rows.shape[1:], jnp.int32)
    depthv = jnp.zeros(rows.shape[1:], jnp.int32)
    firstv = jnp.zeros(rows.shape[1:], jnp.int32)
    codev = jnp.full(codes.shape, -1, jnp.int32)
    pos = []
    for k in range(n_slab):
        s = (k + FIRST) % n_slab
        off = jnp.int32(0)
        for c in range(n_slab):
            off = off + jnp.where(c < me, counts[0, s, c], 0)
        count = counts[0, s, me]
        for r in range(MOST):
            i = k * MOST + r
            slot = jnp.minimum(off + r, slots - 1)
            here = assign[0, blocks[0, s, slot]] - me * LB
            here = jnp.where(r < count, here, -1)
            first = jnp.int32(i)
            for j in reversed(range(i)):
                first = jnp.where(pos[j] == here, j, first)
            pos.append(here)
            firstv = jnp.where(row == i, first, firstv)
            posv = jnp.where(row == i, here, posv)
            depthv = jnp.where(row == i, depth[s], depthv)
            codev = jnp.where(item_lane == i, jnp.where(first == i, here, -1), codev)
    rows[0] = posv
    rows[1] = depthv
    rows[2] = firstv
    codes[...] = codev.astype(jnp.float32).astype(jnp.bfloat16)


def place_kernel(w_in, trans_weight, far_out, far_mid, w_first, w_out, w_later, w_mid, sems):
    copy = pltpu.make_async_copy(far_mid, w_mid, sems.at[0])
    copy.start()
    feats, hidden = w_in.shape
    half_in = (w_in[...].astype(jnp.float32) * 0.5).astype(jnp.bfloat16)
    half_trans = trans_weight[...].astype(jnp.float32) * 0.5
    sub = lax.broadcasted_iota(jnp.int32, (16, hidden), 0)
    w_first[...] = jnp.zeros_like(w_first)
    for a in range(GROUP):
        w_first[a, pl.ds(a * feats, feats), :] = half_in
        tail = jnp.where(sub // 2 == a, half_trans, 0.0)
        w_first[a, pl.ds(GROUP * feats, 16), :] = tail.astype(jnp.bfloat16)
    w_out[...] = far_out[...]
    copy.wait()
    for m in range(w_mid.shape[0]):
        w_later[m] = (w_mid[m].astype(jnp.float32).T * 0.5).astype(jnp.bfloat16)


def silu_half(u):
    return (u + u * jnp.tanh(u)).astype(jnp.bfloat16)


def later_layers(h, w_mid, w_out):
    for m in range(w_mid.shape[0]):
        h = silu_half(jnp.dot(h, w_mid[m], preferred_element_type=jnp.float32))
    y = lax.dot_general(
        w_out[...], h, (((1,), (1,)), ((), ())), preferred_element_type=jnp.float32
    )
    return y.astype(jnp.bfloat16).astype(jnp.float32)


def empty_kernel(trans_weight, w_mid, w_out, out):
    u = trans_weight[...].astype(jnp.float32) * 0.5
    h = silu_half(jnp.broadcast_to(u, (out.shape[1], u.shape[1])))
    y = later_layers(h, w_mid, w_out)
    outs = w_out.shape[0]
    for at in range(0, out.shape[0], outs):
        out[pl.ds(at, outs), :] = y


def shade_kernel(rows, codes, got, w_first, w_mid, w_out, out, acc, xt, ys):
    items, feats, span = acc.shape
    outs = w_out.shape[0]

    posv, depthv = rows[0], rows[1]
    front = jnp.ones((items, span), jnp.float32)
    total = jnp.ones((items, span), jnp.float32)
    for k in range(items // MOST):
        tail = got[k, pl.ds(MOST * feats, ROWS), :].astype(jnp.float32)
        for r in range(MOST):
            j = k * MOST + r
            trans_j = tail[r : r + 1, :]
            same = posv == posv[j : j + 1, :]
            total = jnp.where(same, total * trans_j, total)
            front = jnp.where(same & (depthv > depthv[j : j + 1, :]), front * trans_j, front)
    acc[...] = jnp.zeros_like(acc)
    for j in range(items):
        k, r = divmod(j, MOST)
        color = got[k, pl.ds(r * feats, feats), :].astype(jnp.float32)
        at = rows[2, j, 0]
        acc[at] = acc[at] + front[j : j + 1, :] * color
    total_hi = total.astype(jnp.bfloat16).astype(jnp.float32)
    total_lo = total - total_hi
    groups = items // GROUP
    sub = lax.broadcasted_iota(jnp.int32, (16, span), 0)
    xt[...] = jnp.zeros_like(xt)
    for q in range(groups):
        block = acc[pl.ds(q * GROUP, GROUP)].reshape(GROUP * feats, span)
        tail = jnp.zeros((16, span), jnp.float32)
        for a in range(GROUP):
            i = q * GROUP + a
            tail = jnp.where(sub == 2 * a, total_hi[i : i + 1, :], tail)
            tail = jnp.where(sub == 2 * a + 1, total_lo[i : i + 1, :], tail)
        lines = pl.ds(q * span, span)
        xt[lines, pl.ds(0, GROUP * feats)] = block.T.astype(jnp.bfloat16)
        xt[lines, pl.ds(GROUP * feats, 16)] = tail.T.astype(jnp.bfloat16)

    x = xt[...]
    stride = GROUP
    for start in range(0, GROUP, stride):
        h = jnp.concatenate(
            [
                silu_half(jnp.dot(x, w_first[a], preferred_element_type=jnp.float32))
                for a in range(start, start + stride)
            ]
        )
        y = later_layers(h, w_mid, w_out)
        for a in range(start, start + stride):
            for q in range(groups):
                at = ((a - start) * groups + q) * span
                ys[pl.ds((q * GROUP + a) * outs, outs), :] = y[:, at : at + span]
    out[pl.ds(0, items * outs), :] = ys[...].astype(jnp.bfloat16)
    out[pl.ds(items * outs, ROWS), :] = codes[...]


def join_kernel(*refs):
    *got, empty, out = refs
    _, n_strip, tile, outs, span = out.shape
    lines = tile * outs
    count = got[0].shape[0] - ROWS
    me = lax.axis_index("strip")
    want = lax.broadcasted_iota(jnp.int32, (lines, count), 0) + me * lines
    chan = lax.broadcasted_iota(jnp.int32, (lines, count), 1) % outs
    filler = jnp.concatenate([empty[...]] * (lines // ROWS))
    ones = jnp.ones((count, span), jnp.bfloat16)
    for k in range(n_strip):
        pos = got[k][pl.ds(count, ROWS), :].astype(jnp.float32)[:1, :count].astype(jnp.int32)
        hit = pos * outs + chan == want
        pick = jnp.where(hit, 1.0, 0.0).astype(jnp.bfloat16)
        blocks = got[k][pl.ds(0, count), :]
        placed = jnp.dot(pick, blocks, preferred_element_type=jnp.float32)
        filled = jnp.dot(pick, ones, preferred_element_type=jnp.float32)
        value = jnp.where(filled > 0.5, placed, filler)
        out[0, me ^ ((k + 1) % n_strip)] = value.reshape(tile, outs, span).astype(jnp.bfloat16)


def compact_device(
    n_slab,
    n_strip,
    colors,
    transmit,
    pair_counts,
    slot_block,
    assign,
    depth_rank,
    w_in,
    trans_weight,
    w_mid,
    w_out,
):
    slots, feats, span = colors.shape[2:]
    items = n_slab * MOST
    outs = w_out.shape[0]
    smem = pl.BlockSpec(memory_space=SMEM)
    vmem = pl.BlockSpec(memory_space=VMEM)
    hbm = pl.BlockSpec(memory_space=pltpu.HBM)
    held = functools.partial(pltpu.with_memory_space_constraint, memory_space=pltpu.HBM)
    small = pltpu.CompilerParams(vmem_limit_bytes=4 * 1024 * 1024)
    message = MOST * feats + ROWS
    sends = pl.pallas_call(
        pack_kernel,
        out_shape=jax.ShapeDtypeStruct((n_slab, message, span), jnp.bfloat16),
        in_specs=[hbm] * 3,
        out_specs=vmem,
        scratch_shapes=[
            pltpu.VMEM(pair_counts.shape, jnp.int32),
            pltpu.VMEM(colors.shape, colors.dtype),
            pltpu.VMEM(transmit.shape, transmit.dtype),
            pltpu.SemaphoreType.DMA((3,)),
        ],
        compiler_params=small,
        name="pack",
    )(held(pair_counts), held(colors), held(transmit))
    group = [(k + FIRST) % n_slab for k in range(n_slab)]
    got = lax.all_to_all(
        sends, "slab", split_axis=0, concat_axis=0, axis_index_groups=[group], tiled=True
    )
    hidden = w_in.shape[0]
    rough = pl.CostEstimate(flops=10**5, bytes_accessed=10**6, transcendentals=0)
    roomy = pltpu.CompilerParams(vmem_limit_bytes=16 * 1024 * 1024)
    trans_row = trans_weight[None]
    rows, codes = pl.pallas_call(
        functools.partial(plan_kernel, n_slab, slots),
        out_shape=[
            jax.ShapeDtypeStruct((3, items, span), jnp.int32),
            jax.ShapeDtypeStruct((ROWS, span), jnp.bfloat16),
        ],
        in_specs=[smem] * 4,
        out_specs=[vmem] * 2,
        compiler_params=small,
        cost_estimate=rough,
        name="plan",
    )(pair_counts, slot_block, assign, depth_rank)
    w_first, w_last, w_later = pl.pallas_call(
        place_kernel,
        out_shape=[
            jax.ShapeDtypeStruct((GROUP, 2 * GROUP * feats, hidden), jnp.bfloat16),
            jax.ShapeDtypeStruct(w_out.shape, jnp.bfloat16),
            jax.ShapeDtypeStruct(w_mid.shape, jnp.bfloat16),
        ],
        in_specs=[vmem] * 3 + [hbm],
        out_specs=[vmem] * 3,
        scratch_shapes=[
            pltpu.VMEM(w_mid.shape, jnp.bfloat16),
            pltpu.SemaphoreType.DMA((1,)),
        ],
        compiler_params=small,
        cost_estimate=rough,
        name="place",
    )(w_in.T, trans_row, w_out, held(w_mid))
    empty = pl.pallas_call(
        empty_kernel,
        out_shape=jax.ShapeDtypeStruct((ROWS, span), jnp.float32),
        in_specs=[vmem] * 3,
        out_specs=vmem,
        compiler_params=roomy,
        cost_estimate=rough,
        name="empty",
    )(trans_row, w_later, w_last)
    shaded = pl.pallas_call(
        shade_kernel,
        out_shape=jax.ShapeDtypeStruct((items * outs + ROWS, span), jnp.bfloat16),
        in_specs=[vmem] * 6,
        out_specs=vmem,
        scratch_shapes=[
            pltpu.VMEM((items, feats, span), jnp.float32),
            pltpu.VMEM((items // GROUP * span, 2 * GROUP * feats), jnp.bfloat16),
            pltpu.VMEM((items * outs, span), jnp.float32),
        ],
        compiler_params=roomy,
        name="shade",
    )(rows, codes, got, w_first, w_later, w_last)
    tiles = [
        lax.ppermute(shaded, "strip", [(s, s ^ k) for s in range(n_strip)])
        for k in range(1, n_strip)
    ] + [shaded]
    return pl.pallas_call(
        join_kernel,
        out_shape=jax.ShapeDtypeStruct((1, n_strip, LB // n_strip, outs, span), jnp.bfloat16),
        in_specs=[vmem] * (n_strip + 1),
        out_specs=pl.BlockSpec(),
        compiler_params=small,
        name="join",
    )(*tiles, empty)


def solution(mesh):
    n_slab, n_strip = mesh.shape["slab"], mesh.shape["strip"]
    placed = (
        P("slab", "strip", None, None, None),
        P("slab", "strip", None, None),
        P("strip", None, None),
        P("strip", None, None),
        P("strip", None),
        P(),
        P(),
        P(),
        P(),
        P(),
    )
    compact = n_strip & (n_strip - 1) == 0 and 4 * MOST * n_slab <= LB
    return jax.shard_map(
        functools.partial(compact_device, n_slab, n_strip) if compact else dense_device,
        mesh=mesh,
        in_specs=placed,
        out_specs=P("slab", None, "strip", None, None),
        check_vma=False,
    )
```

```python
import functools

import jax
import jax.numpy as jnp
from jax import lax
from jax.experimental import pallas as pl
from jax.experimental.pallas import tpu as pltpu
from jax.sharding import PartitionSpec as P

MOST = 2
LB = 128


EXACT_PRECISION = lax.Precision.HIGHEST


def shade_blocks(blend_color, trans_field, w_in, trans_weight, w_mid, w_out):
    summed = jnp.einsum("hf,lfp->lhp", w_in, blend_color, preferred_element_type=jnp.float32)
    summed = summed + trans_weight.astype(jnp.float32)[None, :, None] * trans_field[:, None, :]
    hidden = jax.nn.silu(summed).astype(jnp.bfloat16)
    for layer_index in range(w_mid.shape[0]):
        hidden = jax.nn.silu(
            jnp.einsum(
                "hg,lgp->lhp", w_mid[layer_index], hidden, preferred_element_type=jnp.float32
            )
        ).astype(jnp.bfloat16)
    return jnp.einsum("oh,lhp->lop", w_out, hidden, preferred_element_type=jnp.float32).astype(
        jnp.bfloat16
    )


def dense_device(
    colors, transmit, pair_counts, slot_block, assign, depth_rank, w_in, trans_weight, w_mid, w_out
):
    myself = lax.axis_index("slab")
    counts = pair_counts[0]
    blocks_all = slot_block[0]
    assign_row = assign[0]
    offsets = jnp.cumsum(counts, axis=1) - counts
    slot_rank = jnp.arange(MOST, dtype=jnp.int32)
    my_counts = lax.dynamic_index_in_dim(counts, myself, 0, keepdims=False)
    my_offsets = lax.dynamic_index_in_dim(offsets, myself, 0, keepdims=False)
    send_slots = jnp.where(
        slot_rank[None, :] < my_counts[:, None], my_offsets[:, None] + slot_rank[None, :], 0
    )
    send_color = colors[0, 0][send_slots]
    send_trans = transmit[0, 0][send_slots][:, :, None, :]
    incoming = lax.dynamic_index_in_dim(counts, myself, 1, keepdims=False)
    in_offsets = lax.dynamic_index_in_dim(offsets, myself, 1, keepdims=False)
    live_slot = slot_rank[None, :] < incoming[:, None]
    recv_slots = jnp.where(live_slot, in_offsets[:, None] + slot_rank[None, :], 0)
    recv_blocks = jnp.take_along_axis(blocks_all, recv_slots, axis=1)
    local_pos = assign_row[recv_blocks] - myself * LB
    live_flat = live_slot.reshape(-1)
    local_flat = jnp.where(live_flat, local_pos.reshape(-1), -1)
    depth_flat = jnp.repeat(depth_rank, MOST)
    ahead_table = (
        (local_flat[:, None] == local_flat[None, :])
        & (depth_flat[None, :] < depth_flat[:, None])
        & live_flat[None, :]
    )
    ahead_table = ahead_table.astype(jnp.float32)
    owner_table = (jnp.arange(LB, dtype=jnp.int32)[:, None] == local_flat[None, :]).astype(
        jnp.float32
    )
    got_color = lax.all_to_all(send_color, "slab", split_axis=0, concat_axis=0, tiled=True)
    got_trans = lax.all_to_all(send_trans, "slab", split_axis=0, concat_axis=0, tiled=True)
    pixel_count = got_color.shape[3]
    item_count = got_color.shape[0] * got_color.shape[1]
    log_trans = jnp.log(got_trans.reshape(item_count, pixel_count).astype(jnp.float32))
    log_trans = jnp.where(live_flat[:, None], log_trans, 0.0)
    front_log = jnp.dot(ahead_table, log_trans, precision=EXACT_PRECISION)
    front_share = jnp.where(live_flat[:, None], jnp.exp(front_log), 0.0)
    weighted = front_share[:, None, :] * got_color.reshape(item_count, -1, pixel_count).astype(
        jnp.float32
    )
    blend_sum = jnp.dot(owner_table, weighted.reshape(item_count, -1), precision=EXACT_PRECISION)
    blend_color = blend_sum.reshape(LB, -1, pixel_count).astype(jnp.bfloat16)
    trans_field = jnp.exp(jnp.dot(owner_table, log_trans, precision=EXACT_PRECISION))
    shaded = shade_blocks(blend_color, trans_field, w_in, trans_weight, w_mid, w_out)
    display_tiles = lax.all_to_all(shaded[None], "strip", split_axis=1, concat_axis=0, tiled=True)
    return display_tiles[None]


SMEM = pltpu.SMEM
VMEM = pltpu.VMEM
ROWS = 8
GROUP = 4


def exchange_order(n_slab):
    half = n_slab // 2
    flip = 1 if half % 2 == 0 else 0
    return [s for i in range(half) for s in (half + (i ^ flip), i)]


def pack_kernel(far_counts, far_colors, far_transmit, sends, counts, colors, transmit, sems):
    n_slab = sends.shape[0]
    place = [exchange_order(n_slab).index(c) for c in range(n_slab)]
    slots, feats, span = colors.shape[2:]
    me = lax.axis_index("slab")
    copies = [
        pltpu.make_async_copy(far, near, sems.at[i])
        for i, (far, near) in enumerate(
            ((far_counts, counts), (far_transmit, transmit), (far_colors, colors))
        )
    ]
    for copy in copies:
        copy.start()
    copies[0].wait()
    mine = counts[0, pl.ds(me, 1), :].astype(jnp.float32)
    before = lax.broadcasted_iota(jnp.int32, mine.shape, 1)
    row = lax.broadcasted_iota(jnp.int32, (ROWS, slots), 0).astype(jnp.float32)
    lane = lax.broadcasted_iota(jnp.int32, (ROWS, slots), 1).astype(jnp.float32)
    offs, picks = [], []
    for c in range(n_slab):
        off = jnp.sum(jnp.where(before < c, mine, 0.0), axis=1, keepdims=True)
        offs.append(off)
        hit = (row < MOST) & (lane - row == off)
        picks.append(jnp.where(hit, 1.0, 0.0))
    pick = jnp.concatenate(picks).astype(jnp.bfloat16)
    copies[1].wait()
    tails = jnp.dot(pick, transmit[0, 0], preferred_element_type=jnp.float32)
    for c in range(n_slab):
        tail = tails[c * ROWS : (c + 1) * ROWS]
        sends[place[c], pl.ds(MOST * feats, ROWS), :] = tail.astype(jnp.bfloat16)
    copies[2].wait()
    for c in range(n_slab):
        off = jnp.broadcast_to(offs[c], (feats, span)).astype(jnp.bfloat16)
        for r in range(MOST):
            last = min(MOST * c + r, slots - 1)
            block = colors[0, 0, last]
            for slot in range(r, last):
                block = jnp.where(off == slot - r, colors[0, 0, slot], block)
            sends[place[c], pl.ds(r * feats, feats), :] = block


def plan_kernel(n_slab, slots, *refs):
    (counts, blocks, assign, depth), (rows, codes) = refs[:4], refs[4:]
    items = n_slab * MOST
    outs = codes.shape[1] // (2 * items)
    me = lax.axis_index("slab")
    row = lax.broadcasted_iota(jnp.int32, rows.shape[1:], 0)
    item_lane = lax.broadcasted_iota(jnp.int32, codes.shape, 1) // outs
    posv = jnp.zeros(rows.shape[1:], jnp.int32)
    depthv = jnp.zeros(rows.shape[1:], jnp.int32)
    firstv = jnp.zeros(rows.shape[1:], jnp.int32)
    codev = jnp.full(codes.shape, -1, jnp.int32)
    pos = []
    for k, s in enumerate(exchange_order(n_slab)):
        off = jnp.int32(0)
        for c in range(n_slab):
            off = off + jnp.where(c < me, counts[0, s, c], 0)
        count = counts[0, s, me]
        for r in range(MOST):
            i = k * MOST + r
            slot = jnp.minimum(off + r, slots - 1)
            here = assign[0, blocks[0, s, slot]] - me * LB
            here = jnp.where(r < count, here, -1)
            first = jnp.int32(i)
            for j in reversed(range(i)):
                first = jnp.where(pos[j] == here, j, first)
            pos.append(here)
            firstv = jnp.where(row == i, first, firstv)
            posv = jnp.where(row == i, here, posv)
            depthv = jnp.where(row == i, depth[s], depthv)
            codev = jnp.where(item_lane == i, jnp.where(first == i, here, -1), codev)
    rows[0] = posv
    rows[1] = depthv
    rows[2] = firstv
    codes[...] = codev.astype(jnp.float32).astype(jnp.bfloat16)


def place_kernel(w_in, trans_weight, far_out, far_mid, w_first, w_out, w_later, w_mid, sems):
    copy = pltpu.make_async_copy(far_mid, w_mid, sems.at[0])
    copy.start()
    feats, hidden = w_in.shape
    half_in = (w_in[...].astype(jnp.float32) * 0.5).astype(jnp.bfloat16)
    half_trans = trans_weight[...].astype(jnp.float32) * 0.5
    sub = lax.broadcasted_iota(jnp.int32, (16, hidden), 0)
    w_first[...] = jnp.zeros_like(w_first)
    for a in range(GROUP):
        w_first[a, pl.ds(a * feats, feats), :] = half_in
        tail = jnp.where(sub // 2 == a, half_trans, 0.0)
        w_first[a, pl.ds(GROUP * feats, 16), :] = tail.astype(jnp.bfloat16)
    w_out[...] = far_out[...]
    copy.wait()
    for m in range(w_mid.shape[0]):
        w_later[m] = (w_mid[m].astype(jnp.float32).T * 0.5).astype(jnp.bfloat16)


def silu_half(u):
    return (u + u * jnp.tanh(u)).astype(jnp.bfloat16)


def later_layers(h, w_mid, w_out):
    for m in range(w_mid.shape[0]):
        h = silu_half(jnp.dot(h, w_mid[m], preferred_element_type=jnp.float32))
    y = lax.dot_general(
        w_out[...], h, (((1,), (1,)), ((), ())), preferred_element_type=jnp.float32
    )
    return y.astype(jnp.bfloat16).astype(jnp.float32)


def empty_kernel(trans_weight, w_mid, w_out, out):
    u = trans_weight[...].astype(jnp.float32) * 0.5
    h = silu_half(jnp.broadcast_to(u, (out.shape[1], u.shape[1])))
    y = later_layers(h, w_mid, w_out)
    outs = w_out.shape[0]
    for at in range(0, out.shape[0], outs):
        out[pl.ds(at, outs), :] = y


def shade_kernel(rows, codes, got, w_first, w_mid, w_out, out, acc, xt, ys):
    items, feats, span = acc.shape
    outs = w_out.shape[0]

    posv, depthv = rows[0], rows[1]
    front = jnp.ones((items, span), jnp.float32)
    total = jnp.ones((items, span), jnp.float32)
    for k in range(items // MOST):
        tail = got[k, pl.ds(MOST * feats, ROWS), :].astype(jnp.float32)
        for r in range(MOST):
            j = k * MOST + r
            trans_j = tail[r : r + 1, :]
            same = posv == posv[j : j + 1, :]
            total = jnp.where(same, total * trans_j, total)
            front = jnp.where(same & (depthv > depthv[j : j + 1, :]), front * trans_j, front)
    acc[...] = jnp.zeros_like(acc)
    for j in range(items):
        k, r = divmod(j, MOST)
        color = got[k, pl.ds(r * feats, feats), :].astype(jnp.float32)
        at = rows[2, j, 0]
        acc[at] = acc[at] + front[j : j + 1, :] * color
    total_hi = total.astype(jnp.bfloat16).astype(jnp.float32)
    total_lo = total - total_hi
    groups = items // GROUP
    sub = lax.broadcasted_iota(jnp.int32, (16, span), 0)
    xt[...] = jnp.zeros_like(xt)
    for q in range(groups):
        block = acc[pl.ds(q * GROUP, GROUP)].reshape(GROUP * feats, span)
        tail = jnp.zeros((16, span), jnp.float32)
        for a in range(GROUP):
            i = q * GROUP + a
            tail = jnp.where(sub == 2 * a, total_hi[i : i + 1, :], tail)
            tail = jnp.where(sub == 2 * a + 1, total_lo[i : i + 1, :], tail)
        lines = pl.ds(q * span, span)
        xt[lines, pl.ds(0, GROUP * feats)] = block.T.astype(jnp.bfloat16)
        xt[lines, pl.ds(GROUP * feats, 16)] = tail.T.astype(jnp.bfloat16)

    x = xt[...]
    stride = GROUP
    for start in range(0, GROUP, stride):
        h = jnp.concatenate(
            [
                silu_half(jnp.dot(x, w_first[a], preferred_element_type=jnp.float32))
                for a in range(start, start + stride)
            ]
        )
        y = later_layers(h, w_mid, w_out)
        for a in range(start, start + stride):
            for q in range(groups):
                at = ((a - start) * groups + q) * span
                ys[pl.ds((q * GROUP + a) * outs, outs), :] = y[:, at : at + span]
    out[pl.ds(0, items * outs), :] = ys[...].astype(jnp.bfloat16)
    out[pl.ds(items * outs, ROWS), :] = codes[...]


def join_kernel(*refs):
    *got, empty, out = refs
    _, n_strip, tile, outs, span = out.shape
    lines = tile * outs
    count = got[0].shape[0] - ROWS
    me = lax.axis_index("strip")
    want = lax.broadcasted_iota(jnp.int32, (lines, count), 0) + me * lines
    chan = lax.broadcasted_iota(jnp.int32, (lines, count), 1) % outs
    filler = jnp.concatenate([empty[...]] * (lines // ROWS))
    ones = jnp.ones((count, span), jnp.bfloat16)
    for k in range(n_strip):
        pos = got[k][pl.ds(count, ROWS), :].astype(jnp.float32)[:1, :count].astype(jnp.int32)
        hit = pos * outs + chan == want
        pick = jnp.where(hit, 1.0, 0.0).astype(jnp.bfloat16)
        blocks = got[k][pl.ds(0, count), :]
        placed = jnp.dot(pick, blocks, preferred_element_type=jnp.float32)
        filled = jnp.dot(pick, ones, preferred_element_type=jnp.float32)
        value = jnp.where(filled > 0.5, placed, filler)
        out[0, me ^ ((k + 1) % n_strip)] = value.reshape(tile, outs, span).astype(jnp.bfloat16)


def compact_device(
    n_slab,
    n_strip,
    colors,
    transmit,
    pair_counts,
    slot_block,
    assign,
    depth_rank,
    w_in,
    trans_weight,
    w_mid,
    w_out,
):
    slots, feats, span = colors.shape[2:]
    items = n_slab * MOST
    outs = w_out.shape[0]
    smem = pl.BlockSpec(memory_space=SMEM)
    vmem = pl.BlockSpec(memory_space=VMEM)
    hbm = pl.BlockSpec(memory_space=pltpu.HBM)
    held = functools.partial(pltpu.with_memory_space_constraint, memory_space=pltpu.HBM)
    small = pltpu.CompilerParams(vmem_limit_bytes=4 * 1024 * 1024)
    message = MOST * feats + ROWS
    sends = pl.pallas_call(
        pack_kernel,
        out_shape=jax.ShapeDtypeStruct((n_slab, message, span), jnp.bfloat16),
        in_specs=[hbm] * 3,
        out_specs=vmem,
        scratch_shapes=[
            pltpu.VMEM(pair_counts.shape, jnp.int32),
            pltpu.VMEM(colors.shape, colors.dtype),
            pltpu.VMEM(transmit.shape, transmit.dtype),
            pltpu.SemaphoreType.DMA((3,)),
        ],
        compiler_params=small,
        name="pack",
    )(held(pair_counts), held(colors), held(transmit))
    group = exchange_order(n_slab)
    got = lax.all_to_all(
        sends, "slab", split_axis=0, concat_axis=0, axis_index_groups=[group], tiled=True
    )
    hidden = w_in.shape[0]
    rough = pl.CostEstimate(flops=10**5, bytes_accessed=10**6, transcendentals=0)
    roomy = pltpu.CompilerParams(vmem_limit_bytes=16 * 1024 * 1024)
    trans_row = trans_weight[None]
    rows, codes = pl.pallas_call(
        functools.partial(plan_kernel, n_slab, slots),
        out_shape=[
            jax.ShapeDtypeStruct((3, items, span), jnp.int32),
            jax.ShapeDtypeStruct((ROWS, span), jnp.bfloat16),
        ],
        in_specs=[smem] * 4,
        out_specs=[vmem] * 2,
        compiler_params=small,
        cost_estimate=rough,
        name="plan",
    )(pair_counts, slot_block, assign, depth_rank)
    w_first, w_last, w_later = pl.pallas_call(
        place_kernel,
        out_shape=[
            jax.ShapeDtypeStruct((GROUP, 2 * GROUP * feats, hidden), jnp.bfloat16),
            jax.ShapeDtypeStruct(w_out.shape, jnp.bfloat16),
            jax.ShapeDtypeStruct(w_mid.shape, jnp.bfloat16),
        ],
        in_specs=[vmem] * 3 + [hbm],
        out_specs=[vmem] * 3,
        scratch_shapes=[
            pltpu.VMEM(w_mid.shape, jnp.bfloat16),
            pltpu.SemaphoreType.DMA((1,)),
        ],
        compiler_params=small,
        cost_estimate=rough,
        name="place",
    )(w_in.T, trans_row, w_out, held(w_mid))
    empty = pl.pallas_call(
        empty_kernel,
        out_shape=jax.ShapeDtypeStruct((ROWS, span), jnp.float32),
        in_specs=[vmem] * 3,
        out_specs=vmem,
        compiler_params=roomy,
        cost_estimate=rough,
        name="empty",
    )(trans_row, w_later, w_last)
    shaded = pl.pallas_call(
        shade_kernel,
        out_shape=jax.ShapeDtypeStruct((items * outs + ROWS, span), jnp.bfloat16),
        in_specs=[vmem] * 6,
        out_specs=vmem,
        scratch_shapes=[
            pltpu.VMEM((items, feats, span), jnp.float32),
            pltpu.VMEM((items // GROUP * span, 2 * GROUP * feats), jnp.bfloat16),
            pltpu.VMEM((items * outs, span), jnp.float32),
        ],
        compiler_params=roomy,
        name="shade",
    )(rows, codes, got, w_first, w_later, w_last)
    tiles = [
        lax.ppermute(shaded, "strip", [(s, s ^ k) for s in range(n_strip)])
        for k in range(1, n_strip)
    ] + [shaded]
    return pl.pallas_call(
        join_kernel,
        out_shape=jax.ShapeDtypeStruct((1, n_strip, LB // n_strip, outs, span), jnp.bfloat16),
        in_specs=[vmem] * (n_strip + 1),
        out_specs=pl.BlockSpec(),
        compiler_params=small,
        name="join",
    )(*tiles, empty)


def solution(mesh):
    n_slab, n_strip = mesh.shape["slab"], mesh.shape["strip"]
    placed = (
        P("slab", "strip", None, None, None),
        P("slab", "strip", None, None),
        P("strip", None, None),
        P("strip", None, None),
        P("strip", None),
        P(),
        P(),
        P(),
        P(),
        P(),
    )
    compact = n_strip & (n_strip - 1) == 0 and 4 * MOST * n_slab <= LB
    return jax.shard_map(
        functools.partial(compact_device, n_slab, n_strip) if compact else dense_device,
        mesh=mesh,
        in_specs=placed,
        out_specs=P("slab", None, "strip", None, None),
        check_vma=False,
    )
```

```python
import functools

import jax
import jax.numpy as jnp
from jax import lax
from jax.experimental import pallas as pl
from jax.experimental.pallas import tpu as pltpu
from jax.sharding import PartitionSpec as P

MOST = 2
LB = 128


EXACT_PRECISION = lax.Precision.HIGHEST


def shade_blocks(blend_color, trans_field, w_in, trans_weight, w_mid, w_out):
    summed = jnp.einsum("hf,lfp->lhp", w_in, blend_color, preferred_element_type=jnp.float32)
    summed = summed + trans_weight.astype(jnp.float32)[None, :, None] * trans_field[:, None, :]
    hidden = jax.nn.silu(summed).astype(jnp.bfloat16)
    for layer_index in range(w_mid.shape[0]):
        hidden = jax.nn.silu(
            jnp.einsum(
                "hg,lgp->lhp", w_mid[layer_index], hidden, preferred_element_type=jnp.float32
            )
        ).astype(jnp.bfloat16)
    return jnp.einsum("oh,lhp->lop", w_out, hidden, preferred_element_type=jnp.float32).astype(
        jnp.bfloat16
    )


def dense_device(
    colors, transmit, pair_counts, slot_block, assign, depth_rank, w_in, trans_weight, w_mid, w_out
):
    myself = lax.axis_index("slab")
    counts = pair_counts[0]
    blocks_all = slot_block[0]
    assign_row = assign[0]
    offsets = jnp.cumsum(counts, axis=1) - counts
    slot_rank = jnp.arange(MOST, dtype=jnp.int32)
    my_counts = lax.dynamic_index_in_dim(counts, myself, 0, keepdims=False)
    my_offsets = lax.dynamic_index_in_dim(offsets, myself, 0, keepdims=False)
    send_slots = jnp.where(
        slot_rank[None, :] < my_counts[:, None], my_offsets[:, None] + slot_rank[None, :], 0
    )
    send_color = colors[0, 0][send_slots]
    send_trans = transmit[0, 0][send_slots][:, :, None, :]
    incoming = lax.dynamic_index_in_dim(counts, myself, 1, keepdims=False)
    in_offsets = lax.dynamic_index_in_dim(offsets, myself, 1, keepdims=False)
    live_slot = slot_rank[None, :] < incoming[:, None]
    recv_slots = jnp.where(live_slot, in_offsets[:, None] + slot_rank[None, :], 0)
    recv_blocks = jnp.take_along_axis(blocks_all, recv_slots, axis=1)
    local_pos = assign_row[recv_blocks] - myself * LB
    live_flat = live_slot.reshape(-1)
    local_flat = jnp.where(live_flat, local_pos.reshape(-1), -1)
    depth_flat = jnp.repeat(depth_rank, MOST)
    ahead_table = (
        (local_flat[:, None] == local_flat[None, :])
        & (depth_flat[None, :] < depth_flat[:, None])
        & live_flat[None, :]
    )
    ahead_table = ahead_table.astype(jnp.float32)
    owner_table = (jnp.arange(LB, dtype=jnp.int32)[:, None] == local_flat[None, :]).astype(
        jnp.float32
    )
    got_color = lax.all_to_all(send_color, "slab", split_axis=0, concat_axis=0, tiled=True)
    got_trans = lax.all_to_all(send_trans, "slab", split_axis=0, concat_axis=0, tiled=True)
    pixel_count = got_color.shape[3]
    item_count = got_color.shape[0] * got_color.shape[1]
    log_trans = jnp.log(got_trans.reshape(item_count, pixel_count).astype(jnp.float32))
    log_trans = jnp.where(live_flat[:, None], log_trans, 0.0)
    front_log = jnp.dot(ahead_table, log_trans, precision=EXACT_PRECISION)
    front_share = jnp.where(live_flat[:, None], jnp.exp(front_log), 0.0)
    weighted = front_share[:, None, :] * got_color.reshape(item_count, -1, pixel_count).astype(
        jnp.float32
    )
    blend_sum = jnp.dot(owner_table, weighted.reshape(item_count, -1), precision=EXACT_PRECISION)
    blend_color = blend_sum.reshape(LB, -1, pixel_count).astype(jnp.bfloat16)
    trans_field = jnp.exp(jnp.dot(owner_table, log_trans, precision=EXACT_PRECISION))
    shaded = shade_blocks(blend_color, trans_field, w_in, trans_weight, w_mid, w_out)
    display_tiles = lax.all_to_all(shaded[None], "strip", split_axis=1, concat_axis=0, tiled=True)
    return display_tiles[None]


SMEM = pltpu.SMEM
VMEM = pltpu.VMEM
ROWS = 8
GROUP = 4


def exchange_order(n_slab):
    central = n_slab // 2 + 1
    return [central] + [s for s in reversed(range(n_slab)) if s != central]


def pack_kernel(far_counts, far_colors, far_transmit, sends, counts, colors, transmit, sems):
    n_slab = sends.shape[0]
    place = [exchange_order(n_slab).index(c) for c in range(n_slab)]
    slots, feats, span = colors.shape[2:]
    me = lax.axis_index("slab")
    copies = [
        pltpu.make_async_copy(far, near, sems.at[i])
        for i, (far, near) in enumerate(
            ((far_counts, counts), (far_transmit, transmit), (far_colors, colors))
        )
    ]
    for copy in copies:
        copy.start()
    copies[0].wait()
    mine = counts[0, pl.ds(me, 1), :].astype(jnp.float32)
    before = lax.broadcasted_iota(jnp.int32, mine.shape, 1)
    row = lax.broadcasted_iota(jnp.int32, (ROWS, slots), 0).astype(jnp.float32)
    lane = lax.broadcasted_iota(jnp.int32, (ROWS, slots), 1).astype(jnp.float32)
    offs, picks = [], []
    for c in range(n_slab):
        off = jnp.sum(jnp.where(before < c, mine, 0.0), axis=1, keepdims=True)
        offs.append(off)
        hit = (row < MOST) & (lane - row == off)
        picks.append(jnp.where(hit, 1.0, 0.0))
    pick = jnp.concatenate(picks).astype(jnp.bfloat16)
    copies[1].wait()
    tails = jnp.dot(pick, transmit[0, 0], preferred_element_type=jnp.float32)
    for c in range(n_slab):
        tail = tails[c * ROWS : (c + 1) * ROWS]
        sends[place[c], pl.ds(MOST * feats, ROWS), :] = tail.astype(jnp.bfloat16)
    copies[2].wait()
    for c in range(n_slab):
        off = jnp.broadcast_to(offs[c], (feats, span)).astype(jnp.bfloat16)
        for r in range(MOST):
            last = min(MOST * c + r, slots - 1)
            block = colors[0, 0, last]
            for slot in range(r, last):
                block = jnp.where(off == slot - r, colors[0, 0, slot], block)
            sends[place[c], pl.ds(r * feats, feats), :] = block


def plan_kernel(n_slab, slots, *refs):
    (counts, blocks, assign, depth), (rows, codes) = refs[:4], refs[4:]
    items = n_slab * MOST
    outs = codes.shape[1] // (2 * items)
    me = lax.axis_index("slab")
    row = lax.broadcasted_iota(jnp.int32, rows.shape[1:], 0)
    item_lane = lax.broadcasted_iota(jnp.int32, codes.shape, 1) // outs
    posv = jnp.zeros(rows.shape[1:], jnp.int32)
    depthv = jnp.zeros(rows.shape[1:], jnp.int32)
    firstv = jnp.zeros(rows.shape[1:], jnp.int32)
    codev = jnp.full(codes.shape, -1, jnp.int32)
    pos = []
    for k, s in enumerate(exchange_order(n_slab)):
        off = jnp.int32(0)
        for c in range(n_slab):
            off = off + jnp.where(c < me, counts[0, s, c], 0)
        count = counts[0, s, me]
        for r in range(MOST):
            i = k * MOST + r
            slot = jnp.minimum(off + r, slots - 1)
            here = assign[0, blocks[0, s, slot]] - me * LB
            here = jnp.where(r < count, here, -1)
            first = jnp.int32(i)
            for j in reversed(range(i)):
                first = jnp.where(pos[j] == here, j, first)
            pos.append(here)
            firstv = jnp.where(row == i, first, firstv)
            posv = jnp.where(row == i, here, posv)
            depthv = jnp.where(row == i, depth[s], depthv)
            codev = jnp.where(item_lane == i, jnp.where(first == i, here, -1), codev)
    rows[0] = posv
    rows[1] = depthv
    rows[2] = firstv
    codes[...] = codev.astype(jnp.float32).astype(jnp.bfloat16)


def place_kernel(w_in, trans_weight, far_out, far_mid, w_first, w_out, w_later, w_mid, sems):
    copy = pltpu.make_async_copy(far_mid, w_mid, sems.at[0])
    copy.start()
    feats, hidden = w_in.shape
    half_in = (w_in[...].astype(jnp.float32) * 0.5).astype(jnp.bfloat16)
    half_trans = trans_weight[...].astype(jnp.float32) * 0.5
    sub = lax.broadcasted_iota(jnp.int32, (16, hidden), 0)
    w_first[...] = jnp.zeros_like(w_first)
    for a in range(GROUP):
        w_first[a, pl.ds(a * feats, feats), :] = half_in
        tail = jnp.where(sub // 2 == a, half_trans, 0.0)
        w_first[a, pl.ds(GROUP * feats, 16), :] = tail.astype(jnp.bfloat16)
    w_out[...] = far_out[...]
    copy.wait()
    for m in range(w_mid.shape[0]):
        w_later[m] = (w_mid[m].astype(jnp.float32).T * 0.5).astype(jnp.bfloat16)


def silu_half(u):
    return (u + u * jnp.tanh(u)).astype(jnp.bfloat16)


def later_layers(h, w_mid, w_out):
    for m in range(w_mid.shape[0]):
        h = silu_half(jnp.dot(h, w_mid[m], preferred_element_type=jnp.float32))
    y = lax.dot_general(
        w_out[...], h, (((1,), (1,)), ((), ())), preferred_element_type=jnp.float32
    )
    return y.astype(jnp.bfloat16).astype(jnp.float32)


def empty_kernel(trans_weight, w_mid, w_out, out):
    u = trans_weight[...].astype(jnp.float32) * 0.5
    h = silu_half(jnp.broadcast_to(u, (out.shape[1], u.shape[1])))
    y = later_layers(h, w_mid, w_out)
    outs = w_out.shape[0]
    for at in range(0, out.shape[0], outs):
        out[pl.ds(at, outs), :] = y


def shade_kernel(rows, codes, got, w_first, w_mid, w_out, out, acc, xt, ys):
    items, feats, span = acc.shape
    outs = w_out.shape[0]

    posv, depthv = rows[0], rows[1]
    front = jnp.ones((items, span), jnp.float32)
    total = jnp.ones((items, span), jnp.float32)
    for k in range(items // MOST):
        tail = got[k, pl.ds(MOST * feats, ROWS), :].astype(jnp.float32)
        for r in range(MOST):
            j = k * MOST + r
            trans_j = tail[r : r + 1, :]
            same = posv == posv[j : j + 1, :]
            total = jnp.where(same, total * trans_j, total)
            front = jnp.where(same & (depthv > depthv[j : j + 1, :]), front * trans_j, front)
    acc[...] = jnp.zeros_like(acc)
    for j in range(items):
        k, r = divmod(j, MOST)
        color = got[k, pl.ds(r * feats, feats), :].astype(jnp.float32)
        at = rows[2, j, 0]
        acc[at] = acc[at] + front[j : j + 1, :] * color
    total_hi = total.astype(jnp.bfloat16).astype(jnp.float32)
    total_lo = total - total_hi
    groups = items // GROUP
    sub = lax.broadcasted_iota(jnp.int32, (16, span), 0)
    xt[...] = jnp.zeros_like(xt)
    for q in range(groups):
        block = acc[pl.ds(q * GROUP, GROUP)].reshape(GROUP * feats, span)
        tail = jnp.zeros((16, span), jnp.float32)
        for a in range(GROUP):
            i = q * GROUP + a
            tail = jnp.where(sub == 2 * a, total_hi[i : i + 1, :], tail)
            tail = jnp.where(sub == 2 * a + 1, total_lo[i : i + 1, :], tail)
        lines = pl.ds(q * span, span)
        xt[lines, pl.ds(0, GROUP * feats)] = block.T.astype(jnp.bfloat16)
        xt[lines, pl.ds(GROUP * feats, 16)] = tail.T.astype(jnp.bfloat16)

    x = xt[...]
    stride = GROUP
    for start in range(0, GROUP, stride):
        h = jnp.concatenate(
            [
                silu_half(jnp.dot(x, w_first[a], preferred_element_type=jnp.float32))
                for a in range(start, start + stride)
            ]
        )
        y = later_layers(h, w_mid, w_out)
        for a in range(start, start + stride):
            for q in range(groups):
                at = ((a - start) * groups + q) * span
                ys[pl.ds((q * GROUP + a) * outs, outs), :] = y[:, at : at + span]
    out[pl.ds(0, items * outs), :] = ys[...].astype(jnp.bfloat16)
    out[pl.ds(items * outs, ROWS), :] = codes[...]


def join_kernel(*refs):
    *got, empty, out = refs
    _, n_strip, tile, outs, span = out.shape
    lines = tile * outs
    count = got[0].shape[0] - ROWS
    me = lax.axis_index("strip")
    want = lax.broadcasted_iota(jnp.int32, (lines, count), 0) + me * lines
    chan = lax.broadcasted_iota(jnp.int32, (lines, count), 1) % outs
    filler = jnp.concatenate([empty[...]] * (lines // ROWS))
    ones = jnp.ones((count, span), jnp.bfloat16)
    for k in range(n_strip):
        pos = got[k][pl.ds(count, ROWS), :].astype(jnp.float32)[:1, :count].astype(jnp.int32)
        hit = pos * outs + chan == want
        pick = jnp.where(hit, 1.0, 0.0).astype(jnp.bfloat16)
        blocks = got[k][pl.ds(0, count), :]
        placed = jnp.dot(pick, blocks, preferred_element_type=jnp.float32)
        filled = jnp.dot(pick, ones, preferred_element_type=jnp.float32)
        value = jnp.where(filled > 0.5, placed, filler)
        out[0, me ^ ((k + 1) % n_strip)] = value.reshape(tile, outs, span).astype(jnp.bfloat16)


def compact_device(
    n_slab,
    n_strip,
    colors,
    transmit,
    pair_counts,
    slot_block,
    assign,
    depth_rank,
    w_in,
    trans_weight,
    w_mid,
    w_out,
):
    slots, feats, span = colors.shape[2:]
    items = n_slab * MOST
    outs = w_out.shape[0]
    smem = pl.BlockSpec(memory_space=SMEM)
    vmem = pl.BlockSpec(memory_space=VMEM)
    hbm = pl.BlockSpec(memory_space=pltpu.HBM)
    held = functools.partial(pltpu.with_memory_space_constraint, memory_space=pltpu.HBM)
    small = pltpu.CompilerParams(vmem_limit_bytes=4 * 1024 * 1024)
    message = MOST * feats + ROWS
    sends = pl.pallas_call(
        pack_kernel,
        out_shape=jax.ShapeDtypeStruct((n_slab, message, span), jnp.bfloat16),
        in_specs=[hbm] * 3,
        out_specs=vmem,
        scratch_shapes=[
            pltpu.VMEM(pair_counts.shape, jnp.int32),
            pltpu.VMEM(colors.shape, colors.dtype),
            pltpu.VMEM(transmit.shape, transmit.dtype),
            pltpu.SemaphoreType.DMA((3,)),
        ],
        compiler_params=small,
        name="pack",
    )(held(pair_counts), held(colors), held(transmit))
    group = exchange_order(n_slab)
    got = lax.all_to_all(
        sends, "slab", split_axis=0, concat_axis=0, axis_index_groups=[group], tiled=True
    )
    hidden = w_in.shape[0]
    rough = pl.CostEstimate(flops=10**5, bytes_accessed=10**6, transcendentals=0)
    roomy = pltpu.CompilerParams(vmem_limit_bytes=16 * 1024 * 1024)
    trans_row = trans_weight[None]
    rows, codes = pl.pallas_call(
        functools.partial(plan_kernel, n_slab, slots),
        out_shape=[
            jax.ShapeDtypeStruct((3, items, span), jnp.int32),
            jax.ShapeDtypeStruct((ROWS, span), jnp.bfloat16),
        ],
        in_specs=[smem] * 4,
        out_specs=[vmem] * 2,
        compiler_params=small,
        cost_estimate=rough,
        name="plan",
    )(pair_counts, slot_block, assign, depth_rank)
    w_first, w_last, w_later = pl.pallas_call(
        place_kernel,
        out_shape=[
            jax.ShapeDtypeStruct((GROUP, 2 * GROUP * feats, hidden), jnp.bfloat16),
            jax.ShapeDtypeStruct(w_out.shape, jnp.bfloat16),
            jax.ShapeDtypeStruct(w_mid.shape, jnp.bfloat16),
        ],
        in_specs=[vmem] * 3 + [hbm],
        out_specs=[vmem] * 3,
        scratch_shapes=[
            pltpu.VMEM(w_mid.shape, jnp.bfloat16),
            pltpu.SemaphoreType.DMA((1,)),
        ],
        compiler_params=small,
        cost_estimate=rough,
        name="place",
    )(w_in.T, trans_row, w_out, held(w_mid))
    empty = pl.pallas_call(
        empty_kernel,
        out_shape=jax.ShapeDtypeStruct((ROWS, span), jnp.float32),
        in_specs=[vmem] * 3,
        out_specs=vmem,
        compiler_params=roomy,
        cost_estimate=rough,
        name="empty",
    )(trans_row, w_later, w_last)
    shaded = pl.pallas_call(
        shade_kernel,
        out_shape=jax.ShapeDtypeStruct((items * outs + ROWS, span), jnp.bfloat16),
        in_specs=[vmem] * 6,
        out_specs=vmem,
        scratch_shapes=[
            pltpu.VMEM((items, feats, span), jnp.float32),
            pltpu.VMEM((items // GROUP * span, 2 * GROUP * feats), jnp.bfloat16),
            pltpu.VMEM((items * outs, span), jnp.float32),
        ],
        compiler_params=roomy,
        name="shade",
    )(rows, codes, got, w_first, w_later, w_last)
    tiles = [
        lax.ppermute(shaded, "strip", [(s, s ^ k) for s in range(n_strip)])
        for k in range(1, n_strip)
    ] + [shaded]
    return pl.pallas_call(
        join_kernel,
        out_shape=jax.ShapeDtypeStruct((1, n_strip, LB // n_strip, outs, span), jnp.bfloat16),
        in_specs=[vmem] * (n_strip + 1),
        out_specs=pl.BlockSpec(),
        compiler_params=small,
        name="join",
    )(*tiles, empty)


def solution(mesh):
    n_slab, n_strip = mesh.shape["slab"], mesh.shape["strip"]
    placed = (
        P("slab", "strip", None, None, None),
        P("slab", "strip", None, None),
        P("strip", None, None),
        P("strip", None, None),
        P("strip", None),
        P(),
        P(),
        P(),
        P(),
        P(),
    )
    compact = n_strip & (n_strip - 1) == 0 and 4 * MOST * n_slab <= LB
    return jax.shard_map(
        functools.partial(compact_device, n_slab, n_strip) if compact else dense_device,
        mesh=mesh,
        in_specs=placed,
        out_specs=P("slab", None, "strip", None, None),
        check_vma=False,
    )
```

```python
import functools

import jax
import jax.numpy as jnp
from jax import lax
from jax.experimental import pallas as pl
from jax.experimental.pallas import tpu as pltpu
from jax.sharding import PartitionSpec as P

MOST = 2
LB = 128


EXACT_PRECISION = lax.Precision.HIGHEST


def shade_blocks(blend_color, trans_field, w_in, trans_weight, w_mid, w_out):
    summed = jnp.einsum("hf,lfp->lhp", w_in, blend_color, preferred_element_type=jnp.float32)
    summed = summed + trans_weight.astype(jnp.float32)[None, :, None] * trans_field[:, None, :]
    hidden = jax.nn.silu(summed).astype(jnp.bfloat16)
    for layer_index in range(w_mid.shape[0]):
        hidden = jax.nn.silu(
            jnp.einsum(
                "hg,lgp->lhp", w_mid[layer_index], hidden, preferred_element_type=jnp.float32
            )
        ).astype(jnp.bfloat16)
    return jnp.einsum("oh,lhp->lop", w_out, hidden, preferred_element_type=jnp.float32).astype(
        jnp.bfloat16
    )


def dense_device(
    colors, transmit, pair_counts, slot_block, assign, depth_rank, w_in, trans_weight, w_mid, w_out
):
    myself = lax.axis_index("slab")
    counts = pair_counts[0]
    blocks_all = slot_block[0]
    assign_row = assign[0]
    offsets = jnp.cumsum(counts, axis=1) - counts
    slot_rank = jnp.arange(MOST, dtype=jnp.int32)
    my_counts = lax.dynamic_index_in_dim(counts, myself, 0, keepdims=False)
    my_offsets = lax.dynamic_index_in_dim(offsets, myself, 0, keepdims=False)
    send_slots = jnp.where(
        slot_rank[None, :] < my_counts[:, None], my_offsets[:, None] + slot_rank[None, :], 0
    )
    send_color = colors[0, 0][send_slots]
    send_trans = transmit[0, 0][send_slots][:, :, None, :]
    incoming = lax.dynamic_index_in_dim(counts, myself, 1, keepdims=False)
    in_offsets = lax.dynamic_index_in_dim(offsets, myself, 1, keepdims=False)
    live_slot = slot_rank[None, :] < incoming[:, None]
    recv_slots = jnp.where(live_slot, in_offsets[:, None] + slot_rank[None, :], 0)
    recv_blocks = jnp.take_along_axis(blocks_all, recv_slots, axis=1)
    local_pos = assign_row[recv_blocks] - myself * LB
    live_flat = live_slot.reshape(-1)
    local_flat = jnp.where(live_flat, local_pos.reshape(-1), -1)
    depth_flat = jnp.repeat(depth_rank, MOST)
    ahead_table = (
        (local_flat[:, None] == local_flat[None, :])
        & (depth_flat[None, :] < depth_flat[:, None])
        & live_flat[None, :]
    )
    ahead_table = ahead_table.astype(jnp.float32)
    owner_table = (jnp.arange(LB, dtype=jnp.int32)[:, None] == local_flat[None, :]).astype(
        jnp.float32
    )
    got_color = lax.all_to_all(send_color, "slab", split_axis=0, concat_axis=0, tiled=True)
    got_trans = lax.all_to_all(send_trans, "slab", split_axis=0, concat_axis=0, tiled=True)
    pixel_count = got_color.shape[3]
    item_count = got_color.shape[0] * got_color.shape[1]
    log_trans = jnp.log(got_trans.reshape(item_count, pixel_count).astype(jnp.float32))
    log_trans = jnp.where(live_flat[:, None], log_trans, 0.0)
    front_log = jnp.dot(ahead_table, log_trans, precision=EXACT_PRECISION)
    front_share = jnp.where(live_flat[:, None], jnp.exp(front_log), 0.0)
    weighted = front_share[:, None, :] * got_color.reshape(item_count, -1, pixel_count).astype(
        jnp.float32
    )
    blend_sum = jnp.dot(owner_table, weighted.reshape(item_count, -1), precision=EXACT_PRECISION)
    blend_color = blend_sum.reshape(LB, -1, pixel_count).astype(jnp.bfloat16)
    trans_field = jnp.exp(jnp.dot(owner_table, log_trans, precision=EXACT_PRECISION))
    shaded = shade_blocks(blend_color, trans_field, w_in, trans_weight, w_mid, w_out)
    display_tiles = lax.all_to_all(shaded[None], "strip", split_axis=1, concat_axis=0, tiled=True)
    return display_tiles[None]


SMEM = pltpu.SMEM
VMEM = pltpu.VMEM
ROWS = 8
GROUP = 4
PARTS = 4


def exchange_order(n_slab):
    half = n_slab // 2
    flip = 1 if half % 2 == 0 else 0
    return [s for i in range(half) for s in (half + (i ^ flip), i)]


def pack_kernel(far_counts, far_colors, far_transmit, sends, counts, colors, transmit, sems):
    n_slab = sends.shape[0]
    place = [exchange_order(n_slab).index(c) for c in range(n_slab)]
    slots, feats, span = colors.shape
    me = lax.axis_index("slab")
    part = slots // PARTS
    copies = [
        pltpu.make_async_copy(far_counts, counts, sems.at[0]),
        pltpu.make_async_copy(far_transmit, transmit, sems.at[1]),
    ] + [
        pltpu.make_async_copy(
            far_colors.at[0, 0, pl.ds(p * part, part)], colors.at[pl.ds(p * part, part)], sems.at[2 + p]
        )
        for p in range(PARTS)
    ]
    for copy in copies:
        copy.start()
    copies[0].wait()
    mine = counts[0, pl.ds(me, 1), :].astype(jnp.float32)
    before = lax.broadcasted_iota(jnp.int32, mine.shape, 1)
    row = lax.broadcasted_iota(jnp.int32, (ROWS, slots), 0).astype(jnp.float32)
    lane = lax.broadcasted_iota(jnp.int32, (ROWS, slots), 1).astype(jnp.float32)
    offs, picks = [], []
    for c in range(n_slab):
        off = jnp.sum(jnp.where(before < c, mine, 0.0), axis=1, keepdims=True)
        offs.append(off)
        hit = (row < MOST) & (lane - row == off)
        picks.append(jnp.where(hit, 1.0, 0.0))
    pick = jnp.concatenate(picks).astype(jnp.bfloat16)
    copies[1].wait()
    tails = jnp.dot(pick, transmit[0, 0], preferred_element_type=jnp.float32)
    for c in range(n_slab):
        tail = tails[c * ROWS : (c + 1) * ROWS]
        sends[place[c], pl.ds(MOST * feats, ROWS), :] = tail.astype(jnp.bfloat16)
    waited = 0
    for c in range(n_slab):
        off = jnp.broadcast_to(offs[c], (feats, span)).astype(jnp.bfloat16)
        for r in range(MOST):
            last = min(MOST * c + r, slots - 1)
            while waited * part <= last:
                copies[2 + waited].wait()
                waited += 1
            block = colors[last]
            for slot in range(r, last):
                block = jnp.where(off == slot - r, colors[slot], block)
            sends[place[c], pl.ds(r * feats, feats), :] = block
    for copy in copies[2 + waited :]:
        copy.wait()


def plan_kernel(n_slab, slots, *refs):
    (counts, blocks, assign, depth), (rows, codes) = refs[:4], refs[4:]
    items = n_slab * MOST
    outs = codes.shape[1] // (2 * items)
    me = lax.axis_index("slab")
    row = lax.broadcasted_iota(jnp.int32, rows.shape[1:], 0)
    item_lane = lax.broadcasted_iota(jnp.int32, codes.shape, 1) // outs
    posv = jnp.zeros(rows.shape[1:], jnp.int32)
    depthv = jnp.zeros(rows.shape[1:], jnp.int32)
    firstv = jnp.zeros(rows.shape[1:], jnp.int32)
    codev = jnp.full(codes.shape, -1, jnp.int32)
    pos = []
    for k, s in enumerate(exchange_order(n_slab)):
        off = jnp.int32(0)
        for c in range(n_slab):
            off = off + jnp.where(c < me, counts[0, s, c], 0)
        count = counts[0, s, me]
        for r in range(MOST):
            i = k * MOST + r
            slot = jnp.minimum(off + r, slots - 1)
            here = assign[0, blocks[0, s, slot]] - me * LB
            here = jnp.where(r < count, here, -1)
            first = jnp.int32(i)
            for j in reversed(range(i)):
                first = jnp.where(pos[j] == here, j, first)
            pos.append(here)
            firstv = jnp.where(row == i, first, firstv)
            posv = jnp.where(row == i, here, posv)
            depthv = jnp.where(row == i, depth[s], depthv)
            codev = jnp.where(item_lane == i, jnp.where(first == i, here, -1), codev)
    rows[0] = posv
    rows[1] = depthv
    rows[2] = firstv
    codes[...] = codev.astype(jnp.float32).astype(jnp.bfloat16)


def place_kernel(w_in, trans_weight, far_out, far_mid, w_first, w_out, w_later, w_mid, sems):
    copy = pltpu.make_async_copy(far_mid, w_mid, sems.at[0])
    copy.start()
    feats, hidden = w_in.shape
    half_in = (w_in[...].astype(jnp.float32) * 0.5).astype(jnp.bfloat16)
    half_trans = trans_weight[...].astype(jnp.float32) * 0.5
    sub = lax.broadcasted_iota(jnp.int32, (16, hidden), 0)
    w_first[...] = jnp.zeros_like(w_first)
    for a in range(GROUP):
        w_first[a, pl.ds(a * feats, feats), :] = half_in
        tail = jnp.where(sub // 2 == a, half_trans, 0.0)
        w_first[a, pl.ds(GROUP * feats, 16), :] = tail.astype(jnp.bfloat16)
    w_out[...] = far_out[...]
    copy.wait()
    for m in range(w_mid.shape[0]):
        w_later[m] = (w_mid[m].astype(jnp.float32).T * 0.5).astype(jnp.bfloat16)


def silu_half(u):
    return (u + u * jnp.tanh(u)).astype(jnp.bfloat16)


def later_layers(h, w_mid, w_out):
    for m in range(w_mid.shape[0]):
        h = silu_half(jnp.dot(h, w_mid[m], preferred_element_type=jnp.float32))
    y = lax.dot_general(
        w_out[...], h, (((1,), (1,)), ((), ())), preferred_element_type=jnp.float32
    )
    return y.astype(jnp.bfloat16).astype(jnp.float32)


def empty_kernel(trans_weight, w_mid, w_out, out):
    u = trans_weight[...].astype(jnp.float32) * 0.5
    h = silu_half(jnp.broadcast_to(u, (out.shape[1], u.shape[1])))
    y = later_layers(h, w_mid, w_out)
    outs = w_out.shape[0]
    for at in range(0, out.shape[0], outs):
        out[pl.ds(at, outs), :] = y


def shade_kernel(rows, codes, got, w_first, w_mid, w_out, out, acc, xt, ys):
    items, feats, span = acc.shape
    outs = w_out.shape[0]

    posv, depthv = rows[0], rows[1]
    front = jnp.ones((items, span), jnp.float32)
    total = jnp.ones((items, span), jnp.float32)
    for k in range(items // MOST):
        tail = got[k, pl.ds(MOST * feats, ROWS), :].astype(jnp.float32)
        for r in range(MOST):
            j = k * MOST + r
            trans_j = tail[r : r + 1, :]
            same = posv == posv[j : j + 1, :]
            total = jnp.where(same, total * trans_j, total)
            front = jnp.where(same & (depthv > depthv[j : j + 1, :]), front * trans_j, front)
    acc[...] = jnp.zeros_like(acc)
    for j in range(items):
        k, r = divmod(j, MOST)
        color = got[k, pl.ds(r * feats, feats), :].astype(jnp.float32)
        at = rows[2, j, 0]
        acc[at] = acc[at] + front[j : j + 1, :] * color
    total_hi = total.astype(jnp.bfloat16).astype(jnp.float32)
    total_lo = total - total_hi
    groups = items // GROUP
    sub = lax.broadcasted_iota(jnp.int32, (16, span), 0)
    xt[...] = jnp.zeros_like(xt)
    for q in range(groups):
        block = acc[pl.ds(q * GROUP, GROUP)].reshape(GROUP * feats, span)
        tail = jnp.zeros((16, span), jnp.float32)
        for a in range(GROUP):
            i = q * GROUP + a
            tail = jnp.where(sub == 2 * a, total_hi[i : i + 1, :], tail)
            tail = jnp.where(sub == 2 * a + 1, total_lo[i : i + 1, :], tail)
        lines = pl.ds(q * span, span)
        xt[lines, pl.ds(0, GROUP * feats)] = block.T.astype(jnp.bfloat16)
        xt[lines, pl.ds(GROUP * feats, 16)] = tail.T.astype(jnp.bfloat16)

    x = xt[...]
    stride = GROUP
    for start in range(0, GROUP, stride):
        h = jnp.concatenate(
            [
                silu_half(jnp.dot(x, w_first[a], preferred_element_type=jnp.float32))
                for a in range(start, start + stride)
            ]
        )
        y = later_layers(h, w_mid, w_out)
        for a in range(start, start + stride):
            for q in range(groups):
                at = ((a - start) * groups + q) * span
                ys[pl.ds((q * GROUP + a) * outs, outs), :] = y[:, at : at + span]
    out[pl.ds(0, items * outs), :] = ys[...].astype(jnp.bfloat16)
    out[pl.ds(items * outs, ROWS), :] = codes[...]


def join_kernel(*refs):
    *got, empty, out, held, sems = refs
    _, n_strip, tile, outs, span = out.shape
    lines = tile * outs
    count = got[0].shape[0] - ROWS
    me = lax.axis_index("strip")
    want = lax.broadcasted_iota(jnp.int32, (lines, count), 0) + me * lines
    chan = lax.broadcasted_iota(jnp.int32, (lines, count), 1) % outs
    filler = jnp.concatenate([empty[...]] * (lines // ROWS))
    ones = jnp.ones((count, span), jnp.bfloat16)
    copies = []
    for k in range(n_strip):
        pos = got[k][pl.ds(count, ROWS), :].astype(jnp.float32)[:1, :count].astype(jnp.int32)
        hit = pos * outs + chan == want
        pick = jnp.where(hit, 1.0, 0.0).astype(jnp.bfloat16)
        blocks = got[k][pl.ds(0, count), :]
        placed = jnp.dot(pick, blocks, preferred_element_type=jnp.float32)
        filled = jnp.dot(pick, ones, preferred_element_type=jnp.float32)
        value = jnp.where(filled > 0.5, placed, filler)
        held[k] = value.reshape(tile, outs, span).astype(jnp.bfloat16)
        copy = pltpu.make_async_copy(
            held.at[k], out.at[0, me ^ ((k + 1) % n_strip)], sems.at[k]
        )
        copy.start()
        copies.append(copy)
    for copy in copies:
        copy.wait()


def compact_device(
    n_slab,
    n_strip,
    colors,
    transmit,
    pair_counts,
    slot_block,
    assign,
    depth_rank,
    w_in,
    trans_weight,
    w_mid,
    w_out,
):
    slots, feats, span = colors.shape[2:]
    items = n_slab * MOST
    outs = w_out.shape[0]
    smem = pl.BlockSpec(memory_space=SMEM)
    vmem = pl.BlockSpec(memory_space=VMEM)
    hbm = pl.BlockSpec(memory_space=pltpu.HBM)
    held = functools.partial(pltpu.with_memory_space_constraint, memory_space=pltpu.HBM)
    small = pltpu.CompilerParams(vmem_limit_bytes=4 * 1024 * 1024)
    message = MOST * feats + ROWS
    sends = pl.pallas_call(
        pack_kernel,
        out_shape=jax.ShapeDtypeStruct((n_slab, message, span), jnp.bfloat16),
        in_specs=[hbm] * 3,
        out_specs=vmem,
        scratch_shapes=[
            pltpu.VMEM(pair_counts.shape, jnp.int32),
            pltpu.VMEM(colors.shape[2:], colors.dtype),
            pltpu.VMEM(transmit.shape, transmit.dtype),
            pltpu.SemaphoreType.DMA((2 + PARTS,)),
        ],
        compiler_params=small,
        name="pack",
    )(held(pair_counts), held(colors), held(transmit))
    group = exchange_order(n_slab)
    got = lax.all_to_all(
        sends, "slab", split_axis=0, concat_axis=0, axis_index_groups=[group], tiled=True
    )
    hidden = w_in.shape[0]
    rough = pl.CostEstimate(flops=10**5, bytes_accessed=10**6, transcendentals=0)
    roomy = pltpu.CompilerParams(vmem_limit_bytes=16 * 1024 * 1024)
    trans_row = trans_weight[None]
    rows, codes = pl.pallas_call(
        functools.partial(plan_kernel, n_slab, slots),
        out_shape=[
            jax.ShapeDtypeStruct((3, items, span), jnp.int32),
            jax.ShapeDtypeStruct((ROWS, span), jnp.bfloat16),
        ],
        in_specs=[smem] * 4,
        out_specs=[vmem] * 2,
        compiler_params=small,
        cost_estimate=rough,
        name="plan",
    )(pair_counts, slot_block, assign, depth_rank)
    w_first, w_last, w_later = pl.pallas_call(
        place_kernel,
        out_shape=[
            jax.ShapeDtypeStruct((GROUP, 2 * GROUP * feats, hidden), jnp.bfloat16),
            jax.ShapeDtypeStruct(w_out.shape, jnp.bfloat16),
            jax.ShapeDtypeStruct(w_mid.shape, jnp.bfloat16),
        ],
        in_specs=[vmem] * 3 + [hbm],
        out_specs=[vmem] * 3,
        scratch_shapes=[
            pltpu.VMEM(w_mid.shape, jnp.bfloat16),
            pltpu.SemaphoreType.DMA((1,)),
        ],
        compiler_params=small,
        cost_estimate=rough,
        name="place",
    )(w_in.T, trans_row, w_out, held(w_mid))
    empty = pl.pallas_call(
        empty_kernel,
        out_shape=jax.ShapeDtypeStruct((ROWS, span), jnp.float32),
        in_specs=[vmem] * 3,
        out_specs=vmem,
        compiler_params=roomy,
        cost_estimate=rough,
        name="empty",
    )(trans_row, w_later, w_last)
    shaded = pl.pallas_call(
        shade_kernel,
        out_shape=jax.ShapeDtypeStruct((items * outs + ROWS, span), jnp.bfloat16),
        in_specs=[vmem] * 6,
        out_specs=vmem,
        scratch_shapes=[
            pltpu.VMEM((items, feats, span), jnp.float32),
            pltpu.VMEM((items // GROUP * span, 2 * GROUP * feats), jnp.bfloat16),
            pltpu.VMEM((items * outs, span), jnp.float32),
        ],
        compiler_params=roomy,
        name="shade",
    )(rows, codes, got, w_first, w_later, w_last)
    tiles = [
        lax.ppermute(shaded, "strip", [(s, s ^ k) for s in range(n_strip)])
        for k in range(1, n_strip)
    ] + [shaded]
    return pl.pallas_call(
        join_kernel,
        out_shape=jax.ShapeDtypeStruct((1, n_strip, LB // n_strip, outs, span), jnp.bfloat16),
        in_specs=[vmem] * (n_strip + 1),
        out_specs=pl.BlockSpec(memory_space=pl.ANY),
        scratch_shapes=[
            pltpu.VMEM((n_strip, LB // n_strip, outs, span), jnp.bfloat16),
            pltpu.SemaphoreType.DMA((n_strip,)),
        ],
        compiler_params=small,
        name="join",
    )(*tiles, empty)


def solution(mesh):
    n_slab, n_strip = mesh.shape["slab"], mesh.shape["strip"]
    placed = (
        P("slab", "strip", None, None, None),
        P("slab", "strip", None, None),
        P("strip", None, None),
        P("strip", None, None),
        P("strip", None),
        P(),
        P(),
        P(),
        P(),
        P(),
    )
    compact = n_strip & (n_strip - 1) == 0 and 4 * MOST * n_slab <= LB
    return jax.shard_map(
        functools.partial(compact_device, n_slab, n_strip) if compact else dense_device,
        mesh=mesh,
        in_specs=placed,
        out_specs=P("slab", None, "strip", None, None),
        check_vma=False,
    )
```

```python
import functools

import jax
import jax.numpy as jnp
from jax import lax
from jax.experimental import pallas as pl
from jax.experimental.pallas import tpu as pltpu
from jax.sharding import PartitionSpec as P

MOST = 2
LB = 128


EXACT_PRECISION = lax.Precision.HIGHEST


def shade_blocks(blend_color, trans_field, w_in, trans_weight, w_mid, w_out):
    summed = jnp.einsum("hf,lfp->lhp", w_in, blend_color, preferred_element_type=jnp.float32)
    summed = summed + trans_weight.astype(jnp.float32)[None, :, None] * trans_field[:, None, :]
    hidden = jax.nn.silu(summed).astype(jnp.bfloat16)
    for layer_index in range(w_mid.shape[0]):
        hidden = jax.nn.silu(
            jnp.einsum(
                "hg,lgp->lhp", w_mid[layer_index], hidden, preferred_element_type=jnp.float32
            )
        ).astype(jnp.bfloat16)
    return jnp.einsum("oh,lhp->lop", w_out, hidden, preferred_element_type=jnp.float32).astype(
        jnp.bfloat16
    )


def dense_device(
    colors, transmit, pair_counts, slot_block, assign, depth_rank, w_in, trans_weight, w_mid, w_out
):
    myself = lax.axis_index("slab")
    counts = pair_counts[0]
    blocks_all = slot_block[0]
    assign_row = assign[0]
    offsets = jnp.cumsum(counts, axis=1) - counts
    slot_rank = jnp.arange(MOST, dtype=jnp.int32)
    my_counts = lax.dynamic_index_in_dim(counts, myself, 0, keepdims=False)
    my_offsets = lax.dynamic_index_in_dim(offsets, myself, 0, keepdims=False)
    send_slots = jnp.where(
        slot_rank[None, :] < my_counts[:, None], my_offsets[:, None] + slot_rank[None, :], 0
    )
    send_color = colors[0, 0][send_slots]
    send_trans = transmit[0, 0][send_slots][:, :, None, :]
    incoming = lax.dynamic_index_in_dim(counts, myself, 1, keepdims=False)
    in_offsets = lax.dynamic_index_in_dim(offsets, myself, 1, keepdims=False)
    live_slot = slot_rank[None, :] < incoming[:, None]
    recv_slots = jnp.where(live_slot, in_offsets[:, None] + slot_rank[None, :], 0)
    recv_blocks = jnp.take_along_axis(blocks_all, recv_slots, axis=1)
    local_pos = assign_row[recv_blocks] - myself * LB
    live_flat = live_slot.reshape(-1)
    local_flat = jnp.where(live_flat, local_pos.reshape(-1), -1)
    depth_flat = jnp.repeat(depth_rank, MOST)
    ahead_table = (
        (local_flat[:, None] == local_flat[None, :])
        & (depth_flat[None, :] < depth_flat[:, None])
        & live_flat[None, :]
    )
    ahead_table = ahead_table.astype(jnp.float32)
    owner_table = (jnp.arange(LB, dtype=jnp.int32)[:, None] == local_flat[None, :]).astype(
        jnp.float32
    )
    got_color = lax.all_to_all(send_color, "slab", split_axis=0, concat_axis=0, tiled=True)
    got_trans = lax.all_to_all(send_trans, "slab", split_axis=0, concat_axis=0, tiled=True)
    pixel_count = got_color.shape[3]
    item_count = got_color.shape[0] * got_color.shape[1]
    log_trans = jnp.log(got_trans.reshape(item_count, pixel_count).astype(jnp.float32))
    log_trans = jnp.where(live_flat[:, None], log_trans, 0.0)
    front_log = jnp.dot(ahead_table, log_trans, precision=EXACT_PRECISION)
    front_share = jnp.where(live_flat[:, None], jnp.exp(front_log), 0.0)
    weighted = front_share[:, None, :] * got_color.reshape(item_count, -1, pixel_count).astype(
        jnp.float32
    )
    blend_sum = jnp.dot(owner_table, weighted.reshape(item_count, -1), precision=EXACT_PRECISION)
    blend_color = blend_sum.reshape(LB, -1, pixel_count).astype(jnp.bfloat16)
    trans_field = jnp.exp(jnp.dot(owner_table, log_trans, precision=EXACT_PRECISION))
    shaded = shade_blocks(blend_color, trans_field, w_in, trans_weight, w_mid, w_out)
    display_tiles = lax.all_to_all(shaded[None], "strip", split_axis=1, concat_axis=0, tiled=True)
    return display_tiles[None]


SMEM = pltpu.SMEM
VMEM = pltpu.VMEM
ROWS = 8
GROUP = 4
PARTS = 4


def exchange_order(n_slab):
    half = n_slab // 2
    flip = 1 if half % 2 == 0 else 0
    return [s for i in range(half) for s in (half + (i ^ flip), i)]


def pack_kernel(far_counts, far_colors, far_transmit, sends, counts, colors, transmit, sems):
    n_slab = sends.shape[0]
    place = [exchange_order(n_slab).index(c) for c in range(n_slab)]
    slots, feats, span = colors.shape
    me = lax.axis_index("slab")
    part = slots // PARTS
    copies = [
        pltpu.make_async_copy(far_counts, counts, sems.at[0]),
        pltpu.make_async_copy(far_transmit, transmit, sems.at[1]),
    ] + [
        pltpu.make_async_copy(
            far_colors.at[0, 0, pl.ds(p * part, part)], colors.at[pl.ds(p * part, part)], sems.at[2 + p]
        )
        for p in range(PARTS)
    ]
    for copy in copies:
        copy.start()
    copies[0].wait()
    mine = counts[0, pl.ds(me, 1), :].astype(jnp.float32)
    before = lax.broadcasted_iota(jnp.int32, mine.shape, 1)
    row = lax.broadcasted_iota(jnp.int32, (ROWS, slots), 0).astype(jnp.float32)
    lane = lax.broadcasted_iota(jnp.int32, (ROWS, slots), 1).astype(jnp.float32)
    offs, picks = [], []
    for c in range(n_slab):
        off = jnp.sum(jnp.where(before < c, mine, 0.0), axis=1, keepdims=True)
        offs.append(off)
        hit = (row < MOST) & (lane - row == off)
        picks.append(jnp.where(hit, 1.0, 0.0))
    pick = jnp.concatenate(picks).astype(jnp.bfloat16)
    copies[1].wait()
    tails = jnp.dot(pick, transmit[0, 0], preferred_element_type=jnp.float32)
    for c in range(n_slab):
        tail = tails[c * ROWS : (c + 1) * ROWS]
        sends[place[c], pl.ds(MOST * feats, ROWS), :] = tail.astype(jnp.bfloat16)
    waited = 0
    for c in range(n_slab):
        off = jnp.broadcast_to(offs[c], (feats, span)).astype(jnp.bfloat16)
        for r in range(MOST):
            last = min(MOST * c + r, slots - 1)
            while waited * part <= last:
                copies[2 + waited].wait()
                waited += 1
            block = colors[last]
            for slot in range(r, last):
                block = jnp.where(off == slot - r, colors[slot], block)
            sends[place[c], pl.ds(r * feats, feats), :] = block
    for copy in copies[2 + waited :]:
        copy.wait()


def plan_kernel(n_slab, slots, *refs):
    (counts, blocks, assign, depth), (rows, codes) = refs[:4], refs[4:]
    items = n_slab * MOST
    outs = codes.shape[1] // (2 * items)
    me = lax.axis_index("slab")
    row = lax.broadcasted_iota(jnp.int32, rows.shape[1:], 0)
    item_lane = lax.broadcasted_iota(jnp.int32, codes.shape, 1) // outs
    posv = jnp.zeros(rows.shape[1:], jnp.int32)
    depthv = jnp.zeros(rows.shape[1:], jnp.int32)
    firstv = jnp.zeros(rows.shape[1:], jnp.int32)
    codev = jnp.full(codes.shape, -1, jnp.int32)
    pos = []
    for k, s in enumerate(exchange_order(n_slab)):
        off = jnp.int32(0)
        for c in range(n_slab):
            off = off + jnp.where(c < me, counts[0, s, c], 0)
        count = counts[0, s, me]
        for r in range(MOST):
            i = k * MOST + r
            slot = jnp.minimum(off + r, slots - 1)
            here = assign[0, blocks[0, s, slot]] - me * LB
            here = jnp.where(r < count, here, -1)
            first = jnp.int32(i)
            for j in reversed(range(i)):
                first = jnp.where(pos[j] == here, j, first)
            pos.append(here)
            firstv = jnp.where(row == i, first, firstv)
            posv = jnp.where(row == i, here, posv)
            depthv = jnp.where(row == i, depth[s], depthv)
            codev = jnp.where(item_lane == i, jnp.where(first == i, here, -1), codev)
    rows[0] = posv
    rows[1] = depthv
    rows[2] = firstv
    codes[...] = codev.astype(jnp.float32).astype(jnp.bfloat16)


def place_kernel(w_in, trans_weight, far_out, far_mid, w_first, w_out, w_later, w_mid, sems):
    copy = pltpu.make_async_copy(far_mid, w_mid, sems.at[0])
    copy.start()
    feats, hidden = w_in.shape
    half_in = (w_in[...].astype(jnp.float32) * 0.5).astype(jnp.bfloat16)
    half_trans = trans_weight[...].astype(jnp.float32) * 0.5
    sub = lax.broadcasted_iota(jnp.int32, (16, hidden), 0)
    w_first[...] = jnp.zeros_like(w_first)
    for a in range(GROUP):
        w_first[a, pl.ds(a * feats, feats), :] = half_in
        tail = jnp.where(sub // 2 == a, half_trans, 0.0)
        w_first[a, pl.ds(GROUP * feats, 16), :] = tail.astype(jnp.bfloat16)
    w_out[...] = far_out[...]
    copy.wait()
    for m in range(w_mid.shape[0]):
        w_later[m] = (w_mid[m].astype(jnp.float32).T * 0.5).astype(jnp.bfloat16)


def silu_half(u):
    return (u + u * jnp.tanh(u)).astype(jnp.bfloat16)


def silu_half_short(u):
    u = u.astype(jnp.bfloat16)
    return u + u * jnp.tanh(u)


def later_layers(h, w_mid, w_out, silu):
    for m in range(w_mid.shape[0]):
        h = silu(jnp.dot(h, w_mid[m], preferred_element_type=jnp.float32))
    y = lax.dot_general(
        w_out[...], h, (((1,), (1,)), ((), ())), preferred_element_type=jnp.float32
    )
    return y.astype(jnp.bfloat16).astype(jnp.float32)


def empty_kernel(trans_weight, w_mid, w_out, out):
    u = trans_weight[...].astype(jnp.float32) * 0.5
    h = silu_half(jnp.broadcast_to(u, (out.shape[1], u.shape[1])))
    y = later_layers(h, w_mid, w_out, silu_half)
    outs = w_out.shape[0]
    for at in range(0, out.shape[0], outs):
        out[pl.ds(at, outs), :] = y


def shade_kernel(rows, codes, got, w_first, w_mid, w_out, out, acc, xt, ys):
    items, feats, span = acc.shape
    outs = w_out.shape[0]

    posv, depthv = rows[0], rows[1]
    front = jnp.ones((items, span), jnp.float32)
    total = jnp.ones((items, span), jnp.float32)
    for k in range(items // MOST):
        tail = got[k, pl.ds(MOST * feats, ROWS), :].astype(jnp.float32)
        for r in range(MOST):
            j = k * MOST + r
            trans_j = tail[r : r + 1, :]
            same = posv == posv[j : j + 1, :]
            total = jnp.where(same, total * trans_j, total)
            front = jnp.where(same & (depthv > depthv[j : j + 1, :]), front * trans_j, front)
    acc[...] = jnp.zeros_like(acc)
    for j in range(items):
        k, r = divmod(j, MOST)
        color = got[k, pl.ds(r * feats, feats), :].astype(jnp.float32)
        at = rows[2, j, 0]
        acc[at] = acc[at] + front[j : j + 1, :] * color
    total_hi = total.astype(jnp.bfloat16).astype(jnp.float32)
    total_lo = total - total_hi
    groups = items // GROUP
    sub = lax.broadcasted_iota(jnp.int32, (16, span), 0)
    xt[...] = jnp.zeros_like(xt)
    for q in range(groups):
        block = acc[pl.ds(q * GROUP, GROUP)].reshape(GROUP * feats, span)
        tail = jnp.zeros((16, span), jnp.float32)
        for a in range(GROUP):
            i = q * GROUP + a
            tail = jnp.where(sub == 2 * a, total_hi[i : i + 1, :], tail)
            tail = jnp.where(sub == 2 * a + 1, total_lo[i : i + 1, :], tail)
        lines = pl.ds(q * span, span)
        xt[lines, pl.ds(0, GROUP * feats)] = block.T.astype(jnp.bfloat16)
        xt[lines, pl.ds(GROUP * feats, 16)] = tail.T.astype(jnp.bfloat16)

    x = xt[...]
    stride = GROUP
    for start in range(0, GROUP, stride):
        h = jnp.concatenate(
            [
                silu_half_short(jnp.dot(x, w_first[a], preferred_element_type=jnp.float32))
                for a in range(start, start + stride)
            ]
        )
        y = later_layers(h, w_mid, w_out, silu_half_short)
        for a in range(start, start + stride):
            for q in range(groups):
                at = ((a - start) * groups + q) * span
                ys[pl.ds((q * GROUP + a) * outs, outs), :] = y[:, at : at + span]
    out[pl.ds(0, items * outs), :] = ys[...].astype(jnp.bfloat16)
    out[pl.ds(items * outs, ROWS), :] = codes[...]


def join_kernel(*refs):
    *got, empty, out, held, sems = refs
    _, n_strip, tile, outs, span = out.shape
    lines = tile * outs
    count = got[0].shape[0] - ROWS
    me = lax.axis_index("strip")
    want = lax.broadcasted_iota(jnp.int32, (lines, count), 0) + me * lines
    chan = lax.broadcasted_iota(jnp.int32, (lines, count), 1) % outs
    filler = jnp.concatenate([empty[...]] * (lines // ROWS))
    ones = jnp.ones((count, span), jnp.bfloat16)
    copies = []
    for k in range(n_strip):
        pos = got[k][pl.ds(count, ROWS), :].astype(jnp.float32)[:1, :count].astype(jnp.int32)
        hit = pos * outs + chan == want
        pick = jnp.where(hit, 1.0, 0.0).astype(jnp.bfloat16)
        blocks = got[k][pl.ds(0, count), :]
        placed = jnp.dot(pick, blocks, preferred_element_type=jnp.float32)
        filled = jnp.dot(pick, ones, preferred_element_type=jnp.float32)
        value = jnp.where(filled > 0.5, placed, filler)
        held[k] = value.reshape(tile, outs, span).astype(jnp.bfloat16)
        copy = pltpu.make_async_copy(
            held.at[k], out.at[0, me ^ ((k + 1) % n_strip)], sems.at[k]
        )
        copy.start()
        copies.append(copy)
    for copy in copies:
        copy.wait()


def compact_device(
    n_slab,
    n_strip,
    colors,
    transmit,
    pair_counts,
    slot_block,
    assign,
    depth_rank,
    w_in,
    trans_weight,
    w_mid,
    w_out,
):
    slots, feats, span = colors.shape[2:]
    items = n_slab * MOST
    outs = w_out.shape[0]
    smem = pl.BlockSpec(memory_space=SMEM)
    vmem = pl.BlockSpec(memory_space=VMEM)
    hbm = pl.BlockSpec(memory_space=pltpu.HBM)
    held = functools.partial(pltpu.with_memory_space_constraint, memory_space=pltpu.HBM)
    small = pltpu.CompilerParams(vmem_limit_bytes=4 * 1024 * 1024)
    message = MOST * feats + ROWS
    sends = pl.pallas_call(
        pack_kernel,
        out_shape=jax.ShapeDtypeStruct((n_slab, message, span), jnp.bfloat16),
        in_specs=[hbm] * 3,
        out_specs=vmem,
        scratch_shapes=[
            pltpu.VMEM(pair_counts.shape, jnp.int32),
            pltpu.VMEM(colors.shape[2:], colors.dtype),
            pltpu.VMEM(transmit.shape, transmit.dtype),
            pltpu.SemaphoreType.DMA((2 + PARTS,)),
        ],
        compiler_params=small,
        name="pack",
    )(held(pair_counts), held(colors), held(transmit))
    group = exchange_order(n_slab)
    got = lax.all_to_all(
        sends, "slab", split_axis=0, concat_axis=0, axis_index_groups=[group], tiled=True
    )
    hidden = w_in.shape[0]
    rough = pl.CostEstimate(flops=10**5, bytes_accessed=10**6, transcendentals=0)
    roomy = pltpu.CompilerParams(vmem_limit_bytes=16 * 1024 * 1024)
    trans_row = trans_weight[None]
    rows, codes = pl.pallas_call(
        functools.partial(plan_kernel, n_slab, slots),
        out_shape=[
            jax.ShapeDtypeStruct((3, items, span), jnp.int32),
            jax.ShapeDtypeStruct((ROWS, span), jnp.bfloat16),
        ],
        in_specs=[smem] * 4,
        out_specs=[vmem] * 2,
        compiler_params=small,
        cost_estimate=rough,
        name="plan",
    )(pair_counts, slot_block, assign, depth_rank)
    w_first, w_last, w_later = pl.pallas_call(
        place_kernel,
        out_shape=[
            jax.ShapeDtypeStruct((GROUP, 2 * GROUP * feats, hidden), jnp.bfloat16),
            jax.ShapeDtypeStruct(w_out.shape, jnp.bfloat16),
            jax.ShapeDtypeStruct(w_mid.shape, jnp.bfloat16),
        ],
        in_specs=[vmem] * 3 + [hbm],
        out_specs=[vmem] * 3,
        scratch_shapes=[
            pltpu.VMEM(w_mid.shape, jnp.bfloat16),
            pltpu.SemaphoreType.DMA((1,)),
        ],
        compiler_params=small,
        cost_estimate=rough,
        name="place",
    )(w_in.T, trans_row, w_out, held(w_mid))
    empty = pl.pallas_call(
        empty_kernel,
        out_shape=jax.ShapeDtypeStruct((ROWS, span), jnp.float32),
        in_specs=[vmem] * 3,
        out_specs=vmem,
        compiler_params=roomy,
        cost_estimate=rough,
        name="empty",
    )(trans_row, w_later, w_last)
    shaded = pl.pallas_call(
        shade_kernel,
        out_shape=jax.ShapeDtypeStruct((items * outs + ROWS, span), jnp.bfloat16),
        in_specs=[vmem] * 6,
        out_specs=vmem,
        scratch_shapes=[
            pltpu.VMEM((items, feats, span), jnp.float32),
            pltpu.VMEM((items // GROUP * span, 2 * GROUP * feats), jnp.bfloat16),
            pltpu.VMEM((items * outs, span), jnp.float32),
        ],
        compiler_params=roomy,
        name="shade",
    )(rows, codes, got, w_first, w_later, w_last)
    tiles = [
        lax.ppermute(shaded, "strip", [(s, s ^ k) for s in range(n_strip)])
        for k in range(1, n_strip)
    ] + [shaded]
    return pl.pallas_call(
        join_kernel,
        out_shape=jax.ShapeDtypeStruct((1, n_strip, LB // n_strip, outs, span), jnp.bfloat16),
        in_specs=[vmem] * (n_strip + 1),
        out_specs=pl.BlockSpec(memory_space=pl.ANY),
        scratch_shapes=[
            pltpu.VMEM((n_strip, LB // n_strip, outs, span), jnp.bfloat16),
            pltpu.SemaphoreType.DMA((n_strip,)),
        ],
        compiler_params=small,
        name="join",
    )(*tiles, empty)


def solution(mesh):
    n_slab, n_strip = mesh.shape["slab"], mesh.shape["strip"]
    placed = (
        P("slab", "strip", None, None, None),
        P("slab", "strip", None, None),
        P("strip", None, None),
        P("strip", None, None),
        P("strip", None),
        P(),
        P(),
        P(),
        P(),
        P(),
    )
    compact = n_strip & (n_strip - 1) == 0 and 4 * MOST * n_slab <= LB
    return jax.shard_map(
        functools.partial(compact_device, n_slab, n_strip) if compact else dense_device,
        mesh=mesh,
        in_specs=placed,
        out_specs=P("slab", None, "strip", None, None),
        check_vma=False,
    )
```

```python
import functools

import jax
import jax.numpy as jnp
from jax import lax
from jax.experimental import pallas as pl
from jax.experimental.pallas import tpu as pltpu
from jax.sharding import PartitionSpec as P

MOST = 2
LB = 128


EXACT_PRECISION = lax.Precision.HIGHEST


def shade_blocks(blend_color, trans_field, w_in, trans_weight, w_mid, w_out):
    summed = jnp.einsum("hf,lfp->lhp", w_in, blend_color, preferred_element_type=jnp.float32)
    summed = summed + trans_weight.astype(jnp.float32)[None, :, None] * trans_field[:, None, :]
    hidden = jax.nn.silu(summed).astype(jnp.bfloat16)
    for layer_index in range(w_mid.shape[0]):
        hidden = jax.nn.silu(
            jnp.einsum(
                "hg,lgp->lhp", w_mid[layer_index], hidden, preferred_element_type=jnp.float32
            )
        ).astype(jnp.bfloat16)
    return jnp.einsum("oh,lhp->lop", w_out, hidden, preferred_element_type=jnp.float32).astype(
        jnp.bfloat16
    )


def dense_device(
    colors, transmit, pair_counts, slot_block, assign, depth_rank, w_in, trans_weight, w_mid, w_out
):
    myself = lax.axis_index("slab")
    counts = pair_counts[0]
    blocks_all = slot_block[0]
    assign_row = assign[0]
    offsets = jnp.cumsum(counts, axis=1) - counts
    slot_rank = jnp.arange(MOST, dtype=jnp.int32)
    my_counts = lax.dynamic_index_in_dim(counts, myself, 0, keepdims=False)
    my_offsets = lax.dynamic_index_in_dim(offsets, myself, 0, keepdims=False)
    send_slots = jnp.where(
        slot_rank[None, :] < my_counts[:, None], my_offsets[:, None] + slot_rank[None, :], 0
    )
    send_color = colors[0, 0][send_slots]
    send_trans = transmit[0, 0][send_slots][:, :, None, :]
    incoming = lax.dynamic_index_in_dim(counts, myself, 1, keepdims=False)
    in_offsets = lax.dynamic_index_in_dim(offsets, myself, 1, keepdims=False)
    live_slot = slot_rank[None, :] < incoming[:, None]
    recv_slots = jnp.where(live_slot, in_offsets[:, None] + slot_rank[None, :], 0)
    recv_blocks = jnp.take_along_axis(blocks_all, recv_slots, axis=1)
    local_pos = assign_row[recv_blocks] - myself * LB
    live_flat = live_slot.reshape(-1)
    local_flat = jnp.where(live_flat, local_pos.reshape(-1), -1)
    depth_flat = jnp.repeat(depth_rank, MOST)
    ahead_table = (
        (local_flat[:, None] == local_flat[None, :])
        & (depth_flat[None, :] < depth_flat[:, None])
        & live_flat[None, :]
    )
    ahead_table = ahead_table.astype(jnp.float32)
    owner_table = (jnp.arange(LB, dtype=jnp.int32)[:, None] == local_flat[None, :]).astype(
        jnp.float32
    )
    got_color = lax.all_to_all(send_color, "slab", split_axis=0, concat_axis=0, tiled=True)
    got_trans = lax.all_to_all(send_trans, "slab", split_axis=0, concat_axis=0, tiled=True)
    pixel_count = got_color.shape[3]
    item_count = got_color.shape[0] * got_color.shape[1]
    log_trans = jnp.log(got_trans.reshape(item_count, pixel_count).astype(jnp.float32))
    log_trans = jnp.where(live_flat[:, None], log_trans, 0.0)
    front_log = jnp.dot(ahead_table, log_trans, precision=EXACT_PRECISION)
    front_share = jnp.where(live_flat[:, None], jnp.exp(front_log), 0.0)
    weighted = front_share[:, None, :] * got_color.reshape(item_count, -1, pixel_count).astype(
        jnp.float32
    )
    blend_sum = jnp.dot(owner_table, weighted.reshape(item_count, -1), precision=EXACT_PRECISION)
    blend_color = blend_sum.reshape(LB, -1, pixel_count).astype(jnp.bfloat16)
    trans_field = jnp.exp(jnp.dot(owner_table, log_trans, precision=EXACT_PRECISION))
    shaded = shade_blocks(blend_color, trans_field, w_in, trans_weight, w_mid, w_out)
    display_tiles = lax.all_to_all(shaded[None], "strip", split_axis=1, concat_axis=0, tiled=True)
    return display_tiles[None]


SMEM = pltpu.SMEM
VMEM = pltpu.VMEM
ROWS = 8
GROUP = 4
PARTS = 4


def exchange_order(n_slab):
    half = n_slab // 2
    flip = 1 if half % 2 == 0 else 0
    ring = [s for i in range(half) for s in (half + (i ^ flip), i)]
    at = ring.index(n_slab - 1)
    return ring[at:] + ring[:at]


def pack_kernel(far_counts, far_colors, far_transmit, sends, counts, colors, transmit, sems):
    n_slab = sends.shape[0]
    place = [exchange_order(n_slab).index(c) for c in range(n_slab)]
    slots, feats, span = colors.shape
    me = lax.axis_index("slab")
    part = slots // PARTS
    copies = [
        pltpu.make_async_copy(far_counts, counts, sems.at[0]),
        pltpu.make_async_copy(far_transmit, transmit, sems.at[1]),
    ] + [
        pltpu.make_async_copy(
            far_colors.at[0, 0, pl.ds(p * part, part)], colors.at[pl.ds(p * part, part)], sems.at[2 + p]
        )
        for p in range(PARTS)
    ]
    for copy in copies:
        copy.start()
    copies[0].wait()
    mine = counts[0, pl.ds(me, 1), :].astype(jnp.float32)
    before = lax.broadcasted_iota(jnp.int32, mine.shape, 1)
    row = lax.broadcasted_iota(jnp.int32, (ROWS, slots), 0).astype(jnp.float32)
    lane = lax.broadcasted_iota(jnp.int32, (ROWS, slots), 1).astype(jnp.float32)
    offs, picks = [], []
    for c in range(n_slab):
        off = jnp.sum(jnp.where(before < c, mine, 0.0), axis=1, keepdims=True)
        offs.append(off)
        hit = (row < MOST) & (lane - row == off)
        picks.append(jnp.where(hit, 1.0, 0.0))
    pick = jnp.concatenate(picks).astype(jnp.bfloat16)
    copies[1].wait()
    tails = jnp.dot(pick, transmit[0, 0], preferred_element_type=jnp.float32)
    for c in range(n_slab):
        tail = tails[c * ROWS : (c + 1) * ROWS]
        sends[place[c], pl.ds(MOST * feats, ROWS), :] = tail.astype(jnp.bfloat16)
    waited = 0
    for c in range(n_slab):
        off = jnp.broadcast_to(offs[c], (feats, span)).astype(jnp.bfloat16)
        for r in range(MOST):
            last = min(MOST * c + r, slots - 1)
            while waited * part <= last:
                copies[2 + waited].wait()
                waited += 1
            block = colors[last]
            for slot in range(r, last):
                block = jnp.where(off == slot - r, colors[slot], block)
            sends[place[c], pl.ds(r * feats, feats), :] = block
    for copy in copies[2 + waited :]:
        copy.wait()


def plan_kernel(n_slab, slots, *refs):
    (counts, blocks, assign, depth), (rows, codes) = refs[:4], refs[4:]
    items = n_slab * MOST
    outs = codes.shape[1] // (2 * items)
    me = lax.axis_index("slab")
    row = lax.broadcasted_iota(jnp.int32, rows.shape[1:], 0)
    item_lane = lax.broadcasted_iota(jnp.int32, codes.shape, 1) // outs
    posv = jnp.zeros(rows.shape[1:], jnp.int32)
    depthv = jnp.zeros(rows.shape[1:], jnp.int32)
    firstv = jnp.zeros(rows.shape[1:], jnp.int32)
    codev = jnp.full(codes.shape, -1, jnp.int32)
    pos = []
    for k, s in enumerate(exchange_order(n_slab)):
        off = jnp.int32(0)
        for c in range(n_slab):
            off = off + jnp.where(c < me, counts[0, s, c], 0)
        count = counts[0, s, me]
        for r in range(MOST):
            i = k * MOST + r
            slot = jnp.minimum(off + r, slots - 1)
            here = assign[0, blocks[0, s, slot]] - me * LB
            here = jnp.where(r < count, here, -1)
            first = jnp.int32(i)
            for j in reversed(range(i)):
                first = jnp.where(pos[j] == here, j, first)
            pos.append(here)
            firstv = jnp.where(row == i, first, firstv)
            posv = jnp.where(row == i, here, posv)
            depthv = jnp.where(row == i, depth[s], depthv)
            codev = jnp.where(item_lane == i, jnp.where(first == i, here, -1), codev)
    rows[0] = posv
    rows[1] = depthv
    rows[2] = firstv
    codes[...] = codev.astype(jnp.float32).astype(jnp.bfloat16)


def place_kernel(w_in, trans_weight, far_out, far_mid, w_first, w_out, w_later, w_mid, sems):
    copy = pltpu.make_async_copy(far_mid, w_mid, sems.at[0])
    copy.start()
    feats, hidden = w_in.shape
    half_in = (w_in[...].astype(jnp.float32) * 0.5).astype(jnp.bfloat16)
    half_trans = trans_weight[...].astype(jnp.float32) * 0.5
    sub = lax.broadcasted_iota(jnp.int32, (16, hidden), 0)
    w_first[...] = jnp.zeros_like(w_first)
    for a in range(GROUP):
        w_first[a, pl.ds(a * feats, feats), :] = half_in
        tail = jnp.where(sub // 2 == a, half_trans, 0.0)
        w_first[a, pl.ds(GROUP * feats, 16), :] = tail.astype(jnp.bfloat16)
    w_out[...] = far_out[...]
    copy.wait()
    for m in range(w_mid.shape[0]):
        w_later[m] = (w_mid[m].astype(jnp.float32).T * 0.5).astype(jnp.bfloat16)


def silu_half(u):
    return (u + u * jnp.tanh(u)).astype(jnp.bfloat16)


def later_layers(h, w_mid, w_out):
    for m in range(w_mid.shape[0]):
        h = silu_half(jnp.dot(h, w_mid[m], preferred_element_type=jnp.float32))
    y = lax.dot_general(
        w_out[...], h, (((1,), (1,)), ((), ())), preferred_element_type=jnp.float32
    )
    return y.astype(jnp.bfloat16).astype(jnp.float32)


def empty_kernel(trans_weight, w_mid, w_out, out):
    u = trans_weight[...].astype(jnp.float32) * 0.5
    h = silu_half(jnp.broadcast_to(u, (out.shape[1], u.shape[1])))
    y = later_layers(h, w_mid, w_out)
    outs = w_out.shape[0]
    for at in range(0, out.shape[0], outs):
        out[pl.ds(at, outs), :] = y


def shade_kernel(rows, codes, got, w_first, w_mid, w_out, out, acc, xt, ys):
    items, feats, span = acc.shape
    outs = w_out.shape[0]

    posv, depthv = rows[0], rows[1]
    front = jnp.ones((items, span), jnp.float32)
    total = jnp.ones((items, span), jnp.float32)
    for k in range(items // MOST):
        tail = got[k, pl.ds(MOST * feats, ROWS), :].astype(jnp.float32)
        for r in range(MOST):
            j = k * MOST + r
            trans_j = tail[r : r + 1, :]
            same = posv == posv[j : j + 1, :]
            total = jnp.where(same, total * trans_j, total)
            front = jnp.where(same & (depthv > depthv[j : j + 1, :]), front * trans_j, front)
    acc[...] = jnp.zeros_like(acc)
    for j in range(items):
        k, r = divmod(j, MOST)
        color = got[k, pl.ds(r * feats, feats), :].astype(jnp.float32)
        at = rows[2, j, 0]
        acc[at] = acc[at] + front[j : j + 1, :] * color
    total_hi = total.astype(jnp.bfloat16).astype(jnp.float32)
    total_lo = total - total_hi
    groups = items // GROUP
    sub = lax.broadcasted_iota(jnp.int32, (16, span), 0)
    xt[...] = jnp.zeros_like(xt)
    for q in range(groups):
        block = acc[pl.ds(q * GROUP, GROUP)].reshape(GROUP * feats, span)
        tail = jnp.zeros((16, span), jnp.float32)
        for a in range(GROUP):
            i = q * GROUP + a
            tail = jnp.where(sub == 2 * a, total_hi[i : i + 1, :], tail)
            tail = jnp.where(sub == 2 * a + 1, total_lo[i : i + 1, :], tail)
        lines = pl.ds(q * span, span)
        xt[lines, pl.ds(0, GROUP * feats)] = block.T.astype(jnp.bfloat16)
        xt[lines, pl.ds(GROUP * feats, 16)] = tail.T.astype(jnp.bfloat16)

    x = xt[...]
    stride = GROUP
    for start in range(0, GROUP, stride):
        h = jnp.concatenate(
            [
                silu_half(jnp.dot(x, w_first[a], preferred_element_type=jnp.float32))
                for a in range(start, start + stride)
            ]
        )
        y = later_layers(h, w_mid, w_out)
        for a in range(start, start + stride):
            for q in range(groups):
                at = ((a - start) * groups + q) * span
                ys[pl.ds((q * GROUP + a) * outs, outs), :] = y[:, at : at + span]
    out[pl.ds(0, items * outs), :] = ys[...].astype(jnp.bfloat16)
    out[pl.ds(items * outs, ROWS), :] = codes[...]


def join_kernel(*refs):
    *got, empty, out, held, sems = refs
    _, n_strip, tile, outs, span = out.shape
    lines = tile * outs
    count = got[0].shape[0] - ROWS
    me = lax.axis_index("strip")
    want = lax.broadcasted_iota(jnp.int32, (lines, count), 0) + me * lines
    chan = lax.broadcasted_iota(jnp.int32, (lines, count), 1) % outs
    filler = jnp.concatenate([empty[...]] * (lines // ROWS))
    ones = jnp.ones((count, span), jnp.bfloat16)
    copies = []
    for k in range(n_strip):
        pos = got[k][pl.ds(count, ROWS), :].astype(jnp.float32)[:1, :count].astype(jnp.int32)
        hit = pos * outs + chan == want
        pick = jnp.where(hit, 1.0, 0.0).astype(jnp.bfloat16)
        blocks = got[k][pl.ds(0, count), :]
        placed = jnp.dot(pick, blocks, preferred_element_type=jnp.float32)
        filled = jnp.dot(pick, ones, preferred_element_type=jnp.float32)
        value = jnp.where(filled > 0.5, placed, filler)
        held[k] = value.reshape(tile, outs, span).astype(jnp.bfloat16)
        copy = pltpu.make_async_copy(
            held.at[k], out.at[0, me ^ ((k + 1) % n_strip)], sems.at[k]
        )
        copy.start()
        copies.append(copy)
    for copy in copies:
        copy.wait()


def compact_device(
    n_slab,
    n_strip,
    colors,
    transmit,
    pair_counts,
    slot_block,
    assign,
    depth_rank,
    w_in,
    trans_weight,
    w_mid,
    w_out,
):
    slots, feats, span = colors.shape[2:]
    items = n_slab * MOST
    outs = w_out.shape[0]
    smem = pl.BlockSpec(memory_space=SMEM)
    vmem = pl.BlockSpec(memory_space=VMEM)
    hbm = pl.BlockSpec(memory_space=pltpu.HBM)
    held = functools.partial(pltpu.with_memory_space_constraint, memory_space=pltpu.HBM)
    small = pltpu.CompilerParams(vmem_limit_bytes=4 * 1024 * 1024)
    message = MOST * feats + ROWS
    sends = pl.pallas_call(
        pack_kernel,
        out_shape=jax.ShapeDtypeStruct((n_slab, message, span), jnp.bfloat16),
        in_specs=[hbm] * 3,
        out_specs=vmem,
        scratch_shapes=[
            pltpu.VMEM(pair_counts.shape, jnp.int32),
            pltpu.VMEM(colors.shape[2:], colors.dtype),
            pltpu.VMEM(transmit.shape, transmit.dtype),
            pltpu.SemaphoreType.DMA((2 + PARTS,)),
        ],
        compiler_params=small,
        name="pack",
    )(held(pair_counts), held(colors), held(transmit))
    group = exchange_order(n_slab)
    got = lax.all_to_all(
        sends, "slab", split_axis=0, concat_axis=0, axis_index_groups=[group], tiled=True
    )
    hidden = w_in.shape[0]
    rough = pl.CostEstimate(flops=10**5, bytes_accessed=10**6, transcendentals=0)
    roomy = pltpu.CompilerParams(vmem_limit_bytes=16 * 1024 * 1024)
    trans_row = trans_weight[None]
    rows, codes = pl.pallas_call(
        functools.partial(plan_kernel, n_slab, slots),
        out_shape=[
            jax.ShapeDtypeStruct((3, items, span), jnp.int32),
            jax.ShapeDtypeStruct((ROWS, span), jnp.bfloat16),
        ],
        in_specs=[smem] * 4,
        out_specs=[vmem] * 2,
        compiler_params=small,
        cost_estimate=rough,
        name="plan",
    )(pair_counts, slot_block, assign, depth_rank)
    w_first, w_last, w_later = pl.pallas_call(
        place_kernel,
        out_shape=[
            jax.ShapeDtypeStruct((GROUP, 2 * GROUP * feats, hidden), jnp.bfloat16),
            jax.ShapeDtypeStruct(w_out.shape, jnp.bfloat16),
            jax.ShapeDtypeStruct(w_mid.shape, jnp.bfloat16),
        ],
        in_specs=[vmem] * 3 + [hbm],
        out_specs=[vmem] * 3,
        scratch_shapes=[
            pltpu.VMEM(w_mid.shape, jnp.bfloat16),
            pltpu.SemaphoreType.DMA((1,)),
        ],
        compiler_params=small,
        cost_estimate=rough,
        name="place",
    )(w_in.T, trans_row, w_out, held(w_mid))
    empty = pl.pallas_call(
        empty_kernel,
        out_shape=jax.ShapeDtypeStruct((ROWS, span), jnp.float32),
        in_specs=[vmem] * 3,
        out_specs=vmem,
        compiler_params=roomy,
        cost_estimate=rough,
        name="empty",
    )(trans_row, w_later, w_last)
    shaded = pl.pallas_call(
        shade_kernel,
        out_shape=jax.ShapeDtypeStruct((items * outs + ROWS, span), jnp.bfloat16),
        in_specs=[vmem] * 6,
        out_specs=vmem,
        scratch_shapes=[
            pltpu.VMEM((items, feats, span), jnp.float32),
            pltpu.VMEM((items // GROUP * span, 2 * GROUP * feats), jnp.bfloat16),
            pltpu.VMEM((items * outs, span), jnp.float32),
        ],
        compiler_params=roomy,
        name="shade",
    )(rows, codes, got, w_first, w_later, w_last)
    tiles = [
        lax.ppermute(shaded, "strip", [(s, s ^ k) for s in range(n_strip)])
        for k in range(1, n_strip)
    ] + [shaded]
    return pl.pallas_call(
        join_kernel,
        out_shape=jax.ShapeDtypeStruct((1, n_strip, LB // n_strip, outs, span), jnp.bfloat16),
        in_specs=[vmem] * (n_strip + 1),
        out_specs=pl.BlockSpec(memory_space=pl.ANY),
        scratch_shapes=[
            pltpu.VMEM((n_strip, LB // n_strip, outs, span), jnp.bfloat16),
            pltpu.SemaphoreType.DMA((n_strip,)),
        ],
        compiler_params=small,
        name="join",
    )(*tiles, empty)


def solution(mesh):
    n_slab, n_strip = mesh.shape["slab"], mesh.shape["strip"]
    placed = (
        P("slab", "strip", None, None, None),
        P("slab", "strip", None, None),
        P("strip", None, None),
        P("strip", None, None),
        P("strip", None),
        P(),
        P(),
        P(),
        P(),
        P(),
    )
    compact = n_strip & (n_strip - 1) == 0 and 4 * MOST * n_slab <= LB
    return jax.shard_map(
        functools.partial(compact_device, n_slab, n_strip) if compact else dense_device,
        mesh=mesh,
        in_specs=placed,
        out_specs=P("slab", None, "strip", None, None),
        check_vma=False,
    )
```

```python
import functools

import jax
import jax.numpy as jnp
from jax import lax
from jax.experimental import pallas as pl
from jax.experimental.pallas import tpu as pltpu
from jax.sharding import PartitionSpec as P

MOST = 2
LB = 128


EXACT_PRECISION = lax.Precision.HIGHEST


def shade_blocks(blend_color, trans_field, w_in, trans_weight, w_mid, w_out):
    summed = jnp.einsum("hf,lfp->lhp", w_in, blend_color, preferred_element_type=jnp.float32)
    summed = summed + trans_weight.astype(jnp.float32)[None, :, None] * trans_field[:, None, :]
    hidden = jax.nn.silu(summed).astype(jnp.bfloat16)
    for layer_index in range(w_mid.shape[0]):
        hidden = jax.nn.silu(
            jnp.einsum(
                "hg,lgp->lhp", w_mid[layer_index], hidden, preferred_element_type=jnp.float32
            )
        ).astype(jnp.bfloat16)
    return jnp.einsum("oh,lhp->lop", w_out, hidden, preferred_element_type=jnp.float32).astype(
        jnp.bfloat16
    )


def dense_device(
    colors, transmit, pair_counts, slot_block, assign, depth_rank, w_in, trans_weight, w_mid, w_out
):
    myself = lax.axis_index("slab")
    counts = pair_counts[0]
    blocks_all = slot_block[0]
    assign_row = assign[0]
    offsets = jnp.cumsum(counts, axis=1) - counts
    slot_rank = jnp.arange(MOST, dtype=jnp.int32)
    my_counts = lax.dynamic_index_in_dim(counts, myself, 0, keepdims=False)
    my_offsets = lax.dynamic_index_in_dim(offsets, myself, 0, keepdims=False)
    send_slots = jnp.where(
        slot_rank[None, :] < my_counts[:, None], my_offsets[:, None] + slot_rank[None, :], 0
    )
    send_color = colors[0, 0][send_slots]
    send_trans = transmit[0, 0][send_slots][:, :, None, :]
    incoming = lax.dynamic_index_in_dim(counts, myself, 1, keepdims=False)
    in_offsets = lax.dynamic_index_in_dim(offsets, myself, 1, keepdims=False)
    live_slot = slot_rank[None, :] < incoming[:, None]
    recv_slots = jnp.where(live_slot, in_offsets[:, None] + slot_rank[None, :], 0)
    recv_blocks = jnp.take_along_axis(blocks_all, recv_slots, axis=1)
    local_pos = assign_row[recv_blocks] - myself * LB
    live_flat = live_slot.reshape(-1)
    local_flat = jnp.where(live_flat, local_pos.reshape(-1), -1)
    depth_flat = jnp.repeat(depth_rank, MOST)
    ahead_table = (
        (local_flat[:, None] == local_flat[None, :])
        & (depth_flat[None, :] < depth_flat[:, None])
        & live_flat[None, :]
    )
    ahead_table = ahead_table.astype(jnp.float32)
    owner_table = (jnp.arange(LB, dtype=jnp.int32)[:, None] == local_flat[None, :]).astype(
        jnp.float32
    )
    got_color = lax.all_to_all(send_color, "slab", split_axis=0, concat_axis=0, tiled=True)
    got_trans = lax.all_to_all(send_trans, "slab", split_axis=0, concat_axis=0, tiled=True)
    pixel_count = got_color.shape[3]
    item_count = got_color.shape[0] * got_color.shape[1]
    log_trans = jnp.log(got_trans.reshape(item_count, pixel_count).astype(jnp.float32))
    log_trans = jnp.where(live_flat[:, None], log_trans, 0.0)
    front_log = jnp.dot(ahead_table, log_trans, precision=EXACT_PRECISION)
    front_share = jnp.where(live_flat[:, None], jnp.exp(front_log), 0.0)
    weighted = front_share[:, None, :] * got_color.reshape(item_count, -1, pixel_count).astype(
        jnp.float32
    )
    blend_sum = jnp.dot(owner_table, weighted.reshape(item_count, -1), precision=EXACT_PRECISION)
    blend_color = blend_sum.reshape(LB, -1, pixel_count).astype(jnp.bfloat16)
    trans_field = jnp.exp(jnp.dot(owner_table, log_trans, precision=EXACT_PRECISION))
    shaded = shade_blocks(blend_color, trans_field, w_in, trans_weight, w_mid, w_out)
    display_tiles = lax.all_to_all(shaded[None], "strip", split_axis=1, concat_axis=0, tiled=True)
    return display_tiles[None]


SMEM = pltpu.SMEM
VMEM = pltpu.VMEM
ROWS = 8
GROUP = 4


def exchange_place(n_slab, c):
    half = n_slab // 2
    flip = 1 if half % 2 == 0 else 0
    return jnp.where(c < half, 2 * c + 1, 2 * ((c - half) ^ flip))


def exchange_order(n_slab):
    half = n_slab // 2
    flip = 1 if half % 2 == 0 else 0
    return [s for i in range(half) for s in (half + (i ^ flip), i)]


def pack_kernel(far_counts, far_colors, far_transmit, sends, counts, colors, transmit, tall, sems):
    n_slab = sends.shape[0]
    slots, feats, span = colors.shape
    me = lax.axis_index("slab")
    copies = [
        pltpu.make_async_copy(far, near, sems.at[i])
        for i, (far, near) in enumerate(
            (
                (far_counts, counts),
                (far_transmit.at[0, 0], transmit),
                (far_colors.at[0, 0], colors),
            )
        )
    ]
    for copy in copies:
        copy.start()
    row = lax.broadcasted_iota(jnp.int32, (ROWS, span), 0)
    copies[1].wait()
    tall[...] = transmit[...].astype(jnp.float32)
    copies[0].wait()
    copies[2].wait()

    def fill(c, off):
        tail = jnp.ones((ROWS, span), jnp.float32)
        at = exchange_place(n_slab, c)
        for r in range(MOST):
            slot = jnp.minimum(off + r, slots - 1)
            sends[at, pl.ds(r * feats, feats), :] = colors[slot]
            tail = jnp.where(row == r, tall[pl.ds(slot, 1), :], tail)
        sends[at, pl.ds(MOST * feats, ROWS), :] = tail.astype(jnp.bfloat16)
        return off + counts[0, me, c]

    lax.fori_loop(0, n_slab, fill, jnp.int32(0))


def plan_kernel(n_slab, slots, *refs):
    (counts, blocks, assign, depth), (rows, codes) = refs[:4], refs[4:]
    items = n_slab * MOST
    outs = codes.shape[1] // (2 * items)
    me = lax.axis_index("slab")
    row = lax.broadcasted_iota(jnp.int32, rows.shape[1:], 0)
    item_lane = lax.broadcasted_iota(jnp.int32, codes.shape, 1) // outs
    posv = jnp.zeros(rows.shape[1:], jnp.int32)
    depthv = jnp.zeros(rows.shape[1:], jnp.int32)
    firstv = jnp.zeros(rows.shape[1:], jnp.int32)
    codev = jnp.full(codes.shape, -1, jnp.int32)
    pos = []
    for k, s in enumerate(exchange_order(n_slab)):
        off = jnp.int32(0)
        for c in range(n_slab):
            off = off + jnp.where(c < me, counts[0, s, c], 0)
        count = counts[0, s, me]
        for r in range(MOST):
            i = k * MOST + r
            slot = jnp.minimum(off + r, slots - 1)
            here = assign[0, blocks[0, s, slot]] - me * LB
            here = jnp.where(r < count, here, -1)
            first = jnp.int32(i)
            for j in reversed(range(i)):
                first = jnp.where(pos[j] == here, j, first)
            pos.append(here)
            firstv = jnp.where(row == i, first, firstv)
            posv = jnp.where(row == i, here, posv)
            depthv = jnp.where(row == i, depth[s], depthv)
            codev = jnp.where(item_lane == i, jnp.where(first == i, here, -1), codev)
    rows[0] = posv
    rows[1] = depthv
    rows[2] = firstv
    codes[...] = codev.astype(jnp.float32).astype(jnp.bfloat16)


def place_kernel(w_in, trans_weight, far_out, far_mid, w_first, w_out, w_later, w_mid, sems):
    copy = pltpu.make_async_copy(far_mid, w_mid, sems.at[0])
    copy.start()
    feats, hidden = w_in.shape
    half_in = (w_in[...].astype(jnp.float32) * 0.5).astype(jnp.bfloat16)
    half_trans = trans_weight[...].astype(jnp.float32) * 0.5
    sub = lax.broadcasted_iota(jnp.int32, (16, hidden), 0)
    w_first[...] = jnp.zeros_like(w_first)
    for a in range(GROUP):
        w_first[a, pl.ds(a * feats, feats), :] = half_in
        tail = jnp.where(sub // 2 == a, half_trans, 0.0)
        w_first[a, pl.ds(GROUP * feats, 16), :] = tail.astype(jnp.bfloat16)
    w_out[...] = far_out[...]
    copy.wait()
    for m in range(w_mid.shape[0]):
        w_later[m] = (w_mid[m].astype(jnp.float32).T * 0.5).astype(jnp.bfloat16)


def silu_half(u):
    return (u + u * jnp.tanh(u)).astype(jnp.bfloat16)


def later_layers(h, w_mid, w_out):
    for m in range(w_mid.shape[0]):
        h = silu_half(jnp.dot(h, w_mid[m], preferred_element_type=jnp.float32))
    y = lax.dot_general(
        w_out[...], h, (((1,), (1,)), ((), ())), preferred_element_type=jnp.float32
    )
    return y.astype(jnp.bfloat16).astype(jnp.float32)


def empty_kernel(trans_weight, w_mid, w_out, out):
    u = trans_weight[...].astype(jnp.float32) * 0.5
    h = silu_half(jnp.broadcast_to(u, (out.shape[1], u.shape[1])))
    y = later_layers(h, w_mid, w_out)
    outs = w_out.shape[0]
    for at in range(0, out.shape[0], outs):
        out[pl.ds(at, outs), :] = y


def shade_kernel(rows, codes, got, w_first, w_mid, w_out, out, acc, xt, ys):
    items, feats, span = acc.shape
    outs = w_out.shape[0]

    posv, depthv = rows[0], rows[1]
    front = jnp.ones((items, span), jnp.float32)
    total = jnp.ones((items, span), jnp.float32)
    for k in range(items // MOST):
        tail = got[k, pl.ds(MOST * feats, ROWS), :].astype(jnp.float32)
        for r in range(MOST):
            j = k * MOST + r
            trans_j = tail[r : r + 1, :]
            same = posv == posv[j : j + 1, :]
            total = jnp.where(same, total * trans_j, total)
            front = jnp.where(same & (depthv > depthv[j : j + 1, :]), front * trans_j, front)
    acc[...] = jnp.zeros_like(acc)
    for j in range(items):
        k, r = divmod(j, MOST)
        color = got[k, pl.ds(r * feats, feats), :].astype(jnp.float32)
        at = rows[2, j, 0]
        acc[at] = acc[at] + front[j : j + 1, :] * color
    total_hi = total.astype(jnp.bfloat16).astype(jnp.float32)
    total_lo = total - total_hi
    groups = items // GROUP
    sub = lax.broadcasted_iota(jnp.int32, (16, span), 0)
    xt[...] = jnp.zeros_like(xt)
    for q in range(groups):
        block = acc[pl.ds(q * GROUP, GROUP)].reshape(GROUP * feats, span)
        tail = jnp.zeros((16, span), jnp.float32)
        for a in range(GROUP):
            i = q * GROUP + a
            tail = jnp.where(sub == 2 * a, total_hi[i : i + 1, :], tail)
            tail = jnp.where(sub == 2 * a + 1, total_lo[i : i + 1, :], tail)
        lines = pl.ds(q * span, span)
        xt[lines, pl.ds(0, GROUP * feats)] = block.T.astype(jnp.bfloat16)
        xt[lines, pl.ds(GROUP * feats, 16)] = tail.T.astype(jnp.bfloat16)

    x = xt[...]
    stride = GROUP
    for start in range(0, GROUP, stride):
        h = jnp.concatenate(
            [
                silu_half(jnp.dot(x, w_first[a], preferred_element_type=jnp.float32))
                for a in range(start, start + stride)
            ]
        )
        y = later_layers(h, w_mid, w_out)
        for a in range(start, start + stride):
            for q in range(groups):
                at = ((a - start) * groups + q) * span
                ys[pl.ds((q * GROUP + a) * outs, outs), :] = y[:, at : at + span]
    out[pl.ds(0, items * outs), :] = ys[...].astype(jnp.bfloat16)
    out[pl.ds(items * outs, ROWS), :] = codes[...]


def join_kernel(*refs):
    *got, empty, out, held, sems = refs
    _, n_strip, tile, outs, span = out.shape
    lines = tile * outs
    count = got[0].shape[0] - ROWS
    me = lax.axis_index("strip")
    want = lax.broadcasted_iota(jnp.int32, (lines, count), 0) + me * lines
    chan = lax.broadcasted_iota(jnp.int32, (lines, count), 1) % outs
    filler = jnp.concatenate([empty[...]] * (lines // ROWS))
    ones = jnp.ones((count, span), jnp.bfloat16)
    copies = []
    for k in range(n_strip):
        pos = got[k][pl.ds(count, ROWS), :].astype(jnp.float32)[:1, :count].astype(jnp.int32)
        hit = pos * outs + chan == want
        pick = jnp.where(hit, 1.0, 0.0).astype(jnp.bfloat16)
        blocks = got[k][pl.ds(0, count), :]
        placed = jnp.dot(pick, blocks, preferred_element_type=jnp.float32)
        filled = jnp.dot(pick, ones, preferred_element_type=jnp.float32)
        value = jnp.where(filled > 0.5, placed, filler)
        held[k] = value.reshape(tile, outs, span).astype(jnp.bfloat16)
        copy = pltpu.make_async_copy(
            held.at[k], out.at[0, me ^ ((k + 1) % n_strip)], sems.at[k]
        )
        copy.start()
        copies.append(copy)
    for copy in copies:
        copy.wait()


def compact_device(
    n_slab,
    n_strip,
    colors,
    transmit,
    pair_counts,
    slot_block,
    assign,
    depth_rank,
    w_in,
    trans_weight,
    w_mid,
    w_out,
):
    slots, feats, span = colors.shape[2:]
    items = n_slab * MOST
    outs = w_out.shape[0]
    smem = pl.BlockSpec(memory_space=SMEM)
    vmem = pl.BlockSpec(memory_space=VMEM)
    hbm = pl.BlockSpec(memory_space=pltpu.HBM)
    held = functools.partial(pltpu.with_memory_space_constraint, memory_space=pltpu.HBM)
    small = pltpu.CompilerParams(vmem_limit_bytes=4 * 1024 * 1024)
    message = MOST * feats + ROWS
    sends = pl.pallas_call(
        pack_kernel,
        out_shape=jax.ShapeDtypeStruct((n_slab, message, span), jnp.bfloat16),
        in_specs=[hbm] * 3,
        out_specs=vmem,
        scratch_shapes=[
            pltpu.SMEM(pair_counts.shape, jnp.int32),
            pltpu.VMEM(colors.shape[2:], colors.dtype),
            pltpu.VMEM(transmit.shape[2:], transmit.dtype),
            pltpu.VMEM(transmit.shape[2:], jnp.float32),
            pltpu.SemaphoreType.DMA((3,)),
        ],
        compiler_params=small,
        name="pack",
    )(held(pair_counts), held(colors), held(transmit))
    group = exchange_order(n_slab)
    got = lax.all_to_all(
        sends, "slab", split_axis=0, concat_axis=0, axis_index_groups=[group], tiled=True
    )
    hidden = w_in.shape[0]
    rough = pl.CostEstimate(flops=10**5, bytes_accessed=10**6, transcendentals=0)
    roomy = pltpu.CompilerParams(vmem_limit_bytes=16 * 1024 * 1024)
    trans_row = trans_weight[None]
    rows, codes = pl.pallas_call(
        functools.partial(plan_kernel, n_slab, slots),
        out_shape=[
            jax.ShapeDtypeStruct((3, items, span), jnp.int32),
            jax.ShapeDtypeStruct((ROWS, span), jnp.bfloat16),
        ],
        in_specs=[smem] * 4,
        out_specs=[vmem] * 2,
        compiler_params=small,
        cost_estimate=rough,
        name="plan",
    )(pair_counts, slot_block, assign, depth_rank)
    w_first, w_last, w_later = pl.pallas_call(
        place_kernel,
        out_shape=[
            jax.ShapeDtypeStruct((GROUP, 2 * GROUP * feats, hidden), jnp.bfloat16),
            jax.ShapeDtypeStruct(w_out.shape, jnp.bfloat16),
            jax.ShapeDtypeStruct(w_mid.shape, jnp.bfloat16),
        ],
        in_specs=[vmem] * 3 + [hbm],
        out_specs=[vmem] * 3,
        scratch_shapes=[
            pltpu.VMEM(w_mid.shape, jnp.bfloat16),
            pltpu.SemaphoreType.DMA((1,)),
        ],
        compiler_params=small,
        cost_estimate=rough,
        name="place",
    )(w_in.T, trans_row, w_out, held(w_mid))
    empty = pl.pallas_call(
        empty_kernel,
        out_shape=jax.ShapeDtypeStruct((ROWS, span), jnp.float32),
        in_specs=[vmem] * 3,
        out_specs=vmem,
        compiler_params=roomy,
        cost_estimate=rough,
        name="empty",
    )(trans_row, w_later, w_last)
    shaded = pl.pallas_call(
        shade_kernel,
        out_shape=jax.ShapeDtypeStruct((items * outs + ROWS, span), jnp.bfloat16),
        in_specs=[vmem] * 6,
        out_specs=vmem,
        scratch_shapes=[
            pltpu.VMEM((items, feats, span), jnp.float32),
            pltpu.VMEM((items // GROUP * span, 2 * GROUP * feats), jnp.bfloat16),
            pltpu.VMEM((items * outs, span), jnp.float32),
        ],
        compiler_params=roomy,
        name="shade",
    )(rows, codes, got, w_first, w_later, w_last)
    tiles = [
        lax.ppermute(shaded, "strip", [(s, s ^ k) for s in range(n_strip)])
        for k in range(1, n_strip)
    ] + [shaded]
    return pl.pallas_call(
        join_kernel,
        out_shape=jax.ShapeDtypeStruct((1, n_strip, LB // n_strip, outs, span), jnp.bfloat16),
        in_specs=[vmem] * (n_strip + 1),
        out_specs=pl.BlockSpec(memory_space=pl.ANY),
        scratch_shapes=[
            pltpu.VMEM((n_strip, LB // n_strip, outs, span), jnp.bfloat16),
            pltpu.SemaphoreType.DMA((n_strip,)),
        ],
        compiler_params=small,
        name="join",
    )(*tiles, empty)


def solution(mesh):
    n_slab, n_strip = mesh.shape["slab"], mesh.shape["strip"]
    placed = (
        P("slab", "strip", None, None, None),
        P("slab", "strip", None, None),
        P("strip", None, None),
        P("strip", None, None),
        P("strip", None),
        P(),
        P(),
        P(),
        P(),
        P(),
    )
    compact = n_strip & (n_strip - 1) == 0 and 4 * MOST * n_slab <= LB
    return jax.shard_map(
        functools.partial(compact_device, n_slab, n_strip) if compact else dense_device,
        mesh=mesh,
        in_specs=placed,
        out_specs=P("slab", None, "strip", None, None),
        check_vma=False,
    )
```

```python
import functools

import jax
import jax.numpy as jnp
from jax import lax
from jax.experimental import pallas as pl
from jax.experimental.pallas import tpu as pltpu
from jax.sharding import PartitionSpec as P

MOST = 2
LB = 128


EXACT_PRECISION = lax.Precision.HIGHEST


def shade_blocks(blend_color, trans_field, w_in, trans_weight, w_mid, w_out):
    summed = jnp.einsum("hf,lfp->lhp", w_in, blend_color, preferred_element_type=jnp.float32)
    summed = summed + trans_weight.astype(jnp.float32)[None, :, None] * trans_field[:, None, :]
    hidden = jax.nn.silu(summed).astype(jnp.bfloat16)
    for layer_index in range(w_mid.shape[0]):
        hidden = jax.nn.silu(
            jnp.einsum(
                "hg,lgp->lhp", w_mid[layer_index], hidden, preferred_element_type=jnp.float32
            )
        ).astype(jnp.bfloat16)
    return jnp.einsum("oh,lhp->lop", w_out, hidden, preferred_element_type=jnp.float32).astype(
        jnp.bfloat16
    )


def dense_device(
    colors, transmit, pair_counts, slot_block, assign, depth_rank, w_in, trans_weight, w_mid, w_out
):
    myself = lax.axis_index("slab")
    counts = pair_counts[0]
    blocks_all = slot_block[0]
    assign_row = assign[0]
    offsets = jnp.cumsum(counts, axis=1) - counts
    slot_rank = jnp.arange(MOST, dtype=jnp.int32)
    my_counts = lax.dynamic_index_in_dim(counts, myself, 0, keepdims=False)
    my_offsets = lax.dynamic_index_in_dim(offsets, myself, 0, keepdims=False)
    send_slots = jnp.where(
        slot_rank[None, :] < my_counts[:, None], my_offsets[:, None] + slot_rank[None, :], 0
    )
    send_color = colors[0, 0][send_slots]
    send_trans = transmit[0, 0][send_slots][:, :, None, :]
    incoming = lax.dynamic_index_in_dim(counts, myself, 1, keepdims=False)
    in_offsets = lax.dynamic_index_in_dim(offsets, myself, 1, keepdims=False)
    live_slot = slot_rank[None, :] < incoming[:, None]
    recv_slots = jnp.where(live_slot, in_offsets[:, None] + slot_rank[None, :], 0)
    recv_blocks = jnp.take_along_axis(blocks_all, recv_slots, axis=1)
    local_pos = assign_row[recv_blocks] - myself * LB
    live_flat = live_slot.reshape(-1)
    local_flat = jnp.where(live_flat, local_pos.reshape(-1), -1)
    depth_flat = jnp.repeat(depth_rank, MOST)
    ahead_table = (
        (local_flat[:, None] == local_flat[None, :])
        & (depth_flat[None, :] < depth_flat[:, None])
        & live_flat[None, :]
    )
    ahead_table = ahead_table.astype(jnp.float32)
    owner_table = (jnp.arange(LB, dtype=jnp.int32)[:, None] == local_flat[None, :]).astype(
        jnp.float32
    )
    got_color = lax.all_to_all(send_color, "slab", split_axis=0, concat_axis=0, tiled=True)
    got_trans = lax.all_to_all(send_trans, "slab", split_axis=0, concat_axis=0, tiled=True)
    pixel_count = got_color.shape[3]
    item_count = got_color.shape[0] * got_color.shape[1]
    log_trans = jnp.log(got_trans.reshape(item_count, pixel_count).astype(jnp.float32))
    log_trans = jnp.where(live_flat[:, None], log_trans, 0.0)
    front_log = jnp.dot(ahead_table, log_trans, precision=EXACT_PRECISION)
    front_share = jnp.where(live_flat[:, None], jnp.exp(front_log), 0.0)
    weighted = front_share[:, None, :] * got_color.reshape(item_count, -1, pixel_count).astype(
        jnp.float32
    )
    blend_sum = jnp.dot(owner_table, weighted.reshape(item_count, -1), precision=EXACT_PRECISION)
    blend_color = blend_sum.reshape(LB, -1, pixel_count).astype(jnp.bfloat16)
    trans_field = jnp.exp(jnp.dot(owner_table, log_trans, precision=EXACT_PRECISION))
    shaded = shade_blocks(blend_color, trans_field, w_in, trans_weight, w_mid, w_out)
    display_tiles = lax.all_to_all(shaded[None], "strip", split_axis=1, concat_axis=0, tiled=True)
    return display_tiles[None]


SMEM = pltpu.SMEM
VMEM = pltpu.VMEM
ROWS = 8
GROUP = 4
PARTS = 4


def exchange_order(n_slab):
    half = n_slab // 2
    flip = 1 if half % 2 == 0 else 0
    return [s for i in range(half) for s in (half + (i ^ flip), i)]


def pack_kernel(far_counts, far_colors, far_transmit, sends, counts, colors, transmit, sems):
    n_slab = sends.shape[0]
    place = [exchange_order(n_slab).index(c) for c in range(n_slab)]
    slots, feats, span = colors.shape
    part = slots // PARTS
    copies = [
        pltpu.make_async_copy(far_counts, counts, sems.at[0]),
        pltpu.make_async_copy(far_transmit, transmit, sems.at[1]),
    ] + [
        pltpu.make_async_copy(
            far_colors.at[0, 0, pl.ds(p * part, part)], colors.at[pl.ds(p * part, part)], sems.at[2 + p]
        )
        for p in range(PARTS)
    ]
    for copy in copies:
        copy.start()
    me = lax.axis_index("slab")
    copies[0].wait()
    mine = counts[0, pl.ds(me, 1), :].astype(jnp.float32)
    before = lax.broadcasted_iota(jnp.int32, mine.shape, 1)
    row = lax.broadcasted_iota(jnp.int32, (ROWS, slots), 0).astype(jnp.float32)
    lane = lax.broadcasted_iota(jnp.int32, (ROWS, slots), 1).astype(jnp.float32)
    offs, picks = [], []
    for c in range(n_slab):
        off = jnp.sum(jnp.where(before < c, mine, 0.0), axis=1, keepdims=True)
        offs.append(off)
        hit = (row < MOST) & (lane - row == off)
        picks.append(jnp.where(hit, 1.0, 0.0))
    pick = jnp.concatenate(picks).astype(jnp.bfloat16)
    copies[1].wait()
    tails = jnp.dot(pick, transmit[0, 0], preferred_element_type=jnp.float32)
    for c in range(n_slab):
        tail = tails[c * ROWS : (c + 1) * ROWS]
        sends[place[c], pl.ds(MOST * feats, ROWS), :] = tail.astype(jnp.bfloat16)
    waited = 0
    for c in range(n_slab):
        off = jnp.broadcast_to(offs[c], (feats, span)).astype(jnp.bfloat16)
        for r in range(MOST):
            last = min(MOST * c + r, slots - 1)
            while waited * part <= last:
                copies[2 + waited].wait()
                waited += 1
            block = colors[last]
            for slot in range(r, last):
                block = jnp.where(off == slot - r, colors[slot], block)
            sends[place[c], pl.ds(r * feats, feats), :] = block
    for copy in copies[2 + waited :]:
        copy.wait()


def plan_kernel(n_slab, slots, *refs):
    (counts, blocks, assign, depth), (rows, codes, strip) = refs[:4], refs[4:]
    strip[...] = jnp.full(strip.shape, lax.axis_index("strip"), jnp.int32)
    items = n_slab * MOST
    outs = codes.shape[1] // (2 * items)
    me = lax.axis_index("slab")
    row = lax.broadcasted_iota(jnp.int32, rows.shape[1:], 0)
    item_lane = lax.broadcasted_iota(jnp.int32, codes.shape, 1) // outs
    posv = jnp.zeros(rows.shape[1:], jnp.int32)
    depthv = jnp.zeros(rows.shape[1:], jnp.int32)
    firstv = jnp.zeros(rows.shape[1:], jnp.int32)
    codev = jnp.full(codes.shape, -1, jnp.int32)
    pos = []
    for k, s in enumerate(exchange_order(n_slab)):
        off = jnp.int32(0)
        for c in range(n_slab):
            off = off + jnp.where(c < me, counts[0, s, c], 0)
        count = counts[0, s, me]
        for r in range(MOST):
            i = k * MOST + r
            slot = jnp.minimum(off + r, slots - 1)
            here = assign[0, blocks[0, s, slot]] - me * LB
            here = jnp.where(r < count, here, -1)
            first = jnp.int32(i)
            for j in reversed(range(i)):
                first = jnp.where(pos[j] == here, j, first)
            pos.append(here)
            firstv = jnp.where(row == i, first, firstv)
            posv = jnp.where(row == i, here, posv)
            depthv = jnp.where(row == i, depth[s], depthv)
            codev = jnp.where(item_lane == i, jnp.where(first == i, here, -1), codev)
    rows[0] = posv
    rows[1] = depthv
    rows[2] = firstv
    codes[...] = codev.astype(jnp.float32).astype(jnp.bfloat16)


def place_kernel(w_in, trans_weight, far_out, far_mid, w_first, w_out, w_later, w_mid, sems):
    copy = pltpu.make_async_copy(far_mid, w_mid, sems.at[0])
    copy.start()
    feats, hidden = w_in.shape
    half_in = (w_in[...].astype(jnp.float32) * 0.5).astype(jnp.bfloat16)
    half_trans = trans_weight[...].astype(jnp.float32) * 0.5
    sub = lax.broadcasted_iota(jnp.int32, (16, hidden), 0)
    w_first[...] = jnp.zeros_like(w_first)
    for a in range(GROUP):
        w_first[a, pl.ds(a * feats, feats), :] = half_in
        tail = jnp.where(sub // 2 == a, half_trans, 0.0)
        w_first[a, pl.ds(GROUP * feats, 16), :] = tail.astype(jnp.bfloat16)
    w_out[...] = far_out[...]
    copy.wait()
    for m in range(w_mid.shape[0]):
        w_later[m] = (w_mid[m].astype(jnp.float32).T * 0.5).astype(jnp.bfloat16)


def silu_half(u):
    return (u + u * jnp.tanh(u)).astype(jnp.bfloat16)


def later_layers(h, w_mid, w_out):
    for m in range(w_mid.shape[0]):
        h = silu_half(jnp.dot(h, w_mid[m], preferred_element_type=jnp.float32))
    y = lax.dot_general(
        w_out[...], h, (((1,), (1,)), ((), ())), preferred_element_type=jnp.float32
    )
    return y.astype(jnp.bfloat16).astype(jnp.float32)


def empty_kernel(trans_weight, w_mid, w_out, out):
    u = trans_weight[...].astype(jnp.float32) * 0.5
    h = silu_half(jnp.broadcast_to(u, (out.shape[1], u.shape[1])))
    y = later_layers(h, w_mid, w_out)
    outs = w_out.shape[0]
    for at in range(0, out.shape[0], outs):
        out[pl.ds(at, outs), :] = y


def shade_kernel(rows, codes, got, w_first, w_mid, w_out, out, acc, xt, ys):
    items, feats, span = acc.shape
    outs = w_out.shape[0]

    posv, depthv = rows[0], rows[1]
    front = jnp.ones((items, span), jnp.float32)
    total = jnp.ones((items, span), jnp.float32)
    for k in range(items // MOST):
        tail = got[k, pl.ds(MOST * feats, ROWS), :].astype(jnp.float32)
        for r in range(MOST):
            j = k * MOST + r
            trans_j = tail[r : r + 1, :]
            same = posv == posv[j : j + 1, :]
            total = jnp.where(same, total * trans_j, total)
            front = jnp.where(same & (depthv > depthv[j : j + 1, :]), front * trans_j, front)
    acc[...] = jnp.zeros_like(acc)
    for j in range(items):
        k, r = divmod(j, MOST)
        color = got[k, pl.ds(r * feats, feats), :].astype(jnp.float32)
        at = rows[2, j, 0]
        acc[at] = acc[at] + front[j : j + 1, :] * color
    total_hi = total.astype(jnp.bfloat16).astype(jnp.float32)
    total_lo = total - total_hi
    groups = items // GROUP
    sub = lax.broadcasted_iota(jnp.int32, (16, span), 0)
    xt[...] = jnp.zeros_like(xt)
    for q in range(groups):
        block = acc[pl.ds(q * GROUP, GROUP)].reshape(GROUP * feats, span)
        tail = jnp.zeros((16, span), jnp.float32)
        for a in range(GROUP):
            i = q * GROUP + a
            tail = jnp.where(sub == 2 * a, total_hi[i : i + 1, :], tail)
            tail = jnp.where(sub == 2 * a + 1, total_lo[i : i + 1, :], tail)
        lines = pl.ds(q * span, span)
        xt[lines, pl.ds(0, GROUP * feats)] = block.T.astype(jnp.bfloat16)
        xt[lines, pl.ds(GROUP * feats, 16)] = tail.T.astype(jnp.bfloat16)

    x = xt[...]
    stride = GROUP
    for start in range(0, GROUP, stride):
        h = jnp.concatenate(
            [
                silu_half(jnp.dot(x, w_first[a], preferred_element_type=jnp.float32))
                for a in range(start, start + stride)
            ]
        )
        y = later_layers(h, w_mid, w_out)
        for a in range(start, start + stride):
            for q in range(groups):
                at = ((a - start) * groups + q) * span
                ys[pl.ds((q * GROUP + a) * outs, outs), :] = y[:, at : at + span]
    out[pl.ds(0, items * outs), :] = ys[...].astype(jnp.bfloat16)
    out[pl.ds(items * outs, ROWS), :] = codes[...]


def join_kernel(*refs):
    *got, empty, strip, out, held, sems = refs
    _, n_strip, tile, outs, span = out.shape
    lines = tile * outs
    count = got[0].shape[0] - ROWS
    me = strip[0, 0]
    want = lax.broadcasted_iota(jnp.int32, (lines, count), 0) + strip[:1, :count] * lines
    chan = lax.broadcasted_iota(jnp.int32, (lines, count), 1) % outs
    filler = jnp.concatenate([empty[...]] * (lines // ROWS))
    ones = jnp.ones((count, span), jnp.bfloat16)
    copies = []
    for k in range(n_strip):
        pos = got[k][pl.ds(count, ROWS), :].astype(jnp.float32)[:1, :count].astype(jnp.int32)
        hit = pos * outs + chan == want
        pick = jnp.where(hit, 1.0, 0.0).astype(jnp.bfloat16)
        blocks = got[k][pl.ds(0, count), :]
        placed = jnp.dot(pick, blocks, preferred_element_type=jnp.float32)
        filled = jnp.dot(pick, ones, preferred_element_type=jnp.float32)
        value = jnp.where(filled > 0.5, placed, filler)
        held[k] = value.reshape(tile, outs, span).astype(jnp.bfloat16)
        copy = pltpu.make_async_copy(
            held.at[k], out.at[0, me ^ ((k + 1) % n_strip)], sems.at[k]
        )
        copy.start()
        copies.append(copy)
    for copy in copies:
        copy.wait()


def compact_device(
    n_slab,
    n_strip,
    colors,
    transmit,
    pair_counts,
    slot_block,
    assign,
    depth_rank,
    w_in,
    trans_weight,
    w_mid,
    w_out,
):
    slots, feats, span = colors.shape[2:]
    items = n_slab * MOST
    outs = w_out.shape[0]
    smem = pl.BlockSpec(memory_space=SMEM)
    vmem = pl.BlockSpec(memory_space=VMEM)
    hbm = pl.BlockSpec(memory_space=pltpu.HBM)
    held = functools.partial(pltpu.with_memory_space_constraint, memory_space=pltpu.HBM)
    small = pltpu.CompilerParams(vmem_limit_bytes=4 * 1024 * 1024)
    message = MOST * feats + ROWS
    sends = pl.pallas_call(
        pack_kernel,
        out_shape=jax.ShapeDtypeStruct((n_slab, message, span), jnp.bfloat16),
        in_specs=[hbm] * 3,
        out_specs=vmem,
        scratch_shapes=[
            pltpu.VMEM(pair_counts.shape, jnp.int32),
            pltpu.VMEM(colors.shape[2:], colors.dtype),
            pltpu.VMEM(transmit.shape, transmit.dtype),
            pltpu.SemaphoreType.DMA((2 + PARTS,)),
        ],
        compiler_params=small,
        name="pack",
    )(held(pair_counts), held(colors), held(transmit))
    group = exchange_order(n_slab)
    got = lax.all_to_all(
        sends, "slab", split_axis=0, concat_axis=0, axis_index_groups=[group], tiled=True
    )
    hidden = w_in.shape[0]
    rough = pl.CostEstimate(flops=10**5, bytes_accessed=10**6, transcendentals=0)
    roomy = pltpu.CompilerParams(vmem_limit_bytes=16 * 1024 * 1024)
    trans_row = trans_weight[None]
    rows, codes, strip = pl.pallas_call(
        functools.partial(plan_kernel, n_slab, slots),
        out_shape=[
            jax.ShapeDtypeStruct((3, items, span), jnp.int32),
            jax.ShapeDtypeStruct((ROWS, span), jnp.bfloat16),
            jax.ShapeDtypeStruct((ROWS, span), jnp.int32),
        ],
        in_specs=[smem] * 4,
        out_specs=[vmem] * 3,
        compiler_params=small,
        cost_estimate=rough,
        name="plan",
    )(pair_counts, slot_block, assign, depth_rank)
    w_first, w_last, w_later = pl.pallas_call(
        place_kernel,
        out_shape=[
            jax.ShapeDtypeStruct((GROUP, 2 * GROUP * feats, hidden), jnp.bfloat16),
            jax.ShapeDtypeStruct(w_out.shape, jnp.bfloat16),
            jax.ShapeDtypeStruct(w_mid.shape, jnp.bfloat16),
        ],
        in_specs=[vmem] * 3 + [hbm],
        out_specs=[vmem] * 3,
        scratch_shapes=[
            pltpu.VMEM(w_mid.shape, jnp.bfloat16),
            pltpu.SemaphoreType.DMA((1,)),
        ],
        compiler_params=small,
        cost_estimate=rough,
        name="place",
    )(w_in.T, trans_row, w_out, held(w_mid))
    empty = pl.pallas_call(
        empty_kernel,
        out_shape=jax.ShapeDtypeStruct((ROWS, span), jnp.float32),
        in_specs=[vmem] * 3,
        out_specs=vmem,
        compiler_params=roomy,
        cost_estimate=rough,
        name="empty",
    )(trans_row, w_later, w_last)
    shaded = pl.pallas_call(
        shade_kernel,
        out_shape=jax.ShapeDtypeStruct((items * outs + ROWS, span), jnp.bfloat16),
        in_specs=[vmem] * 6,
        out_specs=vmem,
        scratch_shapes=[
            pltpu.VMEM((items, feats, span), jnp.float32),
            pltpu.VMEM((items // GROUP * span, 2 * GROUP * feats), jnp.bfloat16),
            pltpu.VMEM((items * outs, span), jnp.float32),
        ],
        compiler_params=roomy,
        name="shade",
    )(rows, codes, got, w_first, w_later, w_last)
    tiles = [
        lax.ppermute(shaded, "strip", [(s, s ^ k) for s in range(n_strip)])
        for k in range(1, n_strip)
    ] + [shaded]
    return pl.pallas_call(
        join_kernel,
        out_shape=jax.ShapeDtypeStruct((1, n_strip, LB // n_strip, outs, span), jnp.bfloat16),
        in_specs=[vmem] * (n_strip + 2),
        out_specs=pl.BlockSpec(memory_space=pl.ANY),
        scratch_shapes=[
            pltpu.VMEM((n_strip, LB // n_strip, outs, span), jnp.bfloat16),
            pltpu.SemaphoreType.DMA((n_strip,)),
        ],
        compiler_params=small,
        name="join",
    )(*tiles, empty, strip)


def solution(mesh):
    n_slab, n_strip = mesh.shape["slab"], mesh.shape["strip"]
    placed = (
        P("slab", "strip", None, None, None),
        P("slab", "strip", None, None),
        P("strip", None, None),
        P("strip", None, None),
        P("strip", None),
        P(),
        P(),
        P(),
        P(),
        P(),
    )
    compact = n_strip & (n_strip - 1) == 0 and 4 * MOST * n_slab <= LB
    return jax.shard_map(
        functools.partial(compact_device, n_slab, n_strip) if compact else dense_device,
        mesh=mesh,
        in_specs=placed,
        out_specs=P("slab", None, "strip", None, None),
        check_vma=False,
    )
```

```python
import functools

import jax
import jax.numpy as jnp
from jax import lax
from jax.experimental import pallas as pl
from jax.experimental.pallas import tpu as pltpu
from jax.sharding import PartitionSpec as P

MOST = 2
LB = 128


EXACT_PRECISION = lax.Precision.HIGHEST


def shade_blocks(blend_color, trans_field, w_in, trans_weight, w_mid, w_out):
    summed = jnp.einsum("hf,lfp->lhp", w_in, blend_color, preferred_element_type=jnp.float32)
    summed = summed + trans_weight.astype(jnp.float32)[None, :, None] * trans_field[:, None, :]
    hidden = jax.nn.silu(summed).astype(jnp.bfloat16)
    for layer_index in range(w_mid.shape[0]):
        hidden = jax.nn.silu(
            jnp.einsum(
                "hg,lgp->lhp", w_mid[layer_index], hidden, preferred_element_type=jnp.float32
            )
        ).astype(jnp.bfloat16)
    return jnp.einsum("oh,lhp->lop", w_out, hidden, preferred_element_type=jnp.float32).astype(
        jnp.bfloat16
    )


def dense_device(
    colors, transmit, pair_counts, slot_block, assign, depth_rank, w_in, trans_weight, w_mid, w_out
):
    myself = lax.axis_index("slab")
    counts = pair_counts[0]
    blocks_all = slot_block[0]
    assign_row = assign[0]
    offsets = jnp.cumsum(counts, axis=1) - counts
    slot_rank = jnp.arange(MOST, dtype=jnp.int32)
    my_counts = lax.dynamic_index_in_dim(counts, myself, 0, keepdims=False)
    my_offsets = lax.dynamic_index_in_dim(offsets, myself, 0, keepdims=False)
    send_slots = jnp.where(
        slot_rank[None, :] < my_counts[:, None], my_offsets[:, None] + slot_rank[None, :], 0
    )
    send_color = colors[0, 0][send_slots]
    send_trans = transmit[0, 0][send_slots][:, :, None, :]
    incoming = lax.dynamic_index_in_dim(counts, myself, 1, keepdims=False)
    in_offsets = lax.dynamic_index_in_dim(offsets, myself, 1, keepdims=False)
    live_slot = slot_rank[None, :] < incoming[:, None]
    recv_slots = jnp.where(live_slot, in_offsets[:, None] + slot_rank[None, :], 0)
    recv_blocks = jnp.take_along_axis(blocks_all, recv_slots, axis=1)
    local_pos = assign_row[recv_blocks] - myself * LB
    live_flat = live_slot.reshape(-1)
    local_flat = jnp.where(live_flat, local_pos.reshape(-1), -1)
    depth_flat = jnp.repeat(depth_rank, MOST)
    ahead_table = (
        (local_flat[:, None] == local_flat[None, :])
        & (depth_flat[None, :] < depth_flat[:, None])
        & live_flat[None, :]
    )
    ahead_table = ahead_table.astype(jnp.float32)
    owner_table = (jnp.arange(LB, dtype=jnp.int32)[:, None] == local_flat[None, :]).astype(
        jnp.float32
    )
    got_color = lax.all_to_all(send_color, "slab", split_axis=0, concat_axis=0, tiled=True)
    got_trans = lax.all_to_all(send_trans, "slab", split_axis=0, concat_axis=0, tiled=True)
    pixel_count = got_color.shape[3]
    item_count = got_color.shape[0] * got_color.shape[1]
    log_trans = jnp.log(got_trans.reshape(item_count, pixel_count).astype(jnp.float32))
    log_trans = jnp.where(live_flat[:, None], log_trans, 0.0)
    front_log = jnp.dot(ahead_table, log_trans, precision=EXACT_PRECISION)
    front_share = jnp.where(live_flat[:, None], jnp.exp(front_log), 0.0)
    weighted = front_share[:, None, :] * got_color.reshape(item_count, -1, pixel_count).astype(
        jnp.float32
    )
    blend_sum = jnp.dot(owner_table, weighted.reshape(item_count, -1), precision=EXACT_PRECISION)
    blend_color = blend_sum.reshape(LB, -1, pixel_count).astype(jnp.bfloat16)
    trans_field = jnp.exp(jnp.dot(owner_table, log_trans, precision=EXACT_PRECISION))
    shaded = shade_blocks(blend_color, trans_field, w_in, trans_weight, w_mid, w_out)
    display_tiles = lax.all_to_all(shaded[None], "strip", split_axis=1, concat_axis=0, tiled=True)
    return display_tiles[None]


SMEM = pltpu.SMEM
VMEM = pltpu.VMEM
ROWS = 8
GROUP = 4
PARTS = 4


def exchange_order(n_slab):
    half = n_slab // 2
    flip = 1 if half % 2 == 0 else 0
    return [s for i in range(half) for s in (half + (i ^ flip), half - 1 - i)]


def pack_kernel(far_counts, far_colors, far_transmit, sends, counts, colors, transmit, sems):
    n_slab = sends.shape[0]
    place = [exchange_order(n_slab).index(c) for c in range(n_slab)]
    slots, feats, span = colors.shape
    part = slots // PARTS
    copies = [
        pltpu.make_async_copy(far_counts, counts, sems.at[0]),
        pltpu.make_async_copy(far_transmit, transmit, sems.at[1]),
    ] + [
        pltpu.make_async_copy(
            far_colors.at[0, 0, pl.ds(p * part, part)], colors.at[pl.ds(p * part, part)], sems.at[2 + p]
        )
        for p in range(PARTS)
    ]
    for copy in copies:
        copy.start()
    me = lax.axis_index("slab")
    copies[0].wait()
    mine = counts[0, pl.ds(me, 1), :].astype(jnp.float32)
    before = lax.broadcasted_iota(jnp.int32, mine.shape, 1)
    row = lax.broadcasted_iota(jnp.int32, (ROWS, slots), 0).astype(jnp.float32)
    lane = lax.broadcasted_iota(jnp.int32, (ROWS, slots), 1).astype(jnp.float32)
    offs, picks = [], []
    for c in range(n_slab):
        off = jnp.sum(jnp.where(before < c, mine, 0.0), axis=1, keepdims=True)
        offs.append(off)
        hit = (row < MOST) & (lane - row == off)
        picks.append(jnp.where(hit, 1.0, 0.0))
    pick = jnp.concatenate(picks).astype(jnp.bfloat16)
    copies[1].wait()
    tails = jnp.dot(pick, transmit[0, 0], preferred_element_type=jnp.float32)
    for c in range(n_slab):
        tail = tails[c * ROWS : (c + 1) * ROWS]
        sends[place[c], pl.ds(MOST * feats, ROWS), :] = tail.astype(jnp.bfloat16)
    waited = 0
    for c in range(n_slab):
        off = jnp.broadcast_to(offs[c], (feats, span)).astype(jnp.bfloat16)
        for r in range(MOST):
            last = min(MOST * c + r, slots - 1)
            while waited * part <= last:
                copies[2 + waited].wait()
                waited += 1
            block = colors[last]
            for slot in range(r, last):
                block = jnp.where(off == slot - r, colors[slot], block)
            sends[place[c], pl.ds(r * feats, feats), :] = block
    for copy in copies[2 + waited :]:
        copy.wait()


def plan_kernel(n_slab, slots, *refs):
    (counts, blocks, assign, depth), (rows, codes, strip) = refs[:4], refs[4:]
    strip[...] = jnp.full(strip.shape, lax.axis_index("strip"), jnp.int32)
    items = n_slab * MOST
    outs = codes.shape[1] // (2 * items)
    me = lax.axis_index("slab")
    row = lax.broadcasted_iota(jnp.int32, rows.shape[1:], 0)
    item_lane = lax.broadcasted_iota(jnp.int32, codes.shape, 1) // outs
    posv = jnp.zeros(rows.shape[1:], jnp.int32)
    depthv = jnp.zeros(rows.shape[1:], jnp.int32)
    firstv = jnp.zeros(rows.shape[1:], jnp.int32)
    codev = jnp.full(codes.shape, -1, jnp.int32)
    pos = []
    for k, s in enumerate(exchange_order(n_slab)):
        off = jnp.int32(0)
        for c in range(n_slab):
            off = off + jnp.where(c < me, counts[0, s, c], 0)
        count = counts[0, s, me]
        for r in range(MOST):
            i = k * MOST + r
            slot = jnp.minimum(off + r, slots - 1)
            here = assign[0, blocks[0, s, slot]] - me * LB
            here = jnp.where(r < count, here, -1)
            first = jnp.int32(i)
            for j in reversed(range(i)):
                first = jnp.where(pos[j] == here, j, first)
            pos.append(here)
            firstv = jnp.where(row == i, first, firstv)
            posv = jnp.where(row == i, here, posv)
            depthv = jnp.where(row == i, depth[s], depthv)
            codev = jnp.where(item_lane == i, jnp.where(first == i, here, -1), codev)
    rows[0] = posv
    rows[1] = depthv
    rows[2] = firstv
    codes[...] = codev.astype(jnp.float32).astype(jnp.bfloat16)


def place_kernel(w_in, trans_weight, far_out, far_mid, w_first, w_out, w_later, w_mid, sems):
    copy = pltpu.make_async_copy(far_mid, w_mid, sems.at[0])
    copy.start()
    feats, hidden = w_in.shape
    half_in = (w_in[...].astype(jnp.float32) * 0.5).astype(jnp.bfloat16)
    half_trans = trans_weight[...].astype(jnp.float32) * 0.5
    sub = lax.broadcasted_iota(jnp.int32, (16, hidden), 0)
    w_first[...] = jnp.zeros_like(w_first)
    for a in range(GROUP):
        w_first[a, pl.ds(a * feats, feats), :] = half_in
        tail = jnp.where(sub // 2 == a, half_trans, 0.0)
        w_first[a, pl.ds(GROUP * feats, 16), :] = tail.astype(jnp.bfloat16)
    w_out[...] = far_out[...]
    copy.wait()
    for m in range(w_mid.shape[0]):
        w_later[m] = (w_mid[m].astype(jnp.float32).T * 0.5).astype(jnp.bfloat16)


def silu_half(u):
    return (u + u * jnp.tanh(u)).astype(jnp.bfloat16)


def later_layers(h, w_mid, w_out):
    for m in range(w_mid.shape[0]):
        h = silu_half(jnp.dot(h, w_mid[m], preferred_element_type=jnp.float32))
    y = lax.dot_general(
        w_out[...], h, (((1,), (1,)), ((), ())), preferred_element_type=jnp.float32
    )
    return y.astype(jnp.bfloat16).astype(jnp.float32)


def empty_kernel(trans_weight, w_mid, w_out, out):
    u = trans_weight[...].astype(jnp.float32) * 0.5
    h = silu_half(jnp.broadcast_to(u, (out.shape[1], u.shape[1])))
    y = later_layers(h, w_mid, w_out)
    outs = w_out.shape[0]
    for at in range(0, out.shape[0], outs):
        out[pl.ds(at, outs), :] = y


def shade_kernel(rows, codes, got, w_first, w_mid, w_out, out, acc, xt, ys):
    items, feats, span = acc.shape
    outs = w_out.shape[0]

    posv, depthv = rows[0], rows[1]
    front = jnp.ones((items, span), jnp.float32)
    total = jnp.ones((items, span), jnp.float32)
    for k in range(items // MOST):
        tail = got[k, pl.ds(MOST * feats, ROWS), :].astype(jnp.float32)
        for r in range(MOST):
            j = k * MOST + r
            trans_j = tail[r : r + 1, :]
            same = posv == posv[j : j + 1, :]
            total = jnp.where(same, total * trans_j, total)
            front = jnp.where(same & (depthv > depthv[j : j + 1, :]), front * trans_j, front)
    acc[...] = jnp.zeros_like(acc)
    for j in range(items):
        k, r = divmod(j, MOST)
        color = got[k, pl.ds(r * feats, feats), :].astype(jnp.float32)
        at = rows[2, j, 0]
        acc[at] = acc[at] + front[j : j + 1, :] * color
    total_hi = total.astype(jnp.bfloat16).astype(jnp.float32)
    total_lo = total - total_hi
    groups = items // GROUP
    sub = lax.broadcasted_iota(jnp.int32, (16, span), 0)
    xt[...] = jnp.zeros_like(xt)
    for q in range(groups):
        block = acc[pl.ds(q * GROUP, GROUP)].reshape(GROUP * feats, span)
        tail = jnp.zeros((16, span), jnp.float32)
        for a in range(GROUP):
            i = q * GROUP + a
            tail = jnp.where(sub == 2 * a, total_hi[i : i + 1, :], tail)
            tail = jnp.where(sub == 2 * a + 1, total_lo[i : i + 1, :], tail)
        lines = pl.ds(q * span, span)
        xt[lines, pl.ds(0, GROUP * feats)] = block.T.astype(jnp.bfloat16)
        xt[lines, pl.ds(GROUP * feats, 16)] = tail.T.astype(jnp.bfloat16)

    x = xt[...]
    stride = GROUP
    for start in range(0, GROUP, stride):
        h = jnp.concatenate(
            [
                silu_half(jnp.dot(x, w_first[a], preferred_element_type=jnp.float32))
                for a in range(start, start + stride)
            ]
        )
        y = later_layers(h, w_mid, w_out)
        for a in range(start, start + stride):
            for q in range(groups):
                at = ((a - start) * groups + q) * span
                ys[pl.ds((q * GROUP + a) * outs, outs), :] = y[:, at : at + span]
    out[pl.ds(0, items * outs), :] = ys[...].astype(jnp.bfloat16)
    out[pl.ds(items * outs, ROWS), :] = codes[...]


def join_kernel(*refs):
    *got, empty, strip, out, held, sems = refs
    _, n_strip, tile, outs, span = out.shape
    lines = tile * outs
    count = got[0].shape[0] - ROWS
    me = strip[0, 0]
    want = lax.broadcasted_iota(jnp.int32, (lines, count), 0) + strip[:1, :count] * lines
    chan = lax.broadcasted_iota(jnp.int32, (lines, count), 1) % outs
    filler = jnp.concatenate([empty[...]] * (lines // ROWS))
    ones = jnp.ones((count, span), jnp.bfloat16)
    copies = []
    for k in range(n_strip):
        pos = got[k][pl.ds(count, ROWS), :].astype(jnp.float32)[:1, :count].astype(jnp.int32)
        hit = pos * outs + chan == want
        pick = jnp.where(hit, 1.0, 0.0).astype(jnp.bfloat16)
        blocks = got[k][pl.ds(0, count), :]
        placed = jnp.dot(pick, blocks, preferred_element_type=jnp.float32)
        filled = jnp.dot(pick, ones, preferred_element_type=jnp.float32)
        value = jnp.where(filled > 0.5, placed, filler)
        held[k] = value.reshape(tile, outs, span).astype(jnp.bfloat16)
        copy = pltpu.make_async_copy(
            held.at[k], out.at[0, me ^ ((k + 1) % n_strip)], sems.at[k]
        )
        copy.start()
        copies.append(copy)
    for copy in copies:
        copy.wait()


def compact_device(
    n_slab,
    n_strip,
    colors,
    transmit,
    pair_counts,
    slot_block,
    assign,
    depth_rank,
    w_in,
    trans_weight,
    w_mid,
    w_out,
):
    slots, feats, span = colors.shape[2:]
    items = n_slab * MOST
    outs = w_out.shape[0]
    smem = pl.BlockSpec(memory_space=SMEM)
    vmem = pl.BlockSpec(memory_space=VMEM)
    hbm = pl.BlockSpec(memory_space=pltpu.HBM)
    held = functools.partial(pltpu.with_memory_space_constraint, memory_space=pltpu.HBM)
    small = pltpu.CompilerParams(vmem_limit_bytes=4 * 1024 * 1024)
    message = MOST * feats + ROWS
    sends = pl.pallas_call(
        pack_kernel,
        out_shape=jax.ShapeDtypeStruct((n_slab, message, span), jnp.bfloat16),
        in_specs=[hbm] * 3,
        out_specs=vmem,
        scratch_shapes=[
            pltpu.VMEM(pair_counts.shape, jnp.int32),
            pltpu.VMEM(colors.shape[2:], colors.dtype),
            pltpu.VMEM(transmit.shape, transmit.dtype),
            pltpu.SemaphoreType.DMA((2 + PARTS,)),
        ],
        compiler_params=small,
        name="pack",
    )(held(pair_counts), held(colors), held(transmit))
    group = exchange_order(n_slab)
    got = lax.all_to_all(
        sends, "slab", split_axis=0, concat_axis=0, axis_index_groups=[group], tiled=True
    )
    hidden = w_in.shape[0]
    rough = pl.CostEstimate(flops=10**5, bytes_accessed=10**6, transcendentals=0)
    roomy = pltpu.CompilerParams(vmem_limit_bytes=16 * 1024 * 1024)
    trans_row = trans_weight[None]
    rows, codes, strip = pl.pallas_call(
        functools.partial(plan_kernel, n_slab, slots),
        out_shape=[
            jax.ShapeDtypeStruct((3, items, span), jnp.int32),
            jax.ShapeDtypeStruct((ROWS, span), jnp.bfloat16),
            jax.ShapeDtypeStruct((ROWS, span), jnp.int32),
        ],
        in_specs=[smem] * 4,
        out_specs=[vmem] * 3,
        compiler_params=small,
        cost_estimate=rough,
        name="plan",
    )(pair_counts, slot_block, assign, depth_rank)
    w_first, w_last, w_later = pl.pallas_call(
        place_kernel,
        out_shape=[
            jax.ShapeDtypeStruct((GROUP, 2 * GROUP * feats, hidden), jnp.bfloat16),
            jax.ShapeDtypeStruct(w_out.shape, jnp.bfloat16),
            jax.ShapeDtypeStruct(w_mid.shape, jnp.bfloat16),
        ],
        in_specs=[vmem] * 3 + [hbm],
        out_specs=[vmem] * 3,
        scratch_shapes=[
            pltpu.VMEM(w_mid.shape, jnp.bfloat16),
            pltpu.SemaphoreType.DMA((1,)),
        ],
        compiler_params=small,
        cost_estimate=rough,
        name="place",
    )(w_in.T, trans_row, w_out, held(w_mid))
    empty = pl.pallas_call(
        empty_kernel,
        out_shape=jax.ShapeDtypeStruct((ROWS, span), jnp.float32),
        in_specs=[vmem] * 3,
        out_specs=vmem,
        compiler_params=roomy,
        cost_estimate=rough,
        name="empty",
    )(trans_row, w_later, w_last)
    shaded = pl.pallas_call(
        shade_kernel,
        out_shape=jax.ShapeDtypeStruct((items * outs + ROWS, span), jnp.bfloat16),
        in_specs=[vmem] * 6,
        out_specs=vmem,
        scratch_shapes=[
            pltpu.VMEM((items, feats, span), jnp.float32),
            pltpu.VMEM((items // GROUP * span, 2 * GROUP * feats), jnp.bfloat16),
            pltpu.VMEM((items * outs, span), jnp.float32),
        ],
        compiler_params=roomy,
        name="shade",
    )(rows, codes, got, w_first, w_later, w_last)
    tiles = [
        lax.ppermute(shaded, "strip", [(s, s ^ k) for s in range(n_strip)])
        for k in range(1, n_strip)
    ] + [shaded]
    return pl.pallas_call(
        join_kernel,
        out_shape=jax.ShapeDtypeStruct((1, n_strip, LB // n_strip, outs, span), jnp.bfloat16),
        in_specs=[vmem] * (n_strip + 2),
        out_specs=pl.BlockSpec(memory_space=pl.ANY),
        scratch_shapes=[
            pltpu.VMEM((n_strip, LB // n_strip, outs, span), jnp.bfloat16),
            pltpu.SemaphoreType.DMA((n_strip,)),
        ],
        compiler_params=small,
        name="join",
    )(*tiles, empty, strip)


def solution(mesh):
    n_slab, n_strip = mesh.shape["slab"], mesh.shape["strip"]
    placed = (
        P("slab", "strip", None, None, None),
        P("slab", "strip", None, None),
        P("strip", None, None),
        P("strip", None, None),
        P("strip", None),
        P(),
        P(),
        P(),
        P(),
        P(),
    )
    compact = n_strip & (n_strip - 1) == 0 and 4 * MOST * n_slab <= LB
    return jax.shard_map(
        functools.partial(compact_device, n_slab, n_strip) if compact else dense_device,
        mesh=mesh,
        in_specs=placed,
        out_specs=P("slab", None, "strip", None, None),
        check_vma=False,
    )
```

```python
import functools

import jax
import jax.numpy as jnp
from jax import lax
from jax.experimental import pallas as pl
from jax.experimental.pallas import tpu as pltpu
from jax.sharding import PartitionSpec as P

MOST = 2
LB = 128


EXACT_PRECISION = lax.Precision.HIGHEST


def shade_blocks(blend_color, trans_field, w_in, trans_weight, w_mid, w_out):
    summed = jnp.einsum("hf,lfp->lhp", w_in, blend_color, preferred_element_type=jnp.float32)
    summed = summed + trans_weight.astype(jnp.float32)[None, :, None] * trans_field[:, None, :]
    hidden = jax.nn.silu(summed).astype(jnp.bfloat16)
    for layer_index in range(w_mid.shape[0]):
        hidden = jax.nn.silu(
            jnp.einsum(
                "hg,lgp->lhp", w_mid[layer_index], hidden, preferred_element_type=jnp.float32
            )
        ).astype(jnp.bfloat16)
    return jnp.einsum("oh,lhp->lop", w_out, hidden, preferred_element_type=jnp.float32).astype(
        jnp.bfloat16
    )


def dense_device(
    colors, transmit, pair_counts, slot_block, assign, depth_rank, w_in, trans_weight, w_mid, w_out
):
    myself = lax.axis_index("slab")
    counts = pair_counts[0]
    blocks_all = slot_block[0]
    assign_row = assign[0]
    offsets = jnp.cumsum(counts, axis=1) - counts
    slot_rank = jnp.arange(MOST, dtype=jnp.int32)
    my_counts = lax.dynamic_index_in_dim(counts, myself, 0, keepdims=False)
    my_offsets = lax.dynamic_index_in_dim(offsets, myself, 0, keepdims=False)
    send_slots = jnp.where(
        slot_rank[None, :] < my_counts[:, None], my_offsets[:, None] + slot_rank[None, :], 0
    )
    send_color = colors[0, 0][send_slots]
    send_trans = transmit[0, 0][send_slots][:, :, None, :]
    incoming = lax.dynamic_index_in_dim(counts, myself, 1, keepdims=False)
    in_offsets = lax.dynamic_index_in_dim(offsets, myself, 1, keepdims=False)
    live_slot = slot_rank[None, :] < incoming[:, None]
    recv_slots = jnp.where(live_slot, in_offsets[:, None] + slot_rank[None, :], 0)
    recv_blocks = jnp.take_along_axis(blocks_all, recv_slots, axis=1)
    local_pos = assign_row[recv_blocks] - myself * LB
    live_flat = live_slot.reshape(-1)
    local_flat = jnp.where(live_flat, local_pos.reshape(-1), -1)
    depth_flat = jnp.repeat(depth_rank, MOST)
    ahead_table = (
        (local_flat[:, None] == local_flat[None, :])
        & (depth_flat[None, :] < depth_flat[:, None])
        & live_flat[None, :]
    )
    ahead_table = ahead_table.astype(jnp.float32)
    owner_table = (jnp.arange(LB, dtype=jnp.int32)[:, None] == local_flat[None, :]).astype(
        jnp.float32
    )
    got_color = lax.all_to_all(send_color, "slab", split_axis=0, concat_axis=0, tiled=True)
    got_trans = lax.all_to_all(send_trans, "slab", split_axis=0, concat_axis=0, tiled=True)
    pixel_count = got_color.shape[3]
    item_count = got_color.shape[0] * got_color.shape[1]
    log_trans = jnp.log(got_trans.reshape(item_count, pixel_count).astype(jnp.float32))
    log_trans = jnp.where(live_flat[:, None], log_trans, 0.0)
    front_log = jnp.dot(ahead_table, log_trans, precision=EXACT_PRECISION)
    front_share = jnp.where(live_flat[:, None], jnp.exp(front_log), 0.0)
    weighted = front_share[:, None, :] * got_color.reshape(item_count, -1, pixel_count).astype(
        jnp.float32
    )
    blend_sum = jnp.dot(owner_table, weighted.reshape(item_count, -1), precision=EXACT_PRECISION)
    blend_color = blend_sum.reshape(LB, -1, pixel_count).astype(jnp.bfloat16)
    trans_field = jnp.exp(jnp.dot(owner_table, log_trans, precision=EXACT_PRECISION))
    shaded = shade_blocks(blend_color, trans_field, w_in, trans_weight, w_mid, w_out)
    display_tiles = lax.all_to_all(shaded[None], "strip", split_axis=1, concat_axis=0, tiled=True)
    return display_tiles[None]


SMEM = pltpu.SMEM
VMEM = pltpu.VMEM
ROWS = 8
GROUP = 4
PARTS = 4


def exchange_order(n_slab):
    half = n_slab // 2
    return [s for i in range(half) for s in (half + (i + 1) % half, i)]


def pack_kernel(far_counts, far_colors, far_transmit, sends, counts, colors, transmit, sems):
    n_slab = sends.shape[0]
    place = [exchange_order(n_slab).index(c) for c in range(n_slab)]
    slots, feats, span = colors.shape
    part = slots // PARTS
    copies = [
        pltpu.make_async_copy(far_counts, counts, sems.at[0]),
        pltpu.make_async_copy(far_transmit, transmit, sems.at[1]),
    ] + [
        pltpu.make_async_copy(
            far_colors.at[0, 0, pl.ds(p * part, part)], colors.at[pl.ds(p * part, part)], sems.at[2 + p]
        )
        for p in range(PARTS)
    ]
    for copy in copies:
        copy.start()
    me = lax.axis_index("slab")
    copies[0].wait()
    mine = counts[0, pl.ds(me, 1), :].astype(jnp.float32)
    before = lax.broadcasted_iota(jnp.int32, mine.shape, 1)
    row = lax.broadcasted_iota(jnp.int32, (ROWS, slots), 0).astype(jnp.float32)
    lane = lax.broadcasted_iota(jnp.int32, (ROWS, slots), 1).astype(jnp.float32)
    offs, picks = [], []
    for c in range(n_slab):
        off = jnp.sum(jnp.where(before < c, mine, 0.0), axis=1, keepdims=True)
        offs.append(off)
        hit = (row < MOST) & (lane - row == off)
        picks.append(jnp.where(hit, 1.0, 0.0))
    pick = jnp.concatenate(picks).astype(jnp.bfloat16)
    copies[1].wait()
    tails = jnp.dot(pick, transmit[0, 0], preferred_element_type=jnp.float32)
    for c in range(n_slab):
        tail = tails[c * ROWS : (c + 1) * ROWS]
        sends[place[c], pl.ds(MOST * feats, ROWS), :] = tail.astype(jnp.bfloat16)
    waited = 0
    for c in range(n_slab):
        off = jnp.broadcast_to(offs[c], (feats, span)).astype(jnp.bfloat16)
        for r in range(MOST):
            last = min(MOST * c + r, slots - 1)
            while waited * part <= last:
                copies[2 + waited].wait()
                waited += 1
            block = colors[last]
            for slot in range(r, last):
                block = jnp.where(off == slot - r, colors[slot], block)
            sends[place[c], pl.ds(r * feats, feats), :] = block
    for copy in copies[2 + waited :]:
        copy.wait()


def plan_kernel(n_slab, slots, *refs):
    (counts, blocks, assign, depth), (rows, codes, strip) = refs[:4], refs[4:]
    strip[...] = jnp.full(strip.shape, lax.axis_index("strip"), jnp.int32)
    items = n_slab * MOST
    outs = codes.shape[1] // (2 * items)
    me = lax.axis_index("slab")
    row = lax.broadcasted_iota(jnp.int32, rows.shape[1:], 0)
    item_lane = lax.broadcasted_iota(jnp.int32, codes.shape, 1) // outs
    posv = jnp.zeros(rows.shape[1:], jnp.int32)
    depthv = jnp.zeros(rows.shape[1:], jnp.int32)
    firstv = jnp.zeros(rows.shape[1:], jnp.int32)
    codev = jnp.full(codes.shape, -1, jnp.int32)
    pos = []
    for k, s in enumerate(exchange_order(n_slab)):
        off = jnp.int32(0)
        for c in range(n_slab):
            off = off + jnp.where(c < me, counts[0, s, c], 0)
        count = counts[0, s, me]
        for r in range(MOST):
            i = k * MOST + r
            slot = jnp.minimum(off + r, slots - 1)
            here = assign[0, blocks[0, s, slot]] - me * LB
            here = jnp.where(r < count, here, -1)
            first = jnp.int32(i)
            for j in reversed(range(i)):
                first = jnp.where(pos[j] == here, j, first)
            pos.append(here)
            firstv = jnp.where(row == i, first, firstv)
            posv = jnp.where(row == i, here, posv)
            depthv = jnp.where(row == i, depth[s], depthv)
            codev = jnp.where(item_lane == i, jnp.where(first == i, here, -1), codev)
    rows[0] = posv
    rows[1] = depthv
    rows[2] = firstv
    codes[...] = codev.astype(jnp.float32).astype(jnp.bfloat16)


def place_kernel(w_in, trans_weight, far_out, far_mid, w_first, w_out, w_later, w_mid, sems):
    copy = pltpu.make_async_copy(far_mid, w_mid, sems.at[0])
    copy.start()
    feats, hidden = w_in.shape
    half_in = (w_in[...].astype(jnp.float32) * 0.5).astype(jnp.bfloat16)
    half_trans = trans_weight[...].astype(jnp.float32) * 0.5
    sub = lax.broadcasted_iota(jnp.int32, (16, hidden), 0)
    w_first[...] = jnp.zeros_like(w_first)
    for a in range(GROUP):
        w_first[a, pl.ds(a * feats, feats), :] = half_in
        tail = jnp.where(sub // 2 == a, half_trans, 0.0)
        w_first[a, pl.ds(GROUP * feats, 16), :] = tail.astype(jnp.bfloat16)
    w_out[...] = far_out[...]
    copy.wait()
    for m in range(w_mid.shape[0]):
        w_later[m] = (w_mid[m].astype(jnp.float32).T * 0.5).astype(jnp.bfloat16)


def silu_half(u):
    return (u + u * jnp.tanh(u)).astype(jnp.bfloat16)


def later_layers(h, w_mid, w_out):
    for m in range(w_mid.shape[0]):
        h = silu_half(jnp.dot(h, w_mid[m], preferred_element_type=jnp.float32))
    y = lax.dot_general(
        w_out[...], h, (((1,), (1,)), ((), ())), preferred_element_type=jnp.float32
    )
    return y.astype(jnp.bfloat16).astype(jnp.float32)


def empty_kernel(trans_weight, w_mid, w_out, out):
    u = trans_weight[...].astype(jnp.float32) * 0.5
    h = silu_half(jnp.broadcast_to(u, (out.shape[1], u.shape[1])))
    y = later_layers(h, w_mid, w_out)
    outs = w_out.shape[0]
    for at in range(0, out.shape[0], outs):
        out[pl.ds(at, outs), :] = y


def shade_kernel(rows, codes, got, w_first, w_mid, w_out, out, acc, xt, ys):
    items, feats, span = acc.shape
    outs = w_out.shape[0]

    posv, depthv = rows[0], rows[1]
    front = jnp.ones((items, span), jnp.float32)
    total = jnp.ones((items, span), jnp.float32)
    for k in range(items // MOST):
        tail = got[k, pl.ds(MOST * feats, ROWS), :].astype(jnp.float32)
        for r in range(MOST):
            j = k * MOST + r
            trans_j = tail[r : r + 1, :]
            same = posv == posv[j : j + 1, :]
            total = jnp.where(same, total * trans_j, total)
            front = jnp.where(same & (depthv > depthv[j : j + 1, :]), front * trans_j, front)
    acc[...] = jnp.zeros_like(acc)
    for j in range(items):
        k, r = divmod(j, MOST)
        color = got[k, pl.ds(r * feats, feats), :].astype(jnp.float32)
        at = rows[2, j, 0]
        acc[at] = acc[at] + front[j : j + 1, :] * color
    total_hi = total.astype(jnp.bfloat16).astype(jnp.float32)
    total_lo = total - total_hi
    groups = items // GROUP
    sub = lax.broadcasted_iota(jnp.int32, (16, span), 0)
    xt[...] = jnp.zeros_like(xt)
    for q in range(groups):
        block = acc[pl.ds(q * GROUP, GROUP)].reshape(GROUP * feats, span)
        tail = jnp.zeros((16, span), jnp.float32)
        for a in range(GROUP):
            i = q * GROUP + a
            tail = jnp.where(sub == 2 * a, total_hi[i : i + 1, :], tail)
            tail = jnp.where(sub == 2 * a + 1, total_lo[i : i + 1, :], tail)
        lines = pl.ds(q * span, span)
        xt[lines, pl.ds(0, GROUP * feats)] = block.T.astype(jnp.bfloat16)
        xt[lines, pl.ds(GROUP * feats, 16)] = tail.T.astype(jnp.bfloat16)

    x = xt[...]
    stride = GROUP
    for start in range(0, GROUP, stride):
        h = jnp.concatenate(
            [
                silu_half(jnp.dot(x, w_first[a], preferred_element_type=jnp.float32))
                for a in range(start, start + stride)
            ]
        )
        y = later_layers(h, w_mid, w_out)
        for a in range(start, start + stride):
            for q in range(groups):
                at = ((a - start) * groups + q) * span
                ys[pl.ds((q * GROUP + a) * outs, outs), :] = y[:, at : at + span]
    out[pl.ds(0, items * outs), :] = ys[...].astype(jnp.bfloat16)
    out[pl.ds(items * outs, ROWS), :] = codes[...]


def join_kernel(*refs):
    *got, empty, strip, out, held, sems = refs
    _, n_strip, tile, outs, span = out.shape
    lines = tile * outs
    count = got[0].shape[0] - ROWS
    me = strip[0, 0]
    want = lax.broadcasted_iota(jnp.int32, (lines, count), 0) + strip[:1, :count] * lines
    chan = lax.broadcasted_iota(jnp.int32, (lines, count), 1) % outs
    filler = jnp.concatenate([empty[...]] * (lines // ROWS))
    ones = jnp.ones((count, span), jnp.bfloat16)
    copies = []
    for k in range(n_strip):
        pos = got[k][pl.ds(count, ROWS), :].astype(jnp.float32)[:1, :count].astype(jnp.int32)
        hit = pos * outs + chan == want
        pick = jnp.where(hit, 1.0, 0.0).astype(jnp.bfloat16)
        blocks = got[k][pl.ds(0, count), :]
        placed = jnp.dot(pick, blocks, preferred_element_type=jnp.float32)
        filled = jnp.dot(pick, ones, preferred_element_type=jnp.float32)
        value = jnp.where(filled > 0.5, placed, filler)
        held[k] = value.reshape(tile, outs, span).astype(jnp.bfloat16)
        copy = pltpu.make_async_copy(
            held.at[k], out.at[0, me ^ ((k + 1) % n_strip)], sems.at[k]
        )
        copy.start()
        copies.append(copy)
    for copy in copies:
        copy.wait()


def compact_device(
    n_slab,
    n_strip,
    colors,
    transmit,
    pair_counts,
    slot_block,
    assign,
    depth_rank,
    w_in,
    trans_weight,
    w_mid,
    w_out,
):
    slots, feats, span = colors.shape[2:]
    items = n_slab * MOST
    outs = w_out.shape[0]
    smem = pl.BlockSpec(memory_space=SMEM)
    vmem = pl.BlockSpec(memory_space=VMEM)
    hbm = pl.BlockSpec(memory_space=pltpu.HBM)
    held = functools.partial(pltpu.with_memory_space_constraint, memory_space=pltpu.HBM)
    small = pltpu.CompilerParams(vmem_limit_bytes=4 * 1024 * 1024)
    message = MOST * feats + ROWS
    sends = pl.pallas_call(
        pack_kernel,
        out_shape=jax.ShapeDtypeStruct((n_slab, message, span), jnp.bfloat16),
        in_specs=[hbm] * 3,
        out_specs=vmem,
        scratch_shapes=[
            pltpu.VMEM(pair_counts.shape, jnp.int32),
            pltpu.VMEM(colors.shape[2:], colors.dtype),
            pltpu.VMEM(transmit.shape, transmit.dtype),
            pltpu.SemaphoreType.DMA((2 + PARTS,)),
        ],
        compiler_params=small,
        name="pack",
    )(held(pair_counts), held(colors), held(transmit))
    group = exchange_order(n_slab)
    got = lax.all_to_all(
        sends, "slab", split_axis=0, concat_axis=0, axis_index_groups=[group], tiled=True
    )
    hidden = w_in.shape[0]
    rough = pl.CostEstimate(flops=10**5, bytes_accessed=10**6, transcendentals=0)
    roomy = pltpu.CompilerParams(vmem_limit_bytes=16 * 1024 * 1024)
    trans_row = trans_weight[None]
    rows, codes, strip = pl.pallas_call(
        functools.partial(plan_kernel, n_slab, slots),
        out_shape=[
            jax.ShapeDtypeStruct((3, items, span), jnp.int32),
            jax.ShapeDtypeStruct((ROWS, span), jnp.bfloat16),
            jax.ShapeDtypeStruct((ROWS, span), jnp.int32),
        ],
        in_specs=[smem] * 4,
        out_specs=[vmem] * 3,
        compiler_params=small,
        cost_estimate=rough,
        name="plan",
    )(pair_counts, slot_block, assign, depth_rank)
    w_first, w_last, w_later = pl.pallas_call(
        place_kernel,
        out_shape=[
            jax.ShapeDtypeStruct((GROUP, 2 * GROUP * feats, hidden), jnp.bfloat16),
            jax.ShapeDtypeStruct(w_out.shape, jnp.bfloat16),
            jax.ShapeDtypeStruct(w_mid.shape, jnp.bfloat16),
        ],
        in_specs=[vmem] * 3 + [hbm],
        out_specs=[vmem] * 3,
        scratch_shapes=[
            pltpu.VMEM(w_mid.shape, jnp.bfloat16),
            pltpu.SemaphoreType.DMA((1,)),
        ],
        compiler_params=small,
        cost_estimate=rough,
        name="place",
    )(w_in.T, trans_row, w_out, held(w_mid))
    empty = pl.pallas_call(
        empty_kernel,
        out_shape=jax.ShapeDtypeStruct((ROWS, span), jnp.float32),
        in_specs=[vmem] * 3,
        out_specs=vmem,
        compiler_params=roomy,
        cost_estimate=rough,
        name="empty",
    )(trans_row, w_later, w_last)
    shaded = pl.pallas_call(
        shade_kernel,
        out_shape=jax.ShapeDtypeStruct((items * outs + ROWS, span), jnp.bfloat16),
        in_specs=[vmem] * 6,
        out_specs=vmem,
        scratch_shapes=[
            pltpu.VMEM((items, feats, span), jnp.float32),
            pltpu.VMEM((items // GROUP * span, 2 * GROUP * feats), jnp.bfloat16),
            pltpu.VMEM((items * outs, span), jnp.float32),
        ],
        compiler_params=roomy,
        name="shade",
    )(rows, codes, got, w_first, w_later, w_last)
    tiles = [
        lax.ppermute(shaded, "strip", [(s, s ^ k) for s in range(n_strip)])
        for k in range(1, n_strip)
    ] + [shaded]
    return pl.pallas_call(
        join_kernel,
        out_shape=jax.ShapeDtypeStruct((1, n_strip, LB // n_strip, outs, span), jnp.bfloat16),
        in_specs=[vmem] * (n_strip + 2),
        out_specs=pl.BlockSpec(memory_space=pl.ANY),
        scratch_shapes=[
            pltpu.VMEM((n_strip, LB // n_strip, outs, span), jnp.bfloat16),
            pltpu.SemaphoreType.DMA((n_strip,)),
        ],
        compiler_params=small,
        name="join",
    )(*tiles, empty, strip)


def solution(mesh):
    n_slab, n_strip = mesh.shape["slab"], mesh.shape["strip"]
    placed = (
        P("slab", "strip", None, None, None),
        P("slab", "strip", None, None),
        P("strip", None, None),
        P("strip", None, None),
        P("strip", None),
        P(),
        P(),
        P(),
        P(),
        P(),
    )
    compact = n_strip & (n_strip - 1) == 0 and 4 * MOST * n_slab <= LB
    return jax.shard_map(
        functools.partial(compact_device, n_slab, n_strip) if compact else dense_device,
        mesh=mesh,
        in_specs=placed,
        out_specs=P("slab", None, "strip", None, None),
        check_vma=False,
    )
```

```python
import functools

import jax
import jax.numpy as jnp
from jax import lax
from jax.experimental import pallas as pl
from jax.experimental.pallas import tpu as pltpu
from jax.sharding import PartitionSpec as P

MOST = 2
LB = 128


EXACT_PRECISION = lax.Precision.HIGHEST


def shade_blocks(blend_color, trans_field, w_in, trans_weight, w_mid, w_out):
    summed = jnp.einsum("hf,lfp->lhp", w_in, blend_color, preferred_element_type=jnp.float32)
    summed = summed + trans_weight.astype(jnp.float32)[None, :, None] * trans_field[:, None, :]
    hidden = jax.nn.silu(summed).astype(jnp.bfloat16)
    for layer_index in range(w_mid.shape[0]):
        hidden = jax.nn.silu(
            jnp.einsum(
                "hg,lgp->lhp", w_mid[layer_index], hidden, preferred_element_type=jnp.float32
            )
        ).astype(jnp.bfloat16)
    return jnp.einsum("oh,lhp->lop", w_out, hidden, preferred_element_type=jnp.float32).astype(
        jnp.bfloat16
    )


def dense_device(
    colors, transmit, pair_counts, slot_block, assign, depth_rank, w_in, trans_weight, w_mid, w_out
):
    myself = lax.axis_index("slab")
    counts = pair_counts[0]
    blocks_all = slot_block[0]
    assign_row = assign[0]
    offsets = jnp.cumsum(counts, axis=1) - counts
    slot_rank = jnp.arange(MOST, dtype=jnp.int32)
    my_counts = lax.dynamic_index_in_dim(counts, myself, 0, keepdims=False)
    my_offsets = lax.dynamic_index_in_dim(offsets, myself, 0, keepdims=False)
    send_slots = jnp.where(
        slot_rank[None, :] < my_counts[:, None], my_offsets[:, None] + slot_rank[None, :], 0
    )
    send_color = colors[0, 0][send_slots]
    send_trans = transmit[0, 0][send_slots][:, :, None, :]
    incoming = lax.dynamic_index_in_dim(counts, myself, 1, keepdims=False)
    in_offsets = lax.dynamic_index_in_dim(offsets, myself, 1, keepdims=False)
    live_slot = slot_rank[None, :] < incoming[:, None]
    recv_slots = jnp.where(live_slot, in_offsets[:, None] + slot_rank[None, :], 0)
    recv_blocks = jnp.take_along_axis(blocks_all, recv_slots, axis=1)
    local_pos = assign_row[recv_blocks] - myself * LB
    live_flat = live_slot.reshape(-1)
    local_flat = jnp.where(live_flat, local_pos.reshape(-1), -1)
    depth_flat = jnp.repeat(depth_rank, MOST)
    ahead_table = (
        (local_flat[:, None] == local_flat[None, :])
        & (depth_flat[None, :] < depth_flat[:, None])
        & live_flat[None, :]
    )
    ahead_table = ahead_table.astype(jnp.float32)
    owner_table = (jnp.arange(LB, dtype=jnp.int32)[:, None] == local_flat[None, :]).astype(
        jnp.float32
    )
    got_color = lax.all_to_all(send_color, "slab", split_axis=0, concat_axis=0, tiled=True)
    got_trans = lax.all_to_all(send_trans, "slab", split_axis=0, concat_axis=0, tiled=True)
    pixel_count = got_color.shape[3]
    item_count = got_color.shape[0] * got_color.shape[1]
    log_trans = jnp.log(got_trans.reshape(item_count, pixel_count).astype(jnp.float32))
    log_trans = jnp.where(live_flat[:, None], log_trans, 0.0)
    front_log = jnp.dot(ahead_table, log_trans, precision=EXACT_PRECISION)
    front_share = jnp.where(live_flat[:, None], jnp.exp(front_log), 0.0)
    weighted = front_share[:, None, :] * got_color.reshape(item_count, -1, pixel_count).astype(
        jnp.float32
    )
    blend_sum = jnp.dot(owner_table, weighted.reshape(item_count, -1), precision=EXACT_PRECISION)
    blend_color = blend_sum.reshape(LB, -1, pixel_count).astype(jnp.bfloat16)
    trans_field = jnp.exp(jnp.dot(owner_table, log_trans, precision=EXACT_PRECISION))
    shaded = shade_blocks(blend_color, trans_field, w_in, trans_weight, w_mid, w_out)
    display_tiles = lax.all_to_all(shaded[None], "strip", split_axis=1, concat_axis=0, tiled=True)
    return display_tiles[None]


SMEM = pltpu.SMEM
VMEM = pltpu.VMEM
ROWS = 8
GROUP = 4


def exchange_order(n_slab):
    half = n_slab // 2
    return [s for i in range(half) for s in (half + (i + 1) % half, i)]


def pack_kernel(far_counts, far_colors, far_transmit, sends, counts, colors, transmit, tall, sems):
    n_slab = sends.shape[0]
    order = exchange_order(n_slab)
    slots, feats, span = colors.shape[2:]
    copies = [
        pltpu.make_async_copy(far, near, sems.at[i])
        for i, (far, near) in enumerate(
            ((far_counts, counts), (far_colors, colors), (far_transmit, transmit))
        )
    ]
    for copy in copies:
        copy.start()
    me = lax.axis_index("slab")
    for copy in copies:
        copy.wait()
    tall[...] = transmit[0, 0].astype(jnp.float32)
    row = lax.broadcasted_iota(jnp.int32, (ROWS, span), 0)
    off = jnp.int32(0)
    for c in range(n_slab):
        at = order.index(c)
        tail = jnp.ones((ROWS, span), jnp.float32)
        for r in range(MOST):
            slot = jnp.minimum(off + r, slots - 1)
            sends[at, pl.ds(r * feats, feats), :] = colors[0, 0, slot]
            tail = jnp.where(row == r, tall[pl.ds(slot, 1), :], tail)
        sends[at, pl.ds(MOST * feats, ROWS), :] = tail.astype(jnp.bfloat16)
        off = off + counts[0, me, c]


def plan_kernel(n_slab, slots, *refs):
    (counts, blocks, assign, depth), (rows, codes, strip) = refs[:4], refs[4:]
    strip[...] = jnp.full(strip.shape, lax.axis_index("strip"), jnp.int32)
    items = n_slab * MOST
    outs = codes.shape[1] // (2 * items)
    me = lax.axis_index("slab")
    row = lax.broadcasted_iota(jnp.int32, rows.shape[1:], 0)
    item_lane = lax.broadcasted_iota(jnp.int32, codes.shape, 1) // outs
    posv = jnp.zeros(rows.shape[1:], jnp.int32)
    depthv = jnp.zeros(rows.shape[1:], jnp.int32)
    firstv = jnp.zeros(rows.shape[1:], jnp.int32)
    codev = jnp.full(codes.shape, -1, jnp.int32)
    pos = []
    for k, s in enumerate(exchange_order(n_slab)):
        off = jnp.int32(0)
        for c in range(n_slab):
            off = off + jnp.where(c < me, counts[0, s, c], 0)
        count = counts[0, s, me]
        for r in range(MOST):
            i = k * MOST + r
            slot = jnp.minimum(off + r, slots - 1)
            here = assign[0, blocks[0, s, slot]] - me * LB
            here = jnp.where(r < count, here, -1)
            first = jnp.int32(i)
            for j in reversed(range(i)):
                first = jnp.where(pos[j] == here, j, first)
            pos.append(here)
            firstv = jnp.where(row == i, first, firstv)
            posv = jnp.where(row == i, here, posv)
            depthv = jnp.where(row == i, depth[s], depthv)
            codev = jnp.where(item_lane == i, jnp.where(first == i, here, -1), codev)
    rows[0] = posv
    rows[1] = depthv
    rows[2] = firstv
    codes[...] = codev.astype(jnp.float32).astype(jnp.bfloat16)


def place_kernel(w_in, trans_weight, far_out, far_mid, w_first, w_out, w_later, w_mid, sems):
    copy = pltpu.make_async_copy(far_mid, w_mid, sems.at[0])
    copy.start()
    feats, hidden = w_in.shape
    half_in = (w_in[...].astype(jnp.float32) * 0.5).astype(jnp.bfloat16)
    half_trans = trans_weight[...].astype(jnp.float32) * 0.5
    sub = lax.broadcasted_iota(jnp.int32, (16, hidden), 0)
    w_first[...] = jnp.zeros_like(w_first)
    for a in range(GROUP):
        w_first[a, pl.ds(a * feats, feats), :] = half_in
        tail = jnp.where(sub // 2 == a, half_trans, 0.0)
        w_first[a, pl.ds(GROUP * feats, 16), :] = tail.astype(jnp.bfloat16)
    w_out[...] = far_out[...]
    copy.wait()
    for m in range(w_mid.shape[0]):
        w_later[m] = (w_mid[m].astype(jnp.float32).T * 0.5).astype(jnp.bfloat16)


def silu_half(u):
    return (u + u * jnp.tanh(u)).astype(jnp.bfloat16)


def later_layers(h, w_mid, w_out):
    for m in range(w_mid.shape[0]):
        h = silu_half(jnp.dot(h, w_mid[m], preferred_element_type=jnp.float32))
    y = lax.dot_general(
        w_out[...], h, (((1,), (1,)), ((), ())), preferred_element_type=jnp.float32
    )
    return y.astype(jnp.bfloat16).astype(jnp.float32)


def empty_kernel(trans_weight, w_mid, w_out, out):
    u = trans_weight[...].astype(jnp.float32) * 0.5
    h = silu_half(jnp.broadcast_to(u, (out.shape[1], u.shape[1])))
    y = later_layers(h, w_mid, w_out)
    outs = w_out.shape[0]
    for at in range(0, out.shape[0], outs):
        out[pl.ds(at, outs), :] = y


def shade_kernel(rows, codes, got, w_first, w_mid, w_out, out, acc, xt, ys):
    items, feats, span = acc.shape
    outs = w_out.shape[0]

    posv, depthv = rows[0], rows[1]
    front = jnp.ones((items, span), jnp.float32)
    total = jnp.ones((items, span), jnp.float32)
    for k in range(items // MOST):
        tail = got[k, pl.ds(MOST * feats, ROWS), :].astype(jnp.float32)
        for r in range(MOST):
            j = k * MOST + r
            trans_j = tail[r : r + 1, :]
            same = posv == posv[j : j + 1, :]
            total = jnp.where(same, total * trans_j, total)
            front = jnp.where(same & (depthv > depthv[j : j + 1, :]), front * trans_j, front)
    acc[...] = jnp.zeros_like(acc)
    for j in range(items):
        k, r = divmod(j, MOST)
        color = got[k, pl.ds(r * feats, feats), :].astype(jnp.float32)
        at = rows[2, j, 0]
        acc[at] = acc[at] + front[j : j + 1, :] * color
    total_hi = total.astype(jnp.bfloat16).astype(jnp.float32)
    total_lo = total - total_hi
    groups = items // GROUP
    sub = lax.broadcasted_iota(jnp.int32, (16, span), 0)
    xt[...] = jnp.zeros_like(xt)
    for q in range(groups):
        block = acc[pl.ds(q * GROUP, GROUP)].reshape(GROUP * feats, span)
        tail = jnp.zeros((16, span), jnp.float32)
        for a in range(GROUP):
            i = q * GROUP + a
            tail = jnp.where(sub == 2 * a, total_hi[i : i + 1, :], tail)
            tail = jnp.where(sub == 2 * a + 1, total_lo[i : i + 1, :], tail)
        lines = pl.ds(q * span, span)
        xt[lines, pl.ds(0, GROUP * feats)] = block.T.astype(jnp.bfloat16)
        xt[lines, pl.ds(GROUP * feats, 16)] = tail.T.astype(jnp.bfloat16)

    x = xt[...]
    stride = GROUP
    for start in range(0, GROUP, stride):
        h = jnp.concatenate(
            [
                silu_half(jnp.dot(x, w_first[a], preferred_element_type=jnp.float32))
                for a in range(start, start + stride)
            ]
        )
        y = later_layers(h, w_mid, w_out)
        for a in range(start, start + stride):
            for q in range(groups):
                at = ((a - start) * groups + q) * span
                ys[pl.ds((q * GROUP + a) * outs, outs), :] = y[:, at : at + span]
    out[pl.ds(0, items * outs), :] = ys[...].astype(jnp.bfloat16)
    out[pl.ds(items * outs, ROWS), :] = codes[...]


def join_kernel(*refs):
    *got, empty, strip, out, held, sems = refs
    _, n_strip, tile, outs, span = out.shape
    lines = tile * outs
    count = got[0].shape[0] - ROWS
    me = strip[0, 0]
    want = lax.broadcasted_iota(jnp.int32, (lines, count), 0) + strip[:1, :count] * lines
    chan = lax.broadcasted_iota(jnp.int32, (lines, count), 1) % outs
    filler = jnp.concatenate([empty[...]] * (lines // ROWS))
    ones = jnp.ones((count, span), jnp.bfloat16)
    copies = []
    for k in range(n_strip):
        pos = got[k][pl.ds(count, ROWS), :].astype(jnp.float32)[:1, :count].astype(jnp.int32)
        hit = pos * outs + chan == want
        pick = jnp.where(hit, 1.0, 0.0).astype(jnp.bfloat16)
        blocks = got[k][pl.ds(0, count), :]
        placed = jnp.dot(pick, blocks, preferred_element_type=jnp.float32)
        filled = jnp.dot(pick, ones, preferred_element_type=jnp.float32)
        value = jnp.where(filled > 0.5, placed, filler)
        held[k] = value.reshape(tile, outs, span).astype(jnp.bfloat16)
        copy = pltpu.make_async_copy(
            held.at[k], out.at[0, me ^ ((k + 1) % n_strip)], sems.at[k]
        )
        copy.start()
        copies.append(copy)
    for copy in copies:
        copy.wait()


def compact_device(
    n_slab,
    n_strip,
    colors,
    transmit,
    pair_counts,
    slot_block,
    assign,
    depth_rank,
    w_in,
    trans_weight,
    w_mid,
    w_out,
):
    slots, feats, span = colors.shape[2:]
    items = n_slab * MOST
    outs = w_out.shape[0]
    smem = pl.BlockSpec(memory_space=SMEM)
    vmem = pl.BlockSpec(memory_space=VMEM)
    hbm = pl.BlockSpec(memory_space=pltpu.HBM)
    held = functools.partial(pltpu.with_memory_space_constraint, memory_space=pltpu.HBM)
    small = pltpu.CompilerParams(vmem_limit_bytes=4 * 1024 * 1024)
    message = MOST * feats + ROWS
    sends = pl.pallas_call(
        pack_kernel,
        out_shape=jax.ShapeDtypeStruct((n_slab, message, span), jnp.bfloat16),
        in_specs=[hbm] * 3,
        out_specs=vmem,
        scratch_shapes=[
            pltpu.SMEM(pair_counts.shape, jnp.int32),
            pltpu.VMEM(colors.shape, colors.dtype),
            pltpu.VMEM(transmit.shape, transmit.dtype),
            pltpu.VMEM(transmit.shape[2:], jnp.float32),
            pltpu.SemaphoreType.DMA((3,)),
        ],
        compiler_params=small,
        name="pack",
    )(held(pair_counts), held(colors), held(transmit))
    group = exchange_order(n_slab)
    got = lax.all_to_all(
        sends, "slab", split_axis=0, concat_axis=0, axis_index_groups=[group], tiled=True
    )
    hidden = w_in.shape[0]
    rough = pl.CostEstimate(flops=10**5, bytes_accessed=10**6, transcendentals=0)
    roomy = pltpu.CompilerParams(vmem_limit_bytes=16 * 1024 * 1024)
    trans_row = trans_weight[None]
    rows, codes, strip = pl.pallas_call(
        functools.partial(plan_kernel, n_slab, slots),
        out_shape=[
            jax.ShapeDtypeStruct((3, items, span), jnp.int32),
            jax.ShapeDtypeStruct((ROWS, span), jnp.bfloat16),
            jax.ShapeDtypeStruct((ROWS, span), jnp.int32),
        ],
        in_specs=[smem] * 4,
        out_specs=[vmem] * 3,
        compiler_params=small,
        cost_estimate=rough,
        name="plan",
    )(pair_counts, slot_block, assign, depth_rank)
    w_first, w_last, w_later = pl.pallas_call(
        place_kernel,
        out_shape=[
            jax.ShapeDtypeStruct((GROUP, 2 * GROUP * feats, hidden), jnp.bfloat16),
            jax.ShapeDtypeStruct(w_out.shape, jnp.bfloat16),
            jax.ShapeDtypeStruct(w_mid.shape, jnp.bfloat16),
        ],
        in_specs=[vmem] * 3 + [hbm],
        out_specs=[vmem] * 3,
        scratch_shapes=[
            pltpu.VMEM(w_mid.shape, jnp.bfloat16),
            pltpu.SemaphoreType.DMA((1,)),
        ],
        compiler_params=small,
        cost_estimate=rough,
        name="place",
    )(w_in.T, trans_row, w_out, held(w_mid))
    empty = pl.pallas_call(
        empty_kernel,
        out_shape=jax.ShapeDtypeStruct((ROWS, span), jnp.float32),
        in_specs=[vmem] * 3,
        out_specs=vmem,
        compiler_params=roomy,
        cost_estimate=rough,
        name="empty",
    )(trans_row, w_later, w_last)
    shaded = pl.pallas_call(
        shade_kernel,
        out_shape=jax.ShapeDtypeStruct((items * outs + ROWS, span), jnp.bfloat16),
        in_specs=[vmem] * 6,
        out_specs=vmem,
        scratch_shapes=[
            pltpu.VMEM((items, feats, span), jnp.float32),
            pltpu.VMEM((items // GROUP * span, 2 * GROUP * feats), jnp.bfloat16),
            pltpu.VMEM((items * outs, span), jnp.float32),
        ],
        compiler_params=roomy,
        name="shade",
    )(rows, codes, got, w_first, w_later, w_last)
    tiles = [
        lax.ppermute(shaded, "strip", [(s, s ^ k) for s in range(n_strip)])
        for k in range(1, n_strip)
    ] + [shaded]
    return pl.pallas_call(
        join_kernel,
        out_shape=jax.ShapeDtypeStruct((1, n_strip, LB // n_strip, outs, span), jnp.bfloat16),
        in_specs=[vmem] * (n_strip + 2),
        out_specs=pl.BlockSpec(memory_space=pl.ANY),
        scratch_shapes=[
            pltpu.VMEM((n_strip, LB // n_strip, outs, span), jnp.bfloat16),
            pltpu.SemaphoreType.DMA((n_strip,)),
        ],
        compiler_params=small,
        name="join",
    )(*tiles, empty, strip)


def solution(mesh):
    n_slab, n_strip = mesh.shape["slab"], mesh.shape["strip"]
    placed = (
        P("slab", "strip", None, None, None),
        P("slab", "strip", None, None),
        P("strip", None, None),
        P("strip", None, None),
        P("strip", None),
        P(),
        P(),
        P(),
        P(),
        P(),
    )
    compact = n_strip & (n_strip - 1) == 0 and 4 * MOST * n_slab <= LB
    return jax.shard_map(
        functools.partial(compact_device, n_slab, n_strip) if compact else dense_device,
        mesh=mesh,
        in_specs=placed,
        out_specs=P("slab", None, "strip", None, None),
        check_vma=False,
    )
```

```python
import functools

import jax
import jax.numpy as jnp
from jax import lax
from jax.experimental import pallas as pl
from jax.experimental.pallas import tpu as pltpu
from jax.sharding import PartitionSpec as P

MOST = 2
LB = 128


EXACT_PRECISION = lax.Precision.HIGHEST


def shade_blocks(blend_color, trans_field, w_in, trans_weight, w_mid, w_out):
    summed = jnp.einsum("hf,lfp->lhp", w_in, blend_color, preferred_element_type=jnp.float32)
    summed = summed + trans_weight.astype(jnp.float32)[None, :, None] * trans_field[:, None, :]
    hidden = jax.nn.silu(summed).astype(jnp.bfloat16)
    for layer_index in range(w_mid.shape[0]):
        hidden = jax.nn.silu(
            jnp.einsum(
                "hg,lgp->lhp", w_mid[layer_index], hidden, preferred_element_type=jnp.float32
            )
        ).astype(jnp.bfloat16)
    return jnp.einsum("oh,lhp->lop", w_out, hidden, preferred_element_type=jnp.float32).astype(
        jnp.bfloat16
    )


def dense_device(
    colors, transmit, pair_counts, slot_block, assign, depth_rank, w_in, trans_weight, w_mid, w_out
):
    myself = lax.axis_index("slab")
    counts = pair_counts[0]
    blocks_all = slot_block[0]
    assign_row = assign[0]
    offsets = jnp.cumsum(counts, axis=1) - counts
    slot_rank = jnp.arange(MOST, dtype=jnp.int32)
    my_counts = lax.dynamic_index_in_dim(counts, myself, 0, keepdims=False)
    my_offsets = lax.dynamic_index_in_dim(offsets, myself, 0, keepdims=False)
    send_slots = jnp.where(
        slot_rank[None, :] < my_counts[:, None], my_offsets[:, None] + slot_rank[None, :], 0
    )
    send_color = colors[0, 0][send_slots]
    send_trans = transmit[0, 0][send_slots][:, :, None, :]
    incoming = lax.dynamic_index_in_dim(counts, myself, 1, keepdims=False)
    in_offsets = lax.dynamic_index_in_dim(offsets, myself, 1, keepdims=False)
    live_slot = slot_rank[None, :] < incoming[:, None]
    recv_slots = jnp.where(live_slot, in_offsets[:, None] + slot_rank[None, :], 0)
    recv_blocks = jnp.take_along_axis(blocks_all, recv_slots, axis=1)
    local_pos = assign_row[recv_blocks] - myself * LB
    live_flat = live_slot.reshape(-1)
    local_flat = jnp.where(live_flat, local_pos.reshape(-1), -1)
    depth_flat = jnp.repeat(depth_rank, MOST)
    ahead_table = (
        (local_flat[:, None] == local_flat[None, :])
        & (depth_flat[None, :] < depth_flat[:, None])
        & live_flat[None, :]
    )
    ahead_table = ahead_table.astype(jnp.float32)
    owner_table = (jnp.arange(LB, dtype=jnp.int32)[:, None] == local_flat[None, :]).astype(
        jnp.float32
    )
    got_color = lax.all_to_all(send_color, "slab", split_axis=0, concat_axis=0, tiled=True)
    got_trans = lax.all_to_all(send_trans, "slab", split_axis=0, concat_axis=0, tiled=True)
    pixel_count = got_color.shape[3]
    item_count = got_color.shape[0] * got_color.shape[1]
    log_trans = jnp.log(got_trans.reshape(item_count, pixel_count).astype(jnp.float32))
    log_trans = jnp.where(live_flat[:, None], log_trans, 0.0)
    front_log = jnp.dot(ahead_table, log_trans, precision=EXACT_PRECISION)
    front_share = jnp.where(live_flat[:, None], jnp.exp(front_log), 0.0)
    weighted = front_share[:, None, :] * got_color.reshape(item_count, -1, pixel_count).astype(
        jnp.float32
    )
    blend_sum = jnp.dot(owner_table, weighted.reshape(item_count, -1), precision=EXACT_PRECISION)
    blend_color = blend_sum.reshape(LB, -1, pixel_count).astype(jnp.bfloat16)
    trans_field = jnp.exp(jnp.dot(owner_table, log_trans, precision=EXACT_PRECISION))
    shaded = shade_blocks(blend_color, trans_field, w_in, trans_weight, w_mid, w_out)
    display_tiles = lax.all_to_all(shaded[None], "strip", split_axis=1, concat_axis=0, tiled=True)
    return display_tiles[None]


SMEM = pltpu.SMEM
VMEM = pltpu.VMEM
ROWS = 8
GROUP = 4


def exchange_order(n_slab):
    half = n_slab // 2
    back = [half] + list(range(n_slab - 1, half, -1))
    front = list(range(half - 2)) + [half - 1, half - 2] if half > 1 else [0]
    return [s for pair in zip(back, front) for s in pair]


def pack_kernel(far_counts, far_colors, far_transmit, sends, counts, colors, transmit, tall, sems):
    n_slab = sends.shape[0]
    order = exchange_order(n_slab)
    slots, feats, span = colors.shape[2:]
    copies = [
        pltpu.make_async_copy(far, near, sems.at[i])
        for i, (far, near) in enumerate(
            ((far_counts, counts), (far_colors, colors), (far_transmit, transmit))
        )
    ]
    for copy in copies:
        copy.start()
    me = lax.axis_index("slab")
    for copy in copies:
        copy.wait()
    tall[...] = transmit[0, 0].astype(jnp.float32)
    row = lax.broadcasted_iota(jnp.int32, (ROWS, span), 0)
    off = jnp.int32(0)
    for c in range(n_slab):
        at = order.index(c)
        tail = jnp.ones((ROWS, span), jnp.float32)
        for r in range(MOST):
            slot = jnp.minimum(off + r, slots - 1)
            sends[at, pl.ds(r * feats, feats), :] = colors[0, 0, slot]
            tail = jnp.where(row == r, tall[pl.ds(slot, 1), :], tail)
        sends[at, pl.ds(MOST * feats, ROWS), :] = tail.astype(jnp.bfloat16)
        off = off + counts[0, me, c]


def plan_kernel(n_slab, slots, *refs):
    (counts, blocks, assign, depth), (rows, codes, strip) = refs[:4], refs[4:]
    strip[...] = jnp.full(strip.shape, lax.axis_index("strip"), jnp.int32)
    items = n_slab * MOST
    outs = codes.shape[1] // (2 * items)
    me = lax.axis_index("slab")
    row = lax.broadcasted_iota(jnp.int32, rows.shape[1:], 0)
    item_lane = lax.broadcasted_iota(jnp.int32, codes.shape, 1) // outs
    posv = jnp.zeros(rows.shape[1:], jnp.int32)
    depthv = jnp.zeros(rows.shape[1:], jnp.int32)
    firstv = jnp.zeros(rows.shape[1:], jnp.int32)
    codev = jnp.full(codes.shape, -1, jnp.int32)
    pos = []
    for k, s in enumerate(exchange_order(n_slab)):
        off = jnp.int32(0)
        for c in range(n_slab):
            off = off + jnp.where(c < me, counts[0, s, c], 0)
        count = counts[0, s, me]
        for r in range(MOST):
            i = k * MOST + r
            slot = jnp.minimum(off + r, slots - 1)
            here = assign[0, blocks[0, s, slot]] - me * LB
            here = jnp.where(r < count, here, -1)
            first = jnp.int32(i)
            for j in reversed(range(i)):
                first = jnp.where(pos[j] == here, j, first)
            pos.append(here)
            firstv = jnp.where(row == i, first, firstv)
            posv = jnp.where(row == i, here, posv)
            depthv = jnp.where(row == i, depth[s], depthv)
            codev = jnp.where(item_lane == i, jnp.where(first == i, here, -1), codev)
    rows[0] = posv
    rows[1] = depthv
    rows[2] = firstv
    codes[...] = codev.astype(jnp.float32).astype(jnp.bfloat16)


def place_kernel(w_in, trans_weight, far_out, far_mid, w_first, w_out, w_later, w_mid, sems):
    copy = pltpu.make_async_copy(far_mid, w_mid, sems.at[0])
    copy.start()
    feats, hidden = w_in.shape
    half_in = (w_in[...].astype(jnp.float32) * 0.5).astype(jnp.bfloat16)
    half_trans = trans_weight[...].astype(jnp.float32) * 0.5
    sub = lax.broadcasted_iota(jnp.int32, (16, hidden), 0)
    w_first[...] = jnp.zeros_like(w_first)
    for a in range(GROUP):
        w_first[a, pl.ds(a * feats, feats), :] = half_in
        tail = jnp.where(sub // 2 == a, half_trans, 0.0)
        w_first[a, pl.ds(GROUP * feats, 16), :] = tail.astype(jnp.bfloat16)
    w_out[...] = far_out[...]
    copy.wait()
    for m in range(w_mid.shape[0]):
        w_later[m] = (w_mid[m].astype(jnp.float32).T * 0.5).astype(jnp.bfloat16)


def silu_half(u):
    return (u + u * jnp.tanh(u)).astype(jnp.bfloat16)


def later_layers(h, w_mid, w_out):
    for m in range(w_mid.shape[0]):
        h = silu_half(jnp.dot(h, w_mid[m], preferred_element_type=jnp.float32))
    y = lax.dot_general(
        w_out[...], h, (((1,), (1,)), ((), ())), preferred_element_type=jnp.float32
    )
    return y.astype(jnp.bfloat16).astype(jnp.float32)


def empty_kernel(trans_weight, w_mid, w_out, out):
    u = trans_weight[...].astype(jnp.float32) * 0.5
    h = silu_half(jnp.broadcast_to(u, (out.shape[1], u.shape[1])))
    y = later_layers(h, w_mid, w_out)
    outs = w_out.shape[0]
    for at in range(0, out.shape[0], outs):
        out[pl.ds(at, outs), :] = y


def shade_kernel(rows, codes, got, w_first, w_mid, w_out, out, acc, xt, ys):
    items, feats, span = acc.shape
    outs = w_out.shape[0]

    posv, depthv = rows[0], rows[1]
    front = jnp.ones((items, span), jnp.float32)
    total = jnp.ones((items, span), jnp.float32)
    for k in range(items // MOST):
        tail = got[k, pl.ds(MOST * feats, ROWS), :].astype(jnp.float32)
        for r in range(MOST):
            j = k * MOST + r
            trans_j = tail[r : r + 1, :]
            same = posv == posv[j : j + 1, :]
            total = jnp.where(same, total * trans_j, total)
            front = jnp.where(same & (depthv > depthv[j : j + 1, :]), front * trans_j, front)
    acc[...] = jnp.zeros_like(acc)
    for j in range(items):
        k, r = divmod(j, MOST)
        color = got[k, pl.ds(r * feats, feats), :].astype(jnp.float32)
        at = rows[2, j, 0]
        acc[at] = acc[at] + front[j : j + 1, :] * color
    total_hi = total.astype(jnp.bfloat16).astype(jnp.float32)
    total_lo = total - total_hi
    groups = items // GROUP
    sub = lax.broadcasted_iota(jnp.int32, (16, span), 0)
    xt[...] = jnp.zeros_like(xt)
    for q in range(groups):
        block = acc[pl.ds(q * GROUP, GROUP)].reshape(GROUP * feats, span)
        tail = jnp.zeros((16, span), jnp.float32)
        for a in range(GROUP):
            i = q * GROUP + a
            tail = jnp.where(sub == 2 * a, total_hi[i : i + 1, :], tail)
            tail = jnp.where(sub == 2 * a + 1, total_lo[i : i + 1, :], tail)
        lines = pl.ds(q * span, span)
        xt[lines, pl.ds(0, GROUP * feats)] = block.T.astype(jnp.bfloat16)
        xt[lines, pl.ds(GROUP * feats, 16)] = tail.T.astype(jnp.bfloat16)

    x = xt[...]
    stride = GROUP
    for start in range(0, GROUP, stride):
        h = jnp.concatenate(
            [
                silu_half(jnp.dot(x, w_first[a], preferred_element_type=jnp.float32))
                for a in range(start, start + stride)
            ]
        )
        y = later_layers(h, w_mid, w_out)
        for a in range(start, start + stride):
            for q in range(groups):
                at = ((a - start) * groups + q) * span
                ys[pl.ds((q * GROUP + a) * outs, outs), :] = y[:, at : at + span]
    out[pl.ds(0, items * outs), :] = ys[...].astype(jnp.bfloat16)
    out[pl.ds(items * outs, ROWS), :] = codes[...]


def join_kernel(*refs):
    *got, empty, strip, out, held, sems = refs
    _, n_strip, tile, outs, span = out.shape
    lines = tile * outs
    count = got[0].shape[0] - ROWS
    me = strip[0, 0]
    want = lax.broadcasted_iota(jnp.int32, (lines, count), 0) + strip[:1, :count] * lines
    chan = lax.broadcasted_iota(jnp.int32, (lines, count), 1) % outs
    filler = jnp.concatenate([empty[...]] * (lines // ROWS))
    ones = jnp.ones((count, span), jnp.bfloat16)
    copies = []
    for k in range(n_strip):
        pos = got[k][pl.ds(count, ROWS), :].astype(jnp.float32)[:1, :count].astype(jnp.int32)
        hit = pos * outs + chan == want
        pick = jnp.where(hit, 1.0, 0.0).astype(jnp.bfloat16)
        blocks = got[k][pl.ds(0, count), :]
        placed = jnp.dot(pick, blocks, preferred_element_type=jnp.float32)
        filled = jnp.dot(pick, ones, preferred_element_type=jnp.float32)
        value = jnp.where(filled > 0.5, placed, filler)
        held[k] = value.reshape(tile, outs, span).astype(jnp.bfloat16)
        copy = pltpu.make_async_copy(
            held.at[k], out.at[0, me ^ ((k + 1) % n_strip)], sems.at[k]
        )
        copy.start()
        copies.append(copy)
    for copy in copies:
        copy.wait()


def compact_device(
    n_slab,
    n_strip,
    colors,
    transmit,
    pair_counts,
    slot_block,
    assign,
    depth_rank,
    w_in,
    trans_weight,
    w_mid,
    w_out,
):
    slots, feats, span = colors.shape[2:]
    items = n_slab * MOST
    outs = w_out.shape[0]
    smem = pl.BlockSpec(memory_space=SMEM)
    vmem = pl.BlockSpec(memory_space=VMEM)
    hbm = pl.BlockSpec(memory_space=pltpu.HBM)
    held = functools.partial(pltpu.with_memory_space_constraint, memory_space=pltpu.HBM)
    small = pltpu.CompilerParams(vmem_limit_bytes=4 * 1024 * 1024)
    message = MOST * feats + ROWS
    sends = pl.pallas_call(
        pack_kernel,
        out_shape=jax.ShapeDtypeStruct((n_slab, message, span), jnp.bfloat16),
        in_specs=[hbm] * 3,
        out_specs=vmem,
        scratch_shapes=[
            pltpu.SMEM(pair_counts.shape, jnp.int32),
            pltpu.VMEM(colors.shape, colors.dtype),
            pltpu.VMEM(transmit.shape, transmit.dtype),
            pltpu.VMEM(transmit.shape[2:], jnp.float32),
            pltpu.SemaphoreType.DMA((3,)),
        ],
        compiler_params=small,
        name="pack",
    )(held(pair_counts), held(colors), held(transmit))
    group = exchange_order(n_slab)
    got = lax.all_to_all(
        sends, "slab", split_axis=0, concat_axis=0, axis_index_groups=[group], tiled=True
    )
    hidden = w_in.shape[0]
    rough = pl.CostEstimate(flops=10**5, bytes_accessed=10**6, transcendentals=0)
    roomy = pltpu.CompilerParams(vmem_limit_bytes=16 * 1024 * 1024)
    trans_row = trans_weight[None]
    rows, codes, strip = pl.pallas_call(
        functools.partial(plan_kernel, n_slab, slots),
        out_shape=[
            jax.ShapeDtypeStruct((3, items, span), jnp.int32),
            jax.ShapeDtypeStruct((ROWS, span), jnp.bfloat16),
            jax.ShapeDtypeStruct((ROWS, span), jnp.int32),
        ],
        in_specs=[smem] * 4,
        out_specs=[vmem] * 3,
        compiler_params=small,
        cost_estimate=rough,
        name="plan",
    )(pair_counts, slot_block, assign, depth_rank)
    w_first, w_last, w_later = pl.pallas_call(
        place_kernel,
        out_shape=[
            jax.ShapeDtypeStruct((GROUP, 2 * GROUP * feats, hidden), jnp.bfloat16),
            jax.ShapeDtypeStruct(w_out.shape, jnp.bfloat16),
            jax.ShapeDtypeStruct(w_mid.shape, jnp.bfloat16),
        ],
        in_specs=[vmem] * 3 + [hbm],
        out_specs=[vmem] * 3,
        scratch_shapes=[
            pltpu.VMEM(w_mid.shape, jnp.bfloat16),
            pltpu.SemaphoreType.DMA((1,)),
        ],
        compiler_params=small,
        cost_estimate=rough,
        name="place",
    )(w_in.T, trans_row, w_out, held(w_mid))
    empty = pl.pallas_call(
        empty_kernel,
        out_shape=jax.ShapeDtypeStruct((ROWS, span), jnp.float32),
        in_specs=[vmem] * 3,
        out_specs=vmem,
        compiler_params=roomy,
        cost_estimate=rough,
        name="empty",
    )(trans_row, w_later, w_last)
    shaded = pl.pallas_call(
        shade_kernel,
        out_shape=jax.ShapeDtypeStruct((items * outs + ROWS, span), jnp.bfloat16),
        in_specs=[vmem] * 6,
        out_specs=vmem,
        scratch_shapes=[
            pltpu.VMEM((items, feats, span), jnp.float32),
            pltpu.VMEM((items // GROUP * span, 2 * GROUP * feats), jnp.bfloat16),
            pltpu.VMEM((items * outs, span), jnp.float32),
        ],
        compiler_params=roomy,
        name="shade",
    )(rows, codes, got, w_first, w_later, w_last)
    tiles = [
        lax.ppermute(shaded, "strip", [(s, s ^ k) for s in range(n_strip)])
        for k in range(1, n_strip)
    ] + [shaded]
    return pl.pallas_call(
        join_kernel,
        out_shape=jax.ShapeDtypeStruct((1, n_strip, LB // n_strip, outs, span), jnp.bfloat16),
        in_specs=[vmem] * (n_strip + 2),
        out_specs=pl.BlockSpec(memory_space=pl.ANY),
        scratch_shapes=[
            pltpu.VMEM((n_strip, LB // n_strip, outs, span), jnp.bfloat16),
            pltpu.SemaphoreType.DMA((n_strip,)),
        ],
        compiler_params=small,
        name="join",
    )(*tiles, empty, strip)


def solution(mesh):
    n_slab, n_strip = mesh.shape["slab"], mesh.shape["strip"]
    placed = (
        P("slab", "strip", None, None, None),
        P("slab", "strip", None, None),
        P("strip", None, None),
        P("strip", None, None),
        P("strip", None),
        P(),
        P(),
        P(),
        P(),
        P(),
    )
    compact = n_strip & (n_strip - 1) == 0 and 4 * MOST * n_slab <= LB
    return jax.shard_map(
        functools.partial(compact_device, n_slab, n_strip) if compact else dense_device,
        mesh=mesh,
        in_specs=placed,
        out_specs=P("slab", None, "strip", None, None),
        check_vma=False,
    )
```

```python
import functools

import jax
import jax.numpy as jnp
from jax import lax
from jax.experimental import pallas as pl
from jax.experimental.pallas import tpu as pltpu
from jax.sharding import PartitionSpec as P

MOST = 2
LB = 128


EXACT_PRECISION = lax.Precision.HIGHEST


def shade_blocks(blend_color, trans_field, w_in, trans_weight, w_mid, w_out):
    summed = jnp.einsum("hf,lfp->lhp", w_in, blend_color, preferred_element_type=jnp.float32)
    summed = summed + trans_weight.astype(jnp.float32)[None, :, None] * trans_field[:, None, :]
    hidden = jax.nn.silu(summed).astype(jnp.bfloat16)
    for layer_index in range(w_mid.shape[0]):
        hidden = jax.nn.silu(
            jnp.einsum(
                "hg,lgp->lhp", w_mid[layer_index], hidden, preferred_element_type=jnp.float32
            )
        ).astype(jnp.bfloat16)
    return jnp.einsum("oh,lhp->lop", w_out, hidden, preferred_element_type=jnp.float32).astype(
        jnp.bfloat16
    )


def dense_device(
    colors, transmit, pair_counts, slot_block, assign, depth_rank, w_in, trans_weight, w_mid, w_out
):
    myself = lax.axis_index("slab")
    counts = pair_counts[0]
    blocks_all = slot_block[0]
    assign_row = assign[0]
    offsets = jnp.cumsum(counts, axis=1) - counts
    slot_rank = jnp.arange(MOST, dtype=jnp.int32)
    my_counts = lax.dynamic_index_in_dim(counts, myself, 0, keepdims=False)
    my_offsets = lax.dynamic_index_in_dim(offsets, myself, 0, keepdims=False)
    send_slots = jnp.where(
        slot_rank[None, :] < my_counts[:, None], my_offsets[:, None] + slot_rank[None, :], 0
    )
    send_color = colors[0, 0][send_slots]
    send_trans = transmit[0, 0][send_slots][:, :, None, :]
    incoming = lax.dynamic_index_in_dim(counts, myself, 1, keepdims=False)
    in_offsets = lax.dynamic_index_in_dim(offsets, myself, 1, keepdims=False)
    live_slot = slot_rank[None, :] < incoming[:, None]
    recv_slots = jnp.where(live_slot, in_offsets[:, None] + slot_rank[None, :], 0)
    recv_blocks = jnp.take_along_axis(blocks_all, recv_slots, axis=1)
    local_pos = assign_row[recv_blocks] - myself * LB
    live_flat = live_slot.reshape(-1)
    local_flat = jnp.where(live_flat, local_pos.reshape(-1), -1)
    depth_flat = jnp.repeat(depth_rank, MOST)
    ahead_table = (
        (local_flat[:, None] == local_flat[None, :])
        & (depth_flat[None, :] < depth_flat[:, None])
        & live_flat[None, :]
    )
    ahead_table = ahead_table.astype(jnp.float32)
    owner_table = (jnp.arange(LB, dtype=jnp.int32)[:, None] == local_flat[None, :]).astype(
        jnp.float32
    )
    got_color = lax.all_to_all(send_color, "slab", split_axis=0, concat_axis=0, tiled=True)
    got_trans = lax.all_to_all(send_trans, "slab", split_axis=0, concat_axis=0, tiled=True)
    pixel_count = got_color.shape[3]
    item_count = got_color.shape[0] * got_color.shape[1]
    log_trans = jnp.log(got_trans.reshape(item_count, pixel_count).astype(jnp.float32))
    log_trans = jnp.where(live_flat[:, None], log_trans, 0.0)
    front_log = jnp.dot(ahead_table, log_trans, precision=EXACT_PRECISION)
    front_share = jnp.where(live_flat[:, None], jnp.exp(front_log), 0.0)
    weighted = front_share[:, None, :] * got_color.reshape(item_count, -1, pixel_count).astype(
        jnp.float32
    )
    blend_sum = jnp.dot(owner_table, weighted.reshape(item_count, -1), precision=EXACT_PRECISION)
    blend_color = blend_sum.reshape(LB, -1, pixel_count).astype(jnp.bfloat16)
    trans_field = jnp.exp(jnp.dot(owner_table, log_trans, precision=EXACT_PRECISION))
    shaded = shade_blocks(blend_color, trans_field, w_in, trans_weight, w_mid, w_out)
    display_tiles = lax.all_to_all(shaded[None], "strip", split_axis=1, concat_axis=0, tiled=True)
    return display_tiles[None]


SMEM = pltpu.SMEM
VMEM = pltpu.VMEM
ROWS = 8
GROUP = 4


def exchange_order(n_slab):
    half = n_slab // 2
    back = [half] + list(range(n_slab - 1, half, -1))
    front = list(range(half - 2)) + [half - 1, half - 2] if half > 1 else [0]
    return [s for pair in zip(back, front) for s in pair]


def pack_kernel(far_counts, far_colors, far_transmit, sends, counts, colors, transmit, tall, sems):
    n_slab = sends.shape[0]
    order = exchange_order(n_slab)
    slots, feats, span = colors.shape[2:]
    copies = [
        pltpu.make_async_copy(far, near, sems.at[i])
        for i, (far, near) in enumerate(
            ((far_counts, counts), (far_colors, colors), (far_transmit, transmit))
        )
    ]
    for copy in copies:
        copy.start()
    me = lax.axis_index("slab")
    for copy in copies:
        copy.wait()
    tall[...] = transmit[0, 0].astype(jnp.float32)
    row = lax.broadcasted_iota(jnp.int32, (ROWS, span), 0)
    off = jnp.int32(0)
    for c in range(n_slab):
        at = order.index(c)
        tail = jnp.ones((ROWS, span), jnp.float32)
        for r in range(MOST):
            slot = jnp.minimum(off + r, slots - 1)
            sends[at, pl.ds(r * feats, feats), :] = colors[0, 0, slot]
            tail = jnp.where(row == r, tall[pl.ds(slot, 1), :], tail)
        sends[at, pl.ds(MOST * feats, ROWS), :] = tail.astype(jnp.bfloat16)
        off = off + counts[0, me, c]


def plan_kernel(n_slab, slots, *refs):
    (counts, blocks, assign, depth), (rows, codes, strip) = refs[:4], refs[4:]
    strip[...] = jnp.full(strip.shape, lax.axis_index("strip"), jnp.int32)
    items = n_slab * MOST
    outs = codes.shape[1] // (2 * items)
    me = lax.axis_index("slab")
    row = lax.broadcasted_iota(jnp.int32, rows.shape[1:], 0)
    item_lane = lax.broadcasted_iota(jnp.int32, codes.shape, 1) // outs
    posv = jnp.zeros(rows.shape[1:], jnp.int32)
    depthv = jnp.zeros(rows.shape[1:], jnp.int32)
    firstv = jnp.zeros(rows.shape[1:], jnp.int32)
    codev = jnp.full(codes.shape, -1, jnp.int32)
    pos = []
    for k, s in enumerate(exchange_order(n_slab)):
        off = jnp.int32(0)
        for c in range(n_slab):
            off = off + jnp.where(c < me, counts[0, s, c], 0)
        count = counts[0, s, me]
        for r in range(MOST):
            i = k * MOST + r
            slot = jnp.minimum(off + r, slots - 1)
            here = assign[0, blocks[0, s, slot]] - me * LB
            here = jnp.where(r < count, here, -1)
            first = jnp.int32(i)
            for j in reversed(range(i)):
                first = jnp.where(pos[j] == here, j, first)
            pos.append(here)
            firstv = jnp.where(row == i, first, firstv)
            posv = jnp.where(row == i, here, posv)
            depthv = jnp.where(row == i, depth[s], depthv)
            codev = jnp.where(item_lane == i, jnp.where(first == i, here, -1), codev)
    rows[0] = posv
    rows[1] = depthv
    rows[2] = firstv
    codes[...] = codev.astype(jnp.float32).astype(jnp.bfloat16)


def place_kernel(w_in, trans_weight, far_out, far_mid, w_first, w_out, w_later, w_mid, sems):
    copy = pltpu.make_async_copy(far_mid, w_mid, sems.at[0])
    copy.start()
    feats, hidden = w_in.shape
    half_in = (w_in[...].astype(jnp.float32) * 0.5).astype(jnp.bfloat16)
    half_trans = trans_weight[...].astype(jnp.float32) * 0.5
    sub = lax.broadcasted_iota(jnp.int32, (16, hidden), 0)
    w_first[...] = jnp.zeros_like(w_first)
    for a in range(GROUP):
        w_first[a, pl.ds(a * feats, feats), :] = half_in
        tail = jnp.where(sub // 2 == a, half_trans, 0.0)
        w_first[a, pl.ds(GROUP * feats, 16), :] = tail.astype(jnp.bfloat16)
    w_out[...] = far_out[...]
    copy.wait()
    for m in range(w_mid.shape[0]):
        w_later[m] = (w_mid[m].astype(jnp.float32).T * 0.5).astype(jnp.bfloat16)


def silu_half(u):
    return (u + u * jnp.tanh(u)).astype(jnp.bfloat16)


def later_layers(h, w_mid, w_out):
    for m in range(w_mid.shape[0]):
        h = silu_half(jnp.dot(h, w_mid[m], preferred_element_type=jnp.float32))
    y = lax.dot_general(
        w_out[...], h, (((1,), (1,)), ((), ())), preferred_element_type=jnp.float32
    )
    return y.astype(jnp.bfloat16).astype(jnp.float32)


def empty_kernel(trans_weight, w_mid, w_out, out):
    u = trans_weight[...].astype(jnp.float32) * 0.5
    h = silu_half(jnp.broadcast_to(u, (out.shape[1], u.shape[1])))
    y = later_layers(h, w_mid, w_out)
    outs = w_out.shape[0]
    for at in range(0, out.shape[0], outs):
        out[pl.ds(at, outs), :] = y


def shade_kernel(rows, codes, got, w_first, w_mid, w_out, out, acc, xt, ys):
    items, feats, span = acc.shape
    outs = w_out.shape[0]

    posv, depthv = rows[0], rows[1]
    front = jnp.ones((items, span), jnp.float32)
    total = jnp.ones((items, span), jnp.float32)
    for k in range(items // MOST):
        tail = got[k, pl.ds(MOST * feats, ROWS), :].astype(jnp.float32)
        for r in range(MOST):
            j = k * MOST + r
            trans_j = tail[r : r + 1, :]
            same = posv == posv[j : j + 1, :]
            total = jnp.where(same, total * trans_j, total)
            front = jnp.where(same & (depthv > depthv[j : j + 1, :]), front * trans_j, front)
    acc[pl.ds(MOST, items - MOST)] = jnp.zeros((items - MOST, feats, span), jnp.float32)
    for k in range(items // MOST):
        places = [k * MOST + r if k == 0 else rows[2, k * MOST + r, 0] for r in range(MOST)]
        sums = []
        for r in range(MOST):
            j = k * MOST + r
            color = got[k, pl.ds(r * feats, feats), :].astype(jnp.float32)
            share = front[j : j + 1, :] * color
            sums.append(share if k == 0 else acc[places[r]] + share)
        for r in range(MOST):
            acc[places[r]] = sums[r]
    total_hi = total.astype(jnp.bfloat16).astype(jnp.float32)
    total_lo = total - total_hi
    groups = items // GROUP
    sub = lax.broadcasted_iota(jnp.int32, (16, span), 0)
    used = GROUP * feats
    xt[:, pl.ds(used, used)] = jnp.zeros((xt.shape[0], used), jnp.bfloat16)
    for q in range(groups):
        block = acc[pl.ds(q * GROUP, GROUP)].reshape(GROUP * feats, span)
        tail = jnp.zeros((16, span), jnp.float32)
        for a in range(GROUP):
            i = q * GROUP + a
            tail = jnp.where(sub == 2 * a, total_hi[i : i + 1, :], tail)
            tail = jnp.where(sub == 2 * a + 1, total_lo[i : i + 1, :], tail)
        lines = pl.ds(q * span, span)
        xt[lines, pl.ds(0, GROUP * feats)] = block.T.astype(jnp.bfloat16)
        xt[lines, pl.ds(GROUP * feats, 16)] = tail.T.astype(jnp.bfloat16)

    x = xt[...]
    stride = GROUP
    for start in range(0, GROUP, stride):
        h = jnp.concatenate(
            [
                silu_half(jnp.dot(x, w_first[a], preferred_element_type=jnp.float32))
                for a in range(start, start + stride)
            ]
        )
        y = later_layers(h, w_mid, w_out)
        for a in range(start, start + stride):
            for q in range(groups):
                at = ((a - start) * groups + q) * span
                ys[pl.ds((q * GROUP + a) * outs, outs), :] = y[:, at : at + span]
    out[pl.ds(0, items * outs), :] = ys[...].astype(jnp.bfloat16)
    out[pl.ds(items * outs, ROWS), :] = codes[...]


def join_kernel(*refs):
    *got, empty, strip, out, held, sems = refs
    _, n_strip, tile, outs, span = out.shape
    lines = tile * outs
    count = got[0].shape[0] - ROWS
    me = strip[0, 0]
    want = lax.broadcasted_iota(jnp.int32, (lines, count), 0) + strip[:1, :count] * lines
    chan = lax.broadcasted_iota(jnp.int32, (lines, count), 1) % outs
    filler = jnp.concatenate([empty[...]] * (lines // ROWS))
    ones = jnp.ones((count, span), jnp.bfloat16)
    copies = []
    for k in range(n_strip):
        pos = got[k][pl.ds(count, ROWS), :].astype(jnp.float32)[:1, :count].astype(jnp.int32)
        hit = pos * outs + chan == want
        pick = jnp.where(hit, 1.0, 0.0).astype(jnp.bfloat16)
        blocks = got[k][pl.ds(0, count), :]
        placed = jnp.dot(pick, blocks, preferred_element_type=jnp.float32)
        filled = jnp.dot(pick, ones, preferred_element_type=jnp.float32)
        value = jnp.where(filled > 0.5, placed, filler)
        held[k] = value.reshape(tile, outs, span).astype(jnp.bfloat16)
        copy = pltpu.make_async_copy(
            held.at[k], out.at[0, me ^ ((k + 1) % n_strip)], sems.at[k]
        )
        copy.start()
        copies.append(copy)
    for copy in copies:
        copy.wait()


def compact_device(
    n_slab,
    n_strip,
    colors,
    transmit,
    pair_counts,
    slot_block,
    assign,
    depth_rank,
    w_in,
    trans_weight,
    w_mid,
    w_out,
):
    slots, feats, span = colors.shape[2:]
    items = n_slab * MOST
    outs = w_out.shape[0]
    smem = pl.BlockSpec(memory_space=SMEM)
    vmem = pl.BlockSpec(memory_space=VMEM)
    hbm = pl.BlockSpec(memory_space=pltpu.HBM)
    held = functools.partial(pltpu.with_memory_space_constraint, memory_space=pltpu.HBM)
    small = pltpu.CompilerParams(vmem_limit_bytes=4 * 1024 * 1024)
    message = MOST * feats + ROWS
    sends = pl.pallas_call(
        pack_kernel,
        out_shape=jax.ShapeDtypeStruct((n_slab, message, span), jnp.bfloat16),
        in_specs=[hbm] * 3,
        out_specs=vmem,
        scratch_shapes=[
            pltpu.SMEM(pair_counts.shape, jnp.int32),
            pltpu.VMEM(colors.shape, colors.dtype),
            pltpu.VMEM(transmit.shape, transmit.dtype),
            pltpu.VMEM(transmit.shape[2:], jnp.float32),
            pltpu.SemaphoreType.DMA((3,)),
        ],
        compiler_params=small,
        name="pack",
    )(held(pair_counts), held(colors), held(transmit))
    group = exchange_order(n_slab)
    got = lax.all_to_all(
        sends, "slab", split_axis=0, concat_axis=0, axis_index_groups=[group], tiled=True
    )
    hidden = w_in.shape[0]
    rough = pl.CostEstimate(flops=10**5, bytes_accessed=10**6, transcendentals=0)
    roomy = pltpu.CompilerParams(vmem_limit_bytes=16 * 1024 * 1024)
    trans_row = trans_weight[None]
    rows, codes, strip = pl.pallas_call(
        functools.partial(plan_kernel, n_slab, slots),
        out_shape=[
            jax.ShapeDtypeStruct((3, items, span), jnp.int32),
            jax.ShapeDtypeStruct((ROWS, span), jnp.bfloat16),
            jax.ShapeDtypeStruct((ROWS, span), jnp.int32),
        ],
        in_specs=[smem] * 4,
        out_specs=[vmem] * 3,
        compiler_params=small,
        cost_estimate=rough,
        name="plan",
    )(pair_counts, slot_block, assign, depth_rank)
    w_first, w_last, w_later = pl.pallas_call(
        place_kernel,
        out_shape=[
            jax.ShapeDtypeStruct((GROUP, 2 * GROUP * feats, hidden), jnp.bfloat16),
            jax.ShapeDtypeStruct(w_out.shape, jnp.bfloat16),
            jax.ShapeDtypeStruct(w_mid.shape, jnp.bfloat16),
        ],
        in_specs=[vmem] * 3 + [hbm],
        out_specs=[vmem] * 3,
        scratch_shapes=[
            pltpu.VMEM(w_mid.shape, jnp.bfloat16),
            pltpu.SemaphoreType.DMA((1,)),
        ],
        compiler_params=small,
        cost_estimate=rough,
        name="place",
    )(w_in.T, trans_row, w_out, held(w_mid))
    empty = pl.pallas_call(
        empty_kernel,
        out_shape=jax.ShapeDtypeStruct((ROWS, span), jnp.float32),
        in_specs=[vmem] * 3,
        out_specs=vmem,
        compiler_params=roomy,
        cost_estimate=rough,
        name="empty",
    )(trans_row, w_later, w_last)
    shaded = pl.pallas_call(
        shade_kernel,
        out_shape=jax.ShapeDtypeStruct((items * outs + ROWS, span), jnp.bfloat16),
        in_specs=[vmem] * 6,
        out_specs=vmem,
        scratch_shapes=[
            pltpu.VMEM((items, feats, span), jnp.float32),
            pltpu.VMEM((items // GROUP * span, 2 * GROUP * feats), jnp.bfloat16),
            pltpu.VMEM((items * outs, span), jnp.float32),
        ],
        compiler_params=roomy,
        name="shade",
    )(rows, codes, got, w_first, w_later, w_last)
    tiles = [
        lax.ppermute(shaded, "strip", [(s, s ^ k) for s in range(n_strip)])
        for k in range(1, n_strip)
    ] + [shaded]
    return pl.pallas_call(
        join_kernel,
        out_shape=jax.ShapeDtypeStruct((1, n_strip, LB // n_strip, outs, span), jnp.bfloat16),
        in_specs=[vmem] * (n_strip + 2),
        out_specs=pl.BlockSpec(memory_space=pl.ANY),
        scratch_shapes=[
            pltpu.VMEM((n_strip, LB // n_strip, outs, span), jnp.bfloat16),
            pltpu.SemaphoreType.DMA((n_strip,)),
        ],
        compiler_params=small,
        name="join",
    )(*tiles, empty, strip)


def solution(mesh):
    n_slab, n_strip = mesh.shape["slab"], mesh.shape["strip"]
    placed = (
        P("slab", "strip", None, None, None),
        P("slab", "strip", None, None),
        P("strip", None, None),
        P("strip", None, None),
        P("strip", None),
        P(),
        P(),
        P(),
        P(),
        P(),
    )
    compact = n_strip & (n_strip - 1) == 0 and 4 * MOST * n_slab <= LB
    return jax.shard_map(
        functools.partial(compact_device, n_slab, n_strip) if compact else dense_device,
        mesh=mesh,
        in_specs=placed,
        out_specs=P("slab", None, "strip", None, None),
        check_vma=False,
    )
```

```python
import functools

import jax
import jax.numpy as jnp
from jax import lax
from jax.experimental import pallas as pl
from jax.experimental.pallas import tpu as pltpu
from jax.sharding import PartitionSpec as P

MOST = 2
LB = 128


EXACT_PRECISION = lax.Precision.HIGHEST


def shade_blocks(blend_color, trans_field, w_in, trans_weight, w_mid, w_out):
    summed = jnp.einsum("hf,lfp->lhp", w_in, blend_color, preferred_element_type=jnp.float32)
    summed = summed + trans_weight.astype(jnp.float32)[None, :, None] * trans_field[:, None, :]
    hidden = jax.nn.silu(summed).astype(jnp.bfloat16)
    for layer_index in range(w_mid.shape[0]):
        hidden = jax.nn.silu(
            jnp.einsum(
                "hg,lgp->lhp", w_mid[layer_index], hidden, preferred_element_type=jnp.float32
            )
        ).astype(jnp.bfloat16)
    return jnp.einsum("oh,lhp->lop", w_out, hidden, preferred_element_type=jnp.float32).astype(
        jnp.bfloat16
    )


def dense_device(
    colors, transmit, pair_counts, slot_block, assign, depth_rank, w_in, trans_weight, w_mid, w_out
):
    myself = lax.axis_index("slab")
    counts = pair_counts[0]
    blocks_all = slot_block[0]
    assign_row = assign[0]
    offsets = jnp.cumsum(counts, axis=1) - counts
    slot_rank = jnp.arange(MOST, dtype=jnp.int32)
    my_counts = lax.dynamic_index_in_dim(counts, myself, 0, keepdims=False)
    my_offsets = lax.dynamic_index_in_dim(offsets, myself, 0, keepdims=False)
    send_slots = jnp.where(
        slot_rank[None, :] < my_counts[:, None], my_offsets[:, None] + slot_rank[None, :], 0
    )
    send_color = colors[0, 0][send_slots]
    send_trans = transmit[0, 0][send_slots][:, :, None, :]
    incoming = lax.dynamic_index_in_dim(counts, myself, 1, keepdims=False)
    in_offsets = lax.dynamic_index_in_dim(offsets, myself, 1, keepdims=False)
    live_slot = slot_rank[None, :] < incoming[:, None]
    recv_slots = jnp.where(live_slot, in_offsets[:, None] + slot_rank[None, :], 0)
    recv_blocks = jnp.take_along_axis(blocks_all, recv_slots, axis=1)
    local_pos = assign_row[recv_blocks] - myself * LB
    live_flat = live_slot.reshape(-1)
    local_flat = jnp.where(live_flat, local_pos.reshape(-1), -1)
    depth_flat = jnp.repeat(depth_rank, MOST)
    ahead_table = (
        (local_flat[:, None] == local_flat[None, :])
        & (depth_flat[None, :] < depth_flat[:, None])
        & live_flat[None, :]
    )
    ahead_table = ahead_table.astype(jnp.float32)
    owner_table = (jnp.arange(LB, dtype=jnp.int32)[:, None] == local_flat[None, :]).astype(
        jnp.float32
    )
    got_color = lax.all_to_all(send_color, "slab", split_axis=0, concat_axis=0, tiled=True)
    got_trans = lax.all_to_all(send_trans, "slab", split_axis=0, concat_axis=0, tiled=True)
    pixel_count = got_color.shape[3]
    item_count = got_color.shape[0] * got_color.shape[1]
    log_trans = jnp.log(got_trans.reshape(item_count, pixel_count).astype(jnp.float32))
    log_trans = jnp.where(live_flat[:, None], log_trans, 0.0)
    front_log = jnp.dot(ahead_table, log_trans, precision=EXACT_PRECISION)
    front_share = jnp.where(live_flat[:, None], jnp.exp(front_log), 0.0)
    weighted = front_share[:, None, :] * got_color.reshape(item_count, -1, pixel_count).astype(
        jnp.float32
    )
    blend_sum = jnp.dot(owner_table, weighted.reshape(item_count, -1), precision=EXACT_PRECISION)
    blend_color = blend_sum.reshape(LB, -1, pixel_count).astype(jnp.bfloat16)
    trans_field = jnp.exp(jnp.dot(owner_table, log_trans, precision=EXACT_PRECISION))
    shaded = shade_blocks(blend_color, trans_field, w_in, trans_weight, w_mid, w_out)
    display_tiles = lax.all_to_all(shaded[None], "strip", split_axis=1, concat_axis=0, tiled=True)
    return display_tiles[None]


SMEM = pltpu.SMEM
VMEM = pltpu.VMEM
ROWS = 8
GROUP = 4


def exchange_order(n_slab):
    half = n_slab // 2
    back = [half] + list(range(n_slab - 1, half, -1))
    front = list(range(half - 2)) + [half - 1, half - 2] if half > 1 else [0]
    return [s for pair in zip(back, front) for s in pair]


def pack_kernel(far_counts, far_colors, far_transmit, sends, counts, colors, transmit, tall, sems):
    n_slab = sends.shape[0]
    order = exchange_order(n_slab)
    slots, feats, span = colors.shape[2:]
    copies = [
        pltpu.make_async_copy(far, near, sems.at[i])
        for i, (far, near) in enumerate(
            ((far_counts, counts), (far_colors, colors), (far_transmit, transmit))
        )
    ]
    for copy in copies:
        copy.start()
    me = lax.axis_index("slab")
    for copy in copies:
        copy.wait()
    tall[...] = transmit[0, 0].astype(jnp.float32)
    row = lax.broadcasted_iota(jnp.int32, (ROWS, span), 0)
    off = jnp.int32(0)
    for c in range(n_slab):
        at = order.index(c)
        tail = jnp.ones((ROWS, span), jnp.float32)
        for r in range(MOST):
            slot = jnp.minimum(off + r, slots - 1)
            sends[at, pl.ds(r * feats, feats), :] = colors[0, 0, slot]
            tail = jnp.where(row == r, tall[pl.ds(slot, 1), :], tail)
        sends[at, pl.ds(MOST * feats, ROWS), :] = tail.astype(jnp.bfloat16)
        off = off + counts[0, me, c]


def plan_kernel(n_slab, slots, *refs):
    far, (rows, codes, strip) = refs[:4], refs[4:7]
    near, sems = refs[7:11], refs[11]
    counts, blocks, assign, depth = near
    copies = [pltpu.make_async_copy(far[i], near[i], sems.at[i]) for i in range(4)]
    for copy in copies:
        copy.start()
    strip[...] = jnp.full(strip.shape, lax.axis_index("strip"), jnp.int32)
    items = n_slab * MOST
    outs = codes.shape[1] // (2 * items)
    me = lax.axis_index("slab")
    row = lax.broadcasted_iota(jnp.int32, rows.shape[1:], 0)
    item_lane = lax.broadcasted_iota(jnp.int32, codes.shape, 1) // outs
    posv = jnp.zeros(rows.shape[1:], jnp.int32)
    depthv = jnp.zeros(rows.shape[1:], jnp.int32)
    firstv = jnp.zeros(rows.shape[1:], jnp.int32)
    codev = jnp.full(codes.shape, -1, jnp.int32)
    for copy in copies:
        copy.wait()
    pos = []
    for k, s in enumerate(exchange_order(n_slab)):
        off = jnp.int32(0)
        for c in range(n_slab):
            off = off + jnp.where(c < me, counts[0, s, c], 0)
        count = counts[0, s, me]
        for r in range(MOST):
            i = k * MOST + r
            slot = jnp.minimum(off + r, slots - 1)
            here = assign[0, blocks[0, s, slot]] - me * LB
            here = jnp.where(r < count, here, -1)
            first = jnp.int32(i)
            for j in reversed(range(i)):
                first = jnp.where(pos[j] == here, j, first)
            pos.append(here)
            firstv = jnp.where(row == i, first, firstv)
            posv = jnp.where(row == i, here, posv)
            depthv = jnp.where(row == i, depth[s], depthv)
            codev = jnp.where(item_lane == i, jnp.where(first == i, here, -1), codev)
    rows[0] = posv
    rows[1] = depthv
    rows[2] = firstv
    codes[...] = codev.astype(jnp.float32).astype(jnp.bfloat16)


def place_kernel(w_in, trans_weight, far_out, far_mid, w_first, w_out, w_later, w_mid, sems):
    copy = pltpu.make_async_copy(far_mid, w_mid, sems.at[0])
    copy.start()
    feats, hidden = w_in.shape
    half_in = (w_in[...].astype(jnp.float32) * 0.5).astype(jnp.bfloat16)
    half_trans = trans_weight[...].astype(jnp.float32) * 0.5
    sub = lax.broadcasted_iota(jnp.int32, (16, hidden), 0)
    w_first[...] = jnp.zeros_like(w_first)
    for a in range(GROUP):
        w_first[a, pl.ds(a * feats, feats), :] = half_in
        tail = jnp.where(sub // 2 == a, half_trans, 0.0)
        w_first[a, pl.ds(GROUP * feats, 16), :] = tail.astype(jnp.bfloat16)
    w_out[...] = far_out[...]
    copy.wait()
    for m in range(w_mid.shape[0]):
        w_later[m] = (w_mid[m].astype(jnp.float32).T * 0.5).astype(jnp.bfloat16)


def silu_half(u):
    return (u + u * jnp.tanh(u)).astype(jnp.bfloat16)


def later_layers(h, w_mid, w_out):
    for m in range(w_mid.shape[0]):
        h = silu_half(jnp.dot(h, w_mid[m], preferred_element_type=jnp.float32))
    y = lax.dot_general(
        w_out[...], h, (((1,), (1,)), ((), ())), preferred_element_type=jnp.float32
    )
    return y.astype(jnp.bfloat16).astype(jnp.float32)


def empty_kernel(trans_weight, w_mid, w_out, out):
    u = trans_weight[...].astype(jnp.float32) * 0.5
    h = silu_half(jnp.broadcast_to(u, (out.shape[1], u.shape[1])))
    y = later_layers(h, w_mid, w_out)
    outs = w_out.shape[0]
    for at in range(0, out.shape[0], outs):
        out[pl.ds(at, outs), :] = y


def shade_kernel(rows, codes, got, w_first, w_mid, w_out, out, acc, xt, ys):
    items, feats, span = acc.shape
    outs = w_out.shape[0]

    posv, depthv = rows[0], rows[1]
    front = jnp.ones((items, span), jnp.float32)
    total = jnp.ones((items, span), jnp.float32)
    for k in range(items // MOST):
        tail = got[k, pl.ds(MOST * feats, ROWS), :].astype(jnp.float32)
        for r in range(MOST):
            j = k * MOST + r
            trans_j = tail[r : r + 1, :]
            same = posv == posv[j : j + 1, :]
            total = jnp.where(same, total * trans_j, total)
            front = jnp.where(same & (depthv > depthv[j : j + 1, :]), front * trans_j, front)
    acc[pl.ds(MOST, items - MOST)] = jnp.zeros((items - MOST, feats, span), jnp.float32)
    for k in range(items // MOST):
        places = [k * MOST + r if k == 0 else rows[2, k * MOST + r, 0] for r in range(MOST)]
        sums = []
        for r in range(MOST):
            j = k * MOST + r
            color = got[k, pl.ds(r * feats, feats), :].astype(jnp.float32)
            share = front[j : j + 1, :] * color
            sums.append(share if k == 0 else acc[places[r]] + share)
        for r in range(MOST):
            acc[places[r]] = sums[r]
    total_hi = total.astype(jnp.bfloat16).astype(jnp.float32)
    total_lo = total - total_hi
    groups = items // GROUP
    sub = lax.broadcasted_iota(jnp.int32, (16, span), 0)
    used = GROUP * feats
    xt[:, pl.ds(used, used)] = jnp.zeros((xt.shape[0], used), jnp.bfloat16)
    for q in range(groups):
        block = acc[pl.ds(q * GROUP, GROUP)].reshape(GROUP * feats, span)
        tail = jnp.zeros((16, span), jnp.float32)
        for a in range(GROUP):
            i = q * GROUP + a
            tail = jnp.where(sub == 2 * a, total_hi[i : i + 1, :], tail)
            tail = jnp.where(sub == 2 * a + 1, total_lo[i : i + 1, :], tail)
        lines = pl.ds(q * span, span)
        xt[lines, pl.ds(0, GROUP * feats)] = block.T.astype(jnp.bfloat16)
        xt[lines, pl.ds(GROUP * feats, 16)] = tail.T.astype(jnp.bfloat16)

    x = xt[...]
    stride = GROUP // 2
    for start in range(0, GROUP, stride):
        h = jnp.concatenate(
            [
                silu_half(jnp.dot(x, w_first[a], preferred_element_type=jnp.float32))
                for a in range(start, start + stride)
            ]
        )
        y = later_layers(h, w_mid, w_out)
        for a in range(start, start + stride):
            for q in range(groups):
                at = ((a - start) * groups + q) * span
                ys[pl.ds((q * GROUP + a) * outs, outs), :] = y[:, at : at + span]
    out[pl.ds(0, items * outs), :] = ys[...].astype(jnp.bfloat16)
    out[pl.ds(items * outs, ROWS), :] = codes[...]


def join_kernel(*refs):
    *got, empty, strip, out, held, sems = refs
    _, n_strip, tile, outs, span = out.shape
    lines = tile * outs
    count = got[0].shape[0] - ROWS
    me = strip[0, 0]
    want = lax.broadcasted_iota(jnp.int32, (lines, count), 0) + strip[:1, :count] * lines
    chan = lax.broadcasted_iota(jnp.int32, (lines, count), 1) % outs
    filler = jnp.concatenate([empty[...]] * (lines // ROWS))
    ones = jnp.ones((count, span), jnp.bfloat16)
    copies = []
    for k in range(n_strip):
        pos = got[k][pl.ds(count, ROWS), :].astype(jnp.float32)[:1, :count].astype(jnp.int32)
        hit = pos * outs + chan == want
        pick = jnp.where(hit, 1.0, 0.0).astype(jnp.bfloat16)
        blocks = got[k][pl.ds(0, count), :]
        placed = jnp.dot(pick, blocks, preferred_element_type=jnp.float32)
        filled = jnp.dot(pick, ones, preferred_element_type=jnp.float32)
        value = jnp.where(filled > 0.5, placed, filler)
        held[k] = value.reshape(tile, outs, span).astype(jnp.bfloat16)
        copy = pltpu.make_async_copy(
            held.at[k], out.at[0, me ^ ((k + 1) % n_strip)], sems.at[k]
        )
        copy.start()
        copies.append(copy)
    for copy in copies:
        copy.wait()


def compact_device(
    n_slab,
    n_strip,
    colors,
    transmit,
    pair_counts,
    slot_block,
    assign,
    depth_rank,
    w_in,
    trans_weight,
    w_mid,
    w_out,
):
    slots, feats, span = colors.shape[2:]
    items = n_slab * MOST
    outs = w_out.shape[0]
    smem = pl.BlockSpec(memory_space=SMEM)
    vmem = pl.BlockSpec(memory_space=VMEM)
    hbm = pl.BlockSpec(memory_space=pltpu.HBM)
    held = functools.partial(pltpu.with_memory_space_constraint, memory_space=pltpu.HBM)
    small = pltpu.CompilerParams(vmem_limit_bytes=4 * 1024 * 1024)
    message = MOST * feats + ROWS
    sends = pl.pallas_call(
        pack_kernel,
        out_shape=jax.ShapeDtypeStruct((n_slab, message, span), jnp.bfloat16),
        in_specs=[hbm] * 3,
        out_specs=vmem,
        scratch_shapes=[
            pltpu.SMEM(pair_counts.shape, jnp.int32),
            pltpu.VMEM(colors.shape, colors.dtype),
            pltpu.VMEM(transmit.shape, transmit.dtype),
            pltpu.VMEM(transmit.shape[2:], jnp.float32),
            pltpu.SemaphoreType.DMA((3,)),
        ],
        compiler_params=small,
        name="pack",
    )(held(pair_counts), held(colors), held(transmit))
    group = exchange_order(n_slab)
    got = lax.all_to_all(
        sends, "slab", split_axis=0, concat_axis=0, axis_index_groups=[group], tiled=True
    )
    hidden = w_in.shape[0]
    rough = pl.CostEstimate(flops=10**5, bytes_accessed=10**6, transcendentals=0)
    roomy = pltpu.CompilerParams(vmem_limit_bytes=16 * 1024 * 1024)
    trans_row = trans_weight[None]
    rows, codes, strip = pl.pallas_call(
        functools.partial(plan_kernel, n_slab, slots),
        out_shape=[
            jax.ShapeDtypeStruct((3, items, span), jnp.int32),
            jax.ShapeDtypeStruct((ROWS, span), jnp.bfloat16),
            jax.ShapeDtypeStruct((ROWS, span), jnp.int32),
        ],
        in_specs=[hbm] * 4,
        out_specs=[vmem] * 3,
        scratch_shapes=[
            pltpu.SMEM(a.shape, jnp.int32) for a in (pair_counts, slot_block, assign, depth_rank)
        ]
        + [pltpu.SemaphoreType.DMA((4,))],
        compiler_params=small,
        cost_estimate=rough,
        name="plan",
    )(held(pair_counts), held(slot_block), held(assign), held(depth_rank))
    w_first, w_last, w_later = pl.pallas_call(
        place_kernel,
        out_shape=[
            jax.ShapeDtypeStruct((GROUP, 2 * GROUP * feats, hidden), jnp.bfloat16),
            jax.ShapeDtypeStruct(w_out.shape, jnp.bfloat16),
            jax.ShapeDtypeStruct(w_mid.shape, jnp.bfloat16),
        ],
        in_specs=[vmem] * 3 + [hbm],
        out_specs=[vmem] * 3,
        scratch_shapes=[
            pltpu.VMEM(w_mid.shape, jnp.bfloat16),
            pltpu.SemaphoreType.DMA((1,)),
        ],
        compiler_params=small,
        cost_estimate=rough,
        name="place",
    )(w_in.T, trans_row, w_out, held(w_mid))
    empty = pl.pallas_call(
        empty_kernel,
        out_shape=jax.ShapeDtypeStruct((ROWS, span), jnp.float32),
        in_specs=[vmem] * 3,
        out_specs=vmem,
        compiler_params=roomy,
        cost_estimate=rough,
        name="empty",
    )(trans_row, w_later, w_last)
    shaded = pl.pallas_call(
        shade_kernel,
        out_shape=jax.ShapeDtypeStruct((items * outs + ROWS, span), jnp.bfloat16),
        in_specs=[vmem] * 6,
        out_specs=vmem,
        scratch_shapes=[
            pltpu.VMEM((items, feats, span), jnp.float32),
            pltpu.VMEM((items // GROUP * span, 2 * GROUP * feats), jnp.bfloat16),
            pltpu.VMEM((items * outs, span), jnp.float32),
        ],
        compiler_params=roomy,
        name="shade",
    )(rows, codes, got, w_first, w_later, w_last)
    tiles = [
        lax.ppermute(shaded, "strip", [(s, s ^ k) for s in range(n_strip)])
        for k in range(1, n_strip)
    ] + [shaded]
    return pl.pallas_call(
        join_kernel,
        out_shape=jax.ShapeDtypeStruct((1, n_strip, LB // n_strip, outs, span), jnp.bfloat16),
        in_specs=[vmem] * (n_strip + 2),
        out_specs=pl.BlockSpec(memory_space=pl.ANY),
        scratch_shapes=[
            pltpu.VMEM((n_strip, LB // n_strip, outs, span), jnp.bfloat16),
            pltpu.SemaphoreType.DMA((n_strip,)),
        ],
        compiler_params=small,
        name="join",
    )(*tiles, empty, strip)


def solution(mesh):
    n_slab, n_strip = mesh.shape["slab"], mesh.shape["strip"]
    placed = (
        P("slab", "strip", None, None, None),
        P("slab", "strip", None, None),
        P("strip", None, None),
        P("strip", None, None),
        P("strip", None),
        P(),
        P(),
        P(),
        P(),
        P(),
    )
    compact = n_strip & (n_strip - 1) == 0 and 4 * MOST * n_slab <= LB
    return jax.shard_map(
        functools.partial(compact_device, n_slab, n_strip) if compact else dense_device,
        mesh=mesh,
        in_specs=placed,
        out_specs=P("slab", None, "strip", None, None),
        check_vma=False,
    )
```

```python
import functools

import jax
import jax.numpy as jnp
from jax import lax
from jax.experimental import pallas as pl
from jax.experimental.pallas import tpu as pltpu
from jax.sharding import PartitionSpec as P

MOST = 2
LB = 128


EXACT_PRECISION = lax.Precision.HIGHEST


def shade_blocks(blend_color, trans_field, w_in, trans_weight, w_mid, w_out):
    summed = jnp.einsum("hf,lfp->lhp", w_in, blend_color, preferred_element_type=jnp.float32)
    summed = summed + trans_weight.astype(jnp.float32)[None, :, None] * trans_field[:, None, :]
    hidden = jax.nn.silu(summed).astype(jnp.bfloat16)
    for layer_index in range(w_mid.shape[0]):
        hidden = jax.nn.silu(
            jnp.einsum(
                "hg,lgp->lhp", w_mid[layer_index], hidden, preferred_element_type=jnp.float32
            )
        ).astype(jnp.bfloat16)
    return jnp.einsum("oh,lhp->lop", w_out, hidden, preferred_element_type=jnp.float32).astype(
        jnp.bfloat16
    )


def dense_device(
    colors, transmit, pair_counts, slot_block, assign, depth_rank, w_in, trans_weight, w_mid, w_out
):
    myself = lax.axis_index("slab")
    counts = pair_counts[0]
    blocks_all = slot_block[0]
    assign_row = assign[0]
    offsets = jnp.cumsum(counts, axis=1) - counts
    slot_rank = jnp.arange(MOST, dtype=jnp.int32)
    my_counts = lax.dynamic_index_in_dim(counts, myself, 0, keepdims=False)
    my_offsets = lax.dynamic_index_in_dim(offsets, myself, 0, keepdims=False)
    send_slots = jnp.where(
        slot_rank[None, :] < my_counts[:, None], my_offsets[:, None] + slot_rank[None, :], 0
    )
    send_color = colors[0, 0][send_slots]
    send_trans = transmit[0, 0][send_slots][:, :, None, :]
    incoming = lax.dynamic_index_in_dim(counts, myself, 1, keepdims=False)
    in_offsets = lax.dynamic_index_in_dim(offsets, myself, 1, keepdims=False)
    live_slot = slot_rank[None, :] < incoming[:, None]
    recv_slots = jnp.where(live_slot, in_offsets[:, None] + slot_rank[None, :], 0)
    recv_blocks = jnp.take_along_axis(blocks_all, recv_slots, axis=1)
    local_pos = assign_row[recv_blocks] - myself * LB
    live_flat = live_slot.reshape(-1)
    local_flat = jnp.where(live_flat, local_pos.reshape(-1), -1)
    depth_flat = jnp.repeat(depth_rank, MOST)
    ahead_table = (
        (local_flat[:, None] == local_flat[None, :])
        & (depth_flat[None, :] < depth_flat[:, None])
        & live_flat[None, :]
    )
    ahead_table = ahead_table.astype(jnp.float32)
    owner_table = (jnp.arange(LB, dtype=jnp.int32)[:, None] == local_flat[None, :]).astype(
        jnp.float32
    )
    got_color = lax.all_to_all(send_color, "slab", split_axis=0, concat_axis=0, tiled=True)
    got_trans = lax.all_to_all(send_trans, "slab", split_axis=0, concat_axis=0, tiled=True)
    pixel_count = got_color.shape[3]
    item_count = got_color.shape[0] * got_color.shape[1]
    log_trans = jnp.log(got_trans.reshape(item_count, pixel_count).astype(jnp.float32))
    log_trans = jnp.where(live_flat[:, None], log_trans, 0.0)
    front_log = jnp.dot(ahead_table, log_trans, precision=EXACT_PRECISION)
    front_share = jnp.where(live_flat[:, None], jnp.exp(front_log), 0.0)
    weighted = front_share[:, None, :] * got_color.reshape(item_count, -1, pixel_count).astype(
        jnp.float32
    )
    blend_sum = jnp.dot(owner_table, weighted.reshape(item_count, -1), precision=EXACT_PRECISION)
    blend_color = blend_sum.reshape(LB, -1, pixel_count).astype(jnp.bfloat16)
    trans_field = jnp.exp(jnp.dot(owner_table, log_trans, precision=EXACT_PRECISION))
    shaded = shade_blocks(blend_color, trans_field, w_in, trans_weight, w_mid, w_out)
    display_tiles = lax.all_to_all(shaded[None], "strip", split_axis=1, concat_axis=0, tiled=True)
    return display_tiles[None]


SMEM = pltpu.SMEM
VMEM = pltpu.VMEM
ROWS = 8
GROUP = 4


def exchange_order(n_slab):
    half = n_slab // 2
    back = [half] + list(range(n_slab - 1, half, -1))
    front = list(range(half - 2)) + [half - 1, half - 2] if half > 1 else [0]
    return [s for pair in zip(back, front) for s in pair]


def pack_kernel(far_counts, far_colors, far_transmit, sends, counts, colors, transmit, tall, sems):
    n_slab = sends.shape[0]
    order = exchange_order(n_slab)
    slots, feats, span = colors.shape[2:]
    copies = [
        pltpu.make_async_copy(far, near, sems.at[i])
        for i, (far, near) in enumerate(
            ((far_counts, counts), (far_colors, colors), (far_transmit, transmit))
        )
    ]
    for copy in copies:
        copy.start()
    me = lax.axis_index("slab")
    for copy in copies:
        copy.wait()
    tall[...] = transmit[0, 0].astype(jnp.float32)
    row = lax.broadcasted_iota(jnp.int32, (ROWS, span), 0)
    off = jnp.int32(0)
    for c in range(n_slab):
        at = order.index(c)
        tail = jnp.ones((ROWS, span), jnp.float32)
        for r in range(MOST):
            slot = jnp.minimum(off + r, slots - 1)
            sends[at, pl.ds(r * feats, feats), :] = colors[0, 0, slot]
            tail = jnp.where(row == r, tall[pl.ds(slot, 1), :], tail)
        sends[at, pl.ds(MOST * feats, ROWS), :] = tail.astype(jnp.bfloat16)
        off = off + counts[0, me, c]


def plan_kernel(n_slab, slots, *refs):
    far, (rows, codes, strip) = refs[:4], refs[4:7]
    near, sems = refs[7:11], refs[11]
    counts, blocks, assign, depth = near
    copies = [pltpu.make_async_copy(far[i], near[i], sems.at[i]) for i in range(4)]
    for copy in copies:
        copy.start()
    strip[...] = jnp.full(strip.shape, lax.axis_index("strip"), jnp.int32)
    items = n_slab * MOST
    outs = codes.shape[1] // (2 * items)
    me = lax.axis_index("slab")
    row = lax.broadcasted_iota(jnp.int32, rows.shape[1:], 0)
    item_lane = lax.broadcasted_iota(jnp.int32, codes.shape, 1) // outs
    posv = jnp.zeros(rows.shape[1:], jnp.int32)
    depthv = jnp.zeros(rows.shape[1:], jnp.int32)
    firstv = jnp.zeros(rows.shape[1:], jnp.int32)
    codev = jnp.full(codes.shape, -1, jnp.int32)
    for copy in copies:
        copy.wait()
    pos = []
    for k, s in enumerate(exchange_order(n_slab)):
        off = jnp.int32(0)
        for c in range(n_slab):
            off = off + jnp.where(c < me, counts[0, s, c], 0)
        count = counts[0, s, me]
        for r in range(MOST):
            i = k * MOST + r
            slot = jnp.minimum(off + r, slots - 1)
            here = assign[0, blocks[0, s, slot]] - me * LB
            here = jnp.where(r < count, here, -1)
            first = jnp.int32(i)
            for j in reversed(range(i)):
                first = jnp.where(pos[j] == here, j, first)
            pos.append(here)
            firstv = jnp.where(row == i, first, firstv)
            posv = jnp.where(row == i, here, posv)
            depthv = jnp.where(row == i, depth[s], depthv)
            codev = jnp.where(item_lane == i, jnp.where(first == i, here, -1), codev)
    rows[0] = posv
    rows[1] = depthv
    rows[2] = firstv
    codes[...] = codev.astype(jnp.float32).astype(jnp.bfloat16)


def place_kernel(w_in, trans_weight, far_out, far_mid, w_first, w_out, w_later, w_mid, sems):
    copy = pltpu.make_async_copy(far_mid, w_mid, sems.at[0])
    copy.start()
    feats, hidden = w_in.shape
    half_in = (w_in[...].astype(jnp.float32) * 0.5).astype(jnp.bfloat16)
    half_trans = trans_weight[...].astype(jnp.float32) * 0.5
    sub = lax.broadcasted_iota(jnp.int32, (16, hidden), 0)
    w_first[...] = jnp.zeros_like(w_first)
    for a in range(GROUP):
        w_first[a, pl.ds(a * feats, feats), :] = half_in
        tail = jnp.where(sub // 2 == a, half_trans, 0.0)
        w_first[a, pl.ds(GROUP * feats, 16), :] = tail.astype(jnp.bfloat16)
    w_out[...] = far_out[...]
    copy.wait()
    for m in range(w_mid.shape[0]):
        w_later[m] = (w_mid[m].astype(jnp.float32).T * 0.5).astype(jnp.bfloat16)


def silu_half(u):
    return (u + u * jnp.tanh(u)).astype(jnp.bfloat16)


def later_layers(h, w_mid, w_out):
    for m in range(w_mid.shape[0]):
        h = silu_half(jnp.dot(h, w_mid[m], preferred_element_type=jnp.float32))
    y = lax.dot_general(
        w_out[...], h, (((1,), (1,)), ((), ())), preferred_element_type=jnp.float32
    )
    return y.astype(jnp.bfloat16).astype(jnp.float32)


def empty_kernel(trans_weight, w_mid, w_out, out):
    u = trans_weight[...].astype(jnp.float32) * 0.5
    h = silu_half(jnp.broadcast_to(u, (out.shape[1], u.shape[1])))
    y = later_layers(h, w_mid, w_out)
    outs = w_out.shape[0]
    for at in range(0, out.shape[0], outs):
        out[pl.ds(at, outs), :] = y


def shade_kernel(rows, codes, got, w_first, w_mid, w_out, out, acc, xt, ys):
    items, feats, span = acc.shape
    outs = w_out.shape[0]

    posv, depthv = rows[0], rows[1]
    front = jnp.ones((items, span), jnp.float32)
    total = jnp.ones((items, span), jnp.float32)
    for k in range(items // MOST):
        tail = got[k, pl.ds(MOST * feats, ROWS), :].astype(jnp.float32)
        for r in range(MOST):
            j = k * MOST + r
            trans_j = tail[r : r + 1, :]
            same = posv == posv[j : j + 1, :]
            total = jnp.where(same, total * trans_j, total)
            front = jnp.where(same & (depthv > depthv[j : j + 1, :]), front * trans_j, front)
    acc[pl.ds(MOST, items - MOST)] = jnp.zeros((items - MOST, feats, span), jnp.float32)
    for k in range(items // MOST):
        places = [k * MOST + r if k == 0 else rows[2, k * MOST + r, 0] for r in range(MOST)]
        sums = []
        for r in range(MOST):
            j = k * MOST + r
            color = got[k, pl.ds(r * feats, feats), :].astype(jnp.float32)
            share = front[j : j + 1, :] * color
            sums.append(share if k == 0 else acc[places[r]] + share)
        for r in range(MOST):
            acc[places[r]] = sums[r]
    total_hi = total.astype(jnp.bfloat16).astype(jnp.float32)
    total_lo = total - total_hi
    groups = items // GROUP
    sub = lax.broadcasted_iota(jnp.int32, (16, span), 0)
    used = GROUP * feats
    xt[:, pl.ds(used, used)] = jnp.zeros((xt.shape[0], used), jnp.bfloat16)
    for q in range(groups):
        block = acc[pl.ds(q * GROUP, GROUP)].reshape(GROUP * feats, span)
        tail = jnp.zeros((16, span), jnp.float32)
        for a in range(GROUP):
            i = q * GROUP + a
            tail = jnp.where(sub == 2 * a, total_hi[i : i + 1, :], tail)
            tail = jnp.where(sub == 2 * a + 1, total_lo[i : i + 1, :], tail)
        lines = pl.ds(q * span, span)
        xt[lines, pl.ds(0, GROUP * feats)] = block.T.astype(jnp.bfloat16)
        xt[lines, pl.ds(GROUP * feats, 16)] = tail.T.astype(jnp.bfloat16)

    x = xt[...]
    stride = GROUP
    for start in range(0, GROUP, stride):
        h = jnp.concatenate(
            [
                silu_half(jnp.dot(x, w_first[a], preferred_element_type=jnp.float32))
                for a in range(start, start + stride)
            ]
        )
        y = later_layers(h, w_mid, w_out)
        for a in range(start, start + stride):
            for q in range(groups):
                at = ((a - start) * groups + q) * span
                ys[pl.ds((q * GROUP + a) * outs, outs), :] = y[:, at : at + span]
    out[pl.ds(0, items * outs), :] = ys[...].astype(jnp.bfloat16)
    out[pl.ds(items * outs, ROWS), :] = codes[...]


def join_kernel(*refs):
    *got, empty, strip, out, held, sems = refs
    _, n_strip, tile, outs, span = out.shape
    lines = tile * outs
    count = got[0].shape[0] - ROWS
    me = strip[0, 0]
    want = lax.broadcasted_iota(jnp.int32, (lines, count), 0) + strip[:1, :count] * lines
    chan = lax.broadcasted_iota(jnp.int32, (lines, count), 1) % outs
    filler = jnp.concatenate([empty[...]] * (lines // ROWS))
    ones = jnp.ones((count, span), jnp.bfloat16)
    copies = []
    for k in range(n_strip):
        pos = got[k][pl.ds(count, ROWS), :].astype(jnp.float32)[:1, :count].astype(jnp.int32)
        hit = pos * outs + chan == want
        pick = jnp.where(hit, 1.0, 0.0).astype(jnp.bfloat16)
        blocks = got[k][pl.ds(0, count), :]
        placed = jnp.dot(pick, blocks, preferred_element_type=jnp.float32)
        filled = jnp.dot(pick, ones, preferred_element_type=jnp.float32)
        value = jnp.where(filled > 0.5, placed, filler)
        held[k] = value.reshape(tile, outs, span).astype(jnp.bfloat16)
        copy = pltpu.make_async_copy(
            held.at[k], out.at[0, me ^ ((k + 1) % n_strip)], sems.at[k]
        )
        copy.start()
        copies.append(copy)
    for copy in copies:
        copy.wait()


def compact_device(
    n_slab,
    n_strip,
    colors,
    transmit,
    pair_counts,
    slot_block,
    assign,
    depth_rank,
    w_in,
    trans_weight,
    w_mid,
    w_out,
):
    slots, feats, span = colors.shape[2:]
    items = n_slab * MOST
    outs = w_out.shape[0]
    smem = pl.BlockSpec(memory_space=SMEM)
    vmem = pl.BlockSpec(memory_space=VMEM)
    hbm = pl.BlockSpec(memory_space=pltpu.HBM)
    held = functools.partial(pltpu.with_memory_space_constraint, memory_space=pltpu.HBM)
    small = pltpu.CompilerParams(vmem_limit_bytes=4 * 1024 * 1024)
    message = MOST * feats + ROWS
    sends = pl.pallas_call(
        pack_kernel,
        out_shape=jax.ShapeDtypeStruct((n_slab, message, span), jnp.bfloat16),
        in_specs=[hbm] * 3,
        out_specs=vmem,
        scratch_shapes=[
            pltpu.SMEM(pair_counts.shape, jnp.int32),
            pltpu.VMEM(colors.shape, colors.dtype),
            pltpu.VMEM(transmit.shape, transmit.dtype),
            pltpu.VMEM(transmit.shape[2:], jnp.float32),
            pltpu.SemaphoreType.DMA((3,)),
        ],
        compiler_params=small,
        name="pack",
    )(held(pair_counts), held(colors), held(transmit))
    group = exchange_order(n_slab)
    got = lax.all_to_all(
        sends, "slab", split_axis=0, concat_axis=0, axis_index_groups=[group], tiled=True
    )
    hidden = w_in.shape[0]
    rough = pl.CostEstimate(flops=10**5, bytes_accessed=10**6, transcendentals=0)
    roomy = pltpu.CompilerParams(vmem_limit_bytes=16 * 1024 * 1024)
    trans_row = trans_weight[None]
    rows, codes, strip = pl.pallas_call(
        functools.partial(plan_kernel, n_slab, slots),
        out_shape=[
            jax.ShapeDtypeStruct((3, items, span), jnp.int32),
            jax.ShapeDtypeStruct((ROWS, span), jnp.bfloat16),
            jax.ShapeDtypeStruct((ROWS, span), jnp.int32),
        ],
        in_specs=[hbm] * 4,
        out_specs=[vmem] * 3,
        scratch_shapes=[
            pltpu.SMEM(a.shape, jnp.int32) for a in (pair_counts, slot_block, assign, depth_rank)
        ]
        + [pltpu.SemaphoreType.DMA((4,))],
        compiler_params=small,
        cost_estimate=rough,
        name="plan",
    )(held(pair_counts), held(slot_block), held(assign), held(depth_rank))
    w_first, w_last, w_later = pl.pallas_call(
        place_kernel,
        out_shape=[
            jax.ShapeDtypeStruct((GROUP, 2 * GROUP * feats, hidden), jnp.bfloat16),
            jax.ShapeDtypeStruct(w_out.shape, jnp.bfloat16),
            jax.ShapeDtypeStruct(w_mid.shape, jnp.bfloat16),
        ],
        in_specs=[vmem] * 3 + [hbm],
        out_specs=[vmem] * 3,
        scratch_shapes=[
            pltpu.VMEM(w_mid.shape, jnp.bfloat16),
            pltpu.SemaphoreType.DMA((1,)),
        ],
        compiler_params=small,
        cost_estimate=rough,
        name="place",
    )(w_in.T, trans_row, w_out, held(w_mid))
    empty = pl.pallas_call(
        empty_kernel,
        out_shape=jax.ShapeDtypeStruct((ROWS, span), jnp.float32),
        in_specs=[vmem] * 3,
        out_specs=vmem,
        compiler_params=roomy,
        cost_estimate=rough,
        name="empty",
    )(trans_row, w_later, w_last)
    shaded = pl.pallas_call(
        shade_kernel,
        out_shape=jax.ShapeDtypeStruct((items * outs + ROWS, span), jnp.bfloat16),
        in_specs=[vmem] * 6,
        out_specs=vmem,
        scratch_shapes=[
            pltpu.VMEM((items, feats, span), jnp.float32),
            pltpu.VMEM((items // GROUP * span, 2 * GROUP * feats), jnp.bfloat16),
            pltpu.VMEM((items * outs, span), jnp.float32),
        ],
        compiler_params=roomy,
        name="shade",
    )(rows, codes, got, w_first, w_later, w_last)
    tiles = [
        lax.ppermute(shaded, "strip", [(s, s ^ k) for s in range(n_strip)])
        for k in range(1, n_strip)
    ] + [shaded]
    return pl.pallas_call(
        join_kernel,
        out_shape=jax.ShapeDtypeStruct((1, n_strip, LB // n_strip, outs, span), jnp.bfloat16),
        in_specs=[vmem] * (n_strip + 2),
        out_specs=pl.BlockSpec(memory_space=pl.ANY),
        scratch_shapes=[
            pltpu.VMEM((n_strip, LB // n_strip, outs, span), jnp.bfloat16),
            pltpu.SemaphoreType.DMA((n_strip,)),
        ],
        compiler_params=small,
        name="join",
    )(*tiles, empty, strip)


def solution(mesh):
    n_slab, n_strip = mesh.shape["slab"], mesh.shape["strip"]
    placed = (
        P("slab", "strip", None, None, None),
        P("slab", "strip", None, None),
        P("strip", None, None),
        P("strip", None, None),
        P("strip", None),
        P(),
        P(),
        P(),
        P(),
        P(),
    )
    compact = n_strip & (n_strip - 1) == 0 and 4 * MOST * n_slab <= LB
    return jax.shard_map(
        functools.partial(compact_device, n_slab, n_strip) if compact else dense_device,
        mesh=mesh,
        in_specs=placed,
        out_specs=P("slab", None, "strip", None, None),
        check_vma=False,
    )
```

```python
import functools

import jax
import jax.numpy as jnp
from jax import lax
from jax.experimental import pallas as pl
from jax.experimental.pallas import tpu as pltpu
from jax.sharding import PartitionSpec as P

MOST = 2
LB = 128


EXACT_PRECISION = lax.Precision.HIGHEST


def shade_blocks(blend_color, trans_field, w_in, trans_weight, w_mid, w_out):
    summed = jnp.einsum("hf,lfp->lhp", w_in, blend_color, preferred_element_type=jnp.float32)
    summed = summed + trans_weight.astype(jnp.float32)[None, :, None] * trans_field[:, None, :]
    hidden = jax.nn.silu(summed).astype(jnp.bfloat16)
    for layer_index in range(w_mid.shape[0]):
        hidden = jax.nn.silu(
            jnp.einsum(
                "hg,lgp->lhp", w_mid[layer_index], hidden, preferred_element_type=jnp.float32
            )
        ).astype(jnp.bfloat16)
    return jnp.einsum("oh,lhp->lop", w_out, hidden, preferred_element_type=jnp.float32).astype(
        jnp.bfloat16
    )


def dense_device(
    colors, transmit, pair_counts, slot_block, assign, depth_rank, w_in, trans_weight, w_mid, w_out
):
    myself = lax.axis_index("slab")
    counts = pair_counts[0]
    blocks_all = slot_block[0]
    assign_row = assign[0]
    offsets = jnp.cumsum(counts, axis=1) - counts
    slot_rank = jnp.arange(MOST, dtype=jnp.int32)
    my_counts = lax.dynamic_index_in_dim(counts, myself, 0, keepdims=False)
    my_offsets = lax.dynamic_index_in_dim(offsets, myself, 0, keepdims=False)
    send_slots = jnp.where(
        slot_rank[None, :] < my_counts[:, None], my_offsets[:, None] + slot_rank[None, :], 0
    )
    send_color = colors[0, 0][send_slots]
    send_trans = transmit[0, 0][send_slots][:, :, None, :]
    incoming = lax.dynamic_index_in_dim(counts, myself, 1, keepdims=False)
    in_offsets = lax.dynamic_index_in_dim(offsets, myself, 1, keepdims=False)
    live_slot = slot_rank[None, :] < incoming[:, None]
    recv_slots = jnp.where(live_slot, in_offsets[:, None] + slot_rank[None, :], 0)
    recv_blocks = jnp.take_along_axis(blocks_all, recv_slots, axis=1)
    local_pos = assign_row[recv_blocks] - myself * LB
    live_flat = live_slot.reshape(-1)
    local_flat = jnp.where(live_flat, local_pos.reshape(-1), -1)
    depth_flat = jnp.repeat(depth_rank, MOST)
    ahead_table = (
        (local_flat[:, None] == local_flat[None, :])
        & (depth_flat[None, :] < depth_flat[:, None])
        & live_flat[None, :]
    )
    ahead_table = ahead_table.astype(jnp.float32)
    owner_table = (jnp.arange(LB, dtype=jnp.int32)[:, None] == local_flat[None, :]).astype(
        jnp.float32
    )
    got_color = lax.all_to_all(send_color, "slab", split_axis=0, concat_axis=0, tiled=True)
    got_trans = lax.all_to_all(send_trans, "slab", split_axis=0, concat_axis=0, tiled=True)
    pixel_count = got_color.shape[3]
    item_count = got_color.shape[0] * got_color.shape[1]
    log_trans = jnp.log(got_trans.reshape(item_count, pixel_count).astype(jnp.float32))
    log_trans = jnp.where(live_flat[:, None], log_trans, 0.0)
    front_log = jnp.dot(ahead_table, log_trans, precision=EXACT_PRECISION)
    front_share = jnp.where(live_flat[:, None], jnp.exp(front_log), 0.0)
    weighted = front_share[:, None, :] * got_color.reshape(item_count, -1, pixel_count).astype(
        jnp.float32
    )
    blend_sum = jnp.dot(owner_table, weighted.reshape(item_count, -1), precision=EXACT_PRECISION)
    blend_color = blend_sum.reshape(LB, -1, pixel_count).astype(jnp.bfloat16)
    trans_field = jnp.exp(jnp.dot(owner_table, log_trans, precision=EXACT_PRECISION))
    shaded = shade_blocks(blend_color, trans_field, w_in, trans_weight, w_mid, w_out)
    display_tiles = lax.all_to_all(shaded[None], "strip", split_axis=1, concat_axis=0, tiled=True)
    return display_tiles[None]


SMEM = pltpu.SMEM
VMEM = pltpu.VMEM
ROWS = 8
GROUP = 4


def exchange_order(n_slab):
    half = n_slab // 2
    back = [half] + list(range(n_slab - 1, half, -1))
    front = list(range(half - 2)) + [half - 1, half - 2] if half > 1 else [0]
    return [s for pair in zip(back, front) for s in pair]


def pack_kernel(far_counts, far_colors, far_transmit, sends, counts, colors, transmit, tall, sems):
    n_slab = sends.shape[0]
    order = exchange_order(n_slab)
    slots, feats, span = colors.shape[2:]
    copies = [
        pltpu.make_async_copy(far, near, sems.at[i])
        for i, (far, near) in enumerate(
            ((far_counts, counts), (far_colors, colors), (far_transmit, transmit))
        )
    ]
    for copy in copies:
        copy.start()
    me = lax.axis_index("slab")
    for copy in copies:
        copy.wait()
    tall[...] = transmit[0, 0].astype(jnp.float32)
    row = lax.broadcasted_iota(jnp.int32, (ROWS, span), 0)
    off = jnp.int32(0)
    for c in range(n_slab):
        at = order.index(c)
        tail = jnp.ones((ROWS, span), jnp.float32)
        for r in range(MOST):
            slot = jnp.minimum(off + r, slots - 1)
            sends[at, pl.ds(r * feats, feats), :] = colors[0, 0, slot]
            tail = jnp.where(row == r, tall[pl.ds(slot, 1), :], tail)
        sends[at, pl.ds(MOST * feats, ROWS), :] = tail.astype(jnp.bfloat16)
        off = off + counts[0, me, c]


def plan_kernel(n_slab, slots, *refs):
    far, (rows, codes, strip) = refs[:4], refs[4:7]
    near, sems = refs[7:11], refs[11]
    counts, blocks, assign, depth = near
    copies = [pltpu.make_async_copy(far[i], near[i], sems.at[i]) for i in range(4)]
    for copy in copies:
        copy.start()
    strip[...] = jnp.full(strip.shape, lax.axis_index("strip"), jnp.int32)
    items = n_slab * MOST
    outs = codes.shape[1] // (2 * items)
    me = lax.axis_index("slab")
    row = lax.broadcasted_iota(jnp.int32, rows.shape[1:], 0)
    item_lane = lax.broadcasted_iota(jnp.int32, codes.shape, 1) // outs
    posv = jnp.zeros(rows.shape[1:], jnp.int32)
    depthv = jnp.zeros(rows.shape[1:], jnp.int32)
    firstv = jnp.zeros(rows.shape[1:], jnp.int32)
    codev = jnp.full(codes.shape, -1, jnp.int32)
    for copy in copies:
        copy.wait()
    pos = []
    for k, s in enumerate(exchange_order(n_slab)):
        off = jnp.int32(0)
        for c in range(n_slab):
            off = off + jnp.where(c < me, counts[0, s, c], 0)
        count = counts[0, s, me]
        for r in range(MOST):
            i = k * MOST + r
            slot = jnp.minimum(off + r, slots - 1)
            here = assign[0, blocks[0, s, slot]] - me * LB
            here = jnp.where(r < count, here, -1)
            first = jnp.int32(i)
            for j in reversed(range(i)):
                first = jnp.where(pos[j] == here, j, first)
            pos.append(here)
            firstv = jnp.where(row == i, first, firstv)
            posv = jnp.where(row == i, here, posv)
            depthv = jnp.where(row == i, depth[s], depthv)
            codev = jnp.where(item_lane == i, jnp.where(first == i, here, -1), codev)
    rows[0] = posv
    rows[1] = depthv
    rows[2] = firstv
    codes[...] = codev.astype(jnp.float32).astype(jnp.bfloat16)


def place_kernel(w_in, trans_weight, far_out, far_mid, w_first, w_out, w_later, w_mid, sems):
    copy = pltpu.make_async_copy(far_mid, w_mid, sems.at[0])
    copy.start()
    feats, hidden = w_in.shape
    half_in = (w_in[...].astype(jnp.float32) * 0.5).astype(jnp.bfloat16)
    half_trans = trans_weight[...].astype(jnp.float32) * 0.5
    sub = lax.broadcasted_iota(jnp.int32, (16, hidden), 0)
    w_first[...] = jnp.zeros_like(w_first)
    for a in range(GROUP):
        w_first[a, pl.ds(a * feats, feats), :] = half_in
        tail = jnp.where(sub // 2 == a, half_trans, 0.0)
        w_first[a, pl.ds(GROUP * feats, 16), :] = tail.astype(jnp.bfloat16)
    w_out[...] = far_out[...]
    copy.wait()
    for m in range(w_mid.shape[0]):
        w_later[m] = (w_mid[m].astype(jnp.float32).T * 0.5).astype(jnp.bfloat16)


def silu_half(u):
    return (u + u * jnp.tanh(u)).astype(jnp.bfloat16)


def later_layers(h, w_mid, w_out):
    for m in range(w_mid.shape[0]):
        h = silu_half(jnp.dot(h, w_mid[m], preferred_element_type=jnp.float32))
    return lax.dot_general(
        w_out[...], h, (((1,), (1,)), ((), ())), preferred_element_type=jnp.float32
    )


def empty_kernel(trans_weight, w_mid, w_out, out):
    u = trans_weight[...].astype(jnp.float32) * 0.5
    h = silu_half(jnp.broadcast_to(u, (out.shape[1], u.shape[1])))
    y = later_layers(h, w_mid, w_out)
    outs = w_out.shape[0]
    for at in range(0, out.shape[0], outs):
        out[pl.ds(at, outs), :] = y


def shade_kernel(rows, codes, got, w_first, w_mid, w_out, out, acc, xt, ys):
    items, feats, span = acc.shape
    outs = w_out.shape[0]

    posv, depthv = rows[0], rows[1]
    front = jnp.ones((items, span), jnp.float32)
    total = jnp.ones((items, span), jnp.float32)
    for k in range(items // MOST):
        tail = got[k, pl.ds(MOST * feats, ROWS), :].astype(jnp.float32)
        for r in range(MOST):
            j = k * MOST + r
            trans_j = tail[r : r + 1, :]
            same = posv == posv[j : j + 1, :]
            total = jnp.where(same, total * trans_j, total)
            front = jnp.where(same & (depthv > depthv[j : j + 1, :]), front * trans_j, front)
    acc[pl.ds(MOST, items - MOST)] = jnp.zeros((items - MOST, feats, span), jnp.float32)
    for k in range(items // MOST):
        places = [k * MOST + r if k == 0 else rows[2, k * MOST + r, 0] for r in range(MOST)]
        sums = []
        for r in range(MOST):
            j = k * MOST + r
            color = got[k, pl.ds(r * feats, feats), :].astype(jnp.float32)
            share = front[j : j + 1, :] * color
            sums.append(share if k == 0 else acc[places[r]] + share)
        for r in range(MOST):
            acc[places[r]] = sums[r]
    total_hi = total.astype(jnp.bfloat16).astype(jnp.float32)
    total_lo = total - total_hi
    groups = items // GROUP
    sub = lax.broadcasted_iota(jnp.int32, (16, span), 0)
    used = GROUP * feats
    xt[:, pl.ds(used, used)] = jnp.zeros((xt.shape[0], used), jnp.bfloat16)
    for q in range(groups):
        block = acc[pl.ds(q * GROUP, GROUP)].reshape(GROUP * feats, span)
        tail = jnp.zeros((16, span), jnp.float32)
        for a in range(GROUP):
            i = q * GROUP + a
            tail = jnp.where(sub == 2 * a, total_hi[i : i + 1, :], tail)
            tail = jnp.where(sub == 2 * a + 1, total_lo[i : i + 1, :], tail)
        lines = pl.ds(q * span, span)
        xt[lines, pl.ds(0, GROUP * feats)] = block.T.astype(jnp.bfloat16)
        xt[lines, pl.ds(GROUP * feats, 16)] = tail.T.astype(jnp.bfloat16)

    x = xt[...]
    stride = GROUP
    for start in range(0, GROUP, stride):
        h = jnp.concatenate(
            [
                silu_half(jnp.dot(x, w_first[a], preferred_element_type=jnp.float32))
                for a in range(start, start + stride)
            ]
        )
        y = later_layers(h, w_mid, w_out)
        for a in range(start, start + stride):
            for q in range(groups):
                at = ((a - start) * groups + q) * span
                ys[pl.ds((q * GROUP + a) * outs, outs), :] = y[:, at : at + span]
    out[pl.ds(0, items * outs), :] = ys[...].astype(jnp.bfloat16)
    out[pl.ds(items * outs, ROWS), :] = codes[...]


def join_kernel(*refs):
    *got, empty, strip, out, held, sems = refs
    _, n_strip, tile, outs, span = out.shape
    lines = tile * outs
    count = got[0].shape[0] - ROWS
    me = strip[0, 0]
    want = lax.broadcasted_iota(jnp.int32, (lines, count), 0) + strip[:1, :count] * lines
    chan = lax.broadcasted_iota(jnp.int32, (lines, count), 1) % outs
    filler = jnp.concatenate([empty[...]] * (lines // ROWS))
    ones = jnp.ones((count, span), jnp.bfloat16)
    copies = []
    for k in range(n_strip):
        pos = got[k][pl.ds(count, ROWS), :].astype(jnp.float32)[:1, :count].astype(jnp.int32)
        hit = pos * outs + chan == want
        pick = jnp.where(hit, 1.0, 0.0).astype(jnp.bfloat16)
        blocks = jnp.concatenate([got[k][pl.ds(0, count), :], ones], axis=1)
        placed = jnp.dot(pick, blocks, preferred_element_type=jnp.float32)
        value = jnp.where(placed[:, span:] > 0.5, placed[:, :span], filler)
        held[k] = value.reshape(tile, outs, span).astype(jnp.bfloat16)
        copy = pltpu.make_async_copy(
            held.at[k], out.at[0, me ^ ((k + 1) % n_strip)], sems.at[k]
        )
        copy.start()
        copies.append(copy)
    for copy in copies:
        copy.wait()


def compact_device(
    n_slab,
    n_strip,
    colors,
    transmit,
    pair_counts,
    slot_block,
    assign,
    depth_rank,
    w_in,
    trans_weight,
    w_mid,
    w_out,
):
    slots, feats, span = colors.shape[2:]
    items = n_slab * MOST
    outs = w_out.shape[0]
    smem = pl.BlockSpec(memory_space=SMEM)
    vmem = pl.BlockSpec(memory_space=VMEM)
    hbm = pl.BlockSpec(memory_space=pltpu.HBM)
    held = functools.partial(pltpu.with_memory_space_constraint, memory_space=pltpu.HBM)
    small = pltpu.CompilerParams(vmem_limit_bytes=4 * 1024 * 1024)
    message = MOST * feats + ROWS
    sends = pl.pallas_call(
        pack_kernel,
        out_shape=jax.ShapeDtypeStruct((n_slab, message, span), jnp.bfloat16),
        in_specs=[hbm] * 3,
        out_specs=vmem,
        scratch_shapes=[
            pltpu.SMEM(pair_counts.shape, jnp.int32),
            pltpu.VMEM(colors.shape, colors.dtype),
            pltpu.VMEM(transmit.shape, transmit.dtype),
            pltpu.VMEM(transmit.shape[2:], jnp.float32),
            pltpu.SemaphoreType.DMA((3,)),
        ],
        compiler_params=small,
        name="pack",
    )(held(pair_counts), held(colors), held(transmit))
    group = exchange_order(n_slab)
    got = lax.all_to_all(
        sends, "slab", split_axis=0, concat_axis=0, axis_index_groups=[group], tiled=True
    )
    hidden = w_in.shape[0]
    rough = pl.CostEstimate(flops=10**5, bytes_accessed=10**6, transcendentals=0)
    roomy = pltpu.CompilerParams(vmem_limit_bytes=16 * 1024 * 1024)
    trans_row = trans_weight[None]
    rows, codes, strip = pl.pallas_call(
        functools.partial(plan_kernel, n_slab, slots),
        out_shape=[
            jax.ShapeDtypeStruct((3, items, span), jnp.int32),
            jax.ShapeDtypeStruct((ROWS, span), jnp.bfloat16),
            jax.ShapeDtypeStruct((ROWS, span), jnp.int32),
        ],
        in_specs=[hbm] * 4,
        out_specs=[vmem] * 3,
        scratch_shapes=[
            pltpu.SMEM(a.shape, jnp.int32) for a in (pair_counts, slot_block, assign, depth_rank)
        ]
        + [pltpu.SemaphoreType.DMA((4,))],
        compiler_params=small,
        cost_estimate=rough,
        name="plan",
    )(held(pair_counts), held(slot_block), held(assign), held(depth_rank))
    w_first, w_last, w_later = pl.pallas_call(
        place_kernel,
        out_shape=[
            jax.ShapeDtypeStruct((GROUP, 2 * GROUP * feats, hidden), jnp.bfloat16),
            jax.ShapeDtypeStruct(w_out.shape, jnp.bfloat16),
            jax.ShapeDtypeStruct(w_mid.shape, jnp.bfloat16),
        ],
        in_specs=[vmem] * 3 + [hbm],
        out_specs=[vmem] * 3,
        scratch_shapes=[
            pltpu.VMEM(w_mid.shape, jnp.bfloat16),
            pltpu.SemaphoreType.DMA((1,)),
        ],
        compiler_params=small,
        cost_estimate=rough,
        name="place",
    )(w_in.T, trans_row, w_out, held(w_mid))
    empty = pl.pallas_call(
        empty_kernel,
        out_shape=jax.ShapeDtypeStruct((ROWS, span), jnp.float32),
        in_specs=[vmem] * 3,
        out_specs=vmem,
        compiler_params=roomy,
        cost_estimate=rough,
        name="empty",
    )(trans_row, w_later, w_last)
    shaded = pl.pallas_call(
        shade_kernel,
        out_shape=jax.ShapeDtypeStruct((items * outs + ROWS, span), jnp.bfloat16),
        in_specs=[vmem] * 6,
        out_specs=vmem,
        scratch_shapes=[
            pltpu.VMEM((items, feats, span), jnp.float32),
            pltpu.VMEM((items // GROUP * span, 2 * GROUP * feats), jnp.bfloat16),
            pltpu.VMEM((items * outs, span), jnp.float32),
        ],
        compiler_params=roomy,
        name="shade",
    )(rows, codes, got, w_first, w_later, w_last)
    tiles = [
        lax.ppermute(shaded, "strip", [(s, s ^ k) for s in range(n_strip)])
        for k in range(1, n_strip)
    ] + [shaded]
    return pl.pallas_call(
        join_kernel,
        out_shape=jax.ShapeDtypeStruct((1, n_strip, LB // n_strip, outs, span), jnp.bfloat16),
        in_specs=[vmem] * (n_strip + 2),
        out_specs=pl.BlockSpec(memory_space=pl.ANY),
        scratch_shapes=[
            pltpu.VMEM((n_strip, LB // n_strip, outs, span), jnp.bfloat16),
            pltpu.SemaphoreType.DMA((n_strip,)),
        ],
        compiler_params=small,
        name="join",
    )(*tiles, empty, strip)


def solution(mesh):
    n_slab, n_strip = mesh.shape["slab"], mesh.shape["strip"]
    placed = (
        P("slab", "strip", None, None, None),
        P("slab", "strip", None, None),
        P("strip", None, None),
        P("strip", None, None),
        P("strip", None),
        P(),
        P(),
        P(),
        P(),
        P(),
    )
    compact = n_strip & (n_strip - 1) == 0 and 4 * MOST * n_slab <= LB
    return jax.shard_map(
        functools.partial(compact_device, n_slab, n_strip) if compact else dense_device,
        mesh=mesh,
        in_specs=placed,
        out_specs=P("slab", None, "strip", None, None),
        check_vma=False,
    )
```
